32 devices in a mesh: groups: 2 (over x), row: 8 (over z, y), col: 2 (over core).
Axes of the slice: x: 2, y: 2, z: 4, core: 2. Of those that a mesh axis runs over, the one named last changes fastest.
Arguments:
- object_field: float32 [2, 2048, 1536], P(None, ('groups', 'row'), 'col'), parts along dimension 1, may hold values from -5 to 5
- probe: float32 [16, 2, 256, 256], P('groups'), parts along dimension 0, may hold values from -6 to 6
- measured: float32 [32, 256, 256], P(('groups', 'row', 'col')), parts along dimension 0, may hold values from 2 to 40
- offsets: int32 [32, 2], P(('groups', 'row', 'col')), parts along dimension 0, may hold values from 0 to 767, as said below
Outputs:
- new_object: float32 [2, 2048, 1536], P(None, ('groups', 'row'), 'col'), parts along dimension 1
- new_probe: float32 [16, 2, 256, 256], P('groups'), parts along dimension 0
The draws below stay inside these ranges and needn't reach their ends.
There are 2 independent parts, one for each index of `groups`. The reference program is written for one: setup_inputs(seed, part) draws one part's arguments, and reference() takes and returns one part's arrays. A program takes and returns all parts, laid end to end along the dimension named above; each array names one. Nothing has to cross between parts.
Inputs may be any that keep to these rules, and one draw needn't show every extreme that they name: offsets[p, 0] is below 128, and offsets[p, 1] lies in the (p mod 1)-th of 1 equal spans of the tile's 768 columns; both are counted from the first row and column of the tile of device p.
All inputs are finite; a program needn't handle non-finite values.
Results may differ from the reference program's by a relative error of at most 0.00087.
The reference program's roundings to bfloat16 on the way count: a program that leaves them out, or rounds other values in their place, can miss the bound.
Values sent between devices are 32-bit elements; how exact they have to be, the bound alone decides.
No kernel may reach another device: no remote copies, remote signals or barrier semaphores. Data moves between devices by JAX's collectives and lax.ppermute only.
A program may use at most 128 MiB of HBM per device.

```python
import math
import jax
import jax.numpy as jnp
from jax import lax

PS = 256
MODES = 8
TR = 128
TC = 768
POS_DEV = 1
NR = 1024
NC = 1536
NPOS = 16
N_COL = 2


def draw_offsets(key, part):
    key = jax.random.fold_in(key, 11)
    row_key, col_key = jax.random.split(key)
    span = TC // POS_DEV
    rows = jax.random.randint(row_key, (NPOS,), 0, TR, dtype=jnp.int32)
    slots = jnp.arange(NPOS, dtype=jnp.int32) % POS_DEV
    cols = slots * span + jax.random.randint(col_key, (NPOS,), 0, span, dtype=jnp.int32)
    cols = cols.at[0].set(0)
    cols = cols.at[NPOS - 1].set(TC - 1)
    return jnp.stack([rows, cols], axis=1).astype(jnp.int32)


def levels(key, shape, cuts, low, high):
    loudness = 1.0
    for dim, parts in cuts:
        draws = jax.random.uniform(jax.random.fold_in(jax.random.fold_in(key, 6), dim), (parts,), jnp.float32, low / len(cuts), high / len(cuts))
        loudness = loudness * jnp.repeat(jnp.exp(draws), shape[dim] // parts).reshape((-1,) + (1,) * (len(shape) - 1 - dim))
    return loudness


def centred(key, dims, width, most, cuts=(), kind=jnp.bfloat16):
    result = width * jax.random.normal(key, dims, jnp.float32)
    if cuts:
        result = result * levels(key, dims, cuts, -0.22, 0.18)
    return jnp.clip(result, -most, most).astype(kind)


def setup_inputs(seed: int = 0, part: int = 0) -> dict:
    key_of = jax.random.split(jax.random.key(seed), 5)
    own_keys = jax.random.split(jax.random.fold_in(key_of[4], part), 5)
    return {
        "object_field": centred(own_keys[0], (2, NR, NC), 0.7, 5.0, ((1, 8), (2, 2)), jnp.float32),
        "probe": centred(own_keys[1], (MODES, 2, PS, PS), 1.0, 6.0, (), jnp.float32),
        "measured": jnp.clip(jnp.exp(math.log(40.0) - 2.9957323 * jax.random.uniform(own_keys[2], (NPOS, PS, PS), jnp.float32) ** levels(own_keys[2], (NPOS, PS, PS), ((0, 16),), -0.2, 0.2)), 2.0, 40.0),
        "offsets": draw_offsets(jax.random.fold_in(jax.random.fold_in(key_of[4], part), 71), part),
    }


REGULAR = 0.25
AMP_FLOOR = 2.0

def transform_tables(length):
    indices = jnp.arange(length, dtype=jnp.int32)
    phases = indices[:, None] * indices[None, :] % length
    angles = phases.astype(jnp.float32) * (2.0 * math.pi / length)
    factor = 1.0 / math.sqrt(length)
    return ((jnp.cos(angles) * factor).astype(jnp.bfloat16), (-jnp.sin(angles) * factor).astype(jnp.bfloat16))

def left_apply(table_re, table_im, field_re, field_im):
    tab_re = table_re.astype(jnp.float32)
    tab_im = table_im.astype(jnp.float32)
    fld_re = field_re.astype(jnp.float32)
    fld_im = field_im.astype(jnp.float32)
    out_re = jnp.einsum('kn,mnj->mkj', tab_re, fld_re) - jnp.einsum('kn,mnj->mkj', tab_im, fld_im)
    out_im = jnp.einsum('kn,mnj->mkj', tab_re, fld_im) + jnp.einsum('kn,mnj->mkj', tab_im, fld_re)
    return (out_re, out_im)

def right_apply(table_re, table_im, field_re, field_im):
    tab_re = table_re.astype(jnp.float32)
    tab_im = table_im.astype(jnp.float32)
    fld_re = field_re.astype(jnp.float32)
    fld_im = field_im.astype(jnp.float32)
    out_re = jnp.einsum('mnj,jk->mnk', fld_re, tab_re) - jnp.einsum('mnj,jk->mnk', fld_im, tab_im)
    out_im = jnp.einsum('mnj,jk->mnk', fld_im, tab_re) + jnp.einsum('mnj,jk->mnk', fld_re, tab_im)
    return (out_re, out_im)

def position_terms(window, probe_re, probe_im, pattern, cos_table, sin_table):
    win_re = window[0]
    win_im = window[1]
    psi_re = probe_re * win_re[None] - probe_im * win_im[None]
    psi_im = probe_re * win_im[None] + probe_im * win_re[None]
    half_re, half_im = left_apply(cos_table, sin_table, psi_re.astype(jnp.bfloat16), psi_im.astype(jnp.bfloat16))
    far_re, far_im = right_apply(cos_table, sin_table, half_re.astype(jnp.bfloat16), half_im.astype(jnp.bfloat16))
    intensity = lax.optimization_barrier(jnp.sum(far_re * far_re + far_im * far_im, axis=0))
    amp_ratio = jnp.sqrt(pattern) / jnp.maximum(jnp.sqrt(intensity), AMP_FLOOR)
    fixed_re = (far_re * amp_ratio[None]).astype(jnp.bfloat16)
    fixed_im = (far_im * amp_ratio[None]).astype(jnp.bfloat16)
    back_re, back_im = left_apply(cos_table, -sin_table, fixed_re, fixed_im)
    near_re, near_im = right_apply(cos_table, -sin_table, back_re.astype(jnp.bfloat16), back_im.astype(jnp.bfloat16))
    diff_re = near_re - psi_re
    diff_im = near_im - psi_im
    object_terms = jnp.stack([lax.optimization_barrier(jnp.sum(probe_re * diff_re + probe_im * diff_im, axis=0)), lax.optimization_barrier(jnp.sum(probe_re * diff_im - probe_im * diff_re, axis=0)), lax.optimization_barrier(jnp.sum(probe_re * probe_re + probe_im * probe_im, axis=0))])
    probe_terms = jnp.stack([win_re[None] * diff_re + win_im[None] * diff_im, win_re[None] * diff_im - win_im[None] * diff_re], axis=1)
    probe_weight = win_re * win_re + win_im * win_im
    return (object_terms, probe_terms, probe_weight)

def reference(object_field, probe, measured, offsets):
    cos_table, sin_table = transform_tables(PS)
    half_size = PS // 2
    padded = jnp.pad(object_field, ((0, 0), (half_size, half_size), (half_size, half_size)))
    probe_re = probe[:, 0]
    probe_im = probe[:, 1]
    grid_start = jnp.zeros((3, NR + PS, NC + PS), jnp.float32)
    num_start = jnp.zeros(probe.shape, jnp.float32)
    den_start = jnp.zeros((PS, PS), jnp.float32)

    def visit(carry, item):
        grid, probe_num, probe_den = carry
        pattern, position, number = item
        device = (number // POS_DEV).astype(jnp.int32)
        row_start = (device // N_COL * TR + position[0]).astype(jnp.int32)
        col_start = (device % N_COL * TC + position[1]).astype(jnp.int32)
        zero_index = jnp.zeros((), jnp.int32)
        window = lax.dynamic_slice(padded, (zero_index, row_start, col_start), (2, PS, PS))
        object_terms, probe_terms, probe_weight = position_terms(window, probe_re, probe_im, pattern, cos_table, sin_table)
        current = lax.dynamic_slice(grid, (zero_index, row_start, col_start), (3, PS, PS))
        grid = lax.dynamic_update_slice(grid, current + object_terms, (zero_index, row_start, col_start))
        return ((grid, probe_num + probe_terms, probe_den + probe_weight), None)
    numbers = jnp.arange(NPOS, dtype=jnp.int32)
    (grid, probe_num, probe_den), _ = lax.scan(visit, (grid_start, num_start, den_start), (measured, offsets, numbers))
    interior = grid[:, half_size:half_size + NR, half_size:half_size + NC]
    object_den = interior[2]
    object_peak = jnp.max(object_den)
    new_object = object_field + interior[0:2] / ((1.0 - REGULAR) * object_den + REGULAR * object_peak)[None]
    probe_peak = jnp.max(probe_den)
    new_probe = probe + probe_num / ((1.0 - REGULAR) * probe_den + REGULAR * probe_peak)[None, None]
    return (new_object, new_probe)
```

```python
import math

import jax
import jax.numpy as jnp
import ml_dtypes
import numpy as np
from jax import lax
from jax.experimental import pallas as pl
from jax.experimental.pallas import tpu as pltpu
from jax.sharding import PartitionSpec as P

REGULAR = 0.25
AMP_FLOOR = 2.0
RING = 8
VMEM_LIMIT = 56 * 1024 * 1024

SMEM = pl.BlockSpec(memory_space=pltpu.SMEM)
VMEM = pl.BlockSpec(memory_space=pltpu.VMEM)
ANY = pl.BlockSpec(memory_space=pl.ANY)


def transform_blocks(length):
    indices = np.arange(length, dtype=np.int32)
    phases = indices[:, None] * indices[None, :] % length
    angles = phases.astype(np.float32) * np.float32(2.0 * math.pi / length)
    factor = np.float32(1.0 / math.sqrt(length))
    cos = (np.cos(angles) * factor).astype(ml_dtypes.bfloat16)
    sin = (-np.sin(angles) * factor).astype(ml_dtypes.bfloat16)
    one = np.block([[cos, -sin], [sin, cos]])
    return one, np.ascontiguousarray(one.T)


def params():
    return pltpu.CompilerParams(vmem_limit_bytes=VMEM_LIMIT)


def slices_kernel(scal, block, edge, swap_out, far_out, own_out, ext):
    rows, cols = block.shape[1], block.shape[2]
    width = edge.shape[2]
    first = scal[0] == 0
    zero = jnp.zeros(edge.shape, jnp.float32)
    got = edge[...]
    ext[:, :, 0:width] = jnp.where(first, zero, got)
    ext[:, :, width : width + cols] = block[...]
    ext[:, :, width + cols :] = jnp.where(first, got, zero)
    for number, out in enumerate((swap_out, far_out, own_out)):
        start = scal[1 + number]
        base = pl.multiple_of(start // 128 * 128, 128)
        for part in range(2):
            wide = ext[part, :, pl.ds(base, 384)]
            wide = pltpu.roll(wide, (384 - start % 128) % 384, 1)
            out[part] = wide[:, 0:256]


def cut_slices(scal, block, edge):
    rows, cols = block.shape[1], block.shape[2]
    piece = jax.ShapeDtypeStruct((2, rows, 256), jnp.float32)
    return pl.pallas_call(
        slices_kernel,
        out_shape=(piece, piece, piece),
        in_specs=[SMEM, VMEM, VMEM],
        out_specs=(VMEM, VMEM, VMEM),
        scratch_shapes=[pltpu.VMEM((2, rows, cols + 256), jnp.float32)],
        compiler_params=params(),
        name="cut_slices",
    )(scal, block, edge)


def weights_kernel(scal, probe, inner, edge, frame, grid):
    modes = probe.shape[0]
    weight = jnp.zeros((256, 256), jnp.float32)
    for m in range(modes):
        weight = weight + probe[m, 0] * probe[m, 0] + probe[m, 1] * probe[m, 1]
    tall = jnp.concatenate([weight, jnp.zeros((128, 256), jnp.float32)], axis=0)
    grid[...] = jnp.zeros(grid.shape, jnp.float32)
    for number in range(3):
        row, col, there = scal[3 * number], scal[3 * number + 1], scal[3 * number + 2]
        frame[...] = pltpu.roll(tall, row, 0)
        lower = 128 * (2 - number)
        piece = frame[lower : lower + 128, :] * there.astype(jnp.float32)
        wide = jnp.concatenate([piece, jnp.zeros((128, 128), jnp.float32)], axis=1)
        wide = pltpu.roll(wide, col % 128, 1)
        base = pl.multiple_of(col // 128 * 128, 128)
        grid[:, pl.ds(base, 384)] += wide
    inner[...] = grid[:, 128 : grid.shape[1] - 128]
    edge[...] = jnp.where(scal[9] == 0, grid[:, grid.shape[1] - 128 :], grid[:, 0:128])


def weights(scal, probe, rows, cols):
    return pl.pallas_call(
        weights_kernel,
        out_shape=(
            jax.ShapeDtypeStruct((rows, cols), jnp.float32),
            jax.ShapeDtypeStruct((rows, 128), jnp.float32),
        ),
        in_specs=[SMEM, VMEM],
        out_specs=(VMEM, VMEM),
        scratch_shapes=[
            pltpu.VMEM((384, 256), jnp.float32),
            pltpu.VMEM((rows, cols + 256), jnp.float32),
        ],
        compiler_params=params(),
        name="object_weights",
    )(scal, probe)


def position_kernel(
    scal, far_rows, mid_rows, own_rows, probe, pattern, one, two,
    mine_a, mine_b, his1_a, his2_a, his1_b, his2_b, fold_far, fold_mid, fold_own,
    stack, window, far, terms_a, terms_b, update, strength, sems,
):
    modes = probe.shape[0]
    odd, row, core = scal[0], scal[1], scal[2]
    place = (scal[3], scal[4])
    far_at = pl.multiple_of(256 * (1 - odd), 128)
    own_at = pl.multiple_of(256 * odd, 128)
    stack[:, pl.ds(far_at, 128), :] = far_rows[...]
    stack[:, 128:256, :] = mid_rows[...]
    stack[:, pl.ds(own_at, 128), :] = own_rows[...]
    for part in range(2):
        window[part] = pltpu.roll(stack[part], (384 - row) % 384, 0)[0:256]
    strength[...] = jnp.zeros(strength.shape, jnp.float32)
    update[...] = jnp.zeros(update.shape, jnp.float32)

    def exit_wave(m):
        p_re, p_im = probe[m, 0], probe[m, 1]
        w_re, w_im = window[0], window[1]
        return p_re * w_re - p_im * w_im, p_re * w_im + p_im * w_re

    def forward(m, carry):
        e_re, e_im = exit_wave(m)
        field = jnp.concatenate([e_re.astype(jnp.bfloat16), e_im.astype(jnp.bfloat16)], axis=0)
        half = jnp.dot(one[...], field, preferred_element_type=jnp.float32).astype(jnp.bfloat16)
        half = jnp.concatenate([half[0:256], half[256:512]], axis=1)
        out = jnp.dot(half, two[...], preferred_element_type=jnp.float32)
        far[m] = out
        strength[...] += out[:, 0:256] * out[:, 0:256] + out[:, 256:512] * out[:, 256:512]
        return carry

    lax.fori_loop(0, modes, forward, 0, unroll=2)
    strength[...] = jnp.sqrt(pattern[...]) / jnp.maximum(jnp.sqrt(strength[...]), AMP_FLOOR)

    def put(terms, image, value):
        for slab in range(16):
            half = slab // 8
            j = (place[half] + 7 - slab % 8) & 7
            terms[half ^ core, j, image] = value[16 * slab : 16 * slab + 16]

    def backward(terms, first):
        def body(m, carry):
            ratio = strength[...]
            fixed = jnp.concatenate(
                [
                    (far[m, :, 0:256] * ratio).astype(jnp.bfloat16),
                    (far[m, :, 256:512] * ratio).astype(jnp.bfloat16),
                ],
                axis=0,
            )
            back = jnp.dot(two[...], fixed, preferred_element_type=jnp.float32)
            back = back.astype(jnp.bfloat16)
            back = jnp.concatenate([back[0:256], back[256:512]], axis=1)
            near = jnp.dot(back, one[...], preferred_element_type=jnp.float32)
            e_re, e_im = exit_wave(m)
            d_re = near[:, 0:256] - e_re
            d_im = near[:, 256:512] - e_im
            p_re, p_im = probe[m, 0], probe[m, 1]
            w_re, w_im = window[0], window[1]
            update[0] += p_re * d_re + p_im * d_im
            update[1] += p_re * d_im - p_im * d_re
            put(terms, 2 * (m - first), w_re * d_re + w_im * d_im)
            put(terms, 2 * (m - first) + 1, w_re * d_im - w_im * d_re)
            return carry

        return body

    def send(terms, mine, his1, his2, at):
        copies = (
            pltpu.make_async_copy(terms.at[1, 0:2], his1, sems.at[at]),
            pltpu.make_async_copy(terms.at[1, 2:8], his2, sems.at[at + 1]),
            pltpu.make_async_copy(terms.at[0], mine, sems.at[at + 2]),
        )
        for copy in copies:
            copy.start()
        return copies

    cut = modes // 2
    lax.fori_loop(0, cut, backward(terms_a, 0), 0, unroll=2)
    put(terms_a, 2 * cut, window[0] * window[0] + window[1] * window[1])
    copies = send(terms_a, mine_a, his1_a, his2_a, 0)
    lax.fori_loop(cut, modes, backward(terms_b, cut), 0, unroll=2)
    copies += send(terms_b, mine_b, his1_b, his2_b, 3)
    for part in range(2):
        tall = jnp.concatenate([update[part], jnp.zeros((128, 256), jnp.float32)], axis=0)
        stack[part] = pltpu.roll(tall, row, 0)
    fold_far[...] = stack[:, pl.ds(far_at, 128), :]
    fold_mid[...] = stack[:, 128:256, :]
    fold_own[...] = stack[:, pl.ds(own_at, 128), :]
    for copy in copies:
        copy.wait()


def position(scal, far_rows, mid_rows, own_rows, probe, pattern, one, two):
    modes = probe.shape[0]
    n_a, n_b = modes + 1, modes

    def f32(*shape):
        return jax.ShapeDtypeStruct(shape, jnp.float32)

    piece = f32(2, 128, 256)
    return pl.pallas_call(
        position_kernel,
        out_shape=(
            f32(8, n_a, 16, 256), f32(8, n_b, 16, 256),
            f32(2, n_a, 16, 256), f32(6, n_a, 16, 256),
            f32(2, n_b, 16, 256), f32(6, n_b, 16, 256),
            piece, piece, piece,
        ),
        in_specs=[SMEM] + [VMEM] * 7,
        out_specs=(ANY,) * 6 + (VMEM,) * 3,
        scratch_shapes=[
            pltpu.VMEM((2, 384, 256), jnp.float32),
            pltpu.VMEM((2, 256, 256), jnp.float32),
            pltpu.VMEM((modes, 256, 512), jnp.float32),
            pltpu.VMEM((2, 8, n_a, 16, 256), jnp.float32),
            pltpu.VMEM((2, 8, n_b, 16, 256), jnp.float32),
            pltpu.VMEM((2, 256, 256), jnp.float32),
            pltpu.VMEM((256, 256), jnp.float32),
            pltpu.SemaphoreType.DMA((6,)),
        ],
        compiler_params=params(),
        name="position_terms",
    )(scal, far_rows, mid_rows, own_rows, probe, pattern, one, two)


def fold_kernel(scal, above, own, below, inner, edge, grid):
    grid[...] = jnp.zeros(grid.shape, jnp.float32)
    for number, piece in enumerate((above, own, below)):
        col = scal[number]
        base = pl.multiple_of(col // 128 * 128, 128)
        for part in range(2):
            wide = jnp.concatenate([piece[part], jnp.zeros((128, 128), jnp.float32)], axis=1)
            grid[part, :, pl.ds(base, 384)] += pltpu.roll(wide, col % 128, 1)
    size = grid.shape[2]
    inner[...] = grid[:, :, 128 : size - 128]
    edge[...] = jnp.where(scal[3] == 0, grid[:, :, size - 128 :], grid[:, :, 0:128])


def fold(scal, above, own, below, rows, cols):
    return pl.pallas_call(
        fold_kernel,
        out_shape=(
            jax.ShapeDtypeStruct((2, rows, cols), jnp.float32),
            jax.ShapeDtypeStruct((2, rows, 128), jnp.float32),
        ),
        in_specs=[SMEM, VMEM, VMEM, VMEM],
        out_specs=(VMEM, VMEM),
        scratch_shapes=[pltpu.VMEM((2, rows, cols + 256), jnp.float32)],
        compiler_params=params(),
        name="fold_object",
    )(scal, above, own, below)


def finish_kernel(scal, probe, *refs):
    chunks, out = refs[:-1], refs[-1]
    modes = probe.shape[0]
    core = scal[0]
    place = (scal[1], scal[2])
    peak = jnp.zeros((16, 256), jnp.float32)
    for t in range(8):
        peak = jnp.maximum(peak, jnp.maximum(chunks[t][2 * (modes // 2)], chunks[16 + t][2 * (modes // 2)]))
    peak = jnp.max(peak)
    for owner in range(2):
        half = core if owner == 0 else 1 - core
        at = place[owner]
        for t in range(8):
            k = (at + 8 - t) & 7
            start = pl.multiple_of(128 * half + 16 * k, 16)
            part_a, part_b = chunks[16 * owner + t], chunks[16 * owner + 8 + t]
            den = part_a[2 * (modes // 2)]
            scale = 1.0 / ((1.0 - REGULAR) * den + REGULAR * peak)
            for m in range(modes):
                part = part_a if m < modes // 2 else part_b
                image = 2 * (m % (modes // 2))
                for half_part in range(2):
                    out[m, half_part, pl.ds(start, 16), :] = (
                        probe[m, half_part, pl.ds(start, 16), :] + part[image + half_part] * scale
                    )


def finish(scal, probe, chunks):
    return pl.pallas_call(
        finish_kernel,
        out_shape=jax.ShapeDtypeStruct(probe.shape, jnp.float32),
        in_specs=[SMEM] + [VMEM] * (1 + len(chunks)),
        out_specs=VMEM,
        compiler_params=params(),
        name="finish_probe",
    )(scal, probe, *chunks)


def shards(object_field, probe, measured, offsets):
    rows, cols = object_field.shape[1], object_field.shape[2]
    count = lax.axis_size("row")
    r = lax.axis_index("row")
    c = lax.axis_index("col")
    odd = r % 2
    one, two = transform_blocks(probe.shape[-1])
    one, two = jnp.asarray(one), jnp.asarray(two)

    twins = [(i, i ^ 1) for i in range(count)]
    cores = [(0, 1), (1, 0)]
    down = [(i, i + 1) for i in range(count - 1)]
    up = [(i + 1, i) for i in range(count - 1)]
    outward = [(i, i + 2) for i in range(1, count - 2, 2)] + [(i, i - 2) for i in range(2, count, 2)]
    inward = [(b, a) for a, b in outward]

    pattern = lax.ppermute(measured, "row", twins)[0]
    edge = lax.ppermute(
        jnp.where(c == 0, object_field[:, :, cols - 128 :], object_field[:, :, 0:128]), "col", cores
    )
    here = offsets[0]
    above = lax.ppermute(offsets, "row", down)[0]
    below = lax.ppermute(offsets, "row", up)[0]
    twin = jnp.where(odd == 1, above, below)
    beyond = jnp.where(odd == 1, below, above)

    cut_scal = jnp.stack([c, here[1], beyond[1], twin[1]]).astype(jnp.int32)
    to_twin, to_beyond, own_rows = cut_slices(cut_scal, object_field, edge)
    mid_rows = lax.ppermute(to_twin, "row", twins)
    far_rows = lax.ppermute(to_beyond, "row", outward)

    has_above = (r > 0).astype(jnp.int32)
    has_below = (r < count - 1).astype(jnp.int32)
    weight_scal = jnp.stack(
        [above[0], above[1], has_above, here[0], here[1], jnp.ones_like(r), below[0], below[1], has_below, c]
    ).astype(jnp.int32)
    object_den, den_edge = weights(weight_scal, probe, rows, cols)
    den_got = lax.ppermute(den_edge, "col", cores)

    def join(inner, got):
        low = jnp.where(c == 0, 0.0, got)
        high = jnp.where(c == 0, got, 0.0)
        pads = [(0, 0)] * (inner.ndim - 1)
        return inner + jnp.pad(low, pads + [(0, cols - 128)]) + jnp.pad(high, pads + [(cols - 128, 0)])

    object_den = join(object_den, den_got)
    object_peak = jnp.max(object_den).reshape(1, 1)
    object_peak = jnp.maximum(object_peak, lax.ppermute(object_peak, "col", cores))
    step = 1
    while step < count:
        pairs = [(i, i ^ step) for i in range(count)]
        object_peak = jnp.maximum(object_peak, lax.ppermute(object_peak, "row", pairs))
        step *= 2

    order = [0] + list(range(1, RING, 2)) + list(range(RING - 2, 0, -2))
    spot = [order.index(i) for i in range(RING)]
    around = []
    for block in range(0, count, RING):
        for i in range(RING):
            a, b = block + order[i], block + order[(i + 1) % RING]
            around += [(2 * a, 2 * b), (2 * b + 1, 2 * a + 1)]
    here_spot = jnp.asarray(spot, jnp.int32)[r % RING]
    spots = (here_spot, (RING - here_spot) % RING)

    scal = jnp.stack([odd, twin[0], c, spots[0], spots[1]]).astype(jnp.int32)
    mine_a, mine_b, his1_a, his2_a, his1_b, his2_b, fold_far, fold_mid, fold_own = position(
        scal, far_rows, mid_rows, own_rows, probe, pattern, one, two
    )

    def across(x):
        return lax.ppermute(x, "col", cores)

    def onward(x):
        return lax.ppermute(x, ("row", "col"), around)

    got1 = [across(his1_a), across(his1_b)]
    got2 = [across(his2_a), across(his2_b)]
    mine = [mine_a, mine_b]

    def share(which, j):
        got = got1[which][j] if j < 2 else got2[which][j - 2]
        return mine[which][j] + got

    current = [share(0, 0), share(1, 0)]
    for s in range(RING - 1):
        for which in range(2):
            current[which] = onward(current[which]) + share(which, s + 1)
    if count > RING:
        blocks = [[b * RING + i for b in range(count // RING)] for i in range(RING)]
        current = [lax.psum(x, "row", axis_index_groups=blocks) for x in current]

    mid_got = lax.ppermute(fold_mid, "row", twins)
    far_got = lax.ppermute(fold_far, "row", inward)

    gathered = [[current[0]], [current[1]]]
    for s in range(RING - 1):
        for which in range(2):
            gathered[which].append(onward(gathered[which][-1]))
    other = [[across(x) for x in chunks] for chunks in gathered]
    mine_spot = jnp.where(c == 0, spots[0], spots[1])
    his_spot = jnp.where(c == 0, spots[1], spots[0])
    finish_scal = jnp.stack([c, mine_spot, his_spot]).astype(jnp.int32)
    new_probe = finish(finish_scal, probe, gathered[0] + gathered[1] + other[0] + other[1])

    from_above = jnp.where(odd == 1, fold_own, far_got)
    from_below = jnp.where(odd == 1, far_got, fold_own)
    fold_scal = jnp.stack([above[1], here[1], below[1], c]).astype(jnp.int32)
    object_num, num_edge = fold(fold_scal, from_above, mid_got, from_below, rows, cols)
    object_num = join(object_num, lax.ppermute(num_edge, "col", cores))
    new_object = (
        object_field + object_num / ((1.0 - REGULAR) * object_den + REGULAR * object_peak[0, 0])[None]
    )
    return (new_object, new_probe)


def solution(mesh):
    placed = (
        P(None, ("groups", "row"), "col"),
        P("groups", None, None, None),
        P(("groups", "row", "col"), None, None),
        P(("groups", "row", "col"), None),
    )
    return jax.shard_map(
        shards,
        mesh=mesh,
        in_specs=placed,
        out_specs=(P(None, ("groups", "row"), "col"), P("groups", None, None, None)),
        check_vma=False,
    )
```

```python
import functools
import math

import jax
import jax.numpy as jnp
import ml_dtypes
import numpy as np
from jax import lax
from jax.experimental import pallas as pl
from jax.experimental.pallas import tpu as pltpu
from jax.sharding import PartitionSpec as P

REGULAR = 0.25
AMP_FLOOR = 2.0
RING = 8
RING_ORDER = (0, 1, 3, 5, 7, 6, 4, 2)
HOPS = (0, -1, 1, -2, 2, -3, 3, 4)
VMEM_LIMIT = 56 * 1024 * 1024

SMEM = pl.BlockSpec(memory_space=pltpu.SMEM)
VMEM = pl.BlockSpec(memory_space=pltpu.VMEM)
ANY = pl.BlockSpec(memory_space=pl.ANY)


def transform_blocks(length):
    indices = np.arange(length, dtype=np.int32)
    phases = indices[:, None] * indices[None, :] % length
    angles = phases.astype(np.float32) * np.float32(2.0 * math.pi / length)
    factor = np.float32(1.0 / math.sqrt(length))
    cos = (np.cos(angles) * factor).astype(ml_dtypes.bfloat16)
    sin = (-np.sin(angles) * factor).astype(ml_dtypes.bfloat16)
    one = np.block([[cos, -sin], [sin, cos]])
    return one, np.ascontiguousarray(one.T)


def ring_place(r):
    r = lax.rem(r, RING)
    return jnp.where(r == 0, 0, jnp.where(lax.rem(r, 2) == 1, (r + 1) // 2, RING - r // 2))


def params():
    return pltpu.CompilerParams(vmem_limit_bytes=VMEM_LIMIT)


def slices_kernel(here, above, below, block, other, swap_out, far_out, own_out, ext):
    odd = lax.rem(lax.axis_index("row"), 2) == 1
    first = lax.axis_index("col") == 0
    cols = block.shape[2]
    twin = jnp.where(odd, above[0, 1], below[0, 1])
    beyond = jnp.where(odd, below[0, 1], above[0, 1])
    for part in range(2):
        ext[part, :, 0:128] = jnp.where(first, 0.0, other[part, :, cols - 128 :])
        ext[part, :, 128 : 128 + cols] = block[part]
        ext[part, :, 128 + cols :] = jnp.where(first, other[part, :, 0:128], 0.0)
    for start, out in ((here[0, 1], swap_out), (beyond, far_out), (twin, own_out)):
        base = pl.multiple_of(start // 128 * 128, 128)
        for part in range(2):
            wide = ext[part, :, pl.ds(base, 384)]
            wide = pltpu.roll(wide, (384 - start % 128) % 384, 1)
            out[part] = wide[:, 0:256]


def cut_slices(here, above, below, block, other):
    rows, cols = block.shape[1], block.shape[2]
    piece = jax.ShapeDtypeStruct((2, rows, 256), jnp.float32)
    return pl.pallas_call(
        slices_kernel,
        out_shape=(piece, piece, piece),
        in_specs=[SMEM, SMEM, SMEM, VMEM, VMEM],
        out_specs=(VMEM, VMEM, VMEM),
        scratch_shapes=[pltpu.VMEM((2, rows, cols + 256), jnp.float32)],
        compiler_params=params(),
        name="cut_slices",
    )(here, above, below, block, other)


def weights_kernel(count, here, above, below, probe, inner, edge, frame, grid):
    modes = probe.shape[0]
    r = lax.axis_index("row")
    present = ((r > 0).astype(jnp.float32), None, (r < count - 1).astype(jnp.float32))
    weight = jnp.zeros((256, 256), jnp.float32)
    for m in range(modes):
        weight = weight + probe[m, 0] * probe[m, 0] + probe[m, 1] * probe[m, 1]
    tall = jnp.concatenate([weight, jnp.zeros((128, 256), jnp.float32)], axis=0)
    grid[...] = jnp.zeros(grid.shape, jnp.float32)
    for number in range(3):
        spot = (above, here, below)[number]
        row, col = spot[0, 0], spot[0, 1]
        frame[...] = pltpu.roll(tall, row, 0)
        lower = 128 * (2 - number)
        piece = frame[lower : lower + 128, :]
        if present[number] is not None:
            piece = piece * present[number]
        wide = jnp.concatenate([piece, jnp.zeros((128, 128), jnp.float32)], axis=1)
        wide = pltpu.roll(wide, col % 128, 1)
        base = pl.multiple_of(col // 128 * 128, 128)
        grid[:, pl.ds(base, 384)] += wide
    inner[...] = grid[:, 128 : grid.shape[1] - 128]
    edge[...] = jnp.where(lax.axis_index("col") == 0, grid[:, grid.shape[1] - 128 :], grid[:, 0:128])


def weights(count, here, above, below, probe, rows, cols):
    return pl.pallas_call(
        functools.partial(weights_kernel, count),
        out_shape=(
            jax.ShapeDtypeStruct((rows, cols), jnp.float32),
            jax.ShapeDtypeStruct((rows, 128), jnp.float32),
        ),
        in_specs=[SMEM, SMEM, SMEM, VMEM],
        out_specs=(VMEM, VMEM),
        scratch_shapes=[
            pltpu.VMEM((384, 256), jnp.float32),
            pltpu.VMEM((rows, cols + 256), jnp.float32),
        ],
        compiler_params=params(),
        name="object_weights",
    )(here, above, below, probe)


def position_kernel(
    above, below, far_rows, mid_rows, own_rows, probe, pattern, one, two, ordered,
    mine, his0, his1, his2, fold_far, fold_mid, fold_own,
    stack, window, far, terms, update, strength, sems,
):
    del ordered
    modes = probe.shape[0]
    r = lax.axis_index("row")
    core = lax.axis_index("col")
    odd = lax.rem(r, 2)
    row = jnp.where(odd == 1, above[0, 0], below[0, 0])
    place = ring_place(r)
    far_at = pl.multiple_of(256 * (1 - odd), 128)
    own_at = pl.multiple_of(256 * odd, 128)
    stack[:, pl.ds(far_at, 128), :] = far_rows[...]
    stack[:, 128:256, :] = mid_rows[...]
    stack[:, pl.ds(own_at, 128), :] = own_rows[...]
    for part in range(2):
        window[part] = pltpu.roll(stack[part], (384 - row) % 384, 0)[0:256]
    strength[...] = jnp.zeros(strength.shape, jnp.float32)
    update[...] = jnp.zeros(update.shape, jnp.float32)

    def exit_wave(m):
        p_re, p_im = probe[m, 0], probe[m, 1]
        w_re, w_im = window[0], window[1]
        return p_re * w_re - p_im * w_im, p_re * w_im + p_im * w_re

    def forward(m, carry):
        e_re, e_im = exit_wave(m)
        field = jnp.concatenate([e_re.astype(jnp.bfloat16), e_im.astype(jnp.bfloat16)], axis=0)
        half = jnp.dot(one[...], field, preferred_element_type=jnp.float32).astype(jnp.bfloat16)
        half = jnp.concatenate([half[0:256], half[256:512]], axis=1)
        out = jnp.dot(half, two[...], preferred_element_type=jnp.float32)
        far[m] = out
        strength[...] += out[:, 0:256] * out[:, 0:256] + out[:, 256:512] * out[:, 256:512]
        return carry

    lax.fori_loop(0, modes, forward, 0, unroll=2)
    strength[...] = jnp.sqrt(pattern[...]) / jnp.maximum(jnp.sqrt(strength[...]), AMP_FLOOR)

    def put(image, value):
        for slab in range(16):
            ahead = (slab - place) & 7
            spot = jnp.where(ahead < 4, 7 - 2 * ahead, 2 * (ahead - 4))
            terms[(slab // 8) ^ core, spot, image] = value[16 * slab : 16 * slab + 16]

    def backward(m, carry):
        ratio = strength[...]
        fixed = jnp.concatenate(
            [
                (far[m, :, 0:256] * ratio).astype(jnp.bfloat16),
                (far[m, :, 256:512] * ratio).astype(jnp.bfloat16),
            ],
            axis=0,
        )
        back = jnp.dot(two[...], fixed, preferred_element_type=jnp.float32).astype(jnp.bfloat16)
        back = jnp.concatenate([back[0:256], back[256:512]], axis=1)
        near = jnp.dot(back, one[...], preferred_element_type=jnp.float32)
        e_re, e_im = exit_wave(m)
        d_re = near[:, 0:256] - e_re
        d_im = near[:, 256:512] - e_im
        p_re, p_im = probe[m, 0], probe[m, 1]
        w_re, w_im = window[0], window[1]
        update[0] += p_re * d_re + p_im * d_im
        update[1] += p_re * d_im - p_im * d_re
        put(1 + 2 * m, w_re * d_re + w_im * d_im)
        put(2 + 2 * m, w_re * d_im - w_im * d_re)
        return carry

    def send(low, high, at):
        images = pl.ds(low, high - low)
        copies = (
            pltpu.make_async_copy(terms.at[1, 0:1, images], his0.at[:, images], sems.at[at]),
            pltpu.make_async_copy(terms.at[1, 1:3, images], his1.at[:, images], sems.at[at + 1]),
            pltpu.make_async_copy(terms.at[1, 3:8, images], his2.at[:, images], sems.at[at + 2]),
            pltpu.make_async_copy(terms.at[0, :, images], mine.at[:, images], sems.at[at + 3]),
        )
        for copy in copies:
            copy.start()
        return copies

    cut = modes // 2
    put(0, window[0] * window[0] + window[1] * window[1])
    lax.fori_loop(0, cut, backward, 0, unroll=2)
    copies = send(0, 1 + 2 * cut, 0)
    lax.fori_loop(cut, modes, backward, 0, unroll=2)
    copies += send(1 + 2 * cut, 1 + 2 * modes, 4)
    for part in range(2):
        tall = jnp.concatenate([update[part], jnp.zeros((128, 256), jnp.float32)], axis=0)
        stack[part] = pltpu.roll(tall, row, 0)
    fold_far[...] = stack[:, pl.ds(far_at, 128), :]
    fold_mid[...] = stack[:, 128:256, :]
    fold_own[...] = stack[:, pl.ds(own_at, 128), :]
    for copy in copies:
        copy.wait()


def position(above, below, far_rows, mid_rows, own_rows, probe, pattern, one, two, ordered):
    modes = probe.shape[0]
    images = 1 + 2 * modes

    def f32(*shape):
        return jax.ShapeDtypeStruct(shape, jnp.float32)

    piece = f32(2, 128, 256)
    return pl.pallas_call(
        position_kernel,
        out_shape=(
            f32(8, images, 16, 256), f32(1, images, 16, 256), f32(2, images, 16, 256), f32(5, images, 16, 256),
            piece, piece, piece,
        ),
        in_specs=[SMEM] * 2 + [VMEM] * 7 + [ANY],
        out_specs=(ANY,) * 4 + (VMEM,) * 3,
        scratch_shapes=[
            pltpu.VMEM((2, 384, 256), jnp.float32),
            pltpu.VMEM((2, 256, 256), jnp.float32),
            pltpu.VMEM((modes, 256, 512), jnp.float32),
            pltpu.VMEM((2, 8, images, 16, 256), jnp.float32),
            pltpu.VMEM((2, 256, 256), jnp.float32),
            pltpu.VMEM((256, 256), jnp.float32),
            pltpu.SemaphoreType.DMA((8,)),
        ],
        compiler_params=params(),
        name="position_terms",
    )(above, below, far_rows, mid_rows, own_rows, probe, pattern, one, two, ordered)


def fold_kernel(here_at, above_at, below_at, near, middle, far, inner, edge, grid):
    odd = lax.rem(lax.axis_index("row"), 2) == 1
    grid[...] = jnp.zeros(grid.shape, jnp.float32)
    near_col = jnp.where(odd, above_at[0, 1], below_at[0, 1])
    far_col = jnp.where(odd, below_at[0, 1], above_at[0, 1])
    for col, piece in ((near_col, near), (here_at[0, 1], middle), (far_col, far)):
        base = pl.multiple_of(col // 128 * 128, 128)
        for part in range(2):
            wide = jnp.concatenate([piece[part], jnp.zeros((128, 128), jnp.float32)], axis=1)
            grid[part, :, pl.ds(base, 384)] += pltpu.roll(wide, col % 128, 1)
    size = grid.shape[2]
    inner[...] = grid[:, :, 128 : size - 128]
    edge[...] = jnp.where(lax.axis_index("col") == 0, grid[:, :, size - 128 :], grid[:, :, 0:128])


def fold(here, above, below, near, middle, far, rows, cols):
    return pl.pallas_call(
        fold_kernel,
        out_shape=(
            jax.ShapeDtypeStruct((2, rows, cols), jnp.float32),
            jax.ShapeDtypeStruct((2, rows, 128), jnp.float32),
        ),
        in_specs=[SMEM] * 3 + [VMEM] * 3,
        out_specs=(VMEM, VMEM),
        scratch_shapes=[pltpu.VMEM((2, rows, cols + 256), jnp.float32)],
        compiler_params=params(),
        name="fold_object",
    )(here, above, below, near, middle, far)


def finish_kernel(probe, block, inner, edge, den, *refs):
    chunks, (new_block, new_probe) = refs[:-2], refs[-2:]
    modes = probe.shape[0]
    cut = 16 * (1 + modes)
    core = lax.axis_index("col")
    place = ring_place(lax.axis_index("row"))
    cols = block.shape[2]
    peak = jnp.zeros((16, 256), jnp.float32)
    object_peak = jnp.zeros((8, 256), jnp.float32)
    for chunk in chunks:
        if chunk.shape[0] != chunks[8].shape[0]:
            peak = jnp.maximum(peak, chunk[0:16])
        if chunk.shape[0] != chunks[7].shape[0]:
            object_peak = jnp.maximum(object_peak, chunk[chunk.shape[0] - 8 :])
    peak = jnp.max(peak)
    object_peak = jnp.max(object_peak)
    for owner in range(2):
        half = core if owner == 0 else 1 - core
        parts = chunks[9 * owner : 9 * owner + 9]
        for number, hop in enumerate(HOPS):
            start = pl.multiple_of(128 * half + 16 * ((place + hop) & 7), 16)
            scale = 1.0 / ((1.0 - REGULAR) * parts[number][0:16] + REGULAR * peak)
            for m in range(modes):
                for part in range(2):
                    at = 16 * (1 + 2 * m + part)
                    if hop != 4:
                        value = parts[number][at : at + 16]
                    elif at < cut:
                        value = parts[7][at : at + 16]
                    else:
                        value = parts[8][at - cut : at - cut + 16]
                    new_probe[m, part, pl.ds(start, 16), :] = (
                        probe[m, part, pl.ds(start, 16), :] + value * scale
                    )
    side = pl.multiple_of((1 - core) * (cols - 128), 128)
    new_block[...] = inner[...]
    new_block[:, :, pl.ds(side, 128)] += edge[...]
    scale = 1.0 / ((1.0 - REGULAR) * den[...] + REGULAR * object_peak)
    for part in range(2):
        new_block[part] = block[part] + new_block[part] * scale


def finish(probe, block, inner, edge, den, chunks):
    return pl.pallas_call(
        finish_kernel,
        out_shape=(
            jax.ShapeDtypeStruct(block.shape, jnp.float32),
            jax.ShapeDtypeStruct(probe.shape, jnp.float32),
        ),
        in_specs=[VMEM] * (5 + len(chunks)),
        out_specs=(VMEM, VMEM),
        compiler_params=params(),
        name="finish",
    )(probe, block, inner, edge, den, *chunks)


def shards(object_field, probe, measured, offsets):
    rows, cols = object_field.shape[1], object_field.shape[2]
    count = lax.axis_size("row")
    r = lax.axis_index("row")
    c = lax.axis_index("col")
    odd = r % 2
    one, two = transform_blocks(probe.shape[-1])
    one, two = jnp.asarray(one), jnp.asarray(two)

    twins = [(i, i ^ 1) for i in range(count)]
    cores = [(0, 1), (1, 0)]
    down = [(i, i + 1) for i in range(count - 1)]
    up = [(i + 1, i) for i in range(count - 1)]
    outward = [(i, i + 2) for i in range(1, count - 2, 2)] + [(i, i - 2) for i in range(2, count, 2)]
    inward = [(b, a) for a, b in outward]
    forward = [
        (block + RING_ORDER[i], block + RING_ORDER[(i + 1) % RING])
        for block in range(0, count, RING)
        for i in range(RING)
    ]
    reverse = [(b, a) for a, b in forward]

    def across(x):
        return lax.ppermute(x, "col", cores)

    def send(x, pairs):
        return lax.ppermute(x, "row", pairs)

    above = send(offsets, down)
    below = send(offsets, up)
    other = across(object_field)
    pattern = send(measured, twins)[0]

    to_twin, to_beyond, own_rows = cut_slices(offsets, above, below, object_field, other)
    mid_rows = send(to_twin, twins)
    far_rows = send(to_beyond, outward)

    def join(inner, got):
        low = jnp.where(c == 0, 0.0, got)
        high = jnp.where(c == 0, got, 0.0)
        pads = [(0, 0)] * (inner.ndim - 1)
        return inner + jnp.pad(low, pads + [(0, cols - 128)]) + jnp.pad(high, pads + [(cols - 128, 0)])

    object_den, den_edge = weights(count, offsets, above, below, probe, rows, cols)
    object_den = join(object_den, across(den_edge))
    object_peak = jnp.max(object_den)

    mine, his0, his1, his2, fold_far, fold_mid, fold_own = position(
        above, below, far_rows, mid_rows, own_rows, probe, pattern, one, two, object_den
    )
    images = mine.shape[1]
    cut = images // 2 + 1
    theirs = [across(his0), across(his1), across(his2)]

    def share(leg):
        got = theirs[0][0] if leg == 0 else theirs[1][leg - 1] if leg < 3 else theirs[2][leg - 3]
        return mine[leg] + got

    farthest = share(0)
    ahead, behind = send(farthest[:cut], forward), send(farthest[cut:], reverse)
    rest = [(0, 0), (0, 0)]
    ahead = share(1) + jnp.pad(ahead, [(0, images - cut)] + rest)
    behind = share(2) + jnp.pad(behind, [(cut, 0)] + rest)
    for leg in (3, 5):
        ahead = share(leg) + send(ahead, forward)
        behind = share(leg + 1) + send(behind, reverse)
    total = share(7) + send(ahead, forward) + send(behind, reverse)
    if count > RING:
        blocks = [[b * RING + i for b in range(count // RING)] for i in range(RING)]
        total = lax.psum(total, "row", axis_index_groups=blocks)
        object_peak = lax.pmax(object_peak, "row", axis_index_groups=blocks)

    mid_got = send(fold_mid, twins)
    far_got = send(fold_far, inward)

    message = jnp.concatenate(
        [total.reshape(16 * images, 256), jnp.broadcast_to(object_peak, (8, 256))], axis=0
    )
    chunks = [message]
    ahead = behind = message
    for hop in range(3):
        ahead, behind = send(ahead, forward), send(behind, reverse)
        chunks += [ahead, behind]
    chunks += [send(ahead[: 16 * cut], forward), send(behind[16 * cut :], reverse)]
    chunks += [across(x) for x in chunks]

    inner, edge = fold(offsets, above, below, fold_own, mid_got, far_got, rows, cols)
    return finish(probe, object_field, inner, across(edge), object_den, chunks)


def solution(mesh):
    placed = (
        P(None, ("groups", "row"), "col"),
        P("groups", None, None, None),
        P(("groups", "row", "col"), None, None),
        P(("groups", "row", "col"), None),
    )
    return jax.shard_map(
        shards,
        mesh=mesh,
        in_specs=placed,
        out_specs=(P(None, ("groups", "row"), "col"), P("groups", None, None, None)),
        check_vma=False,
    )
```

```python
import functools
import math

import jax
import jax.numpy as jnp
import ml_dtypes
import numpy as np
from jax import lax
from jax.experimental import pallas as pl
from jax.experimental.pallas import tpu as pltpu
from jax.sharding import PartitionSpec as P

REGULAR = 0.25
AMP_FLOOR = 2.0
RING = 8
RING_ORDER = (0, 1, 3, 5, 7, 6, 4, 2)
HOPS = (0, -1, 1, -2, 2, -3, 3, 4)
VMEM_LIMIT = 56 * 1024 * 1024

SMEM = pl.BlockSpec(memory_space=pltpu.SMEM)
VMEM = pl.BlockSpec(memory_space=pltpu.VMEM)
ANY = pl.BlockSpec(memory_space=pl.ANY)


def transform_blocks(length):
    indices = np.arange(length, dtype=np.int32)
    phases = indices[:, None] * indices[None, :] % length
    angles = phases.astype(np.float32) * np.float32(2.0 * math.pi / length)
    factor = np.float32(1.0 / math.sqrt(length))
    cos = (np.cos(angles) * factor).astype(ml_dtypes.bfloat16)
    sin = (-np.sin(angles) * factor).astype(ml_dtypes.bfloat16)
    one = np.block([[cos, -sin], [sin, cos]])
    return one, np.ascontiguousarray(one.T)


def ring_place(r):
    r = lax.rem(r, RING)
    return jnp.where(r == 0, 0, jnp.where(lax.rem(r, 2) == 1, (r + 1) // 2, RING - r // 2))


def params():
    return pltpu.CompilerParams(vmem_limit_bytes=VMEM_LIMIT)


def slices_kernel(here, above, below, block, other, swap_out, far_out, own_out, ext):
    odd = lax.rem(lax.axis_index("row"), 2) == 1
    first = lax.axis_index("col") == 0
    cols = block.shape[2]
    twin = jnp.where(odd, above[0, 1], below[0, 1])
    beyond = jnp.where(odd, below[0, 1], above[0, 1])
    for part in range(2):
        ext[part, :, 0:128] = jnp.where(first, 0.0, other[part, :, cols - 128 :])
        ext[part, :, 128 : 128 + cols] = block[part]
        ext[part, :, 128 + cols :] = jnp.where(first, other[part, :, 0:128], 0.0)
    for start, out in ((here[0, 1], swap_out), (beyond, far_out), (twin, own_out)):
        base = pl.multiple_of(start // 128 * 128, 128)
        for part in range(2):
            wide = ext[part, :, pl.ds(base, 384)]
            wide = pltpu.roll(wide, (384 - start % 128) % 384, 1)
            out[part] = wide[:, 0:256]


def cut_slices(here, above, below, block, other):
    rows, cols = block.shape[1], block.shape[2]
    piece = jax.ShapeDtypeStruct((2, rows, 256), jnp.float32)
    return pl.pallas_call(
        slices_kernel,
        out_shape=(piece, piece, piece),
        in_specs=[SMEM, SMEM, SMEM, VMEM, VMEM],
        out_specs=(VMEM, VMEM, VMEM),
        scratch_shapes=[pltpu.VMEM((2, rows, cols + 256), jnp.float32)],
        compiler_params=params(),
        name="cut_slices",
    )(here, above, below, block, other)


def weights_kernel(count, here, above, below, probe, ordered, inner, edge, frame, grid):
    del ordered
    modes = probe.shape[0]
    r = lax.axis_index("row")
    present = ((r > 0).astype(jnp.float32), None, (r < count - 1).astype(jnp.float32))
    weight = jnp.zeros((256, 256), jnp.float32)
    for m in range(modes):
        weight = weight + probe[m, 0] * probe[m, 0] + probe[m, 1] * probe[m, 1]
    tall = jnp.concatenate([weight, jnp.zeros((128, 256), jnp.float32)], axis=0)
    grid[...] = jnp.zeros(grid.shape, jnp.float32)
    for number in range(3):
        spot = (above, here, below)[number]
        row, col = spot[0, 0], spot[0, 1]
        frame[...] = pltpu.roll(tall, row, 0)
        lower = 128 * (2 - number)
        piece = frame[lower : lower + 128, :]
        if present[number] is not None:
            piece = piece * present[number]
        wide = jnp.concatenate([piece, jnp.zeros((128, 128), jnp.float32)], axis=1)
        wide = pltpu.roll(wide, col % 128, 1)
        base = pl.multiple_of(col // 128 * 128, 128)
        grid[:, pl.ds(base, 384)] += wide
    inner[...] = grid[:, 128 : grid.shape[1] - 128]
    edge[...] = jnp.where(lax.axis_index("col") == 0, grid[:, grid.shape[1] - 128 :], grid[:, 0:128])


def weights(count, here, above, below, probe, ordered, rows, cols):
    return pl.pallas_call(
        functools.partial(weights_kernel, count),
        out_shape=(
            jax.ShapeDtypeStruct((rows, cols), jnp.float32),
            jax.ShapeDtypeStruct((rows, 128), jnp.float32),
        ),
        in_specs=[SMEM, SMEM, SMEM, VMEM, ANY],
        out_specs=(VMEM, VMEM),
        scratch_shapes=[
            pltpu.VMEM((384, 256), jnp.float32),
            pltpu.VMEM((rows, cols + 256), jnp.float32),
        ],
        compiler_params=params(),
        name="object_weights",
    )(here, above, below, probe, ordered)


def position_kernel(
    above, below, far_rows, mid_rows, own_rows, probe, pattern, one, two, ordered,
    mine, his0, his1, his2, fold_far, fold_mid, fold_own,
    stack, window, far, terms, update, strength, sems,
):
    del ordered
    modes = probe.shape[0]
    r = lax.axis_index("row")
    core = lax.axis_index("col")
    odd = lax.rem(r, 2)
    row = jnp.where(odd == 1, above[0, 0], below[0, 0])
    place = ring_place(r)
    far_at = pl.multiple_of(256 * (1 - odd), 128)
    own_at = pl.multiple_of(256 * odd, 128)
    stack[:, pl.ds(far_at, 128), :] = far_rows[...]
    stack[:, 128:256, :] = mid_rows[...]
    stack[:, pl.ds(own_at, 128), :] = own_rows[...]
    for part in range(2):
        window[part] = pltpu.roll(stack[part], (384 - row) % 384, 0)[0:256]
    strength[...] = jnp.zeros(strength.shape, jnp.float32)
    update[...] = jnp.zeros(update.shape, jnp.float32)

    def exit_wave(m):
        p_re, p_im = probe[m, 0], probe[m, 1]
        w_re, w_im = window[0], window[1]
        return p_re * w_re - p_im * w_im, p_re * w_im + p_im * w_re

    def forward(m, carry):
        e_re, e_im = exit_wave(m)
        field = jnp.concatenate([e_re.astype(jnp.bfloat16), e_im.astype(jnp.bfloat16)], axis=0)
        half = jnp.dot(one[...], field, preferred_element_type=jnp.float32).astype(jnp.bfloat16)
        half = jnp.concatenate([half[0:256], half[256:512]], axis=1)
        out = jnp.dot(half, two[...], preferred_element_type=jnp.float32)
        far[m] = out
        strength[...] += out[:, 0:256] * out[:, 0:256] + out[:, 256:512] * out[:, 256:512]
        return carry

    lax.fori_loop(0, modes, forward, 0, unroll=2)
    strength[...] = jnp.sqrt(pattern[...]) / jnp.maximum(jnp.sqrt(strength[...]), AMP_FLOOR)

    def put(image, value):
        for slab in range(16):
            ahead = (slab - place) & 7
            spot = jnp.where(ahead < 4, 7 - 2 * ahead, 2 * (ahead - 4))
            terms[(slab // 8) ^ core, spot, image] = value[16 * slab : 16 * slab + 16]

    def backward(m, carry):
        ratio = strength[...]
        fixed = jnp.concatenate(
            [
                (far[m, :, 0:256] * ratio).astype(jnp.bfloat16),
                (far[m, :, 256:512] * ratio).astype(jnp.bfloat16),
            ],
            axis=0,
        )
        back = jnp.dot(two[...], fixed, preferred_element_type=jnp.float32).astype(jnp.bfloat16)
        back = jnp.concatenate([back[0:256], back[256:512]], axis=1)
        near = jnp.dot(back, one[...], preferred_element_type=jnp.float32)
        e_re, e_im = exit_wave(m)
        d_re = near[:, 0:256] - e_re
        d_im = near[:, 256:512] - e_im
        p_re, p_im = probe[m, 0], probe[m, 1]
        w_re, w_im = window[0], window[1]
        update[0] += p_re * d_re + p_im * d_im
        update[1] += p_re * d_im - p_im * d_re
        put(1 + 2 * m, w_re * d_re + w_im * d_im)
        put(2 + 2 * m, w_re * d_im - w_im * d_re)
        return carry

    def send(low, high, at):
        images = pl.ds(low, high - low)
        copies = (
            pltpu.make_async_copy(terms.at[1, 0:1, images], his0.at[:, images], sems.at[at]),
            pltpu.make_async_copy(terms.at[1, 1:3, images], his1.at[:, images], sems.at[at + 1]),
            pltpu.make_async_copy(terms.at[1, 3:8, images], his2.at[:, images], sems.at[at + 2]),
            pltpu.make_async_copy(terms.at[0, :, images], mine.at[:, images], sems.at[at + 3]),
        )
        for copy in copies:
            copy.start()
        return copies

    cut = modes // 2
    put(0, window[0] * window[0] + window[1] * window[1])
    lax.fori_loop(0, cut, backward, 0, unroll=2)
    copies = send(0, 1 + 2 * cut, 0)
    lax.fori_loop(cut, modes, backward, 0, unroll=2)
    copies += send(1 + 2 * cut, 1 + 2 * modes, 4)
    for part in range(2):
        tall = jnp.concatenate([update[part], jnp.zeros((128, 256), jnp.float32)], axis=0)
        stack[part] = pltpu.roll(tall, row, 0)
    fold_far[...] = stack[:, pl.ds(far_at, 128), :]
    fold_mid[...] = stack[:, 128:256, :]
    fold_own[...] = stack[:, pl.ds(own_at, 128), :]
    for copy in copies:
        copy.wait()


def position(above, below, far_rows, mid_rows, own_rows, probe, pattern, one, two, ordered):
    modes = probe.shape[0]
    images = 1 + 2 * modes

    def f32(*shape):
        return jax.ShapeDtypeStruct(shape, jnp.float32)

    piece = f32(2, 128, 256)
    return pl.pallas_call(
        position_kernel,
        out_shape=(
            f32(8, images, 16, 256), f32(1, images, 16, 256), f32(2, images, 16, 256), f32(5, images, 16, 256),
            piece, piece, piece,
        ),
        in_specs=[SMEM] * 2 + [VMEM] * 7 + [ANY],
        out_specs=(ANY,) * 4 + (VMEM,) * 3,
        scratch_shapes=[
            pltpu.VMEM((2, 384, 256), jnp.float32),
            pltpu.VMEM((2, 256, 256), jnp.float32),
            pltpu.VMEM((modes, 256, 512), jnp.float32),
            pltpu.VMEM((2, 8, images, 16, 256), jnp.float32),
            pltpu.VMEM((2, 256, 256), jnp.float32),
            pltpu.VMEM((256, 256), jnp.float32),
            pltpu.SemaphoreType.DMA((8,)),
        ],
        compiler_params=params(),
        name="position_terms",
    )(above, below, far_rows, mid_rows, own_rows, probe, pattern, one, two, ordered)


def fold_kernel(here_at, above_at, below_at, near, middle, far, inner, edge, grid):
    odd = lax.rem(lax.axis_index("row"), 2) == 1
    grid[...] = jnp.zeros(grid.shape, jnp.float32)
    near_col = jnp.where(odd, above_at[0, 1], below_at[0, 1])
    far_col = jnp.where(odd, below_at[0, 1], above_at[0, 1])
    for col, piece in ((near_col, near), (here_at[0, 1], middle), (far_col, far)):
        base = pl.multiple_of(col // 128 * 128, 128)
        for part in range(2):
            wide = jnp.concatenate([piece[part], jnp.zeros((128, 128), jnp.float32)], axis=1)
            grid[part, :, pl.ds(base, 384)] += pltpu.roll(wide, col % 128, 1)
    size = grid.shape[2]
    inner[...] = grid[:, :, 128 : size - 128]
    edge[...] = jnp.where(lax.axis_index("col") == 0, grid[:, :, size - 128 :], grid[:, :, 0:128])


def fold(here, above, below, near, middle, far, rows, cols):
    return pl.pallas_call(
        fold_kernel,
        out_shape=(
            jax.ShapeDtypeStruct((2, rows, cols), jnp.float32),
            jax.ShapeDtypeStruct((2, rows, 128), jnp.float32),
        ),
        in_specs=[SMEM] * 3 + [VMEM] * 3,
        out_specs=(VMEM, VMEM),
        scratch_shapes=[pltpu.VMEM((2, rows, cols + 256), jnp.float32)],
        compiler_params=params(),
        name="fold_object",
    )(here, above, below, near, middle, far)


def finish_kernel(probe, block, inner, edge, den, *refs):
    chunks, (new_block, new_probe) = refs[:-2], refs[-2:]
    modes = probe.shape[0]
    cut = 16 * (1 + modes)
    core = lax.axis_index("col")
    place = ring_place(lax.axis_index("row"))
    cols = block.shape[2]
    peak = jnp.zeros((16, 256), jnp.float32)
    object_peak = jnp.zeros((8, 256), jnp.float32)
    for chunk in chunks:
        if chunk.shape[0] != chunks[8].shape[0]:
            peak = jnp.maximum(peak, chunk[0:16])
        if chunk.shape[0] != chunks[7].shape[0]:
            object_peak = jnp.maximum(object_peak, chunk[chunk.shape[0] - 8 :])
    peak = jnp.max(peak)
    object_peak = jnp.max(object_peak)
    for owner in range(2):
        half = core if owner == 0 else 1 - core
        parts = chunks[9 * owner : 9 * owner + 9]
        for number, hop in enumerate(HOPS):
            start = pl.multiple_of(128 * half + 16 * ((place + hop) & 7), 16)
            scale = 1.0 / ((1.0 - REGULAR) * parts[number][0:16] + REGULAR * peak)
            for m in range(modes):
                for part in range(2):
                    at = 16 * (1 + 2 * m + part)
                    if hop != 4:
                        value = parts[number][at : at + 16]
                    elif at < cut:
                        value = parts[7][at : at + 16]
                    else:
                        value = parts[8][at - cut : at - cut + 16]
                    new_probe[m, part, pl.ds(start, 16), :] = (
                        probe[m, part, pl.ds(start, 16), :] + value * scale
                    )
    side = pl.multiple_of((1 - core) * (cols - 128), 128)
    new_block[...] = inner[...]
    new_block[:, :, pl.ds(side, 128)] += edge[...]
    scale = 1.0 / ((1.0 - REGULAR) * den[...] + REGULAR * object_peak)
    for part in range(2):
        new_block[part] = block[part] + new_block[part] * scale


def finish(probe, block, inner, edge, den, chunks):
    return pl.pallas_call(
        finish_kernel,
        out_shape=(
            jax.ShapeDtypeStruct(block.shape, jnp.float32),
            jax.ShapeDtypeStruct(probe.shape, jnp.float32),
        ),
        in_specs=[VMEM] * (5 + len(chunks)),
        out_specs=(VMEM, VMEM),
        compiler_params=params(),
        name="finish",
    )(probe, block, inner, edge, den, *chunks)


def shards(object_field, probe, measured, offsets):
    rows, cols = object_field.shape[1], object_field.shape[2]
    count = lax.axis_size("row")
    r = lax.axis_index("row")
    c = lax.axis_index("col")
    odd = r % 2
    one, two = transform_blocks(probe.shape[-1])
    one, two = jnp.asarray(one), jnp.asarray(two)

    twins = [(i, i ^ 1) for i in range(count)]
    cores = [(0, 1), (1, 0)]
    down = [(i, i + 1) for i in range(count - 1)]
    up = [(i + 1, i) for i in range(count - 1)]
    outward = [(i, i + 2) for i in range(1, count - 2, 2)] + [(i, i - 2) for i in range(2, count, 2)]
    inward = [(b, a) for a, b in outward]
    forward = [
        (block + RING_ORDER[i], block + RING_ORDER[(i + 1) % RING])
        for block in range(0, count, RING)
        for i in range(RING)
    ]
    reverse = [(b, a) for a, b in forward]

    def across(x):
        return lax.ppermute(x, "col", cores)

    def send(x, pairs):
        return lax.ppermute(x, "row", pairs)

    above = send(offsets, down)
    below = send(offsets, up)
    other = across(object_field)
    pattern = send(measured, twins)
    above, below, other, pattern = lax.optimization_barrier((above, below, other, pattern))

    to_twin, to_beyond, own_rows = cut_slices(offsets, above, below, object_field, other)
    mid_rows = send(to_twin, twins)
    far_rows = send(to_beyond, outward)

    def join(inner, got):
        low = jnp.where(c == 0, 0.0, got)
        high = jnp.where(c == 0, got, 0.0)
        pads = [(0, 0)] * (inner.ndim - 1)
        return inner + jnp.pad(low, pads + [(0, cols - 128)]) + jnp.pad(high, pads + [(cols - 128, 0)])

    object_den, den_edge = weights(count, offsets, above, below, probe, own_rows, rows, cols)
    object_den = join(object_den, across(den_edge))
    object_peak = jnp.max(object_den)

    mine, his0, his1, his2, fold_far, fold_mid, fold_own = position(
        above, below, far_rows, mid_rows, own_rows, probe, pattern[0], one, two, object_den
    )
    images = mine.shape[1]
    cut = images // 2 + 1
    theirs = [across(his0), across(his1), across(his2)]

    def share(leg):
        got = theirs[0][0] if leg == 0 else theirs[1][leg - 1] if leg < 3 else theirs[2][leg - 3]
        return mine[leg] + got

    mid_got = send(fold_mid, twins)
    far_got = send(fold_far, inward)

    farthest = share(0)
    ahead, behind = farthest[:cut], farthest[cut:]
    ahead, behind = send(ahead, forward), send(behind, reverse)
    ahead, behind, mid_got, far_got = lax.optimization_barrier((ahead, behind, mid_got, far_got))
    rest = [(0, 0), (0, 0)]
    ahead = share(1) + jnp.pad(ahead, [(0, images - cut)] + rest)
    behind = share(2) + jnp.pad(behind, [(cut, 0)] + rest)
    for leg in (3, 5, 7):
        ahead, behind = lax.optimization_barrier((ahead, behind))
        ahead, behind = send(ahead, forward), send(behind, reverse)
        ahead, behind = lax.optimization_barrier((ahead, behind))
        if leg < 7:
            ahead, behind = share(leg) + ahead, share(leg + 1) + behind
    total = share(7) + ahead + behind
    if count > RING:
        blocks = [[b * RING + i for b in range(count // RING)] for i in range(RING)]
        total = lax.psum(total, "row", axis_index_groups=blocks)
        object_peak = lax.pmax(object_peak, "row", axis_index_groups=blocks)

    message = jnp.concatenate(
        [total.reshape(16 * images, 256), jnp.broadcast_to(object_peak, (8, 256))], axis=0
    )
    chunks = [message]
    ahead = behind = message
    for hop in range(3):
        ahead, behind = send(ahead, forward), send(behind, reverse)
        ahead, behind = lax.optimization_barrier((ahead, behind))
        chunks += [ahead, behind]
    ahead, behind = lax.optimization_barrier((ahead[: 16 * cut], behind[16 * cut :]))
    chunks += [send(ahead, forward), send(behind, reverse)]
    chunks += [across(x) for x in chunks]

    inner, edge = fold(offsets, above, below, fold_own, mid_got, far_got, rows, cols)
    return finish(probe, object_field, inner, across(edge), object_den, chunks)


def solution(mesh):
    placed = (
        P(None, ("groups", "row"), "col"),
        P("groups", None, None, None),
        P(("groups", "row", "col"), None, None),
        P(("groups", "row", "col"), None),
    )
    return jax.shard_map(
        shards,
        mesh=mesh,
        in_specs=placed,
        out_specs=(P(None, ("groups", "row"), "col"), P("groups", None, None, None)),
        check_vma=False,
    )
```

```python
import functools
import math

import jax
import jax.numpy as jnp
import ml_dtypes
import numpy as np
from jax import lax
from jax.experimental import pallas as pl
from jax.experimental.pallas import tpu as pltpu
from jax.sharding import PartitionSpec as P

REGULAR = 0.25
AMP_FLOOR = 2.0
RING = 8
RING_ORDER = (0, 1, 3, 5, 7, 6, 4, 2)
HOPS = (0, -1, 1, -2, 2, -3, 3, 4)

SMEM = pl.BlockSpec(memory_space=pltpu.SMEM)
VMEM = pl.BlockSpec(memory_space=pltpu.VMEM)
ANY = pl.BlockSpec(memory_space=pl.ANY)


def transform_blocks(length):
    indices = np.arange(length, dtype=np.int32)
    phases = indices[:, None] * indices[None, :] % length
    angles = phases.astype(np.float32) * np.float32(2.0 * math.pi / length)
    factor = np.float32(1.0 / math.sqrt(length))
    cos = (np.cos(angles) * factor).astype(ml_dtypes.bfloat16)
    sin = (-np.sin(angles) * factor).astype(ml_dtypes.bfloat16)
    one = np.block([[cos, -sin], [sin, cos]])
    return one, np.ascontiguousarray(one.T)


def ring_place(r):
    r = lax.rem(r, RING)
    return jnp.where(r == 0, 0, jnp.where(lax.rem(r, 2) == 1, (r + 1) // 2, RING - r // 2))


def params(mib):
    return pltpu.CompilerParams(vmem_limit_bytes=mib * 1024 * 1024)


def f32(*shape):
    return jax.ShapeDtypeStruct(shape, jnp.float32)


def begin(copies):
    for copy in copies:
        copy.start()
    return copies


def end(copies):
    for copy in copies:
        copy.wait()


def slices_kernel(offsets_at, *refs):
    offsets, (block, other, _), outs, (ext, cuts, sems) = refs[:3], refs[3:6], refs[6:-3], refs[-3:]
    odd = lax.rem(lax.axis_index("row"), 2) == 1
    core = lax.axis_index("col")
    cols = block.shape[2]
    end_of = cols + 128
    source = pl.multiple_of(core * (cols - 128), 128)
    target = pl.multiple_of((1 - core) * end_of, 128)
    blank = pl.multiple_of(core * end_of, 128)
    copies = begin(
        (
            pltpu.make_async_copy(block, ext.at[:, :, 128:end_of], sems.at[0]),
            pltpu.make_async_copy(
                other.at[:, :, pl.ds(source, 128)], ext.at[:, :, pl.ds(target, 128)], sems.at[1]
            ),
        )
    )
    ext[:, :, pl.ds(blank, 128)] = jnp.zeros((2, block.shape[1], 128), jnp.float32)
    end(copies)
    here, above, below = offsets[0][0, 1], offsets[1][0, 1], offsets[2][0, 1]
    columns = {
        "here": here,
        "twin": jnp.where(odd, above, below),
        "beyond": jnp.where(odd, below, above),
    }
    copies = ()
    for number, (which, out) in enumerate(zip(offsets_at, outs)):
        start = columns[which]
        base = pl.multiple_of(start // 128 * 128, 128)
        for part in range(2):
            wide = ext[part, :, pl.ds(base, 384)]
            wide = pltpu.roll(wide, (384 - start % 128) % 384, 1)
            cuts[number, part] = wide[:, 0:256]
        copies += begin((pltpu.make_async_copy(cuts.at[number], out, sems.at[2 + number]),))
    end(copies)


def cut_slices(offsets_at, here, above, below, block, other, ordered):
    rows, cols = block.shape[1], block.shape[2]
    count = len(offsets_at)
    return pl.pallas_call(
        functools.partial(slices_kernel, offsets_at),
        out_shape=(f32(2, rows, 256),) * count,
        in_specs=[SMEM] * 3 + [ANY] * 3,
        out_specs=(ANY,) * count,
        scratch_shapes=[
            pltpu.VMEM((2, rows, cols + 256), jnp.float32),
            pltpu.VMEM((count, 2, rows, 256), jnp.float32),
            pltpu.SemaphoreType.DMA((4,)),
        ],
        compiler_params=params(6),
        name="cut_slices",
    )(here, above, below, block, other, ordered)


def power_kernel(probe, out, held, sems):
    modes = probe.shape[0]
    copies = begin([pltpu.make_async_copy(probe.at[m], held.at[m], sems.at[m]) for m in range(modes)])
    for m in range(modes):
        copies[m].wait()
        power = held[m, 0] * held[m, 0] + held[m, 1] * held[m, 1]
        out[...] = power if m == 0 else out[...] + power


def probe_power(probe):
    return pl.pallas_call(
        power_kernel,
        out_shape=f32(*probe.shape[2:]),
        in_specs=[ANY],
        out_specs=VMEM,
        scratch_shapes=[pltpu.VMEM(probe.shape, jnp.float32), pltpu.SemaphoreType.DMA((probe.shape[0],))],
        compiler_params=params(8),
        name="probe_power",
    )(probe)


def weights_kernel(count, here, above, below, power, inner, edge, frame, grid):
    r = lax.axis_index("row")
    present = ((r > 0).astype(jnp.float32), None, (r < count - 1).astype(jnp.float32))
    tall = jnp.concatenate([power[...], jnp.zeros((128, 256), jnp.float32)], axis=0)
    grid[...] = jnp.zeros(grid.shape, jnp.float32)
    for number, spot in enumerate((above, here, below)):
        row, col = spot[0, 0], spot[0, 1]
        frame[...] = pltpu.roll(tall, row, 0)
        lower = 128 * (2 - number)
        piece = frame[lower : lower + 128, :]
        if present[number] is not None:
            piece = piece * present[number]
        wide = jnp.concatenate([piece, jnp.zeros((128, 128), jnp.float32)], axis=1)
        base = pl.multiple_of(col // 128 * 128, 128)
        grid[:, pl.ds(base, 384)] += pltpu.roll(wide, col % 128, 1)
    size = grid.shape[1]
    inner[...] = grid[:, 128 : size - 128]
    edge[...] = jnp.where(lax.axis_index("col") == 0, grid[:, size - 128 :], grid[:, 0:128])


def weights(count, here, above, below, power, rows, cols):
    return pl.pallas_call(
        functools.partial(weights_kernel, count),
        out_shape=(f32(rows, cols), f32(rows, 128)),
        in_specs=[SMEM] * 3 + [VMEM],
        out_specs=(VMEM, VMEM),
        scratch_shapes=[
            pltpu.VMEM((384, 256), jnp.float32),
            pltpu.VMEM((rows, cols + 256), jnp.float32),
        ],
        compiler_params=params(6),
        name="object_weights",
    )(here, above, below, power)


def position_kernel(
    above, below, far_rows, mid_rows, own_rows, probe_at, pattern_at, one_at, two_at,
    mine, his0, his1, his2, fold_far, fold_mid, fold_own,
    probe, pattern, one, two, stack, window, far, terms, update, strength, sems, probe_sems, out_sems,
):
    modes = probe.shape[0]
    r = lax.axis_index("row")
    core = lax.axis_index("col")
    odd = lax.rem(r, 2)
    row = jnp.where(odd == 1, above[0, 0], below[0, 0])
    place = ring_place(r)
    far_at = pl.multiple_of(256 * (1 - odd), 128)
    own_at = pl.multiple_of(256 * odd, 128)

    def load(source, target, number):
        return pltpu.make_async_copy(source, target, sems.at[number])

    rows_in = begin(
        (
            load(far_rows, stack.at[:, pl.ds(far_at, 128), :], 0),
            load(mid_rows, stack.at[:, 128:256, :], 1),
            load(own_rows, stack.at[:, pl.ds(own_at, 128), :], 2),
        )
    )
    tables_in = begin((load(one_at, one, 3), load(two_at, two, 4)))
    probe_in = begin(
        [pltpu.make_async_copy(probe_at.at[m], probe.at[m], probe_sems.at[m]) for m in range(modes)]
    )
    pattern_in = begin((load(pattern_at, pattern, 5),))
    end(rows_in)
    for part in range(2):
        window[part] = pltpu.roll(stack[part], (384 - row) % 384, 0)[0:256]
    end(tables_in)

    def exit_wave(m):
        p_re, p_im = probe[m, 0], probe[m, 1]
        w_re, w_im = window[0], window[1]
        return p_re * w_re - p_im * w_im, p_re * w_im + p_im * w_re

    for m in range(modes):
        probe_in[m].wait()
        e_re, e_im = exit_wave(m)
        field = jnp.concatenate([e_re.astype(jnp.bfloat16), e_im.astype(jnp.bfloat16)], axis=0)
        half = jnp.dot(one[...], field, preferred_element_type=jnp.float32).astype(jnp.bfloat16)
        half = jnp.concatenate([half[0:256], half[256:512]], axis=1)
        out = jnp.dot(half, two[...], preferred_element_type=jnp.float32)
        far[m] = out
        power = out[:, 0:256] * out[:, 0:256] + out[:, 256:512] * out[:, 256:512]
        strength[...] = power if m == 0 else strength[...] + power

    end(pattern_in)
    strength[...] = jnp.sqrt(pattern[...]) / jnp.maximum(jnp.sqrt(strength[...]), AMP_FLOOR)

    def put(image, value):
        for slab in range(16):
            ahead = (slab - place) & 7
            spot = jnp.where(ahead < 4, 7 - 2 * ahead, 2 * (ahead - 4))
            terms[(slab // 8) ^ core, spot, image] = value[16 * slab : 16 * slab + 16]

    def give(low, high, at):
        images = pl.ds(low, high - low)
        return begin(
            (
                pltpu.make_async_copy(terms.at[1, 0:1, images], his0.at[:, images], out_sems.at[at]),
                pltpu.make_async_copy(terms.at[1, 1:3, images], his1.at[:, images], out_sems.at[at + 1]),
                pltpu.make_async_copy(terms.at[1, 3:8, images], his2.at[:, images], out_sems.at[at + 2]),
                pltpu.make_async_copy(terms.at[0, :, images], mine.at[:, images], out_sems.at[at + 3]),
            )
        )

    put(0, window[0] * window[0] + window[1] * window[1])
    given, copies = 0, ()
    for m in range(modes):
        ratio = strength[...]
        fixed = jnp.concatenate(
            [
                (far[m, :, 0:256] * ratio).astype(jnp.bfloat16),
                (far[m, :, 256:512] * ratio).astype(jnp.bfloat16),
            ],
            axis=0,
        )
        back = jnp.dot(two[...], fixed, preferred_element_type=jnp.float32).astype(jnp.bfloat16)
        back = jnp.concatenate([back[0:256], back[256:512]], axis=1)
        near = jnp.dot(back, one[...], preferred_element_type=jnp.float32)
        e_re, e_im = exit_wave(m)
        d_re = near[:, 0:256] - e_re
        d_im = near[:, 256:512] - e_im
        p_re, p_im = probe[m, 0], probe[m, 1]
        w_re, w_im = window[0], window[1]
        u_re = p_re * d_re + p_im * d_im
        u_im = p_re * d_im - p_im * d_re
        update[0] = u_re if m == 0 else update[0] + u_re
        update[1] = u_im if m == 0 else update[1] + u_im
        put(1 + 2 * m, w_re * d_re + w_im * d_im)
        put(2 + 2 * m, w_re * d_im - w_im * d_re)
        if m % 2 == 1:
            copies += give(given, 3 + 2 * m, 2 * (m - 1))
            given = 3 + 2 * m

    for part in range(2):
        tall = jnp.concatenate([update[part], jnp.zeros((128, 256), jnp.float32)], axis=0)
        stack[part] = pltpu.roll(tall, row, 0)
    copies += begin(
        (
            load(stack.at[:, pl.ds(far_at, 128), :], fold_far, 0),
            load(stack.at[:, 128:256, :], fold_mid, 1),
            load(stack.at[:, pl.ds(own_at, 128), :], fold_own, 2),
        )
    )
    end(copies)


def position(above, below, far_rows, mid_rows, own_rows, probe, pattern, one, two):
    modes = probe.shape[0]
    images = 1 + 2 * modes
    return pl.pallas_call(
        position_kernel,
        out_shape=tuple(f32(legs, images, 16, 256) for legs in (8, 1, 2, 5)) + (f32(2, 128, 256),) * 3,
        in_specs=[SMEM] * 2 + [ANY] * 7,
        out_specs=(ANY,) * 7,
        scratch_shapes=[
            pltpu.VMEM(probe.shape, jnp.float32),
            pltpu.VMEM((256, 256), jnp.float32),
            pltpu.VMEM(one.shape, jnp.bfloat16),
            pltpu.VMEM(two.shape, jnp.bfloat16),
            pltpu.VMEM((2, 384, 256), jnp.float32),
            pltpu.VMEM((2, 256, 256), jnp.float32),
            pltpu.VMEM((modes, 256, 512), jnp.float32),
            pltpu.VMEM((2, 8, images, 16, 256), jnp.float32),
            pltpu.VMEM((2, 256, 256), jnp.float32),
            pltpu.VMEM((256, 256), jnp.float32),
            pltpu.SemaphoreType.DMA((6,)),
            pltpu.SemaphoreType.DMA((modes,)),
            pltpu.SemaphoreType.DMA((2 * modes,)),
        ],
        compiler_params=params(32),
        name="position_terms",
    )(above, below, far_rows, mid_rows, own_rows, probe, pattern, one, two)


def fold_kernel(here_at, above_at, below_at, near, middle, far, inner, edge, grid):
    odd = lax.rem(lax.axis_index("row"), 2) == 1
    grid[...] = jnp.zeros(grid.shape, jnp.float32)
    near_col = jnp.where(odd, above_at[0, 1], below_at[0, 1])
    far_col = jnp.where(odd, below_at[0, 1], above_at[0, 1])
    for col, piece in ((near_col, near), (here_at[0, 1], middle), (far_col, far)):
        base = pl.multiple_of(col // 128 * 128, 128)
        for part in range(2):
            wide = jnp.concatenate([piece[part], jnp.zeros((128, 128), jnp.float32)], axis=1)
            grid[part, :, pl.ds(base, 384)] += pltpu.roll(wide, col % 128, 1)
    size = grid.shape[2]
    inner[...] = grid[:, :, 128 : size - 128]
    edge[...] = jnp.where(lax.axis_index("col") == 0, grid[:, :, size - 128 :], grid[:, :, 0:128])


def fold(here, above, below, near, middle, far, rows, cols):
    return pl.pallas_call(
        fold_kernel,
        out_shape=(f32(2, rows, cols), f32(2, rows, 128)),
        in_specs=[SMEM] * 3 + [VMEM] * 3,
        out_specs=(VMEM, VMEM),
        scratch_shapes=[pltpu.VMEM((2, rows, cols + 256), jnp.float32)],
        compiler_params=params(8),
        name="fold_object",
    )(here, above, below, near, middle, far)


def close_kernel(ahead_at, behind_at, mine_at, theirs_at, den_at, edge_at, message, maxima, ahead, behind, mine, theirs, den, edge, sems):
    pairs = (
        (den_at, den), (edge_at, edge),
        (ahead_at, ahead), (behind_at, behind),
        (mine_at.at[mine_at.shape[0] - 1], mine), (theirs_at.at[theirs_at.shape[0] - 1], theirs),
    )
    copies = begin([pltpu.make_async_copy(a, b, sems.at[n]) for n, (a, b) in enumerate(pairs)])
    end(copies[:2])
    cols = den.shape[1]
    side = pl.multiple_of((1 - lax.axis_index("col")) * (cols - 128), 128)
    den[:, pl.ds(side, 128)] += edge[...]
    object_peak = jnp.max(den[...])
    end(copies[2:])
    images = ahead.shape[0]
    for image in range(images):
        total = (mine[image] + theirs[image]) + (ahead[image] + behind[image])
        message[16 * image : 16 * image + 16] = total
        if image == 0:
            maxima[0:8] = jnp.full((8, 256), jnp.max(total), jnp.float32)
    message[16 * images :] = jnp.full((8, 256), object_peak, jnp.float32)
    maxima[8:16] = jnp.full((8, 256), object_peak, jnp.float32)


def close(ahead, behind, mine, theirs, den, edge):
    shape = ahead.shape
    return pl.pallas_call(
        close_kernel,
        out_shape=(f32(16 * shape[0] + 8, 256), f32(16, 256)),
        in_specs=[ANY] * 6,
        out_specs=(VMEM, VMEM),
        scratch_shapes=[pltpu.VMEM(shape, jnp.float32)] * 4
        + [
            pltpu.VMEM(den.shape, jnp.float32),
            pltpu.VMEM(edge.shape, jnp.float32),
            pltpu.SemaphoreType.DMA((6,)),
        ],
        compiler_params=params(6),
        name="close_sum",
    )(ahead, behind, mine, theirs, den, edge)


def finish_kernel(probe_at, block_at, inner_at, edge_at, den_at, den_edge_at, opposite, opposite_twin, *refs):
    number = 2 * (len(HOPS) - 1)
    messages, refs = refs[:number], refs[number:]
    new_block_at, new_probe_at, peaks, probe, block, inner, edge, den, den_edge, new_probe, held = refs[:11]
    sems, out_sems = refs[11:]
    modes = probe.shape[0]
    core = lax.axis_index("col")
    place = ring_place(lax.axis_index("row"))
    cols = block.shape[2]
    pairs = [(messages[n], held.at[n]) for n in range(number)]
    pairs += [(probe_at.at[m], probe.at[m]) for m in range(modes)]
    pairs += [(block_at, block), (inner_at, inner), (edge_at, edge), (den_at, den), (den_edge_at, den_edge)]
    copies = begin([pltpu.make_async_copy(a, b, sems.at[n]) for n, (a, b) in enumerate(pairs)])
    end(copies[:number])
    peak = jnp.maximum(opposite[0:8], opposite_twin[0:8])
    object_peak = jnp.maximum(opposite[8:16], opposite_twin[8:16])
    for n in range(number):
        peak = jnp.maximum(peak, jnp.maximum(held[n, 0:8], held[n, 8:16]))
        object_peak = jnp.maximum(object_peak, held[n, held.shape[1] - 8 :])
    peak = jnp.max(peak)
    object_peak = jnp.max(object_peak)
    peaks[...] = jnp.full((8, 128), peak, jnp.float32)
    scales, starts = [], []
    for n in range(number):
        half = core if n < number // 2 else 1 - core
        starts.append(pl.multiple_of(128 * half + 16 * ((place + HOPS[n % (number // 2)]) & 7), 16))
        held[n, 0:16] = 1.0 / ((1.0 - REGULAR) * held[n, 0:16] + REGULAR * peak)
    outs = ()
    for m in range(modes):
        copies[number + m].wait()
        for part in range(2):
            at = 16 * (1 + 2 * m + part)
            for n in range(number):
                rows = pl.ds(starts[n], 16)
                new_probe[m, part, rows, :] = probe[m, part, rows, :] + held[n, at : at + 16] * held[n, 0:16]
            for half in range(2):
                rows = pl.ds(pl.multiple_of(128 * half + 16 * ((place + 4) & 7), 16), 16)
                new_probe[m, part, rows, :] = probe[m, part, rows, :]
        outs += begin((pltpu.make_async_copy(new_probe.at[m], new_probe_at.at[m], out_sems.at[m]),))
    end(copies[number + modes :])
    side = pl.multiple_of((1 - core) * (cols - 128), 128)
    inner[:, :, pl.ds(side, 128)] += edge[...]
    den[:, pl.ds(side, 128)] += den_edge[...]
    scale = 1.0 / ((1.0 - REGULAR) * den[...] + REGULAR * object_peak)
    for part in range(2):
        block[part] = block[part] + inner[part] * scale
    outs += begin((pltpu.make_async_copy(block, new_block_at, out_sems.at[modes]),))
    end(outs)


def finish(probe, block, inner, edge, den, den_edge, opposite, opposite_twin, messages):
    modes = probe.shape[0]
    number = len(messages)
    return pl.pallas_call(
        finish_kernel,
        out_shape=(f32(*block.shape), f32(*probe.shape), f32(8, 128)),
        in_specs=[ANY] * 6 + [VMEM] * 2 + [ANY] * number,
        out_specs=(ANY, ANY, VMEM),
        scratch_shapes=[
            pltpu.VMEM(x.shape, jnp.float32) for x in (probe, block, inner, edge, den, den_edge, probe)
        ]
        + [
            pltpu.VMEM((number,) + messages[0].shape, jnp.float32),
            pltpu.SemaphoreType.DMA((number + modes + 5,)),
            pltpu.SemaphoreType.DMA((modes + 1,)),
        ],
        compiler_params=params(24),
        name="finish_most",
    )(probe, block, inner, edge, den, den_edge, opposite, opposite_twin, *messages)


def last_kernel(started, probe_at, peaks, low_at, high_at, low_twin_at, high_twin_at, out_at, probe, low, high, sems):
    del started
    modes = probe.shape[1]
    cut = low.shape[1]
    core = lax.axis_index("col")
    place = ring_place(lax.axis_index("row"))
    peak = jnp.max(peaks[...])
    rows = []
    pairs = [(low_at, low.at[0]), (high_at, high.at[0]), (low_twin_at, low.at[1]), (high_twin_at, high.at[1])]
    for owner in range(2):
        half = core if owner == 0 else 1 - core
        rows.append(pl.ds(pl.multiple_of(128 * half + 16 * ((place + 4) & 7), 16), 16))
        pairs.append((probe_at.at[:, :, rows[owner], :], probe.at[owner]))
    end(begin([pltpu.make_async_copy(a, b, sems.at[n]) for n, (a, b) in enumerate(pairs)]))
    outs = ()
    for owner in range(2):
        scale = 1.0 / ((1.0 - REGULAR) * low[owner, 0:16] + REGULAR * peak)
        for m in range(modes):
            for part in range(2):
                at = 16 * (1 + 2 * m + part)
                value = low[owner, at : at + 16] if at < cut else high[owner, at - cut : at - cut + 16]
                probe[owner, m, part] = probe[owner, m, part] + value * scale
        outs += begin((pltpu.make_async_copy(probe.at[owner], out_at.at[:, :, rows[owner], :], sems.at[owner]),))
    end(outs)


def finish_rest(started, probe, peaks, parts):
    modes = probe.shape[0]
    return pl.pallas_call(
        last_kernel,
        out_shape=f32(*probe.shape),
        in_specs=[ANY, ANY, VMEM] + [ANY] * 4,
        out_specs=ANY,
        input_output_aliases={0: 0},
        scratch_shapes=[
            pltpu.VMEM((2, modes, 2, 16, 256), jnp.float32),
            pltpu.VMEM((2,) + parts[0].shape, jnp.float32),
            pltpu.VMEM((2,) + parts[1].shape, jnp.float32),
            pltpu.SemaphoreType.DMA((6,)),
        ],
        compiler_params=params(6),
        name="finish_rest",
    )(started, probe, peaks, *parts)


def shards(object_field, probe, measured, offsets):
    rows, cols = object_field.shape[1], object_field.shape[2]
    count = lax.axis_size("row")
    one, two = transform_blocks(probe.shape[-1])
    one, two = jnp.asarray(one), jnp.asarray(two)

    twins = [(i, i ^ 1) for i in range(count)]
    cores = [(0, 1), (1, 0)]
    down = [(i, i + 1) for i in range(count - 1)]
    up = [(i + 1, i) for i in range(count - 1)]
    outward = [(i, i + 2) for i in range(1, count - 2, 2)] + [(i, i - 2) for i in range(2, count, 2)]
    inward = [(b, a) for a, b in outward]
    forward = [
        (block + RING_ORDER[i], block + RING_ORDER[(i + 1) % RING])
        for block in range(0, count, RING)
        for i in range(RING)
    ]
    reverse = [(b, a) for a, b in forward]
    across_ring = [
        (block + RING_ORDER[i], block + RING_ORDER[(i + RING // 2) % RING])
        for block in range(0, count, RING)
        for i in range(RING)
    ]

    def across(x):
        return lax.ppermute(x, "col", cores)

    def send(x, pairs):
        return lax.ppermute(x, "row", pairs)

    other = across(object_field)
    above = send(offsets, down)
    below = send(offsets, up)
    pattern = send(measured, twins)
    power = probe_power(probe)

    (to_twin,) = cut_slices(("here",), offsets, offsets, offsets, object_field, other, offsets)
    mid_rows = send(to_twin, twins)
    to_beyond, own_rows = cut_slices(
        ("beyond", "twin"), offsets, above, below, object_field, other, power
    )
    far_rows = send(to_beyond, outward)

    mine, his0, his1, his2, fold_far, fold_mid, fold_own = position(
        above, below, far_rows, mid_rows, own_rows, probe, pattern[0], one, two
    )
    images = mine.shape[1]
    cut = images // 2 + 1
    theirs = [across(his0), across(his1), across(his2)]

    def share(leg):
        got = theirs[0][0] if leg == 0 else theirs[1][leg - 1] if leg < 3 else theirs[2][leg - 3]
        return mine[leg] + got

    mid_got = send(fold_mid, twins)
    far_got = send(fold_far, inward)

    farthest = share(0)
    ahead, behind = farthest[:cut], farthest[cut:]
    ahead, behind = send(ahead, forward), send(behind, reverse)
    ahead, behind, power, theirs[1] = lax.optimization_barrier((ahead, behind, power, theirs[1]))
    object_den, den_edge = weights(count, offsets, above, below, power, rows, cols)
    den_edge = across(den_edge)
    rest = [(0, 0), (0, 0)]
    ahead = share(1) + jnp.pad(ahead, [(0, images - cut)] + rest)
    behind = share(2) + jnp.pad(behind, [(cut, 0)] + rest)
    for leg in (3, 5, 7):
        ahead, behind = lax.optimization_barrier((ahead, behind))
        ahead, behind = send(ahead, forward), send(behind, reverse)
        if leg < 7:
            ahead, behind, mid_got, far_got = lax.optimization_barrier((ahead, behind, mid_got, far_got))
            ahead, behind = share(leg) + ahead, share(leg + 1) + behind
    message, maxima = close(ahead, behind, mine, theirs[2], object_den, den_edge)
    if count > RING:
        blocks = [[b * RING + i for b in range(count // RING)] for i in range(RING)]
        total = lax.psum(message[: 16 * images], "row", axis_index_groups=blocks)
        top = lax.pmax(message[16 * images :], "row", axis_index_groups=blocks)
        message = jnp.concatenate([total, top], axis=0)
        maxima = jnp.concatenate([jnp.full_like(top, jnp.max(total[0:16])), top], axis=0)

    opposite = send(maxima, across_ring)
    messages = [message]
    ahead = behind = message
    for hop in range(3):
        ahead, behind = send(ahead, forward), send(behind, reverse)
        ahead, behind = lax.optimization_barrier((ahead, behind))
        messages += [ahead, behind]
    ahead, behind = lax.optimization_barrier((ahead[: 16 * cut], behind[16 * cut :]))
    parts = [send(ahead, forward), send(behind, reverse)]
    messages += [across(x) for x in messages]
    parts += [across(x) for x in parts]

    mid_got, far_got, messages[8] = lax.optimization_barrier((mid_got, far_got, messages[8]))
    inner, edge = fold(offsets, above, below, fold_own, mid_got, far_got, rows, cols)
    new_object, started, peaks = finish(
        probe, object_field, inner, across(edge), object_den, den_edge, opposite, across(opposite), messages
    )
    return new_object, finish_rest(started, probe, peaks, parts)


def solution(mesh):
    placed = (
        P(None, ("groups", "row"), "col"),
        P("groups", None, None, None),
        P(("groups", "row", "col"), None, None),
        P(("groups", "row", "col"), None),
    )
    return jax.shard_map(
        shards,
        mesh=mesh,
        in_specs=placed,
        out_specs=(P(None, ("groups", "row"), "col"), P("groups", None, None, None)),
        check_vma=False,
    )
```

```python
import functools
import math

import jax
import jax.numpy as jnp
import ml_dtypes
import numpy as np
from jax import lax
from jax.experimental import pallas as pl
from jax.experimental.pallas import tpu as pltpu
from jax.sharding import PartitionSpec as P

REGULAR = 0.25
AMP_FLOOR = 2.0
RING = 8
RING_ORDER = (0, 1, 3, 5, 7, 6, 4, 2)
HOPS = (0, -1, 1, -2, 2, -3, 3, 4)

SMEM = pl.BlockSpec(memory_space=pltpu.SMEM)
VMEM = pl.BlockSpec(memory_space=pltpu.VMEM)
ANY = pl.BlockSpec(memory_space=pl.ANY)


def transform_blocks(length):
    indices = np.arange(length, dtype=np.int32)
    phases = indices[:, None] * indices[None, :] % length
    angles = phases.astype(np.float32) * np.float32(2.0 * math.pi / length)
    factor = np.float32(1.0 / math.sqrt(length))
    cos = (np.cos(angles) * factor).astype(ml_dtypes.bfloat16)
    sin = (-np.sin(angles) * factor).astype(ml_dtypes.bfloat16)
    one = np.block([[cos, -sin], [sin, cos]])
    return one, np.ascontiguousarray(one.T)


def ring_places(r):
    r = lax.rem(r, RING)
    place = jnp.where(r == 0, 0, jnp.where(lax.rem(r, 2) == 1, (r + 1) // 2, RING - r // 2))
    return place, (RING - place) & 7


def either(core, pair):
    return jnp.where(core == 0, pair[0], pair[1])


def params(mib):
    return pltpu.CompilerParams(vmem_limit_bytes=mib * 1024 * 1024)


def f32(*shape):
    return jax.ShapeDtypeStruct(shape, jnp.float32)


def begin(copies):
    for copy in copies:
        copy.start()
    return copies


def end(copies):
    for copy in copies:
        copy.wait()


def slices_kernel(offsets_at, *refs):
    offsets, (block, other, _), outs, (ext, cuts, sems) = refs[:3], refs[3:6], refs[6:-3], refs[-3:]
    odd = lax.rem(lax.axis_index("row"), 2) == 1
    core = lax.axis_index("col")
    cols = block.shape[2]
    end_of = cols + 128
    source = pl.multiple_of(core * (cols - 128), 128)
    target = pl.multiple_of((1 - core) * end_of, 128)
    blank = pl.multiple_of(core * end_of, 128)
    copies = begin(
        (
            pltpu.make_async_copy(block, ext.at[:, :, 128:end_of], sems.at[0]),
            pltpu.make_async_copy(
                other.at[:, :, pl.ds(source, 128)], ext.at[:, :, pl.ds(target, 128)], sems.at[1]
            ),
        )
    )
    ext[:, :, pl.ds(blank, 128)] = jnp.zeros((2, block.shape[1], 128), jnp.float32)
    end(copies)
    here, above, below = offsets[0][0, 1], offsets[1][0, 1], offsets[2][0, 1]
    columns = {
        "here": here,
        "twin": jnp.where(odd, above, below),
        "beyond": jnp.where(odd, below, above),
    }
    copies = ()
    for number, (which, out) in enumerate(zip(offsets_at, outs)):
        start = columns[which]
        base = pl.multiple_of(start // 128 * 128, 128)
        for part in range(2):
            wide = ext[part, :, pl.ds(base, 384)]
            wide = pltpu.roll(wide, (384 - start % 128) % 384, 1)
            cuts[number, part] = wide[:, 0:256]
        copies += begin((pltpu.make_async_copy(cuts.at[number], out, sems.at[2 + number]),))
    end(copies)


def cut_slices(offsets_at, here, above, below, block, other, ordered):
    rows, cols = block.shape[1], block.shape[2]
    count = len(offsets_at)
    return pl.pallas_call(
        functools.partial(slices_kernel, offsets_at),
        out_shape=(f32(2, rows, 256),) * count,
        in_specs=[SMEM] * 3 + [ANY] * 3,
        out_specs=(ANY,) * count,
        scratch_shapes=[
            pltpu.VMEM((2, rows, cols + 256), jnp.float32),
            pltpu.VMEM((count, 2, rows, 256), jnp.float32),
            pltpu.SemaphoreType.DMA((4,)),
        ],
        compiler_params=params(6),
        name="cut_slices",
    )(here, above, below, block, other, ordered)


def power_kernel(probe, out, held, sems):
    modes = probe.shape[0]
    copies = begin([pltpu.make_async_copy(probe.at[m], held.at[m], sems.at[m]) for m in range(modes)])
    for m in range(modes):
        copies[m].wait()
        power = held[m, 0] * held[m, 0] + held[m, 1] * held[m, 1]
        out[...] = power if m == 0 else out[...] + power


def probe_power(probe):
    return pl.pallas_call(
        power_kernel,
        out_shape=f32(*probe.shape[2:]),
        in_specs=[ANY],
        out_specs=VMEM,
        scratch_shapes=[pltpu.VMEM(probe.shape, jnp.float32), pltpu.SemaphoreType.DMA((probe.shape[0],))],
        compiler_params=params(8),
        name="probe_power",
    )(probe)


def weights_kernel(count, here, above, below, power, inner, edge, frame, grid):
    r = lax.axis_index("row")
    present = ((r > 0).astype(jnp.float32), None, (r < count - 1).astype(jnp.float32))
    tall = jnp.concatenate([power[...], jnp.zeros((128, 256), jnp.float32)], axis=0)
    grid[...] = jnp.zeros(grid.shape, jnp.float32)
    for number, spot in enumerate((above, here, below)):
        row, col = spot[0, 0], spot[0, 1]
        frame[...] = pltpu.roll(tall, row, 0)
        lower = 128 * (2 - number)
        piece = frame[lower : lower + 128, :]
        if present[number] is not None:
            piece = piece * present[number]
        wide = jnp.concatenate([piece, jnp.zeros((128, 128), jnp.float32)], axis=1)
        base = pl.multiple_of(col // 128 * 128, 128)
        grid[:, pl.ds(base, 384)] += pltpu.roll(wide, col % 128, 1)
    size = grid.shape[1]
    inner[...] = grid[:, 128 : size - 128]
    edge[...] = jnp.where(lax.axis_index("col") == 0, grid[:, size - 128 :], grid[:, 0:128])


def weights(count, here, above, below, power, rows, cols):
    return pl.pallas_call(
        functools.partial(weights_kernel, count),
        out_shape=(f32(rows, cols), f32(rows, 128)),
        in_specs=[SMEM] * 3 + [VMEM],
        out_specs=(VMEM, VMEM),
        scratch_shapes=[
            pltpu.VMEM((384, 256), jnp.float32),
            pltpu.VMEM((rows, cols + 256), jnp.float32),
        ],
        compiler_params=params(6),
        name="object_weights",
    )(here, above, below, power)


def position_kernel(
    above, below, far_rows, mid_rows, own_rows, probe_at, pattern_at, one_at, two_at,
    mine, his0, his1, his2, fold_far, fold_mid, fold_own,
    probe, pattern, one, two, stack, window, far, terms, update, strength, sems, probe_sems, out_sems,
):
    modes = probe.shape[0]
    r = lax.axis_index("row")
    core = lax.axis_index("col")
    odd = lax.rem(r, 2)
    row = jnp.where(odd == 1, above[0, 0], below[0, 0])
    places = ring_places(r)
    far_at = pl.multiple_of(256 * (1 - odd), 128)
    own_at = pl.multiple_of(256 * odd, 128)

    def load(source, target, number):
        return pltpu.make_async_copy(source, target, sems.at[number])

    rows_in = begin(
        (
            load(far_rows, stack.at[:, pl.ds(far_at, 128), :], 0),
            load(mid_rows, stack.at[:, 128:256, :], 1),
            load(own_rows, stack.at[:, pl.ds(own_at, 128), :], 2),
        )
    )
    tables_in = begin((load(one_at, one, 3), load(two_at, two, 4)))
    probe_in = begin(
        [pltpu.make_async_copy(probe_at.at[m], probe.at[m], probe_sems.at[m]) for m in range(modes)]
    )
    pattern_in = begin((load(pattern_at, pattern, 5),))
    end(rows_in)
    for part in range(2):
        window[part] = pltpu.roll(stack[part], (384 - row) % 384, 0)[0:256]
    end(tables_in)

    def exit_wave(m):
        p_re, p_im = probe[m, 0], probe[m, 1]
        w_re, w_im = window[0], window[1]
        return p_re * w_re - p_im * w_im, p_re * w_im + p_im * w_re

    for m in range(modes):
        probe_in[m].wait()
        e_re, e_im = exit_wave(m)
        field = jnp.concatenate([e_re.astype(jnp.bfloat16), e_im.astype(jnp.bfloat16)], axis=0)
        half = jnp.dot(one[...], field, preferred_element_type=jnp.float32).astype(jnp.bfloat16)
        half = jnp.concatenate([half[0:256], half[256:512]], axis=1)
        out = jnp.dot(half, two[...], preferred_element_type=jnp.float32)
        far[m] = out
        power = out[:, 0:256] * out[:, 0:256] + out[:, 256:512] * out[:, 256:512]
        strength[...] = power if m == 0 else strength[...] + power

    end(pattern_in)
    strength[...] = jnp.sqrt(pattern[...]) / jnp.maximum(jnp.sqrt(strength[...]), AMP_FLOOR)

    def put(image, value):
        for slab in range(16):
            ahead = (slab - places[slab // 8]) & 7
            spot = jnp.where(ahead < 4, 7 - 2 * ahead, 2 * (ahead - 4))
            terms[(slab // 8) ^ core, spot, image] = value[16 * slab : 16 * slab + 16]

    def give(low, high, at):
        images = pl.ds(low, high - low)
        return begin(
            (
                pltpu.make_async_copy(terms.at[1, 0:1, images], his0.at[:, images], out_sems.at[at]),
                pltpu.make_async_copy(terms.at[1, 1:3, images], his1.at[:, images], out_sems.at[at + 1]),
                pltpu.make_async_copy(terms.at[1, 3:8, images], his2.at[:, images], out_sems.at[at + 2]),
                pltpu.make_async_copy(terms.at[0, :, images], mine.at[:, images], out_sems.at[at + 3]),
            )
        )

    put(0, window[0] * window[0] + window[1] * window[1])
    given, copies = 0, ()
    for m in range(modes):
        ratio = strength[...]
        fixed = jnp.concatenate(
            [
                (far[m, :, 0:256] * ratio).astype(jnp.bfloat16),
                (far[m, :, 256:512] * ratio).astype(jnp.bfloat16),
            ],
            axis=0,
        )
        back = jnp.dot(two[...], fixed, preferred_element_type=jnp.float32).astype(jnp.bfloat16)
        back = jnp.concatenate([back[0:256], back[256:512]], axis=1)
        near = jnp.dot(back, one[...], preferred_element_type=jnp.float32)
        e_re, e_im = exit_wave(m)
        d_re = near[:, 0:256] - e_re
        d_im = near[:, 256:512] - e_im
        p_re, p_im = probe[m, 0], probe[m, 1]
        w_re, w_im = window[0], window[1]
        u_re = p_re * d_re + p_im * d_im
        u_im = p_re * d_im - p_im * d_re
        update[0] = u_re if m == 0 else update[0] + u_re
        update[1] = u_im if m == 0 else update[1] + u_im
        put(1 + 2 * m, w_re * d_re + w_im * d_im)
        put(2 + 2 * m, w_re * d_im - w_im * d_re)
        if m % 2 == 1:
            copies += give(given, 3 + 2 * m, 2 * (m - 1))
            given = 3 + 2 * m

    for part in range(2):
        tall = jnp.concatenate([update[part], jnp.zeros((128, 256), jnp.float32)], axis=0)
        stack[part] = pltpu.roll(tall, row, 0)
    copies += begin(
        (
            load(stack.at[:, pl.ds(far_at, 128), :], fold_far, 0),
            load(stack.at[:, 128:256, :], fold_mid, 1),
            load(stack.at[:, pl.ds(own_at, 128), :], fold_own, 2),
        )
    )
    end(copies)


def position(above, below, far_rows, mid_rows, own_rows, probe, pattern, one, two):
    modes = probe.shape[0]
    images = 1 + 2 * modes
    return pl.pallas_call(
        position_kernel,
        out_shape=tuple(f32(legs, images, 16, 256) for legs in (8, 1, 2, 5)) + (f32(2, 128, 256),) * 3,
        in_specs=[SMEM] * 2 + [ANY] * 7,
        out_specs=(ANY,) * 7,
        scratch_shapes=[
            pltpu.VMEM(probe.shape, jnp.float32),
            pltpu.VMEM((256, 256), jnp.float32),
            pltpu.VMEM(one.shape, jnp.bfloat16),
            pltpu.VMEM(two.shape, jnp.bfloat16),
            pltpu.VMEM((2, 384, 256), jnp.float32),
            pltpu.VMEM((2, 256, 256), jnp.float32),
            pltpu.VMEM((modes, 256, 512), jnp.float32),
            pltpu.VMEM((2, 8, images, 16, 256), jnp.float32),
            pltpu.VMEM((2, 256, 256), jnp.float32),
            pltpu.VMEM((256, 256), jnp.float32),
            pltpu.SemaphoreType.DMA((6,)),
            pltpu.SemaphoreType.DMA((modes,)),
            pltpu.SemaphoreType.DMA((2 * modes,)),
        ],
        compiler_params=params(32),
        name="position_terms",
    )(above, below, far_rows, mid_rows, own_rows, probe, pattern, one, two)


def fold_kernel(here_at, above_at, below_at, near, middle, far, inner, edge, grid):
    odd = lax.rem(lax.axis_index("row"), 2) == 1
    grid[...] = jnp.zeros(grid.shape, jnp.float32)
    near_col = jnp.where(odd, above_at[0, 1], below_at[0, 1])
    far_col = jnp.where(odd, below_at[0, 1], above_at[0, 1])
    for col, piece in ((near_col, near), (here_at[0, 1], middle), (far_col, far)):
        base = pl.multiple_of(col // 128 * 128, 128)
        for part in range(2):
            wide = jnp.concatenate([piece[part], jnp.zeros((128, 128), jnp.float32)], axis=1)
            grid[part, :, pl.ds(base, 384)] += pltpu.roll(wide, col % 128, 1)
    size = grid.shape[2]
    inner[...] = grid[:, :, 128 : size - 128]
    edge[...] = jnp.where(lax.axis_index("col") == 0, grid[:, :, size - 128 :], grid[:, :, 0:128])


def fold(here, above, below, near, middle, far, rows, cols):
    return pl.pallas_call(
        fold_kernel,
        out_shape=(f32(2, rows, cols), f32(2, rows, 128)),
        in_specs=[SMEM] * 3 + [VMEM] * 3,
        out_specs=(VMEM, VMEM),
        scratch_shapes=[pltpu.VMEM((2, rows, cols + 256), jnp.float32)],
        compiler_params=params(8),
        name="fold_object",
    )(here, above, below, near, middle, far)


def close_kernel(ahead_at, behind_at, mine_at, theirs_at, den_at, edge_at, message, maxima, ahead, behind, mine, theirs, den, edge, sems):
    pairs = (
        (den_at, den), (edge_at, edge),
        (ahead_at, ahead), (behind_at, behind),
        (mine_at.at[mine_at.shape[0] - 1], mine), (theirs_at.at[theirs_at.shape[0] - 1], theirs),
    )
    copies = begin([pltpu.make_async_copy(a, b, sems.at[n]) for n, (a, b) in enumerate(pairs)])
    end(copies[:2])
    cols = den.shape[1]
    side = pl.multiple_of((1 - lax.axis_index("col")) * (cols - 128), 128)
    den[:, pl.ds(side, 128)] += edge[...]
    object_peak = jnp.max(den[...])
    end(copies[2:])
    images = ahead.shape[0]
    for image in range(images):
        total = (mine[image] + theirs[image]) + (ahead[image] + behind[image])
        message[16 * image : 16 * image + 16] = total
        if image == 0:
            maxima[0:8] = jnp.full((8, 256), jnp.max(total), jnp.float32)
    message[16 * images :] = jnp.full((8, 256), object_peak, jnp.float32)
    maxima[8:16] = jnp.full((8, 256), object_peak, jnp.float32)


def close(ahead, behind, mine, theirs, den, edge):
    shape = ahead.shape
    return pl.pallas_call(
        close_kernel,
        out_shape=(f32(16 * shape[0] + 8, 256), f32(16, 256)),
        in_specs=[ANY] * 6,
        out_specs=(VMEM, VMEM),
        scratch_shapes=[pltpu.VMEM(shape, jnp.float32)] * 4
        + [
            pltpu.VMEM(den.shape, jnp.float32),
            pltpu.VMEM(edge.shape, jnp.float32),
            pltpu.SemaphoreType.DMA((6,)),
        ],
        compiler_params=params(6),
        name="close_sum",
    )(ahead, behind, mine, theirs, den, edge)


def finish_kernel(probe_at, block_at, inner_at, edge_at, den_at, den_edge_at, opposite, opposite_twin, *refs):
    number = 2 * (len(HOPS) - 1)
    messages, refs = refs[:number], refs[number:]
    new_block_at, new_probe_at, peaks, probe, block, inner, edge, den, den_edge, new_probe, held = refs[:11]
    sems, out_sems = refs[11:]
    modes = probe.shape[0]
    core = lax.axis_index("col")
    places = ring_places(lax.axis_index("row"))
    cols = block.shape[2]
    pairs = [(messages[n], held.at[n]) for n in range(number)]
    pairs += [(probe_at.at[m], probe.at[m]) for m in range(modes)]
    pairs += [(block_at, block), (inner_at, inner), (edge_at, edge), (den_at, den), (den_edge_at, den_edge)]
    copies = begin([pltpu.make_async_copy(a, b, sems.at[n]) for n, (a, b) in enumerate(pairs)])
    end(copies[:number])
    peak = jnp.maximum(opposite[0:8], opposite_twin[0:8])
    object_peak = jnp.maximum(opposite[8:16], opposite_twin[8:16])
    for n in range(number):
        peak = jnp.maximum(peak, jnp.maximum(held[n, 0:8], held[n, 8:16]))
        object_peak = jnp.maximum(object_peak, held[n, held.shape[1] - 8 :])
    peak = jnp.max(peak)
    object_peak = jnp.max(object_peak)
    peaks[...] = jnp.full((8, 128), peak, jnp.float32)
    scales, starts = [], []
    for n in range(number):
        half = core if n < number // 2 else 1 - core
        place = either(half, places)
        starts.append(pl.multiple_of(128 * half + 16 * ((place + HOPS[n % (number // 2)]) & 7), 16))
        held[n, 0:16] = 1.0 / ((1.0 - REGULAR) * held[n, 0:16] + REGULAR * peak)
    outs = ()
    for m in range(modes):
        copies[number + m].wait()
        for part in range(2):
            at = 16 * (1 + 2 * m + part)
            for n in range(number):
                rows = pl.ds(starts[n], 16)
                new_probe[m, part, rows, :] = probe[m, part, rows, :] + held[n, at : at + 16] * held[n, 0:16]
            for half in range(2):
                rows = pl.ds(pl.multiple_of(128 * half + 16 * ((places[half] + 4) & 7), 16), 16)
                new_probe[m, part, rows, :] = probe[m, part, rows, :]
        outs += begin((pltpu.make_async_copy(new_probe.at[m], new_probe_at.at[m], out_sems.at[m]),))
    end(copies[number + modes :])
    side = pl.multiple_of((1 - core) * (cols - 128), 128)
    inner[:, :, pl.ds(side, 128)] += edge[...]
    den[:, pl.ds(side, 128)] += den_edge[...]
    scale = 1.0 / ((1.0 - REGULAR) * den[...] + REGULAR * object_peak)
    for part in range(2):
        block[part] = block[part] + inner[part] * scale
    outs += begin((pltpu.make_async_copy(block, new_block_at, out_sems.at[modes]),))
    end(outs)


def finish(probe, block, inner, edge, den, den_edge, opposite, opposite_twin, messages):
    modes = probe.shape[0]
    number = len(messages)
    return pl.pallas_call(
        finish_kernel,
        out_shape=(f32(*block.shape), f32(*probe.shape), f32(8, 128)),
        in_specs=[ANY] * 6 + [VMEM] * 2 + [ANY] * number,
        out_specs=(ANY, ANY, VMEM),
        scratch_shapes=[
            pltpu.VMEM(x.shape, jnp.float32) for x in (probe, block, inner, edge, den, den_edge, probe)
        ]
        + [
            pltpu.VMEM((number,) + messages[0].shape, jnp.float32),
            pltpu.SemaphoreType.DMA((number + modes + 5,)),
            pltpu.SemaphoreType.DMA((modes + 1,)),
        ],
        compiler_params=params(24),
        name="finish_most",
    )(probe, block, inner, edge, den, den_edge, opposite, opposite_twin, *messages)


def last_kernel(started, probe_at, peaks, low_at, high_at, low_twin_at, high_twin_at, out_at, probe, low, high, sems):
    del started
    modes = probe.shape[1]
    cut = low.shape[1]
    core = lax.axis_index("col")
    places = ring_places(lax.axis_index("row"))
    peak = jnp.max(peaks[...])
    rows = []
    pairs = [(low_at, low.at[0]), (high_at, high.at[0]), (low_twin_at, low.at[1]), (high_twin_at, high.at[1])]
    for owner in range(2):
        half = core if owner == 0 else 1 - core
        rows.append(pl.ds(pl.multiple_of(128 * half + 16 * ((either(half, places) + 4) & 7), 16), 16))
        pairs.append((probe_at.at[:, :, rows[owner], :], probe.at[owner]))
    end(begin([pltpu.make_async_copy(a, b, sems.at[n]) for n, (a, b) in enumerate(pairs)]))
    outs = ()
    for owner in range(2):
        scale = 1.0 / ((1.0 - REGULAR) * low[owner, 0:16] + REGULAR * peak)
        for m in range(modes):
            for part in range(2):
                at = 16 * (1 + 2 * m + part)
                value = low[owner, at : at + 16] if at < cut else high[owner, at - cut : at - cut + 16]
                probe[owner, m, part] = probe[owner, m, part] + value * scale
        outs += begin((pltpu.make_async_copy(probe.at[owner], out_at.at[:, :, rows[owner], :], sems.at[owner]),))
    end(outs)


def finish_rest(started, probe, peaks, parts):
    modes = probe.shape[0]
    return pl.pallas_call(
        last_kernel,
        out_shape=f32(*probe.shape),
        in_specs=[ANY, ANY, VMEM] + [ANY] * 4,
        out_specs=ANY,
        input_output_aliases={0: 0},
        scratch_shapes=[
            pltpu.VMEM((2, modes, 2, 16, 256), jnp.float32),
            pltpu.VMEM((2,) + parts[0].shape, jnp.float32),
            pltpu.VMEM((2,) + parts[1].shape, jnp.float32),
            pltpu.SemaphoreType.DMA((6,)),
        ],
        compiler_params=params(6),
        name="finish_rest",
    )(started, probe, peaks, *parts)


def shards(object_field, probe, measured, offsets):
    rows, cols = object_field.shape[1], object_field.shape[2]
    count = lax.axis_size("row")
    one, two = transform_blocks(probe.shape[-1])
    one, two = jnp.asarray(one), jnp.asarray(two)

    twins = [(i, i ^ 1) for i in range(count)]
    cores = [(0, 1), (1, 0)]
    down = [(i, i + 1) for i in range(count - 1)]
    up = [(i + 1, i) for i in range(count - 1)]
    outward = [(i, i + 2) for i in range(1, count - 2, 2)] + [(i, i - 2) for i in range(2, count, 2)]
    inward = [(b, a) for a, b in outward]
    steps = [
        (block + RING_ORDER[i], block + RING_ORDER[(i + 1) % RING])
        for block in range(0, count, RING)
        for i in range(RING)
    ]
    forward = [(2 * a, 2 * b) for a, b in steps] + [(2 * b + 1, 2 * a + 1) for a, b in steps]
    reverse = [(b, a) for a, b in forward]
    across_ring = [
        (block + RING_ORDER[i], block + RING_ORDER[(i + RING // 2) % RING])
        for block in range(0, count, RING)
        for i in range(RING)
    ]

    def across(x):
        return lax.ppermute(x, "col", cores)

    def send(x, pairs):
        return lax.ppermute(x, "row", pairs)

    def turn(x, pairs):
        return lax.ppermute(x, ("row", "col"), pairs)

    def after(x, y):
        return lax.optimization_barrier((x, y))[0]

    other = across(object_field)
    above = send(offsets, down)
    below = send(offsets, up)
    pattern = send(measured, twins)

    (to_twin,) = cut_slices(("here",), offsets, offsets, offsets, object_field, other, offsets)
    mid_rows = send(to_twin, twins)
    to_beyond, own_rows = cut_slices(
        ("beyond", "twin"), offsets, above, below, object_field, other, to_twin
    )
    far_rows = send(to_beyond, outward)
    power = probe_power(after(probe, own_rows))

    mine, his0, his1, his2, fold_far, fold_mid, fold_own = position(
        above, below, far_rows, after(mid_rows, power), own_rows, probe, pattern[0], one, two
    )
    images = mine.shape[1]
    cut = images // 2 + 1
    theirs = [across(his0), across(his1), across(his2)]

    def share(leg):
        got = theirs[0][0] if leg == 0 else theirs[1][leg - 1] if leg < 3 else theirs[2][leg - 3]
        return mine[leg] + got

    mid_got = send(fold_mid, twins)
    far_got = send(fold_far, inward)

    farthest = share(0)
    ahead, behind = turn(farthest[:cut], forward), turn(farthest[cut:], reverse)
    behind, power, theirs[1] = lax.optimization_barrier((behind, power, theirs[1]))
    object_den, den_edge = weights(count, offsets, above, below, power, rows, cols)
    den_edge = across(den_edge)
    rest = [(0, 0), (0, 0)]
    ahead = jnp.pad(ahead, [(0, images - cut)] + rest)
    behind = jnp.pad(behind, [(cut, 0)] + rest)
    for leg in (1, 3, 5):
        onward = share(leg) + ahead
        ahead = turn(onward, forward)
        onward = share(leg + 1) + after(behind, onward)
        behind = turn(onward, reverse)
        ahead = after(ahead, onward)
        if leg == 3:
            ahead, mid_got, far_got = lax.optimization_barrier((ahead, mid_got, far_got))
    message, maxima = close(ahead, behind, mine, theirs[2], object_den, den_edge)
    if count > RING:
        blocks = [[b * RING + i for b in range(count // RING)] for i in range(RING)]
        total = lax.psum(message[: 16 * images], "row", axis_index_groups=blocks)
        top = lax.pmax(message[16 * images :], "row", axis_index_groups=blocks)
        message = jnp.concatenate([total, top], axis=0)
        maxima = jnp.concatenate([jnp.full_like(top, jnp.max(total[0:16])), top], axis=0)

    opposite = send(maxima, across_ring)
    messages = [message]
    ahead, behind = turn(message, forward), turn(message, reverse)
    ahead, opposite = lax.optimization_barrier((ahead, opposite))
    inner, edge = fold(offsets, above, below, fold_own, mid_got, far_got, rows, cols)
    edge = across(edge)
    for hop in range(2):
        messages += [ahead, behind]
        behind = after(behind, ahead)
        if hop == 1:
            ahead, edge, inner = lax.optimization_barrier((ahead, edge, inner))
        ahead = turn(ahead, forward)
        ahead = after(ahead, behind)
        behind = turn(behind, reverse)
    messages += [ahead, behind]
    parts = [turn(ahead[: 16 * cut], forward), turn(after(behind, ahead)[16 * cut :], reverse)]
    messages += [across(x) for x in messages]

    new_object, started, peaks = finish(
        probe, object_field, inner, edge, object_den, den_edge, opposite, across(opposite), messages
    )
    parts = [after(x, peaks) for x in parts]
    parts += [across(x) for x in parts]
    return new_object, finish_rest(started, probe, peaks, parts)


def solution(mesh):
    placed = (
        P(None, ("groups", "row"), "col"),
        P("groups", None, None, None),
        P(("groups", "row", "col"), None, None),
        P(("groups", "row", "col"), None),
    )
    return jax.shard_map(
        shards,
        mesh=mesh,
        in_specs=placed,
        out_specs=(P(None, ("groups", "row"), "col"), P("groups", None, None, None)),
        check_vma=False,
    )
```

```python
import functools
import math

import jax
import jax.numpy as jnp
import ml_dtypes
import numpy as np
from jax import lax
from jax.experimental import pallas as pl
from jax.experimental.pallas import tpu as pltpu
from jax.sharding import PartitionSpec as P

REGULAR = 0.25
AMP_FLOOR = 2.0
RING = 8
RING_ORDER = (0, 1, 3, 5, 7, 6, 4, 2)
HOPS = (0, -1, 1, -2, 2, -3, 3, 4)

SMEM = pl.BlockSpec(memory_space=pltpu.SMEM)
VMEM = pl.BlockSpec(memory_space=pltpu.VMEM)
ANY = pl.BlockSpec(memory_space=pl.ANY)


def transform_blocks(length):
    indices = np.arange(length, dtype=np.int32)
    phases = indices[:, None] * indices[None, :] % length
    angles = phases.astype(np.float32) * np.float32(2.0 * math.pi / length)
    factor = np.float32(1.0 / math.sqrt(length))
    cos = (np.cos(angles) * factor).astype(ml_dtypes.bfloat16)
    sin = (-np.sin(angles) * factor).astype(ml_dtypes.bfloat16)
    one = np.block([[cos, -sin], [sin, cos]])
    return one, np.ascontiguousarray(one.T)


def ring_place(r):
    r = lax.rem(r, RING)
    return jnp.where(r == 0, 0, jnp.where(lax.rem(r, 2) == 1, (r + 1) // 2, RING - r // 2))


def params(mib):
    return pltpu.CompilerParams(vmem_limit_bytes=mib * 1024 * 1024)


def f32(*shape):
    return jax.ShapeDtypeStruct(shape, jnp.float32)


def begin(copies):
    for copy in copies:
        copy.start()
    return copies


def end(copies):
    for copy in copies:
        copy.wait()


def slices_kernel(offsets_at, *refs):
    offsets, (block, other, _), outs, (ext, cuts, sems) = refs[:3], refs[3:6], refs[6:-3], refs[-3:]
    odd = lax.rem(lax.axis_index("row"), 2) == 1
    core = lax.axis_index("col")
    cols = block.shape[2]
    end_of = cols + 128
    source = pl.multiple_of(core * (cols - 128), 128)
    target = pl.multiple_of((1 - core) * end_of, 128)
    blank = pl.multiple_of(core * end_of, 128)
    copies = begin(
        (
            pltpu.make_async_copy(block, ext.at[:, :, 128:end_of], sems.at[0]),
            pltpu.make_async_copy(
                other.at[:, :, pl.ds(source, 128)], ext.at[:, :, pl.ds(target, 128)], sems.at[1]
            ),
        )
    )
    ext[:, :, pl.ds(blank, 128)] = jnp.zeros((2, block.shape[1], 128), jnp.float32)
    end(copies)
    here, above, below = offsets[0][0, 1], offsets[1][0, 1], offsets[2][0, 1]
    columns = {
        "here": here,
        "twin": jnp.where(odd, above, below),
        "beyond": jnp.where(odd, below, above),
    }
    copies = ()
    for number, (which, out) in enumerate(zip(offsets_at, outs)):
        start = columns[which]
        base = pl.multiple_of(start // 128 * 128, 128)
        for part in range(2):
            wide = ext[part, :, pl.ds(base, 384)]
            wide = pltpu.roll(wide, (384 - start % 128) % 384, 1)
            cuts[number, part] = wide[:, 0:256]
        copies += begin((pltpu.make_async_copy(cuts.at[number], out, sems.at[2 + number]),))
    end(copies)


def cut_slices(offsets_at, here, above, below, block, other, ordered):
    rows, cols = block.shape[1], block.shape[2]
    count = len(offsets_at)
    return pl.pallas_call(
        functools.partial(slices_kernel, offsets_at),
        out_shape=(f32(2, rows, 256),) * count,
        in_specs=[SMEM] * 3 + [ANY] * 3,
        out_specs=(ANY,) * count,
        scratch_shapes=[
            pltpu.VMEM((2, rows, cols + 256), jnp.float32),
            pltpu.VMEM((count, 2, rows, 256), jnp.float32),
            pltpu.SemaphoreType.DMA((4,)),
        ],
        compiler_params=params(6),
        name="cut_slices",
    )(here, above, below, block, other, ordered)


def power_kernel(probe, out, held, sems):
    modes = probe.shape[0]
    copies = begin([pltpu.make_async_copy(probe.at[m], held.at[m], sems.at[m]) for m in range(modes)])
    for m in range(modes):
        copies[m].wait()
        power = held[m, 0] * held[m, 0] + held[m, 1] * held[m, 1]
        out[...] = power if m == 0 else out[...] + power


def probe_power(probe):
    return pl.pallas_call(
        power_kernel,
        out_shape=f32(*probe.shape[2:]),
        in_specs=[ANY],
        out_specs=VMEM,
        scratch_shapes=[pltpu.VMEM(probe.shape, jnp.float32), pltpu.SemaphoreType.DMA((probe.shape[0],))],
        compiler_params=params(8),
        name="probe_power",
    )(probe)


def weights_kernel(count, here, above, below, power, inner, edge, frame, grid):
    r = lax.axis_index("row")
    present = ((r > 0).astype(jnp.float32), None, (r < count - 1).astype(jnp.float32))
    tall = jnp.concatenate([power[...], jnp.zeros((128, 256), jnp.float32)], axis=0)
    grid[...] = jnp.zeros(grid.shape, jnp.float32)
    for number, spot in enumerate((above, here, below)):
        row, col = spot[0, 0], spot[0, 1]
        frame[...] = pltpu.roll(tall, row, 0)
        lower = 128 * (2 - number)
        piece = frame[lower : lower + 128, :]
        if present[number] is not None:
            piece = piece * present[number]
        wide = jnp.concatenate([piece, jnp.zeros((128, 128), jnp.float32)], axis=1)
        base = pl.multiple_of(col // 128 * 128, 128)
        grid[:, pl.ds(base, 384)] += pltpu.roll(wide, col % 128, 1)
    size = grid.shape[1]
    inner[...] = grid[:, 128 : size - 128]
    edge[...] = jnp.where(lax.axis_index("col") == 0, grid[:, size - 128 :], grid[:, 0:128])


def weights(count, here, above, below, power, rows, cols):
    return pl.pallas_call(
        functools.partial(weights_kernel, count),
        out_shape=(f32(rows, cols), f32(rows, 128)),
        in_specs=[SMEM] * 3 + [VMEM],
        out_specs=(VMEM, VMEM),
        scratch_shapes=[
            pltpu.VMEM((384, 256), jnp.float32),
            pltpu.VMEM((rows, cols + 256), jnp.float32),
        ],
        compiler_params=params(6),
        name="object_weights",
    )(here, above, below, power)


def position_kernel(
    above, below, far_rows, mid_rows, own_rows, probe_at, pattern_at, one_at, two_at,
    mine, his0, his1, his2, fold_far, fold_mid, fold_own,
    probe, pattern, one, two, stack, window, far, terms, update, strength, sems, probe_sems, out_sems,
):
    modes = probe.shape[0]
    r = lax.axis_index("row")
    core = lax.axis_index("col")
    odd = lax.rem(r, 2)
    row = jnp.where(odd == 1, above[0, 0], below[0, 0])
    place = ring_place(r)
    far_at = pl.multiple_of(256 * (1 - odd), 128)
    own_at = pl.multiple_of(256 * odd, 128)

    def load(source, target, number):
        return pltpu.make_async_copy(source, target, sems.at[number])

    rows_in = begin(
        (
            load(far_rows, stack.at[:, pl.ds(far_at, 128), :], 0),
            load(mid_rows, stack.at[:, 128:256, :], 1),
            load(own_rows, stack.at[:, pl.ds(own_at, 128), :], 2),
        )
    )
    tables_in = begin((load(one_at, one, 3), load(two_at, two, 4)))
    probe_in = begin(
        [pltpu.make_async_copy(probe_at.at[m], probe.at[m], probe_sems.at[m]) for m in range(modes)]
    )
    pattern_in = begin((load(pattern_at, pattern, 5),))
    end(rows_in)
    for part in range(2):
        window[part] = pltpu.roll(stack[part], (384 - row) % 384, 0)[0:256]
    end(tables_in)

    def exit_wave(m):
        p_re, p_im = probe[m, 0], probe[m, 1]
        w_re, w_im = window[0], window[1]
        return p_re * w_re - p_im * w_im, p_re * w_im + p_im * w_re

    end(probe_in)
    for m in range(modes):
        e_re, e_im = exit_wave(m)
        field = jnp.concatenate([e_re.astype(jnp.bfloat16), e_im.astype(jnp.bfloat16)], axis=0)
        half = jnp.dot(one[...], field, preferred_element_type=jnp.float32).astype(jnp.bfloat16)
        half = jnp.concatenate([half[0:256], half[256:512]], axis=1)
        out = jnp.dot(half, two[...], preferred_element_type=jnp.float32)
        far[m] = out
        power = out[:, 0:256] * out[:, 0:256] + out[:, 256:512] * out[:, 256:512]
        strength[...] = power if m == 0 else strength[...] + power

    end(pattern_in)
    strength[...] = jnp.sqrt(pattern[...]) / jnp.maximum(jnp.sqrt(strength[...]), AMP_FLOOR)

    def put(image, value):
        for slab in range(16):
            ahead = (slab - place) & 7
            spot = jnp.where(ahead < 4, 7 - 2 * ahead, 2 * (ahead - 4))
            terms[(slab // 8) ^ core, spot, image] = value[16 * slab : 16 * slab + 16]

    def give(low, high, at):
        images = pl.ds(low, high - low)
        return begin(
            (
                pltpu.make_async_copy(terms.at[1, 0:1, images], his0.at[:, images], out_sems.at[at]),
                pltpu.make_async_copy(terms.at[1, 1:3, images], his1.at[:, images], out_sems.at[at + 1]),
                pltpu.make_async_copy(terms.at[1, 3:8, images], his2.at[:, images], out_sems.at[at + 2]),
                pltpu.make_async_copy(terms.at[0, :, images], mine.at[:, images], out_sems.at[at + 3]),
            )
        )

    put(0, window[0] * window[0] + window[1] * window[1])
    given, copies = 0, ()
    for m in range(modes):
        ratio = strength[...]
        fixed = jnp.concatenate(
            [
                (far[m, :, 0:256] * ratio).astype(jnp.bfloat16),
                (far[m, :, 256:512] * ratio).astype(jnp.bfloat16),
            ],
            axis=0,
        )
        back = jnp.dot(two[...], fixed, preferred_element_type=jnp.float32).astype(jnp.bfloat16)
        back = jnp.concatenate([back[0:256], back[256:512]], axis=1)
        near = jnp.dot(back, one[...], preferred_element_type=jnp.float32)
        e_re, e_im = exit_wave(m)
        d_re = near[:, 0:256] - e_re
        d_im = near[:, 256:512] - e_im
        p_re, p_im = probe[m, 0], probe[m, 1]
        w_re, w_im = window[0], window[1]
        u_re = p_re * d_re + p_im * d_im
        u_im = p_re * d_im - p_im * d_re
        update[0] = u_re if m == 0 else update[0] + u_re
        update[1] = u_im if m == 0 else update[1] + u_im
        put(1 + 2 * m, w_re * d_re + w_im * d_im)
        put(2 + 2 * m, w_re * d_im - w_im * d_re)
        if m % 2 == 1:
            copies += give(given, 3 + 2 * m, 2 * (m - 1))
            given = 3 + 2 * m

    for part in range(2):
        tall = jnp.concatenate([update[part], jnp.zeros((128, 256), jnp.float32)], axis=0)
        stack[part] = pltpu.roll(tall, row, 0)
    copies += begin(
        (
            load(stack.at[:, pl.ds(far_at, 128), :], fold_far, 0),
            load(stack.at[:, 128:256, :], fold_mid, 1),
            load(stack.at[:, pl.ds(own_at, 128), :], fold_own, 2),
        )
    )
    end(copies)


def position(above, below, far_rows, mid_rows, own_rows, probe, pattern, one, two):
    modes = probe.shape[0]
    images = 1 + 2 * modes
    return pl.pallas_call(
        position_kernel,
        out_shape=tuple(f32(legs, images, 16, 256) for legs in (8, 1, 2, 5)) + (f32(2, 128, 256),) * 3,
        in_specs=[SMEM] * 2 + [ANY] * 7,
        out_specs=(ANY,) * 7,
        scratch_shapes=[
            pltpu.VMEM(probe.shape, jnp.float32),
            pltpu.VMEM((256, 256), jnp.float32),
            pltpu.VMEM(one.shape, jnp.bfloat16),
            pltpu.VMEM(two.shape, jnp.bfloat16),
            pltpu.VMEM((2, 384, 256), jnp.float32),
            pltpu.VMEM((2, 256, 256), jnp.float32),
            pltpu.VMEM((modes, 256, 512), jnp.float32),
            pltpu.VMEM((2, 8, images, 16, 256), jnp.float32),
            pltpu.VMEM((2, 256, 256), jnp.float32),
            pltpu.VMEM((256, 256), jnp.float32),
            pltpu.SemaphoreType.DMA((6,)),
            pltpu.SemaphoreType.DMA((modes,)),
            pltpu.SemaphoreType.DMA((2 * modes,)),
        ],
        compiler_params=params(32),
        name="position_terms",
    )(above, below, far_rows, mid_rows, own_rows, probe, pattern, one, two)


def fold_kernel(here_at, above_at, below_at, near, middle, far, inner, edge, grid):
    odd = lax.rem(lax.axis_index("row"), 2) == 1
    grid[...] = jnp.zeros(grid.shape, jnp.float32)
    near_col = jnp.where(odd, above_at[0, 1], below_at[0, 1])
    far_col = jnp.where(odd, below_at[0, 1], above_at[0, 1])
    for col, piece in ((near_col, near), (here_at[0, 1], middle), (far_col, far)):
        base = pl.multiple_of(col // 128 * 128, 128)
        for part in range(2):
            wide = jnp.concatenate([piece[part], jnp.zeros((128, 128), jnp.float32)], axis=1)
            grid[part, :, pl.ds(base, 384)] += pltpu.roll(wide, col % 128, 1)
    size = grid.shape[2]
    inner[...] = grid[:, :, 128 : size - 128]
    edge[...] = jnp.where(lax.axis_index("col") == 0, grid[:, :, size - 128 :], grid[:, :, 0:128])


def fold(here, above, below, near, middle, far, rows, cols):
    return pl.pallas_call(
        fold_kernel,
        out_shape=(f32(2, rows, cols), f32(2, rows, 128)),
        in_specs=[SMEM] * 3 + [VMEM] * 3,
        out_specs=(VMEM, VMEM),
        scratch_shapes=[pltpu.VMEM((2, rows, cols + 256), jnp.float32)],
        compiler_params=params(8),
        name="fold_object",
    )(here, above, below, near, middle, far)


def leg_kernel(low, mine_spot, theirs_spot, came_at, mine_at, theirs_at, out, came, mine, theirs, sems):
    pairs = ((came_at, came), (mine_at.at[mine_spot], mine), (theirs_at.at[theirs_spot], theirs))
    end(begin([pltpu.make_async_copy(a, b, sems.at[n]) for n, (a, b) in enumerate(pairs)]))
    out[...] = mine[...] + theirs[...]
    out[low : low + came.shape[0]] = out[low : low + came.shape[0]] + came[...]


def add_leg(came, low, mine, mine_spot, theirs, theirs_spot):
    whole = mine.shape[1:]
    return pl.pallas_call(
        functools.partial(leg_kernel, low, mine_spot, theirs_spot),
        out_shape=f32(*whole),
        in_specs=[ANY] * 3,
        out_specs=VMEM,
        scratch_shapes=[
            pltpu.VMEM(came.shape, jnp.float32),
            pltpu.VMEM(whole, jnp.float32),
            pltpu.VMEM(whole, jnp.float32),
            pltpu.SemaphoreType.DMA((3,)),
        ],
        compiler_params=params(4),
        name="add_leg",
    )(came, mine, theirs)


def close_kernel(ahead_at, behind_at, mine_at, theirs_at, den_at, edge_at, message, maxima, ahead, behind, mine, theirs, den, edge, sems):
    pairs = (
        (den_at, den), (edge_at, edge),
        (ahead_at, ahead), (behind_at, behind),
        (mine_at.at[mine_at.shape[0] - 1], mine), (theirs_at.at[theirs_at.shape[0] - 1], theirs),
    )
    copies = begin([pltpu.make_async_copy(a, b, sems.at[n]) for n, (a, b) in enumerate(pairs)])
    end(copies[:2])
    cols = den.shape[1]
    side = pl.multiple_of((1 - lax.axis_index("col")) * (cols - 128), 128)
    den[:, pl.ds(side, 128)] += edge[...]
    object_peak = jnp.max(den[...])
    end(copies[2:])
    images = ahead.shape[0]
    for image in range(images):
        total = (mine[image] + theirs[image]) + (ahead[image] + behind[image])
        message[16 * image : 16 * image + 16] = total
        if image == 0:
            maxima[0:8] = jnp.full((8, 256), jnp.max(total), jnp.float32)
    message[16 * images :] = jnp.full((8, 256), object_peak, jnp.float32)
    maxima[8:16] = jnp.full((8, 256), object_peak, jnp.float32)


def close(ahead, behind, mine, theirs, den, edge):
    shape = ahead.shape
    return pl.pallas_call(
        close_kernel,
        out_shape=(f32(16 * shape[0] + 8, 256), f32(16, 256)),
        in_specs=[ANY] * 6,
        out_specs=(VMEM, VMEM),
        scratch_shapes=[pltpu.VMEM(shape, jnp.float32)] * 4
        + [
            pltpu.VMEM(den.shape, jnp.float32),
            pltpu.VMEM(edge.shape, jnp.float32),
            pltpu.SemaphoreType.DMA((6,)),
        ],
        compiler_params=params(6),
        name="close_sum",
    )(ahead, behind, mine, theirs, den, edge)


def finish_kernel(probe_at, block_at, inner_at, edge_at, den_at, den_edge_at, opposite, opposite_twin, *refs):
    number = 2 * (len(HOPS) - 1)
    messages, refs = refs[:number], refs[number:]
    new_block_at, new_probe_at, peaks, probe, block, inner, edge, den, den_edge, new_probe, held = refs[:11]
    sems, out_sems = refs[11:]
    modes = probe.shape[0]
    core = lax.axis_index("col")
    place = ring_place(lax.axis_index("row"))
    cols = block.shape[2]
    pairs = [(messages[n], held.at[n]) for n in range(number)]
    pairs += [(probe_at.at[m], probe.at[m]) for m in range(modes)]
    pairs += [(block_at, block), (inner_at, inner), (edge_at, edge), (den_at, den), (den_edge_at, den_edge)]
    copies = begin([pltpu.make_async_copy(a, b, sems.at[n]) for n, (a, b) in enumerate(pairs)])
    end(copies[:number])
    peak = jnp.maximum(opposite[0:8], opposite_twin[0:8])
    object_peak = jnp.maximum(opposite[8:16], opposite_twin[8:16])
    for n in range(number):
        peak = jnp.maximum(peak, jnp.maximum(held[n, 0:8], held[n, 8:16]))
        object_peak = jnp.maximum(object_peak, held[n, held.shape[1] - 8 :])
    peak = jnp.max(peak)
    object_peak = jnp.max(object_peak)
    peaks[...] = jnp.full((8, 128), peak, jnp.float32)
    scales, starts = [], []
    for n in range(number):
        half = core if n < number // 2 else 1 - core
        starts.append(pl.multiple_of(128 * half + 16 * ((place + HOPS[n % (number // 2)]) & 7), 16))
        held[n, 0:16] = 1.0 / ((1.0 - REGULAR) * held[n, 0:16] + REGULAR * peak)
    outs = ()
    for m in range(modes):
        copies[number + m].wait()
        for part in range(2):
            at = 16 * (1 + 2 * m + part)
            for n in range(number):
                rows = pl.ds(starts[n], 16)
                new_probe[m, part, rows, :] = probe[m, part, rows, :] + held[n, at : at + 16] * held[n, 0:16]
            for half in range(2):
                rows = pl.ds(pl.multiple_of(128 * half + 16 * ((place + 4) & 7), 16), 16)
                new_probe[m, part, rows, :] = probe[m, part, rows, :]
        outs += begin((pltpu.make_async_copy(new_probe.at[m], new_probe_at.at[m], out_sems.at[m]),))
    end(copies[number + modes :])
    side = pl.multiple_of((1 - core) * (cols - 128), 128)
    inner[:, :, pl.ds(side, 128)] += edge[...]
    den[:, pl.ds(side, 128)] += den_edge[...]
    scale = 1.0 / ((1.0 - REGULAR) * den[...] + REGULAR * object_peak)
    for part in range(2):
        block[part] = block[part] + inner[part] * scale
    outs += begin((pltpu.make_async_copy(block, new_block_at, out_sems.at[modes]),))
    end(outs)


def finish(probe, block, inner, edge, den, den_edge, opposite, opposite_twin, messages):
    modes = probe.shape[0]
    number = len(messages)
    return pl.pallas_call(
        finish_kernel,
        out_shape=(f32(*block.shape), f32(*probe.shape), f32(8, 128)),
        in_specs=[ANY] * 6 + [VMEM] * 2 + [ANY] * number,
        out_specs=(ANY, ANY, VMEM),
        scratch_shapes=[
            pltpu.VMEM(x.shape, jnp.float32) for x in (probe, block, inner, edge, den, den_edge, probe)
        ]
        + [
            pltpu.VMEM((number,) + messages[0].shape, jnp.float32),
            pltpu.SemaphoreType.DMA((number + modes + 5,)),
            pltpu.SemaphoreType.DMA((modes + 1,)),
        ],
        compiler_params=params(24),
        name="finish_most",
    )(probe, block, inner, edge, den, den_edge, opposite, opposite_twin, *messages)


def last_kernel(started, probe_at, peaks, low_at, high_at, low_twin_at, high_twin_at, out_at, probe, low, high, sems):
    del started
    modes = probe.shape[1]
    cut = low.shape[1]
    core = lax.axis_index("col")
    place = ring_place(lax.axis_index("row"))
    peak = jnp.max(peaks[...])
    rows = []
    pairs = [(low_at, low.at[0]), (high_at, high.at[0]), (low_twin_at, low.at[1]), (high_twin_at, high.at[1])]
    for owner in range(2):
        half = core if owner == 0 else 1 - core
        rows.append(pl.ds(pl.multiple_of(128 * half + 16 * ((place + 4) & 7), 16), 16))
        pairs.append((probe_at.at[:, :, rows[owner], :], probe.at[owner]))
    end(begin([pltpu.make_async_copy(a, b, sems.at[n]) for n, (a, b) in enumerate(pairs)]))
    outs = ()
    for owner in range(2):
        scale = 1.0 / ((1.0 - REGULAR) * low[owner, 0:16] + REGULAR * peak)
        for m in range(modes):
            for part in range(2):
                at = 16 * (1 + 2 * m + part)
                value = low[owner, at : at + 16] if at < cut else high[owner, at - cut : at - cut + 16]
                probe[owner, m, part] = probe[owner, m, part] + value * scale
        outs += begin((pltpu.make_async_copy(probe.at[owner], out_at.at[:, :, rows[owner], :], sems.at[owner]),))
    end(outs)


def finish_rest(started, probe, peaks, parts):
    modes = probe.shape[0]
    return pl.pallas_call(
        last_kernel,
        out_shape=f32(*probe.shape),
        in_specs=[ANY, ANY, VMEM] + [ANY] * 4,
        out_specs=ANY,
        input_output_aliases={0: 0},
        scratch_shapes=[
            pltpu.VMEM((2, modes, 2, 16, 256), jnp.float32),
            pltpu.VMEM((2,) + parts[0].shape, jnp.float32),
            pltpu.VMEM((2,) + parts[1].shape, jnp.float32),
            pltpu.SemaphoreType.DMA((6,)),
        ],
        compiler_params=params(6),
        name="finish_rest",
    )(started, probe, peaks, *parts)


def shards(object_field, probe, measured, offsets):
    rows, cols = object_field.shape[1], object_field.shape[2]
    count = lax.axis_size("row")
    one, two = transform_blocks(probe.shape[-1])
    one, two = jnp.asarray(one), jnp.asarray(two)

    twins = [(i, i ^ 1) for i in range(count)]
    cores = [(0, 1), (1, 0)]
    down = [(i, i + 1) for i in range(count - 1)]
    up = [(i + 1, i) for i in range(count - 1)]
    outward = [(i, i + 2) for i in range(1, count - 2, 2)] + [(i, i - 2) for i in range(2, count, 2)]
    inward = [(b, a) for a, b in outward]
    forward = [
        (block + RING_ORDER[i], block + RING_ORDER[(i + 1) % RING])
        for block in range(0, count, RING)
        for i in range(RING)
    ]
    reverse = [(b, a) for a, b in forward]
    across_ring = [
        (block + RING_ORDER[i], block + RING_ORDER[(i + RING // 2) % RING])
        for block in range(0, count, RING)
        for i in range(RING)
    ]

    def across(x):
        return lax.ppermute(x, "col", cores)

    def send(x, pairs):
        return lax.ppermute(x, "row", pairs)

    def after(x, y):
        return lax.optimization_barrier((x, y))[0]

    other = across(object_field)
    above = send(offsets, down)
    below = send(offsets, up)
    pattern = send(measured, twins)

    above, below, pattern = lax.optimization_barrier((above, below, pattern))
    (to_twin,) = cut_slices(("here",), offsets, offsets, offsets, object_field, other, offsets)
    mid_rows = send(to_twin, twins)
    to_beyond, own_rows = cut_slices(
        ("beyond", "twin"), offsets, above, below, object_field, other, to_twin
    )
    far_rows = send(to_beyond, outward)
    power = probe_power(after(probe, own_rows))

    mine, his0, his1, his2, fold_far, fold_mid, fold_own = position(
        above, below, far_rows, after(mid_rows, power), own_rows, probe, pattern[0], one, two
    )
    images = mine.shape[1]
    cut = images // 2 + 1
    theirs = [across(his0), across(his1), across(his2)]

    mid_got = send(fold_mid, twins)
    far_got = send(fold_far, inward)

    farthest = mine[0] + theirs[0][0]
    ahead, behind = send(farthest[:cut], forward), send(farthest[cut:], reverse)
    power, theirs[1] = lax.optimization_barrier((power, theirs[1]))
    object_den, den_edge = weights(count, offsets, above, below, power, rows, cols)
    den_edge = across(den_edge)
    low = cut
    for leg in (1, 3, 5):
        got, spot = (theirs[1], 0) if leg == 1 else (theirs[2], leg - 3)
        ahead = send(add_leg(ahead, 0, mine, leg, got, spot), forward)
        behind = send(add_leg(behind, low, mine, leg + 1, got, spot + 1), reverse)
        low = 0
    message, maxima = close(ahead, behind, mine, theirs[2], object_den, den_edge)
    if count > RING:
        blocks = [[b * RING + i for b in range(count // RING)] for i in range(RING)]
        total = lax.psum(message[: 16 * images], "row", axis_index_groups=blocks)
        top = lax.pmax(message[16 * images :], "row", axis_index_groups=blocks)
        message = jnp.concatenate([total, top], axis=0)
        maxima = jnp.concatenate([jnp.full_like(top, jnp.max(total[0:16])), top], axis=0)

    opposite = send(maxima, across_ring)
    messages = [message]
    ahead, behind = send(message, forward), send(message, reverse)
    messages += [ahead, behind]
    ahead, mid_got, far_got = lax.optimization_barrier((ahead, mid_got, far_got))
    inner, edge = fold(offsets, above, below, fold_own, mid_got, far_got, rows, cols)
    edge = across(edge)
    ahead, behind = send(ahead, forward), send(behind, reverse)
    messages += [ahead, behind]
    ahead, opposite = lax.optimization_barrier((ahead, opposite))
    ahead, behind = send(ahead, forward), send(behind, reverse)
    messages += [ahead, behind]
    behind, edge = lax.optimization_barrier((behind, edge))
    parts = [send(ahead[: 16 * cut], forward), send(behind[16 * cut :], reverse)]
    messages += [across(x) for x in messages]

    new_object, started, peaks = finish(
        probe, object_field, inner, edge, object_den, den_edge, opposite, across(opposite), messages
    )
    parts = [after(x, peaks) for x in parts]
    parts += [across(x) for x in parts]
    return new_object, finish_rest(started, probe, peaks, parts)


def solution(mesh):
    placed = (
        P(None, ("groups", "row"), "col"),
        P("groups", None, None, None),
        P(("groups", "row", "col"), None, None),
        P(("groups", "row", "col"), None),
    )
    return jax.shard_map(
        shards,
        mesh=mesh,
        in_specs=placed,
        out_specs=(P(None, ("groups", "row"), "col"), P("groups", None, None, None)),
        check_vma=False,
    )
```

```python
import functools
import math

import jax
import jax.numpy as jnp
import ml_dtypes
import numpy as np
from jax import lax
from jax.experimental import pallas as pl
from jax.experimental.pallas import tpu as pltpu
from jax.sharding import PartitionSpec as P

REGULAR = 0.25
AMP_FLOOR = 2.0
RING = 8
RING_ORDER = (0, 1, 3, 5, 7, 6, 4, 2)
HOPS = (0, -1, 1, -2, 2, -3, 3, 4)

SMEM = pl.BlockSpec(memory_space=pltpu.SMEM)
VMEM = pl.BlockSpec(memory_space=pltpu.VMEM)
ANY = pl.BlockSpec(memory_space=pl.ANY)
HBM = pl.BlockSpec(memory_space=pltpu.HBM)


def transform_blocks(length):
    indices = np.arange(length, dtype=np.int32)
    phases = indices[:, None] * indices[None, :] % length
    angles = phases.astype(np.float32) * np.float32(2.0 * math.pi / length)
    factor = np.float32(1.0 / math.sqrt(length))
    cos = (np.cos(angles) * factor).astype(ml_dtypes.bfloat16)
    sin = (-np.sin(angles) * factor).astype(ml_dtypes.bfloat16)
    one = np.block([[cos, -sin], [sin, cos]])
    return one, np.ascontiguousarray(one.T)


def ring_place(r):
    r = lax.rem(r, RING)
    return jnp.where(r == 0, 0, jnp.where(lax.rem(r, 2) == 1, (r + 1) // 2, RING - r // 2))


def params(mib):
    return pltpu.CompilerParams(vmem_limit_bytes=mib * 1024 * 1024)


def f32(*shape):
    return jax.ShapeDtypeStruct(shape, jnp.float32)


def begin(copies):
    for copy in copies:
        copy.start()
    return copies


def end(copies):
    for copy in copies:
        copy.wait()


def slices_kernel(offsets_at, *refs):
    offsets_in, (block, other, _), outs, (ext, cuts, offsets, sems) = refs[:3], refs[3:6], refs[6:-4], refs[-4:]
    odd = lax.rem(lax.axis_index("row"), 2) == 1
    core = lax.axis_index("col")
    cols = block.shape[2]
    end_of = cols + 128
    source = pl.multiple_of(core * (cols - 128), 128)
    target = pl.multiple_of((1 - core) * end_of, 128)
    blank = pl.multiple_of(core * end_of, 128)
    copies = begin(
        (
            pltpu.make_async_copy(block, ext.at[:, :, 128:end_of], sems.at[0]),
            pltpu.make_async_copy(
                other.at[:, :, pl.ds(source, 128)], ext.at[:, :, pl.ds(target, 128)], sems.at[1]
            ),
        )
        + tuple(
            pltpu.make_async_copy(spot, offsets.at[n], sems.at[4 + n]) for n, spot in enumerate(offsets_in)
        )
    )
    ext[:, :, pl.ds(blank, 128)] = jnp.zeros((2, block.shape[1], 128), jnp.float32)
    end(copies)
    here, above, below = offsets[0, 0, 1], offsets[1, 0, 1], offsets[2, 0, 1]
    columns = {
        "here": here,
        "twin": jnp.where(odd, above, below),
        "beyond": jnp.where(odd, below, above),
    }
    copies = ()
    for number, (which, out) in enumerate(zip(offsets_at, outs)):
        start = columns[which]
        base = pl.multiple_of(start // 128 * 128, 128)
        for part in range(2):
            wide = ext[part, :, pl.ds(base, 384)]
            wide = pltpu.roll(wide, (384 - start % 128) % 384, 1)
            cuts[number, part] = wide[:, 0:256]
        copies += begin((pltpu.make_async_copy(cuts.at[number], out, sems.at[2 + number]),))
    end(copies)


def cut_slices(offsets_at, here, above, below, block, other, ordered):
    rows, cols = block.shape[1], block.shape[2]
    count = len(offsets_at)
    return pl.pallas_call(
        functools.partial(slices_kernel, offsets_at),
        out_shape=(f32(2, rows, 256),) * count,
        in_specs=[ANY] * 3 + [HBM] + [ANY] * 2,
        out_specs=(ANY,) * count,
        scratch_shapes=[
            pltpu.VMEM((2, rows, cols + 256), jnp.float32),
            pltpu.VMEM((count, 2, rows, 256), jnp.float32),
            pltpu.SMEM((3, 1, 2), jnp.int32),
            pltpu.SemaphoreType.DMA((7,)),
        ],
        compiler_params=params(6),
        name="cut_slices",
    )(here, above, below, block, other, ordered)


def power_kernel(probe, out, held, sems):
    modes = probe.shape[0]
    copies = begin([pltpu.make_async_copy(probe.at[m], held.at[m], sems.at[m]) for m in range(modes)])
    for m in range(modes):
        copies[m].wait()
        power = held[m, 0] * held[m, 0] + held[m, 1] * held[m, 1]
        out[...] = power if m == 0 else out[...] + power


def probe_power(probe):
    return pl.pallas_call(
        power_kernel,
        out_shape=f32(*probe.shape[2:]),
        in_specs=[ANY],
        out_specs=VMEM,
        scratch_shapes=[pltpu.VMEM(probe.shape, jnp.float32), pltpu.SemaphoreType.DMA((probe.shape[0],))],
        compiler_params=params(8),
        name="probe_power",
    )(probe)


def weights_kernel(count, here, above, below, power, inner, edge, frame, grid):
    r = lax.axis_index("row")
    present = ((r > 0).astype(jnp.float32), None, (r < count - 1).astype(jnp.float32))
    tall = jnp.concatenate([power[...], jnp.zeros((128, 256), jnp.float32)], axis=0)
    grid[...] = jnp.zeros(grid.shape, jnp.float32)
    for number, spot in enumerate((above, here, below)):
        row, col = spot[0, 0], spot[0, 1]
        frame[...] = pltpu.roll(tall, row, 0)
        lower = 128 * (2 - number)
        piece = frame[lower : lower + 128, :]
        if present[number] is not None:
            piece = piece * present[number]
        wide = jnp.concatenate([piece, jnp.zeros((128, 128), jnp.float32)], axis=1)
        base = pl.multiple_of(col // 128 * 128, 128)
        grid[:, pl.ds(base, 384)] += pltpu.roll(wide, col % 128, 1)
    size = grid.shape[1]
    inner[...] = grid[:, 128 : size - 128]
    edge[...] = jnp.where(lax.axis_index("col") == 0, grid[:, size - 128 :], grid[:, 0:128])


def weights(count, here, above, below, power, rows, cols):
    return pl.pallas_call(
        functools.partial(weights_kernel, count),
        out_shape=(f32(rows, cols), f32(rows, 128)),
        in_specs=[SMEM] * 3 + [VMEM],
        out_specs=(VMEM, VMEM),
        scratch_shapes=[
            pltpu.VMEM((384, 256), jnp.float32),
            pltpu.VMEM((rows, cols + 256), jnp.float32),
        ],
        compiler_params=params(6),
        name="object_weights",
    )(here, above, below, power)


def position_kernel(
    above, below, far_rows, mid_rows, own_rows, probe, pattern, one, two,
    mine, his0, his1, his2, fold_far, fold_mid, fold_own,
    stack, window, far, terms, update, strength, sems, out_sems,
):
    modes = probe.shape[0]
    r = lax.axis_index("row")
    core = lax.axis_index("col")
    odd = lax.rem(r, 2)
    row = jnp.where(odd == 1, above[0, 0], below[0, 0])
    place = ring_place(r)
    far_at = pl.multiple_of(256 * (1 - odd), 128)
    own_at = pl.multiple_of(256 * odd, 128)
    stack[:, pl.ds(far_at, 128), :] = far_rows[...]
    stack[:, 128:256, :] = mid_rows[...]
    stack[:, pl.ds(own_at, 128), :] = own_rows[...]
    for part in range(2):
        window[part] = pltpu.roll(stack[part], (384 - row) % 384, 0)[0:256]

    def exit_wave(m):
        p_re, p_im = probe[m, 0], probe[m, 1]
        w_re, w_im = window[0], window[1]
        return p_re * w_re - p_im * w_im, p_re * w_im + p_im * w_re

    for m in range(modes):
        e_re, e_im = exit_wave(m)
        field = jnp.concatenate([e_re.astype(jnp.bfloat16), e_im.astype(jnp.bfloat16)], axis=0)
        half = jnp.dot(one[...], field, preferred_element_type=jnp.float32).astype(jnp.bfloat16)
        half = jnp.concatenate([half[0:256], half[256:512]], axis=1)
        out = jnp.dot(half, two[...], preferred_element_type=jnp.float32)
        far[m] = out
        power = out[:, 0:256] * out[:, 0:256] + out[:, 256:512] * out[:, 256:512]
        strength[...] = power if m == 0 else strength[...] + power

    strength[...] = jnp.sqrt(pattern[...]) / jnp.maximum(jnp.sqrt(strength[...]), AMP_FLOOR)

    def put(image, value):
        for slab in range(16):
            ahead = (slab - place) & 7
            spot = jnp.where(ahead < 4, 7 - 2 * ahead, 2 * (ahead - 4))
            terms[(slab // 8) ^ core, spot, image] = value[16 * slab : 16 * slab + 16]

    def give(low, high, at):
        images = pl.ds(low, high - low)
        return begin(
            (
                pltpu.make_async_copy(terms.at[1, 0:1, images], his0.at[:, images], out_sems.at[at]),
                pltpu.make_async_copy(terms.at[1, 1:3, images], his1.at[:, images], out_sems.at[at + 1]),
                pltpu.make_async_copy(terms.at[1, 3:8, images], his2.at[:, images], out_sems.at[at + 2]),
                pltpu.make_async_copy(terms.at[0, :, images], mine.at[:, images], out_sems.at[at + 3]),
            )
        )

    put(0, window[0] * window[0] + window[1] * window[1])
    given, copies = 0, ()
    for m in range(modes):
        ratio = strength[...]
        fixed = jnp.concatenate(
            [
                (far[m, :, 0:256] * ratio).astype(jnp.bfloat16),
                (far[m, :, 256:512] * ratio).astype(jnp.bfloat16),
            ],
            axis=0,
        )
        back = jnp.dot(two[...], fixed, preferred_element_type=jnp.float32).astype(jnp.bfloat16)
        back = jnp.concatenate([back[0:256], back[256:512]], axis=1)
        near = jnp.dot(back, one[...], preferred_element_type=jnp.float32)
        e_re, e_im = exit_wave(m)
        d_re = near[:, 0:256] - e_re
        d_im = near[:, 256:512] - e_im
        p_re, p_im = probe[m, 0], probe[m, 1]
        w_re, w_im = window[0], window[1]
        u_re = p_re * d_re + p_im * d_im
        u_im = p_re * d_im - p_im * d_re
        update[0] = u_re if m == 0 else update[0] + u_re
        update[1] = u_im if m == 0 else update[1] + u_im
        put(1 + 2 * m, w_re * d_re + w_im * d_im)
        put(2 + 2 * m, w_re * d_im - w_im * d_re)
        if m % 2 == 1:
            copies += give(given, 3 + 2 * m, 2 * (m - 1))
            given = 3 + 2 * m

    for part in range(2):
        tall = jnp.concatenate([update[part], jnp.zeros((128, 256), jnp.float32)], axis=0)
        stack[part] = pltpu.roll(tall, row, 0)
    copies += begin(
        (
            pltpu.make_async_copy(stack.at[:, pl.ds(far_at, 128), :], fold_far, sems.at[0]),
            pltpu.make_async_copy(stack.at[:, 128:256, :], fold_mid, sems.at[1]),
            pltpu.make_async_copy(stack.at[:, pl.ds(own_at, 128), :], fold_own, sems.at[2]),
        )
    )
    end(copies)


def position(above, below, far_rows, mid_rows, own_rows, probe, pattern, one, two):
    modes = probe.shape[0]
    images = 1 + 2 * modes
    return pl.pallas_call(
        position_kernel,
        out_shape=tuple(f32(legs, images, 16, 256) for legs in (8, 1, 2, 5)) + (f32(2, 128, 256),) * 3,
        in_specs=[SMEM] * 2 + [VMEM] * 7,
        out_specs=(ANY,) * 7,
        scratch_shapes=[
            pltpu.VMEM((2, 384, 256), jnp.float32),
            pltpu.VMEM((2, 256, 256), jnp.float32),
            pltpu.VMEM((modes, 256, 512), jnp.float32),
            pltpu.VMEM((2, 8, images, 16, 256), jnp.float32),
            pltpu.VMEM((2, 256, 256), jnp.float32),
            pltpu.VMEM((256, 256), jnp.float32),
            pltpu.SemaphoreType.DMA((3,)),
            pltpu.SemaphoreType.DMA((2 * modes,)),
        ],
        compiler_params=params(20),
        name="position_terms",
    )(above, below, far_rows, mid_rows, own_rows, probe, pattern, one, two)


def fold_kernel(here_at, above_at, below_at, near, middle, far, inner, edge, grid):
    odd = lax.rem(lax.axis_index("row"), 2) == 1
    grid[...] = jnp.zeros(grid.shape, jnp.float32)
    near_col = jnp.where(odd, above_at[0, 1], below_at[0, 1])
    far_col = jnp.where(odd, below_at[0, 1], above_at[0, 1])
    for col, piece in ((near_col, near), (here_at[0, 1], middle), (far_col, far)):
        base = pl.multiple_of(col // 128 * 128, 128)
        for part in range(2):
            wide = jnp.concatenate([piece[part], jnp.zeros((128, 128), jnp.float32)], axis=1)
            grid[part, :, pl.ds(base, 384)] += pltpu.roll(wide, col % 128, 1)
    size = grid.shape[2]
    inner[...] = grid[:, :, 128 : size - 128]
    edge[...] = jnp.where(lax.axis_index("col") == 0, grid[:, :, size - 128 :], grid[:, :, 0:128])


def fold(here, above, below, near, middle, far, rows, cols):
    return pl.pallas_call(
        fold_kernel,
        out_shape=(f32(2, rows, cols), f32(2, rows, 128)),
        in_specs=[SMEM] * 3 + [VMEM] * 3,
        out_specs=(VMEM, VMEM),
        scratch_shapes=[pltpu.VMEM((2, rows, cols + 256), jnp.float32)],
        compiler_params=params(8),
        name="fold_object",
    )(here, above, below, near, middle, far)


def leg_kernel(low, mine_spot, theirs_spot, came, mine_at, theirs_at, out, mine, theirs, sems):
    pairs = ((mine_at.at[mine_spot], mine), (theirs_at.at[theirs_spot], theirs))
    end(begin([pltpu.make_async_copy(a, b, sems.at[n]) for n, (a, b) in enumerate(pairs)]))
    out[...] = mine[...] + theirs[...]
    out[low : low + came.shape[0]] = out[low : low + came.shape[0]] + came[...]


def add_leg(came, low, mine, mine_spot, theirs, theirs_spot):
    whole = mine.shape[1:]
    return pl.pallas_call(
        functools.partial(leg_kernel, low, mine_spot, theirs_spot),
        out_shape=f32(*whole),
        in_specs=[VMEM] + [ANY] * 2,
        out_specs=VMEM,
        scratch_shapes=[
            pltpu.VMEM(whole, jnp.float32),
            pltpu.VMEM(whole, jnp.float32),
            pltpu.SemaphoreType.DMA((2,)),
        ],
        compiler_params=params(4),
        name="add_leg",
    )(came, mine, theirs)


def close_kernel(ahead, behind, mine_at, theirs_at, den_in, edge, message, maxima, mine, theirs, den, sems):
    pairs = ((mine_at.at[mine_at.shape[0] - 1], mine), (theirs_at.at[theirs_at.shape[0] - 1], theirs))
    copies = begin([pltpu.make_async_copy(a, b, sems.at[n]) for n, (a, b) in enumerate(pairs)])
    den[...] = den_in[...]
    cols = den.shape[1]
    side = pl.multiple_of((1 - lax.axis_index("col")) * (cols - 128), 128)
    den[:, pl.ds(side, 128)] += edge[...]
    object_peak = jnp.max(den[...])
    end(copies)
    images = ahead.shape[0]
    for image in range(images):
        total = (mine[image] + theirs[image]) + (ahead[image] + behind[image])
        message[16 * image : 16 * image + 16] = total
        if image == 0:
            maxima[0:8] = jnp.full((8, 256), jnp.max(total), jnp.float32)
    message[16 * images :] = jnp.full((8, 256), object_peak, jnp.float32)
    maxima[8:16] = jnp.full((8, 256), object_peak, jnp.float32)


def close(ahead, behind, mine, theirs, den, edge):
    shape = ahead.shape
    return pl.pallas_call(
        close_kernel,
        out_shape=(f32(16 * shape[0] + 8, 256), f32(16, 256)),
        in_specs=[VMEM] * 2 + [ANY] * 2 + [VMEM] * 2,
        out_specs=(VMEM, VMEM),
        scratch_shapes=[pltpu.VMEM(shape, jnp.float32)] * 2
        + [pltpu.VMEM(den.shape, jnp.float32), pltpu.SemaphoreType.DMA((2,))],
        compiler_params=params(6),
        name="close_sum",
    )(ahead, behind, mine, theirs, den, edge)


def finish_kernel(probe, block, inner, edge, den, den_edge, opposite, opposite_twin, *refs):
    number = 2 * (len(HOPS) - 1)
    messages, refs = refs[:number], refs[number:]
    new_block_at, new_probe_at, peaks, new_probe, new_block, whole_den, scales, sems = refs
    modes = probe.shape[0]
    core = lax.axis_index("col")
    place = ring_place(lax.axis_index("row"))
    cols = block.shape[2]
    peak = jnp.maximum(opposite[0:8], opposite_twin[0:8])
    object_peak = jnp.maximum(opposite[8:16], opposite_twin[8:16])
    for message in messages:
        peak = jnp.maximum(peak, jnp.maximum(message[0:8], message[8:16]))
        object_peak = jnp.maximum(object_peak, message[message.shape[0] - 8 :])
    peak = jnp.max(peak)
    object_peak = jnp.max(object_peak)
    peaks[...] = jnp.full((8, 128), peak, jnp.float32)
    starts = []
    for n, message in enumerate(messages):
        half = core if n < number // 2 else 1 - core
        starts.append(pl.multiple_of(128 * half + 16 * ((place + HOPS[n % (number // 2)]) & 7), 16))
        scales[n] = 1.0 / ((1.0 - REGULAR) * message[0:16] + REGULAR * peak)
    outs = ()
    for m in range(modes):
        for part in range(2):
            at = 16 * (1 + 2 * m + part)
            for n, message in enumerate(messages):
                rows = pl.ds(starts[n], 16)
                new_probe[m, part, rows, :] = probe[m, part, rows, :] + message[at : at + 16] * scales[n]
            for half in range(2):
                rows = pl.ds(pl.multiple_of(128 * half + 16 * ((place + 4) & 7), 16), 16)
                new_probe[m, part, rows, :] = probe[m, part, rows, :]
        outs += begin((pltpu.make_async_copy(new_probe.at[m], new_probe_at.at[m], sems.at[m]),))
    side = pl.multiple_of((1 - core) * (cols - 128), 128)
    new_block[...] = inner[...]
    new_block[:, :, pl.ds(side, 128)] += edge[...]
    whole_den[...] = den[...]
    whole_den[:, pl.ds(side, 128)] += den_edge[...]
    scale = 1.0 / ((1.0 - REGULAR) * whole_den[...] + REGULAR * object_peak)
    for part in range(2):
        new_block[part] = block[part] + new_block[part] * scale
    outs += begin((pltpu.make_async_copy(new_block, new_block_at, sems.at[modes]),))
    end(outs)


def finish(probe, block, inner, edge, den, den_edge, opposite, opposite_twin, messages):
    modes = probe.shape[0]
    number = len(messages)
    return pl.pallas_call(
        finish_kernel,
        out_shape=(f32(*block.shape), f32(*probe.shape), f32(8, 128)),
        in_specs=[VMEM] * (8 + number),
        out_specs=(ANY, ANY, VMEM),
        scratch_shapes=[pltpu.VMEM(x.shape, jnp.float32) for x in (probe, block, den)]
        + [
            pltpu.VMEM((number, 16, 256), jnp.float32),
            pltpu.SemaphoreType.DMA((modes + 1,)),
        ],
        compiler_params=params(12),
        name="finish_most",
    )(probe, block, inner, edge, den, den_edge, opposite, opposite_twin, *messages)


def last_kernel(started, whole, peaks, low, high, low_twin, high_twin, out_at, probe, sems):
    del started
    modes = probe.shape[1]
    cut = low.shape[0]
    core = lax.axis_index("col")
    place = ring_place(lax.axis_index("row"))
    peak = jnp.max(peaks[...])
    outs = ()
    for owner, (first, second) in enumerate(((low, high), (low_twin, high_twin))):
        half = core if owner == 0 else 1 - core
        rows = pl.ds(pl.multiple_of(128 * half + 16 * ((place + 4) & 7), 16), 16)
        scale = 1.0 / ((1.0 - REGULAR) * first[0:16] + REGULAR * peak)
        for m in range(modes):
            for part in range(2):
                at = 16 * (1 + 2 * m + part)
                value = first[at : at + 16] if at < cut else second[at - cut : at - cut + 16]
                probe[owner, m, part] = whole[m, part, rows, :] + value * scale
        outs += begin((pltpu.make_async_copy(probe.at[owner], out_at.at[:, :, rows, :], sems.at[owner]),))
    end(outs)


def finish_rest(started, probe, peaks, parts):
    modes = probe.shape[0]
    return pl.pallas_call(
        last_kernel,
        out_shape=f32(*probe.shape),
        in_specs=[ANY] + [VMEM] * 6,
        out_specs=ANY,
        input_output_aliases={0: 0},
        scratch_shapes=[
            pltpu.VMEM((2, modes, 2, 16, 256), jnp.float32),
            pltpu.SemaphoreType.DMA((2,)),
        ],
        compiler_params=params(4),
        name="finish_rest",
    )(started, probe, peaks, *parts)


def shards(object_field, probe, measured, offsets):
    rows, cols = object_field.shape[1], object_field.shape[2]
    count = lax.axis_size("row")
    one, two = transform_blocks(probe.shape[-1])
    one, two = jnp.asarray(one), jnp.asarray(two)

    twins = [(i, i ^ 1) for i in range(count)]
    cores = [(0, 1), (1, 0)]
    down = [(i, i + 1) for i in range(count - 1)]
    up = [(i + 1, i) for i in range(count - 1)]
    outward = [(i, i + 2) for i in range(1, count - 2, 2)] + [(i, i - 2) for i in range(2, count, 2)]
    inward = [(b, a) for a, b in outward]
    forward = [
        (block + RING_ORDER[i], block + RING_ORDER[(i + 1) % RING])
        for block in range(0, count, RING)
        for i in range(RING)
    ]
    reverse = [(b, a) for a, b in forward]
    across_ring = [
        (block + RING_ORDER[i], block + RING_ORDER[(i + RING // 2) % RING])
        for block in range(0, count, RING)
        for i in range(RING)
    ]

    def across(x):
        return lax.ppermute(x, "col", cores)

    def send(x, pairs):
        return lax.ppermute(x, "row", pairs)

    def after(x, y):
        return lax.optimization_barrier((x, y))[0]

    other = across(object_field)
    above = send(offsets, down)
    below = send(offsets, up)

    (to_twin,) = cut_slices(("here",), offsets, offsets, offsets, object_field, other, offsets)
    mid_rows = send(to_twin, twins)
    to_beyond, own_rows = cut_slices(
        ("beyond", "twin"), offsets, above, below, object_field, other, to_twin
    )
    far_rows = send(to_beyond, outward)
    pattern = send(after(measured, own_rows), twins)
    power = probe_power(after(probe, own_rows))

    mine, his0, his1, his2, fold_far, fold_mid, fold_own = position(
        above, below, far_rows, after(mid_rows, power), own_rows, probe, pattern[0], one, two
    )
    images = mine.shape[1]
    cut = images // 2 + 1
    theirs = [across(his0), across(his1), across(his2)]

    mid_got = send(fold_mid, twins)
    far_got = send(fold_far, inward)

    farthest = mine[0] + theirs[0][0]
    ahead, behind = send(farthest[:cut], forward), send(farthest[cut:], reverse)
    power, theirs[1] = lax.optimization_barrier((power, theirs[1]))
    object_den, den_edge = weights(count, offsets, above, below, power, rows, cols)
    den_edge = across(den_edge)
    low = cut
    for leg in (1, 3, 5):
        got, spot = (theirs[1], 0) if leg == 1 else (theirs[2], leg - 3)
        ahead = send(add_leg(ahead, 0, mine, leg, got, spot), forward)
        behind = send(add_leg(behind, low, mine, leg + 1, got, spot + 1), reverse)
        low = 0
    message, maxima = close(ahead, behind, mine, theirs[2], object_den, den_edge)
    if count > RING:
        blocks = [[b * RING + i for b in range(count // RING)] for i in range(RING)]
        total = lax.psum(message[: 16 * images], "row", axis_index_groups=blocks)
        top = lax.pmax(message[16 * images :], "row", axis_index_groups=blocks)
        message = jnp.concatenate([total, top], axis=0)
        maxima = jnp.concatenate([jnp.full_like(top, jnp.max(total[0:16])), top], axis=0)

    opposite = send(maxima, across_ring)
    messages = [message]
    ahead, behind = send(message, forward), send(message, reverse)
    messages += [ahead, behind]
    mid_got, far_got, opposite = lax.optimization_barrier((mid_got, far_got, opposite))
    inner, edge = fold(offsets, above, below, fold_own, mid_got, far_got, rows, cols)
    edge = across(edge)
    for hop in range(2):
        ahead, behind = send(ahead, forward), send(behind, reverse)
        messages += [ahead, behind]
    behind, edge = lax.optimization_barrier((behind, edge))
    parts = [send(ahead[: 16 * cut], forward), send(behind[16 * cut :], reverse)]
    messages += [across(x) for x in messages]

    new_object, started, peaks = finish(
        probe, object_field, inner, edge, object_den, den_edge, opposite, across(opposite), messages
    )
    parts = [after(x, peaks) for x in parts]
    parts += [across(x) for x in parts]
    return new_object, finish_rest(started, probe, peaks, parts)


def solution(mesh):
    placed = (
        P(None, ("groups", "row"), "col"),
        P("groups", None, None, None),
        P(("groups", "row", "col"), None, None),
        P(("groups", "row", "col"), None),
    )
    return jax.shard_map(
        shards,
        mesh=mesh,
        in_specs=placed,
        out_specs=(P(None, ("groups", "row"), "col"), P("groups", None, None, None)),
        check_vma=False,
    )
```

```python
import functools
import math

import jax
import jax.numpy as jnp
import ml_dtypes
import numpy as np
from jax import lax
from jax.experimental import pallas as pl
from jax.experimental.pallas import tpu as pltpu
from jax.sharding import PartitionSpec as P

REGULAR = 0.25
AMP_FLOOR = 2.0
RING = 8
RING_ORDER = (0, 1, 3, 5, 7, 6, 4, 2)
HOPS = (0, -1, 1, -2, 2, -3, 3, 4)

SMEM = pl.BlockSpec(memory_space=pltpu.SMEM)
VMEM = pl.BlockSpec(memory_space=pltpu.VMEM)
ANY = pl.BlockSpec(memory_space=pl.ANY)
HBM = pl.BlockSpec(memory_space=pltpu.HBM)


def transform_blocks(length):
    indices = np.arange(length, dtype=np.int32)
    phases = indices[:, None] * indices[None, :] % length
    angles = phases.astype(np.float32) * np.float32(2.0 * math.pi / length)
    factor = np.float32(1.0 / math.sqrt(length))
    cos = (np.cos(angles) * factor).astype(ml_dtypes.bfloat16)
    sin = (-np.sin(angles) * factor).astype(ml_dtypes.bfloat16)
    one = np.block([[cos, -sin], [sin, cos]])
    return one, np.ascontiguousarray(one.T)


def ring_place(r):
    r = lax.rem(r, RING)
    return jnp.where(r == 0, 0, jnp.where(lax.rem(r, 2) == 1, (r + 1) // 2, RING - r // 2))


def params(mib):
    return pltpu.CompilerParams(vmem_limit_bytes=mib * 1024 * 1024)


def f32(*shape):
    return jax.ShapeDtypeStruct(shape, jnp.float32)


def begin(copies):
    for copy in copies:
        copy.start()
    return copies


def end(copies):
    for copy in copies:
        copy.wait()


def slices_kernel(offsets_at, *refs):
    offsets_in, (block, other, _), outs, (ext, cuts, offsets, sems) = refs[:3], refs[3:6], refs[6:-4], refs[-4:]
    odd = lax.rem(lax.axis_index("row"), 2) == 1
    core = lax.axis_index("col")
    cols = block.shape[2]
    end_of = cols + 128
    source = pl.multiple_of(core * (cols - 128), 128)
    target = pl.multiple_of((1 - core) * end_of, 128)
    blank = pl.multiple_of(core * end_of, 128)
    copies = begin(
        (
            pltpu.make_async_copy(block, ext.at[:, :, 128:end_of], sems.at[0]),
            pltpu.make_async_copy(
                other.at[:, :, pl.ds(source, 128)], ext.at[:, :, pl.ds(target, 128)], sems.at[1]
            ),
        )
        + tuple(
            pltpu.make_async_copy(spot, offsets.at[n], sems.at[4 + n]) for n, spot in enumerate(offsets_in)
        )
    )
    ext[:, :, pl.ds(blank, 128)] = jnp.zeros((2, block.shape[1], 128), jnp.float32)
    end(copies)
    here, above, below = offsets[0, 0, 1], offsets[1, 0, 1], offsets[2, 0, 1]
    columns = {
        "here": here,
        "twin": jnp.where(odd, above, below),
        "beyond": jnp.where(odd, below, above),
    }
    copies = ()
    for number, (which, out) in enumerate(zip(offsets_at, outs)):
        start = columns[which]
        base = pl.multiple_of(start // 128 * 128, 128)
        for part in range(2):
            wide = ext[part, :, pl.ds(base, 384)]
            wide = pltpu.roll(wide, (384 - start % 128) % 384, 1)
            cuts[number, part] = wide[:, 0:256]
        copies += begin((pltpu.make_async_copy(cuts.at[number], out, sems.at[2 + number]),))
    end(copies)


def cut_slices(offsets_at, here, above, below, block, other, ordered):
    rows, cols = block.shape[1], block.shape[2]
    count = len(offsets_at)
    return pl.pallas_call(
        functools.partial(slices_kernel, offsets_at),
        out_shape=(f32(2, rows, 256),) * count,
        in_specs=[ANY] * 3 + [HBM] + [ANY] * 2,
        out_specs=(ANY,) * count,
        scratch_shapes=[
            pltpu.VMEM((2, rows, cols + 256), jnp.float32),
            pltpu.VMEM((count, 2, rows, 256), jnp.float32),
            pltpu.SMEM((3, 1, 2), jnp.int32),
            pltpu.SemaphoreType.DMA((7,)),
        ],
        compiler_params=params(6),
        name="cut_slices",
    )(here, above, below, block, other, ordered)


def power_kernel(probe, out, held, sems):
    modes = probe.shape[0]
    copies = begin([pltpu.make_async_copy(probe.at[m], held.at[m], sems.at[m]) for m in range(modes)])
    for m in range(modes):
        copies[m].wait()
        power = held[m, 0] * held[m, 0] + held[m, 1] * held[m, 1]
        out[...] = power if m == 0 else out[...] + power


def probe_power(probe):
    return pl.pallas_call(
        power_kernel,
        out_shape=f32(*probe.shape[2:]),
        in_specs=[ANY],
        out_specs=VMEM,
        scratch_shapes=[pltpu.VMEM(probe.shape, jnp.float32), pltpu.SemaphoreType.DMA((probe.shape[0],))],
        compiler_params=params(8),
        name="probe_power",
    )(probe)


def weights_kernel(count, here, above, below, power, inner, edge, frame, grid):
    r = lax.axis_index("row")
    present = ((r > 0).astype(jnp.float32), None, (r < count - 1).astype(jnp.float32))
    tall = jnp.concatenate([power[...], jnp.zeros((128, 256), jnp.float32)], axis=0)
    grid[...] = jnp.zeros(grid.shape, jnp.float32)
    for number, spot in enumerate((above, here, below)):
        row, col = spot[0, 0], spot[0, 1]
        frame[...] = pltpu.roll(tall, row, 0)
        lower = 128 * (2 - number)
        piece = frame[lower : lower + 128, :]
        if present[number] is not None:
            piece = piece * present[number]
        wide = jnp.concatenate([piece, jnp.zeros((128, 128), jnp.float32)], axis=1)
        base = pl.multiple_of(col // 128 * 128, 128)
        grid[:, pl.ds(base, 384)] += pltpu.roll(wide, col % 128, 1)
    size = grid.shape[1]
    inner[...] = grid[:, 128 : size - 128]
    edge[...] = jnp.where(lax.axis_index("col") == 0, grid[:, size - 128 :], grid[:, 0:128])


def weights(count, here, above, below, power, rows, cols):
    return pl.pallas_call(
        functools.partial(weights_kernel, count),
        out_shape=(f32(rows, cols), f32(rows, 128)),
        in_specs=[SMEM] * 3 + [VMEM],
        out_specs=(VMEM, VMEM),
        scratch_shapes=[
            pltpu.VMEM((384, 256), jnp.float32),
            pltpu.VMEM((rows, cols + 256), jnp.float32),
        ],
        compiler_params=params(6),
        name="object_weights",
    )(here, above, below, power)


def position_kernel(
    above, below, far_rows, mid_rows, own_rows, probe, pattern, one, two,
    mine, his0, his1, fold_far, fold_mid, fold_own,
    stack, window, far, terms, update, strength, sems, out_sems,
):
    modes = probe.shape[0]
    r = lax.axis_index("row")
    core = lax.axis_index("col")
    odd = lax.rem(r, 2)
    row = jnp.where(odd == 1, above[0, 0], below[0, 0])
    place = ring_place(r)
    far_at = pl.multiple_of(256 * (1 - odd), 128)
    own_at = pl.multiple_of(256 * odd, 128)
    stack[:, pl.ds(far_at, 128), :] = far_rows[...]
    stack[:, 128:256, :] = mid_rows[...]
    stack[:, pl.ds(own_at, 128), :] = own_rows[...]
    for part in range(2):
        window[part] = pltpu.roll(stack[part], (384 - row) % 384, 0)[0:256]

    def exit_wave(m):
        p_re, p_im = probe[m, 0], probe[m, 1]
        w_re, w_im = window[0], window[1]
        return p_re * w_re - p_im * w_im, p_re * w_im + p_im * w_re

    for m in range(modes):
        e_re, e_im = exit_wave(m)
        field = jnp.concatenate([e_re.astype(jnp.bfloat16), e_im.astype(jnp.bfloat16)], axis=0)
        half = jnp.dot(one[...], field, preferred_element_type=jnp.float32).astype(jnp.bfloat16)
        half = jnp.concatenate([half[0:256], half[256:512]], axis=1)
        out = jnp.dot(half, two[...], preferred_element_type=jnp.float32)
        far[m] = out
        power = out[:, 0:256] * out[:, 0:256] + out[:, 256:512] * out[:, 256:512]
        strength[...] = power if m == 0 else strength[...] + power

    strength[...] = jnp.sqrt(pattern[...]) / jnp.maximum(jnp.sqrt(strength[...]), AMP_FLOOR)

    def put(image, value):
        for slab in range(16):
            ahead = (slab - place) & 7
            spot = jnp.where(ahead < 4, 7 - 2 * ahead, 2 * (ahead - 4))
            terms[(slab // 8) ^ core, spot, image] = value[16 * slab : 16 * slab + 16]

    def give(low, high, at):
        images = pl.ds(low, high - low)
        return begin(
            (
                pltpu.make_async_copy(terms.at[1, 0:1, images], his0.at[:, images], out_sems.at[at]),
                pltpu.make_async_copy(terms.at[1, 1:8, images], his1.at[:, images], out_sems.at[at + 1]),
                pltpu.make_async_copy(terms.at[0, :, images], mine.at[:, images], out_sems.at[at + 2]),
            )
        )

    put(0, window[0] * window[0] + window[1] * window[1])
    given, copies = 0, ()
    for m in range(modes):
        ratio = strength[...]
        fixed = jnp.concatenate(
            [
                (far[m, :, 0:256] * ratio).astype(jnp.bfloat16),
                (far[m, :, 256:512] * ratio).astype(jnp.bfloat16),
            ],
            axis=0,
        )
        back = jnp.dot(two[...], fixed, preferred_element_type=jnp.float32).astype(jnp.bfloat16)
        back = jnp.concatenate([back[0:256], back[256:512]], axis=1)
        near = jnp.dot(back, one[...], preferred_element_type=jnp.float32)
        e_re, e_im = exit_wave(m)
        d_re = near[:, 0:256] - e_re
        d_im = near[:, 256:512] - e_im
        p_re, p_im = probe[m, 0], probe[m, 1]
        w_re, w_im = window[0], window[1]
        u_re = p_re * d_re + p_im * d_im
        u_im = p_re * d_im - p_im * d_re
        update[0] = u_re if m == 0 else update[0] + u_re
        update[1] = u_im if m == 0 else update[1] + u_im
        put(1 + 2 * m, w_re * d_re + w_im * d_im)
        put(2 + 2 * m, w_re * d_im - w_im * d_re)
        if m % 2 == 1:
            copies += give(given, 3 + 2 * m, 3 * (m // 2))
            given = 3 + 2 * m

    for part in range(2):
        tall = jnp.concatenate([update[part], jnp.zeros((128, 256), jnp.float32)], axis=0)
        stack[part] = pltpu.roll(tall, row, 0)
    copies += begin(
        (
            pltpu.make_async_copy(stack.at[:, pl.ds(far_at, 128), :], fold_far, sems.at[0]),
            pltpu.make_async_copy(stack.at[:, 128:256, :], fold_mid, sems.at[1]),
            pltpu.make_async_copy(stack.at[:, pl.ds(own_at, 128), :], fold_own, sems.at[2]),
        )
    )
    end(copies)


def position(above, below, far_rows, mid_rows, own_rows, probe, pattern, one, two):
    modes = probe.shape[0]
    images = 1 + 2 * modes
    return pl.pallas_call(
        position_kernel,
        out_shape=tuple(f32(legs, images, 16, 256) for legs in (8, 1, 7)) + (f32(2, 128, 256),) * 3,
        in_specs=[SMEM] * 2 + [VMEM] * 7,
        out_specs=(ANY,) * 6,
        scratch_shapes=[
            pltpu.VMEM((2, 384, 256), jnp.float32),
            pltpu.VMEM((2, 256, 256), jnp.float32),
            pltpu.VMEM((modes, 256, 512), jnp.float32),
            pltpu.VMEM((2, 8, images, 16, 256), jnp.float32),
            pltpu.VMEM((2, 256, 256), jnp.float32),
            pltpu.VMEM((256, 256), jnp.float32),
            pltpu.SemaphoreType.DMA((3,)),
            pltpu.SemaphoreType.DMA((3 * (modes // 2),)),
        ],
        compiler_params=params(20),
        name="position_terms",
    )(above, below, far_rows, mid_rows, own_rows, probe, pattern, one, two)


def fold_kernel(here_at, above_at, below_at, near, middle, far, inner, edge, grid):
    odd = lax.rem(lax.axis_index("row"), 2) == 1
    grid[...] = jnp.zeros(grid.shape, jnp.float32)
    near_col = jnp.where(odd, above_at[0, 1], below_at[0, 1])
    far_col = jnp.where(odd, below_at[0, 1], above_at[0, 1])
    for col, piece in ((near_col, near), (here_at[0, 1], middle), (far_col, far)):
        base = pl.multiple_of(col // 128 * 128, 128)
        for part in range(2):
            wide = jnp.concatenate([piece[part], jnp.zeros((128, 128), jnp.float32)], axis=1)
            grid[part, :, pl.ds(base, 384)] += pltpu.roll(wide, col % 128, 1)
    size = grid.shape[2]
    inner[...] = grid[:, :, 128 : size - 128]
    edge[...] = jnp.where(lax.axis_index("col") == 0, grid[:, :, size - 128 :], grid[:, :, 0:128])


def fold(here, above, below, near, middle, far, rows, cols):
    return pl.pallas_call(
        fold_kernel,
        out_shape=(f32(2, rows, cols), f32(2, rows, 128)),
        in_specs=[SMEM] * 3 + [VMEM] * 3,
        out_specs=(VMEM, VMEM),
        scratch_shapes=[pltpu.VMEM((2, rows, cols + 256), jnp.float32)],
        compiler_params=params(8),
        name="fold_object",
    )(here, above, below, near, middle, far)


def leg_kernel(low, mine_spot, theirs_spot, came, mine_at, theirs_at, out, mine, theirs, sems):
    pairs = ((mine_at.at[mine_spot], mine), (theirs_at.at[theirs_spot], theirs))
    end(begin([pltpu.make_async_copy(a, b, sems.at[n]) for n, (a, b) in enumerate(pairs)]))
    out[...] = mine[...] + theirs[...]
    out[low : low + came.shape[0]] = out[low : low + came.shape[0]] + came[...]


def add_leg(came, low, mine, mine_spot, theirs, theirs_spot):
    whole = mine.shape[1:]
    return pl.pallas_call(
        functools.partial(leg_kernel, low, mine_spot, theirs_spot),
        out_shape=f32(*whole),
        in_specs=[VMEM] + [ANY] * 2,
        out_specs=VMEM,
        scratch_shapes=[
            pltpu.VMEM(whole, jnp.float32),
            pltpu.VMEM(whole, jnp.float32),
            pltpu.SemaphoreType.DMA((2,)),
        ],
        compiler_params=params(4),
        name="add_leg",
    )(came, mine, theirs)


def close_kernel(ahead, behind, mine_at, theirs_at, den_in, edge, message, mine, theirs, den, sems):
    pairs = ((mine_at.at[mine_at.shape[0] - 1], mine), (theirs_at.at[theirs_at.shape[0] - 1], theirs))
    copies = begin([pltpu.make_async_copy(a, b, sems.at[n]) for n, (a, b) in enumerate(pairs)])
    den[...] = den_in[...]
    cols = den.shape[1]
    side = pl.multiple_of((1 - lax.axis_index("col")) * (cols - 128), 128)
    den[:, pl.ds(side, 128)] += edge[...]
    object_peak = jnp.max(den[...])
    end(copies)
    images = ahead.shape[0]
    for image in range(images):
        total = (mine[image] + theirs[image]) + (ahead[image] + behind[image])
        message[16 * image : 16 * image + 16] = total
    message[16 * images :] = jnp.full((8, 256), object_peak, jnp.float32)


def close(ahead, behind, mine, theirs, den, edge):
    shape = ahead.shape
    return pl.pallas_call(
        close_kernel,
        out_shape=f32(16 * shape[0] + 8, 256),
        in_specs=[VMEM] * 2 + [ANY] * 2 + [VMEM] * 2,
        out_specs=VMEM,
        scratch_shapes=[pltpu.VMEM(shape, jnp.float32)] * 2
        + [pltpu.VMEM(den.shape, jnp.float32), pltpu.SemaphoreType.DMA((2,))],
        compiler_params=params(6),
        name="close_sum",
    )(ahead, behind, mine, theirs, den, edge)


def finish_kernel(probe, block, inner, edge, den, den_edge, *refs):
    per_owner = len(HOPS) + 1
    messages, refs = refs[: 2 * per_owner], refs[2 * per_owner :]
    new_block_at, new_probe_at, new_probe, new_block, whole_den, scales, sems = refs
    modes = probe.shape[0]
    core = lax.axis_index("col")
    place = ring_place(lax.axis_index("row"))
    cols = block.shape[2]
    cut = messages[per_owner - 2].shape[0]
    peak = jnp.zeros((8, 256), jnp.float32)
    object_peak = jnp.zeros((8, 256), jnp.float32)
    for n, message in enumerate(messages):
        if n % per_owner != per_owner - 1:
            peak = jnp.maximum(peak, jnp.maximum(message[0:8], message[8:16]))
        if n % per_owner != per_owner - 2:
            object_peak = jnp.maximum(object_peak, message[message.shape[0] - 8 :])
    peak = jnp.max(peak)
    object_peak = jnp.max(object_peak)
    starts = []
    for owner in range(2):
        half = core if owner == 0 else 1 - core
        for n, hop in enumerate(HOPS):
            starts.append(pl.multiple_of(128 * half + 16 * ((place + hop) & 7), 16))
            den_rows = messages[per_owner * owner + n][0:16]
            scales[len(HOPS) * owner + n] = 1.0 / ((1.0 - REGULAR) * den_rows + REGULAR * peak)
    outs = ()
    for m in range(modes):
        for part in range(2):
            at = 16 * (1 + 2 * m + part)
            for owner in range(2):
                for n, hop in enumerate(HOPS):
                    first = per_owner * owner
                    if hop != 4 or at < cut:
                        value = messages[first + n][at : at + 16]
                    else:
                        value = messages[first + n + 1][at - cut : at - cut + 16]
                    spot = len(HOPS) * owner + n
                    rows = pl.ds(starts[spot], 16)
                    new_probe[m, part, rows, :] = probe[m, part, rows, :] + value * scales[spot]
        outs += begin((pltpu.make_async_copy(new_probe.at[m], new_probe_at.at[m], sems.at[m]),))
    side = pl.multiple_of((1 - core) * (cols - 128), 128)
    new_block[...] = inner[...]
    new_block[:, :, pl.ds(side, 128)] += edge[...]
    whole_den[...] = den[...]
    whole_den[:, pl.ds(side, 128)] += den_edge[...]
    scale = 1.0 / ((1.0 - REGULAR) * whole_den[...] + REGULAR * object_peak)
    for part in range(2):
        new_block[part] = block[part] + new_block[part] * scale
    outs += begin((pltpu.make_async_copy(new_block, new_block_at, sems.at[modes]),))
    end(outs)


def finish(probe, block, inner, edge, den, den_edge, messages):
    modes = probe.shape[0]
    return pl.pallas_call(
        finish_kernel,
        out_shape=(f32(*block.shape), f32(*probe.shape)),
        in_specs=[VMEM] * (6 + len(messages)),
        out_specs=(ANY, ANY),
        scratch_shapes=[pltpu.VMEM(x.shape, jnp.float32) for x in (probe, block, den)]
        + [
            pltpu.VMEM((2 * len(HOPS), 16, 256), jnp.float32),
            pltpu.SemaphoreType.DMA((modes + 1,)),
        ],
        compiler_params=params(12),
        name="finish",
    )(probe, block, inner, edge, den, den_edge, *messages)


def shards(object_field, probe, measured, offsets):
    rows, cols = object_field.shape[1], object_field.shape[2]
    count = lax.axis_size("row")
    one, two = transform_blocks(probe.shape[-1])
    one, two = jnp.asarray(one), jnp.asarray(two)

    twins = [(i, i ^ 1) for i in range(count)]
    cores = [(0, 1), (1, 0)]
    down = [(i, i + 1) for i in range(count - 1)]
    up = [(i + 1, i) for i in range(count - 1)]
    outward = [(i, i + 2) for i in range(1, count - 2, 2)] + [(i, i - 2) for i in range(2, count, 2)]
    inward = [(b, a) for a, b in outward]
    forward = [
        (block + RING_ORDER[i], block + RING_ORDER[(i + 1) % RING])
        for block in range(0, count, RING)
        for i in range(RING)
    ]
    reverse = [(b, a) for a, b in forward]

    def across(x):
        return lax.ppermute(x, "col", cores)

    def send(x, pairs):
        return lax.ppermute(x, "row", pairs)

    def after(x, y):
        return lax.optimization_barrier((x, y))[0]

    other = across(object_field)
    above = send(offsets, down)
    below = send(offsets, up)

    (to_twin,) = cut_slices(("here",), offsets, offsets, offsets, object_field, other, offsets)
    mid_rows = send(to_twin, twins)
    to_beyond, own_rows = cut_slices(
        ("beyond", "twin"), offsets, above, below, object_field, other, to_twin
    )
    far_rows = send(to_beyond, outward)
    pattern = send(after(measured, own_rows), twins)
    power = probe_power(after(probe, own_rows))

    mine, his0, his1, fold_far, fold_mid, fold_own = position(
        above, below, far_rows, after(mid_rows, power), own_rows, probe, pattern[0], one, two
    )
    images = mine.shape[1]
    cut = images // 2 + 1
    theirs = [across(his0), across(his1)]

    mid_got = send(fold_mid, twins)
    far_got = send(fold_far, inward)

    farthest = mine[0] + theirs[0][0]
    ahead, behind = send(farthest[:cut], forward), send(farthest[cut:], reverse)
    power, theirs[1] = lax.optimization_barrier((power, theirs[1]))
    behind, mid_got, far_got = lax.optimization_barrier((behind, mid_got, far_got))
    object_den, den_edge = weights(count, offsets, above, below, power, rows, cols)
    den_edge = across(den_edge)
    low = cut
    for leg in (1, 3, 5):
        ahead = send(add_leg(ahead, 0, mine, leg, theirs[1], leg - 1), forward)
        behind = send(add_leg(behind, low, mine, leg + 1, theirs[1], leg), reverse)
        low = 0
    message = close(ahead, behind, mine, theirs[1], object_den, den_edge)
    if count > RING:
        blocks = [[b * RING + i for b in range(count // RING)] for i in range(RING)]
        total = lax.psum(message[: 16 * images], "row", axis_index_groups=blocks)
        top = lax.pmax(message[16 * images :], "row", axis_index_groups=blocks)
        message = jnp.concatenate([total, top], axis=0)

    messages = [message]
    ahead, behind = send(message, forward), send(message, reverse)
    messages += [ahead, behind]
    inner, edge = fold(offsets, above, below, fold_own, mid_got, far_got, rows, cols)
    edge = across(edge)
    for hop in range(2):
        ahead, behind = send(ahead, forward), send(behind, reverse)
        messages += [ahead, behind]
    behind, edge = lax.optimization_barrier((behind, edge))
    messages += [send(ahead[: 16 * cut], forward), send(behind[16 * cut :], reverse)]
    messages += [across(x) for x in messages]
    return finish(probe, object_field, inner, edge, object_den, den_edge, messages)


def solution(mesh):
    placed = (
        P(None, ("groups", "row"), "col"),
        P("groups", None, None, None),
        P(("groups", "row", "col"), None, None),
        P(("groups", "row", "col"), None),
    )
    return jax.shard_map(
        shards,
        mesh=mesh,
        in_specs=placed,
        out_specs=(P(None, ("groups", "row"), "col"), P("groups", None, None, None)),
        check_vma=False,
    )
```

```python
import functools
import math

import jax
import jax.numpy as jnp
import ml_dtypes
import numpy as np
from jax import lax
from jax.experimental import pallas as pl
from jax.experimental.pallas import tpu as pltpu
from jax.sharding import PartitionSpec as P

REGULAR = 0.25
AMP_FLOOR = 2.0
RING = 8
RING_ORDER = (0, 1, 3, 5, 7, 6, 4, 2)
HOPS = (0, -1, 1, -2, 2, -3, 3, 4)

SMEM = pl.BlockSpec(memory_space=pltpu.SMEM)
VMEM = pl.BlockSpec(memory_space=pltpu.VMEM)
ANY = pl.BlockSpec(memory_space=pl.ANY)
HBM = pl.BlockSpec(memory_space=pltpu.HBM)


def transform_blocks(length):
    indices = np.arange(length, dtype=np.int32)
    phases = indices[:, None] * indices[None, :] % length
    angles = phases.astype(np.float32) * np.float32(2.0 * math.pi / length)
    factor = np.float32(1.0 / math.sqrt(length))
    cos = (np.cos(angles) * factor).astype(ml_dtypes.bfloat16)
    sin = (-np.sin(angles) * factor).astype(ml_dtypes.bfloat16)
    one = np.block([[cos, -sin], [sin, cos]])
    return one, np.ascontiguousarray(one.T)


def ring_place(r):
    r = lax.rem(r, RING)
    return jnp.where(r == 0, 0, jnp.where(lax.rem(r, 2) == 1, (r + 1) // 2, RING - r // 2))


def params(mib):
    return pltpu.CompilerParams(vmem_limit_bytes=mib * 1024 * 1024)


def f32(*shape):
    return jax.ShapeDtypeStruct(shape, jnp.float32)


def begin(copies):
    for copy in copies:
        copy.start()
    return copies


def end(copies):
    for copy in copies:
        copy.wait()


def slices_kernel(offsets_at, *refs):
    offsets_in, (block, other, _), outs, (ext, cuts, offsets, sems) = refs[:3], refs[3:6], refs[6:-4], refs[-4:]
    odd = lax.rem(lax.axis_index("row"), 2) == 1
    core = lax.axis_index("col")
    cols = block.shape[2]
    end_of = cols + 128
    source = pl.multiple_of(core * (cols - 128), 128)
    target = pl.multiple_of((1 - core) * end_of, 128)
    blank = pl.multiple_of(core * end_of, 128)
    copies = begin(
        (
            pltpu.make_async_copy(block, ext.at[:, :, 128:end_of], sems.at[0]),
            pltpu.make_async_copy(
                other.at[:, :, pl.ds(source, 128)], ext.at[:, :, pl.ds(target, 128)], sems.at[1]
            ),
        )
        + tuple(
            pltpu.make_async_copy(spot, offsets.at[n], sems.at[4 + n]) for n, spot in enumerate(offsets_in)
        )
    )
    ext[:, :, pl.ds(blank, 128)] = jnp.zeros((2, block.shape[1], 128), jnp.float32)
    end(copies)
    here, above, below = offsets[0, 0, 1], offsets[1, 0, 1], offsets[2, 0, 1]
    columns = {
        "here": here,
        "twin": jnp.where(odd, above, below),
        "beyond": jnp.where(odd, below, above),
    }
    copies = ()
    for number, (which, out) in enumerate(zip(offsets_at, outs)):
        start = columns[which]
        base = pl.multiple_of(start // 128 * 128, 128)
        for part in range(2):
            wide = ext[part, :, pl.ds(base, 384)]
            wide = pltpu.roll(wide, (384 - start % 128) % 384, 1)
            cuts[number, part] = wide[:, 0:256]
        copies += begin((pltpu.make_async_copy(cuts.at[number], out, sems.at[2 + number]),))
    end(copies)


def cut_slices(offsets_at, here, above, below, block, other, ordered):
    rows, cols = block.shape[1], block.shape[2]
    count = len(offsets_at)
    return pl.pallas_call(
        functools.partial(slices_kernel, offsets_at),
        out_shape=(f32(2, rows, 256),) * count,
        in_specs=[ANY] * 3 + [HBM] + [ANY] * 2,
        out_specs=(ANY,) * count,
        scratch_shapes=[
            pltpu.VMEM((2, rows, cols + 256), jnp.float32),
            pltpu.VMEM((count, 2, rows, 256), jnp.float32),
            pltpu.SMEM((3, 1, 2), jnp.int32),
            pltpu.SemaphoreType.DMA((7,)),
        ],
        compiler_params=params(6),
        name="cut_slices",
    )(here, above, below, block, other, ordered)


def power_kernel(probe, out, held, sems):
    modes = probe.shape[0]
    copies = begin([pltpu.make_async_copy(probe.at[m], held.at[m], sems.at[m]) for m in range(modes)])
    for m in range(modes):
        copies[m].wait()
        power = held[m, 0] * held[m, 0] + held[m, 1] * held[m, 1]
        out[...] = power if m == 0 else out[...] + power


def probe_power(probe):
    return pl.pallas_call(
        power_kernel,
        out_shape=f32(*probe.shape[2:]),
        in_specs=[ANY],
        out_specs=VMEM,
        scratch_shapes=[pltpu.VMEM(probe.shape, jnp.float32), pltpu.SemaphoreType.DMA((probe.shape[0],))],
        compiler_params=params(8),
        name="probe_power",
    )(probe)


def weights_kernel(count, here, above, below, power, inner, edge, frame, grid):
    r = lax.axis_index("row")
    present = ((r > 0).astype(jnp.float32), None, (r < count - 1).astype(jnp.float32))
    tall = jnp.concatenate([power[...], jnp.zeros((128, 256), jnp.float32)], axis=0)
    grid[...] = jnp.zeros(grid.shape, jnp.float32)
    for number, spot in enumerate((above, here, below)):
        row, col = spot[0, 0], spot[0, 1]
        frame[...] = pltpu.roll(tall, row, 0)
        lower = 128 * (2 - number)
        piece = frame[lower : lower + 128, :]
        if present[number] is not None:
            piece = piece * present[number]
        wide = jnp.concatenate([piece, jnp.zeros((128, 128), jnp.float32)], axis=1)
        base = pl.multiple_of(col // 128 * 128, 128)
        grid[:, pl.ds(base, 384)] += pltpu.roll(wide, col % 128, 1)
    size = grid.shape[1]
    inner[...] = grid[:, 128 : size - 128]
    edge[...] = jnp.where(lax.axis_index("col") == 0, grid[:, size - 128 :], grid[:, 0:128])


def weights(count, here, above, below, power, rows, cols):
    return pl.pallas_call(
        functools.partial(weights_kernel, count),
        out_shape=(f32(rows, cols), f32(rows, 128)),
        in_specs=[SMEM] * 3 + [VMEM],
        out_specs=(VMEM, VMEM),
        scratch_shapes=[
            pltpu.VMEM((384, 256), jnp.float32),
            pltpu.VMEM((rows, cols + 256), jnp.float32),
        ],
        compiler_params=params(6),
        name="object_weights",
    )(here, above, below, power)


def position_kernel(
    above, below, far_rows, mid_rows, own_rows, probe, pattern, one, two,
    mine, his0, his1, fold_far, fold_mid, fold_own,
    stack, window, far, terms, update, strength, sems, out_sems,
):
    modes = probe.shape[0]
    r = lax.axis_index("row")
    core = lax.axis_index("col")
    odd = lax.rem(r, 2)
    row = jnp.where(odd == 1, above[0, 0], below[0, 0])
    place = ring_place(r)
    far_at = pl.multiple_of(256 * (1 - odd), 128)
    own_at = pl.multiple_of(256 * odd, 128)
    stack[:, pl.ds(far_at, 128), :] = far_rows[...]
    stack[:, 128:256, :] = mid_rows[...]
    stack[:, pl.ds(own_at, 128), :] = own_rows[...]
    for part in range(2):
        window[part] = pltpu.roll(stack[part], (384 - row) % 384, 0)[0:256]

    def exit_wave(m):
        p_re, p_im = probe[m, 0], probe[m, 1]
        w_re, w_im = window[0], window[1]
        return p_re * w_re - p_im * w_im, p_re * w_im + p_im * w_re

    for m in range(modes):
        e_re, e_im = exit_wave(m)
        field = jnp.concatenate([e_re.astype(jnp.bfloat16), e_im.astype(jnp.bfloat16)], axis=0)
        half = jnp.dot(one[...], field, preferred_element_type=jnp.float32).astype(jnp.bfloat16)
        half = jnp.concatenate([half[0:256], half[256:512]], axis=1)
        out = jnp.dot(half, two[...], preferred_element_type=jnp.float32)
        far[m] = out
        power = out[:, 0:256] * out[:, 0:256] + out[:, 256:512] * out[:, 256:512]
        strength[...] = power if m == 0 else strength[...] + power

    strength[...] = jnp.sqrt(pattern[...]) / jnp.maximum(jnp.sqrt(strength[...]), AMP_FLOOR)

    def put(image, value):
        for slab in range(16):
            ahead = (slab - place) & 7
            spot = jnp.where(ahead < 4, 7 - 2 * ahead, 2 * (ahead - 4))
            terms[(slab // 8) ^ core, spot, image] = value[16 * slab : 16 * slab + 16]

    def give(low, high, at):
        images = pl.ds(low, high - low)
        return begin(
            (
                pltpu.make_async_copy(terms.at[1, 0:1, images], his0.at[:, images], out_sems.at[at]),
                pltpu.make_async_copy(terms.at[1, 1:8, images], his1.at[:, images], out_sems.at[at + 1]),
                pltpu.make_async_copy(terms.at[0, :, images], mine.at[:, images], out_sems.at[at + 2]),
            )
        )

    put(0, window[0] * window[0] + window[1] * window[1])
    given, copies = 0, ()
    for m in range(modes):
        ratio = strength[...]
        fixed = jnp.concatenate(
            [
                (far[m, :, 0:256] * ratio).astype(jnp.bfloat16),
                (far[m, :, 256:512] * ratio).astype(jnp.bfloat16),
            ],
            axis=0,
        )
        back = jnp.dot(two[...], fixed, preferred_element_type=jnp.float32).astype(jnp.bfloat16)
        back = jnp.concatenate([back[0:256], back[256:512]], axis=1)
        near = jnp.dot(back, one[...], preferred_element_type=jnp.float32)
        e_re, e_im = exit_wave(m)
        d_re = near[:, 0:256] - e_re
        d_im = near[:, 256:512] - e_im
        p_re, p_im = probe[m, 0], probe[m, 1]
        w_re, w_im = window[0], window[1]
        u_re = p_re * d_re + p_im * d_im
        u_im = p_re * d_im - p_im * d_re
        update[0] = u_re if m == 0 else update[0] + u_re
        update[1] = u_im if m == 0 else update[1] + u_im
        put(1 + 2 * m, w_re * d_re + w_im * d_im)
        put(2 + 2 * m, w_re * d_im - w_im * d_re)
        if m % 2 == 1:
            copies += give(given, 3 + 2 * m, 3 * (m // 2))
            given = 3 + 2 * m

    for part in range(2):
        tall = jnp.concatenate([update[part], jnp.zeros((128, 256), jnp.float32)], axis=0)
        stack[part] = pltpu.roll(tall, row, 0)
    copies += begin(
        (
            pltpu.make_async_copy(stack.at[:, pl.ds(far_at, 128), :], fold_far, sems.at[0]),
            pltpu.make_async_copy(stack.at[:, 128:256, :], fold_mid, sems.at[1]),
            pltpu.make_async_copy(stack.at[:, pl.ds(own_at, 128), :], fold_own, sems.at[2]),
        )
    )
    end(copies)


def position(above, below, far_rows, mid_rows, own_rows, probe, pattern, one, two):
    modes = probe.shape[0]
    images = 1 + 2 * modes
    return pl.pallas_call(
        position_kernel,
        out_shape=tuple(f32(legs, images, 16, 256) for legs in (8, 1, 7)) + (f32(2, 128, 256),) * 3,
        in_specs=[SMEM] * 2 + [VMEM] * 7,
        out_specs=(ANY,) * 6,
        scratch_shapes=[
            pltpu.VMEM((2, 384, 256), jnp.float32),
            pltpu.VMEM((2, 256, 256), jnp.float32),
            pltpu.VMEM((modes, 256, 512), jnp.float32),
            pltpu.VMEM((2, 8, images, 16, 256), jnp.float32),
            pltpu.VMEM((2, 256, 256), jnp.float32),
            pltpu.VMEM((256, 256), jnp.float32),
            pltpu.SemaphoreType.DMA((3,)),
            pltpu.SemaphoreType.DMA((3 * (modes // 2),)),
        ],
        compiler_params=params(20),
        name="position_terms",
    )(above, below, far_rows, mid_rows, own_rows, probe, pattern, one, two)


def fold_kernel(here_at, above_at, below_at, near, middle, far, inner, edge, grid):
    odd = lax.rem(lax.axis_index("row"), 2) == 1
    grid[...] = jnp.zeros(grid.shape, jnp.float32)
    near_col = jnp.where(odd, above_at[0, 1], below_at[0, 1])
    far_col = jnp.where(odd, below_at[0, 1], above_at[0, 1])
    for col, piece in ((near_col, near), (here_at[0, 1], middle), (far_col, far)):
        base = pl.multiple_of(col // 128 * 128, 128)
        for part in range(2):
            wide = jnp.concatenate([piece[part], jnp.zeros((128, 128), jnp.float32)], axis=1)
            grid[part, :, pl.ds(base, 384)] += pltpu.roll(wide, col % 128, 1)
    size = grid.shape[2]
    inner[...] = grid[:, :, 128 : size - 128]
    edge[...] = jnp.where(lax.axis_index("col") == 0, grid[:, :, size - 128 :], grid[:, :, 0:128])


def fold(here, above, below, near, middle, far, rows, cols):
    return pl.pallas_call(
        fold_kernel,
        out_shape=(f32(2, rows, cols), f32(2, rows, 128)),
        in_specs=[SMEM] * 3 + [VMEM] * 3,
        out_specs=(VMEM, VMEM),
        scratch_shapes=[pltpu.VMEM((2, rows, cols + 256), jnp.float32)],
        compiler_params=params(8),
        name="fold_object",
    )(here, above, below, near, middle, far)


def leg_kernel(low, mine_spot, theirs_spot, came, mine_at, theirs_at, out, mine, theirs, sems):
    pairs = ((mine_at.at[mine_spot], mine), (theirs_at.at[theirs_spot], theirs))
    end(begin([pltpu.make_async_copy(a, b, sems.at[n]) for n, (a, b) in enumerate(pairs)]))
    out[...] = mine[...] + theirs[...]
    out[low : low + came.shape[0]] = out[low : low + came.shape[0]] + came[...]


def add_leg(came, low, mine, mine_spot, theirs, theirs_spot):
    whole = mine.shape[1:]
    return pl.pallas_call(
        functools.partial(leg_kernel, low, mine_spot, theirs_spot),
        out_shape=f32(*whole),
        in_specs=[VMEM] + [ANY] * 2,
        out_specs=VMEM,
        scratch_shapes=[
            pltpu.VMEM(whole, jnp.float32),
            pltpu.VMEM(whole, jnp.float32),
            pltpu.SemaphoreType.DMA((2,)),
        ],
        compiler_params=params(4),
        name="add_leg",
    )(came, mine, theirs)


def close_kernel(ahead, behind, mine_at, theirs_at, den_in, edge, message, mine, theirs, den, sems):
    pairs = ((mine_at.at[mine_at.shape[0] - 1], mine), (theirs_at.at[theirs_at.shape[0] - 1], theirs))
    copies = begin([pltpu.make_async_copy(a, b, sems.at[n]) for n, (a, b) in enumerate(pairs)])
    den[...] = den_in[...]
    cols = den.shape[1]
    side = pl.multiple_of((1 - lax.axis_index("col")) * (cols - 128), 128)
    den[:, pl.ds(side, 128)] += edge[...]
    object_peak = jnp.max(den[...])
    end(copies)
    images = ahead.shape[0]
    for image in range(images):
        total = (mine[image] + theirs[image]) + (ahead[image] + behind[image])
        message[16 * image : 16 * image + 16] = total
    message[16 * images :] = jnp.full((8, 256), object_peak, jnp.float32)


def close(ahead, behind, mine, theirs, den, edge):
    shape = ahead.shape
    return pl.pallas_call(
        close_kernel,
        out_shape=f32(16 * shape[0] + 8, 256),
        in_specs=[VMEM] * 2 + [ANY] * 2 + [VMEM] * 2,
        out_specs=VMEM,
        scratch_shapes=[pltpu.VMEM(shape, jnp.float32)] * 2
        + [pltpu.VMEM(den.shape, jnp.float32), pltpu.SemaphoreType.DMA((2,))],
        compiler_params=params(6),
        name="close_sum",
    )(ahead, behind, mine, theirs, den, edge)


def pack_kernel(*refs):
    edge, messages, out = refs[0], refs[1:-1], refs[-1]
    size = messages[0].shape[0]
    for n, message in enumerate(messages):
        out[size * n : size * n + size] = message[...]
    for part in range(2):
        out[size * len(messages) :, 128 * part : 128 * part + 128] = edge[part]


def pack(edge, messages):
    size = sum(x.shape[0] for x in messages) + edge.shape[1]
    return pl.pallas_call(
        pack_kernel,
        out_shape=f32(size, 256),
        in_specs=[VMEM] * (1 + len(messages)),
        out_specs=VMEM,
        compiler_params=params(4),
        name="pack",
    )(edge, *messages)


def finish_kernel(probe, block, inner, den, den_edge, packed, packed_parts, *refs):
    per_owner = len(HOPS) + 1
    messages, refs = refs[:per_owner], refs[per_owner:]
    size, cut = messages[0].shape[0], messages[per_owner - 2].shape[0]
    messages += tuple(packed.at[size * n : size * n + size] for n in range(per_owner - 2))
    messages += (packed_parts.at[0:cut], packed_parts.at[cut:size])
    edge = packed.at[size * (per_owner - 2) :]
    new_block_at, new_probe_at, new_probe, new_block, whole_den, scales, sems = refs
    modes = probe.shape[0]
    core = lax.axis_index("col")
    place = ring_place(lax.axis_index("row"))
    cols = block.shape[2]
    peak = jnp.zeros((8, 256), jnp.float32)
    object_peak = jnp.zeros((8, 256), jnp.float32)
    for n, message in enumerate(messages):
        if n % per_owner != per_owner - 1:
            peak = jnp.maximum(peak, jnp.maximum(message[0:8], message[8:16]))
        if n % per_owner != per_owner - 2:
            object_peak = jnp.maximum(object_peak, message[message.shape[0] - 8 :])
    peak = jnp.max(peak)
    object_peak = jnp.max(object_peak)
    starts = []
    for owner in range(2):
        half = core if owner == 0 else 1 - core
        for n, hop in enumerate(HOPS):
            starts.append(pl.multiple_of(128 * half + 16 * ((place + hop) & 7), 16))
            den_rows = messages[per_owner * owner + n][0:16]
            scales[len(HOPS) * owner + n] = 1.0 / ((1.0 - REGULAR) * den_rows + REGULAR * peak)
    outs = ()
    for m in range(modes):
        for part in range(2):
            at = 16 * (1 + 2 * m + part)
            for owner in range(2):
                for n, hop in enumerate(HOPS):
                    first = per_owner * owner
                    if hop != 4 or at < cut:
                        value = messages[first + n][at : at + 16]
                    else:
                        value = messages[first + n + 1][at - cut : at - cut + 16]
                    spot = len(HOPS) * owner + n
                    rows = pl.ds(starts[spot], 16)
                    new_probe[m, part, rows, :] = probe[m, part, rows, :] + value * scales[spot]
        outs += begin((pltpu.make_async_copy(new_probe.at[m], new_probe_at.at[m], sems.at[m]),))
    side = pl.multiple_of((1 - core) * (cols - 128), 128)
    new_block[...] = inner[...]
    for part in range(2):
        new_block[part, :, pl.ds(side, 128)] += edge[:, 128 * part : 128 * part + 128]
    whole_den[...] = den[...]
    whole_den[:, pl.ds(side, 128)] += den_edge[...]
    scale = 1.0 / ((1.0 - REGULAR) * whole_den[...] + REGULAR * object_peak)
    for part in range(2):
        new_block[part] = block[part] + new_block[part] * scale
    outs += begin((pltpu.make_async_copy(new_block, new_block_at, sems.at[modes]),))
    end(outs)


def finish(probe, block, inner, den, den_edge, packed, packed_parts, messages):
    modes = probe.shape[0]
    return pl.pallas_call(
        finish_kernel,
        out_shape=(f32(*block.shape), f32(*probe.shape)),
        in_specs=[VMEM] * (7 + len(messages)),
        out_specs=(ANY, ANY),
        scratch_shapes=[pltpu.VMEM(x.shape, jnp.float32) for x in (probe, block, den)]
        + [
            pltpu.VMEM((2 * len(HOPS), 16, 256), jnp.float32),
            pltpu.SemaphoreType.DMA((modes + 1,)),
        ],
        compiler_params=params(12),
        name="finish",
    )(probe, block, inner, den, den_edge, packed, packed_parts, *messages)


def shards(object_field, probe, measured, offsets):
    rows, cols = object_field.shape[1], object_field.shape[2]
    count = lax.axis_size("row")
    one, two = transform_blocks(probe.shape[-1])
    one, two = jnp.asarray(one), jnp.asarray(two)

    twins = [(i, i ^ 1) for i in range(count)]
    cores = [(0, 1), (1, 0)]
    down = [(i, i + 1) for i in range(count - 1)]
    up = [(i + 1, i) for i in range(count - 1)]
    outward = [(i, i + 2) for i in range(1, count - 2, 2)] + [(i, i - 2) for i in range(2, count, 2)]
    inward = [(b, a) for a, b in outward]
    forward = [
        (block + RING_ORDER[i], block + RING_ORDER[(i + 1) % RING])
        for block in range(0, count, RING)
        for i in range(RING)
    ]
    reverse = [(b, a) for a, b in forward]

    def across(x):
        return lax.ppermute(x, "col", cores)

    def send(x, pairs):
        return lax.ppermute(x, "row", pairs)

    def after(x, y):
        return lax.optimization_barrier((x, y))[0]

    other = across(object_field)
    above = send(offsets, down)
    below = send(offsets, up)

    (to_twin,) = cut_slices(("here",), offsets, offsets, offsets, object_field, other, offsets)
    mid_rows = send(to_twin, twins)
    to_beyond, own_rows = cut_slices(
        ("beyond", "twin"), offsets, above, below, object_field, other, to_twin
    )
    far_rows = send(to_beyond, outward)
    pattern = send(after(measured, own_rows), twins)
    power = probe_power(after(probe, own_rows))
    object_den, den_edge = weights(count, offsets, above, below, power, rows, cols)
    den_edge = across(den_edge)

    mine, his0, his1, fold_far, fold_mid, fold_own = position(
        above, below, far_rows, after(mid_rows, den_edge), own_rows, probe, pattern[0], one, two
    )
    images = mine.shape[1]
    cut = images // 2 + 1
    theirs = [across(his0), across(his1)]

    mid_got = send(fold_mid, twins)
    far_got = send(fold_far, inward)

    farthest = mine[0] + theirs[0][0]
    ahead, behind = send(farthest[:cut], forward), send(farthest[cut:], reverse)
    low = cut
    for leg in (1, 3, 5):
        ahead = send(add_leg(ahead, 0, mine, leg, theirs[1], leg - 1), forward)
        behind = send(add_leg(behind, low, mine, leg + 1, theirs[1], leg), reverse)
        low = 0
    message = close(ahead, behind, mine, theirs[1], object_den, den_edge)
    if count > RING:
        blocks = [[b * RING + i for b in range(count // RING)] for i in range(RING)]
        total = lax.psum(message[: 16 * images], "row", axis_index_groups=blocks)
        top = lax.pmax(message[16 * images :], "row", axis_index_groups=blocks)
        message = jnp.concatenate([total, top], axis=0)

    messages = [message]
    ahead, behind = send(message, forward), send(message, reverse)
    messages += [ahead, behind]
    inner, edge = fold(offsets, above, below, fold_own, mid_got, far_got, rows, cols)
    for hop in range(2):
        ahead, behind = send(ahead, forward), send(behind, reverse)
        messages += [ahead, behind]
    parts = [send(ahead[: 16 * cut], forward), send(behind[16 * cut :], reverse)]
    packed = across(pack(edge, messages))
    packed_parts = across(jnp.concatenate(parts, axis=0))
    return finish(probe, object_field, inner, object_den, den_edge, packed, packed_parts, messages + parts)


def solution(mesh):
    placed = (
        P(None, ("groups", "row"), "col"),
        P("groups", None, None, None),
        P(("groups", "row", "col"), None, None),
        P(("groups", "row", "col"), None),
    )
    return jax.shard_map(
        shards,
        mesh=mesh,
        in_specs=placed,
        out_specs=(P(None, ("groups", "row"), "col"), P("groups", None, None, None)),
        check_vma=False,
    )
```

```python
import functools
import math

import jax
import jax.numpy as jnp
import ml_dtypes
import numpy as np
from jax import lax
from jax.experimental import pallas as pl
from jax.experimental.pallas import tpu as pltpu
from jax.sharding import PartitionSpec as P

REGULAR = 0.25
AMP_FLOOR = 2.0
RING = 8
RING_ORDER = (0, 1, 3, 5, 7, 6, 4, 2)
HOPS = (0, -1, 1, -2, 2, -3, 3, 4)

SMEM = pl.BlockSpec(memory_space=pltpu.SMEM)
VMEM = pl.BlockSpec(memory_space=pltpu.VMEM)
ANY = pl.BlockSpec(memory_space=pl.ANY)
HBM = pl.BlockSpec(memory_space=pltpu.HBM)


def transform_blocks(length):
    indices = np.arange(length, dtype=np.int32)
    phases = indices[:, None] * indices[None, :] % length
    angles = phases.astype(np.float32) * np.float32(2.0 * math.pi / length)
    factor = np.float32(1.0 / math.sqrt(length))
    cos = (np.cos(angles) * factor).astype(ml_dtypes.bfloat16)
    sin = (-np.sin(angles) * factor).astype(ml_dtypes.bfloat16)
    one = np.block([[cos, -sin], [sin, cos]])
    return one, np.ascontiguousarray(one.T)


def ring_place(r):
    r = lax.rem(r, RING)
    return jnp.where(r == 0, 0, jnp.where(lax.rem(r, 2) == 1, (r + 1) // 2, RING - r // 2))


def params(mib):
    return pltpu.CompilerParams(vmem_limit_bytes=mib * 1024 * 1024)


def f32(*shape):
    return jax.ShapeDtypeStruct(shape, jnp.float32)


def begin(copies):
    for copy in copies:
        copy.start()
    return copies


def end(copies):
    for copy in copies:
        copy.wait()


def slices_kernel(offsets_at, *refs):
    offsets_in, (block, other, _), outs, (ext, cuts, offsets, sems) = refs[:3], refs[3:6], refs[6:-4], refs[-4:]
    odd = lax.rem(lax.axis_index("row"), 2) == 1
    core = lax.axis_index("col")
    cols = block.shape[2]
    end_of = cols + 128
    source = pl.multiple_of(core * (cols - 128), 128)
    target = pl.multiple_of((1 - core) * end_of, 128)
    blank = pl.multiple_of(core * end_of, 128)
    copies = begin(
        (
            pltpu.make_async_copy(block, ext.at[:, :, 128:end_of], sems.at[0]),
            pltpu.make_async_copy(
                other.at[:, :, pl.ds(source, 128)], ext.at[:, :, pl.ds(target, 128)], sems.at[1]
            ),
        )
        + tuple(
            pltpu.make_async_copy(spot, offsets.at[n], sems.at[4 + n]) for n, spot in enumerate(offsets_in)
        )
    )
    ext[:, :, pl.ds(blank, 128)] = jnp.zeros((2, block.shape[1], 128), jnp.float32)
    end(copies)
    here, above, below = offsets[0, 0, 1], offsets[1, 0, 1], offsets[2, 0, 1]
    columns = {
        "here": here,
        "twin": jnp.where(odd, above, below),
        "beyond": jnp.where(odd, below, above),
    }
    copies = ()
    for number, (which, out) in enumerate(zip(offsets_at, outs)):
        start = columns[which]
        base = pl.multiple_of(start // 128 * 128, 128)
        for part in range(2):
            wide = ext[part, :, pl.ds(base, 384)]
            wide = pltpu.roll(wide, (384 - start % 128) % 384, 1)
            cuts[number, part] = wide[:, 0:256]
        copies += begin((pltpu.make_async_copy(cuts.at[number], out, sems.at[2 + number]),))
    end(copies)


def cut_slices(offsets_at, here, above, below, block, other, ordered):
    rows, cols = block.shape[1], block.shape[2]
    count = len(offsets_at)
    return pl.pallas_call(
        functools.partial(slices_kernel, offsets_at),
        out_shape=(f32(2, rows, 256),) * count,
        in_specs=[ANY] * 3 + [HBM] + [ANY] * 2,
        out_specs=(ANY,) * count,
        scratch_shapes=[
            pltpu.VMEM((2, rows, cols + 256), jnp.float32),
            pltpu.VMEM((count, 2, rows, 256), jnp.float32),
            pltpu.SMEM((3, 1, 2), jnp.int32),
            pltpu.SemaphoreType.DMA((7,)),
        ],
        compiler_params=params(6),
        name="cut_slices",
    )(here, above, below, block, other, ordered)


def power_kernel(probe, out, held, sems):
    modes = probe.shape[0]
    copies = begin([pltpu.make_async_copy(probe.at[m], held.at[m], sems.at[m]) for m in range(modes)])
    for m in range(modes):
        copies[m].wait()
        power = held[m, 0] * held[m, 0] + held[m, 1] * held[m, 1]
        out[...] = power if m == 0 else out[...] + power


def probe_power(probe):
    return pl.pallas_call(
        power_kernel,
        out_shape=f32(*probe.shape[2:]),
        in_specs=[ANY],
        out_specs=VMEM,
        scratch_shapes=[pltpu.VMEM(probe.shape, jnp.float32), pltpu.SemaphoreType.DMA((probe.shape[0],))],
        compiler_params=params(8),
        name="probe_power",
    )(probe)


def weights_kernel(count, here, above, below, power, inner, edge, frame, grid):
    r = lax.axis_index("row")
    present = ((r > 0).astype(jnp.float32), None, (r < count - 1).astype(jnp.float32))
    tall = jnp.concatenate([power[...], jnp.zeros((128, 256), jnp.float32)], axis=0)
    grid[...] = jnp.zeros(grid.shape, jnp.float32)
    for number, spot in enumerate((above, here, below)):
        row, col = spot[0, 0], spot[0, 1]
        frame[...] = pltpu.roll(tall, row, 0)
        lower = 128 * (2 - number)
        piece = frame[lower : lower + 128, :]
        if present[number] is not None:
            piece = piece * present[number]
        wide = jnp.concatenate([piece, jnp.zeros((128, 128), jnp.float32)], axis=1)
        base = pl.multiple_of(col // 128 * 128, 128)
        grid[:, pl.ds(base, 384)] += pltpu.roll(wide, col % 128, 1)
    size = grid.shape[1]
    inner[...] = grid[:, 128 : size - 128]
    edge[...] = jnp.where(lax.axis_index("col") == 0, grid[:, size - 128 :], grid[:, 0:128])


def weights(count, here, above, below, power, rows, cols):
    return pl.pallas_call(
        functools.partial(weights_kernel, count),
        out_shape=(f32(rows, cols), f32(rows, 128)),
        in_specs=[SMEM] * 3 + [VMEM],
        out_specs=(VMEM, VMEM),
        scratch_shapes=[
            pltpu.VMEM((384, 256), jnp.float32),
            pltpu.VMEM((rows, cols + 256), jnp.float32),
        ],
        compiler_params=params(6),
        name="object_weights",
    )(here, above, below, power)


def position_kernel(
    above, below, far_rows, mid_rows, own_rows, probe, pattern, one, two,
    mine, his0, his1, fold_far, fold_mid, fold_own,
    stack, window, far, terms, update, strength, sems, out_sems,
):
    modes = probe.shape[0]
    r = lax.axis_index("row")
    core = lax.axis_index("col")
    odd = lax.rem(r, 2)
    row = jnp.where(odd == 1, above[0, 0], below[0, 0])
    place = ring_place(r)
    far_at = pl.multiple_of(256 * (1 - odd), 128)
    own_at = pl.multiple_of(256 * odd, 128)
    stack[:, pl.ds(far_at, 128), :] = far_rows[...]
    stack[:, 128:256, :] = mid_rows[...]
    stack[:, pl.ds(own_at, 128), :] = own_rows[...]
    for part in range(2):
        window[part] = pltpu.roll(stack[part], (384 - row) % 384, 0)[0:256]

    def exit_wave(m):
        p_re, p_im = probe[m, 0], probe[m, 1]
        w_re, w_im = window[0], window[1]
        return p_re * w_re - p_im * w_im, p_re * w_im + p_im * w_re

    for m in range(modes):
        e_re, e_im = exit_wave(m)
        field = jnp.concatenate([e_re.astype(jnp.bfloat16), e_im.astype(jnp.bfloat16)], axis=0)
        half = jnp.dot(one[...], field, preferred_element_type=jnp.float32).astype(jnp.bfloat16)
        half = jnp.concatenate([half[0:256], half[256:512]], axis=1)
        out = jnp.dot(half, two[...], preferred_element_type=jnp.float32)
        far[m] = out
        power = out[:, 0:256] * out[:, 0:256] + out[:, 256:512] * out[:, 256:512]
        strength[...] = power if m == 0 else strength[...] + power

    strength[...] = jnp.sqrt(pattern[...]) / jnp.maximum(jnp.sqrt(strength[...]), AMP_FLOOR)

    def put(image, value):
        for slab in range(16):
            ahead = (slab - place) & 7
            spot = jnp.where(ahead < 4, 7 - 2 * ahead, 2 * (ahead - 4))
            terms[(slab // 8) ^ core, spot, image] = value[16 * slab : 16 * slab + 16]

    def give(low, high, at):
        images = pl.ds(low, high - low)
        return begin(
            (
                pltpu.make_async_copy(terms.at[1, 0:1, images], his0.at[:, images], out_sems.at[at]),
                pltpu.make_async_copy(terms.at[1, 1:8, images], his1.at[:, images], out_sems.at[at + 1]),
                pltpu.make_async_copy(terms.at[0, :, images], mine.at[:, images], out_sems.at[at + 2]),
            )
        )

    put(0, window[0] * window[0] + window[1] * window[1])
    given, copies = 0, ()
    for m in range(modes):
        ratio = strength[...]
        fixed = jnp.concatenate(
            [
                (far[m, :, 0:256] * ratio).astype(jnp.bfloat16),
                (far[m, :, 256:512] * ratio).astype(jnp.bfloat16),
            ],
            axis=0,
        )
        back = jnp.dot(two[...], fixed, preferred_element_type=jnp.float32).astype(jnp.bfloat16)
        back = jnp.concatenate([back[0:256], back[256:512]], axis=1)
        near = jnp.dot(back, one[...], preferred_element_type=jnp.float32)
        e_re, e_im = exit_wave(m)
        d_re = near[:, 0:256] - e_re
        d_im = near[:, 256:512] - e_im
        p_re, p_im = probe[m, 0], probe[m, 1]
        w_re, w_im = window[0], window[1]
        u_re = p_re * d_re + p_im * d_im
        u_im = p_re * d_im - p_im * d_re
        update[0] = u_re if m == 0 else update[0] + u_re
        update[1] = u_im if m == 0 else update[1] + u_im
        put(1 + 2 * m, w_re * d_re + w_im * d_im)
        put(2 + 2 * m, w_re * d_im - w_im * d_re)
        if m % 2 == 1:
            copies += give(given, 3 + 2 * m, 3 * (m // 2))
            given = 3 + 2 * m

    for part in range(2):
        tall = jnp.concatenate([update[part], jnp.zeros((128, 256), jnp.float32)], axis=0)
        stack[part] = pltpu.roll(tall, row, 0)
    copies += begin(
        (
            pltpu.make_async_copy(stack.at[:, pl.ds(far_at, 128), :], fold_far, sems.at[0]),
            pltpu.make_async_copy(stack.at[:, 128:256, :], fold_mid, sems.at[1]),
            pltpu.make_async_copy(stack.at[:, pl.ds(own_at, 128), :], fold_own, sems.at[2]),
        )
    )
    end(copies)


def position(above, below, far_rows, mid_rows, own_rows, probe, pattern, one, two):
    modes = probe.shape[0]
    images = 1 + 2 * modes
    return pl.pallas_call(
        position_kernel,
        out_shape=tuple(f32(legs, images, 16, 256) for legs in (8, 1, 7)) + (f32(2, 128, 256),) * 3,
        in_specs=[SMEM] * 2 + [VMEM] * 7,
        out_specs=(ANY,) * 6,
        scratch_shapes=[
            pltpu.VMEM((2, 384, 256), jnp.float32),
            pltpu.VMEM((2, 256, 256), jnp.float32),
            pltpu.VMEM((modes, 256, 512), jnp.float32),
            pltpu.VMEM((2, 8, images, 16, 256), jnp.float32),
            pltpu.VMEM((2, 256, 256), jnp.float32),
            pltpu.VMEM((256, 256), jnp.float32),
            pltpu.SemaphoreType.DMA((3,)),
            pltpu.SemaphoreType.DMA((3 * (modes // 2),)),
        ],
        compiler_params=params(20),
        name="position_terms",
    )(above, below, far_rows, mid_rows, own_rows, probe, pattern, one, two)


def fold_kernel(here_at, above_at, below_at, near, middle, far, inner, edge, grid):
    odd = lax.rem(lax.axis_index("row"), 2) == 1
    grid[...] = jnp.zeros(grid.shape, jnp.float32)
    near_col = jnp.where(odd, above_at[0, 1], below_at[0, 1])
    far_col = jnp.where(odd, below_at[0, 1], above_at[0, 1])
    for col, piece in ((near_col, near), (here_at[0, 1], middle), (far_col, far)):
        base = pl.multiple_of(col // 128 * 128, 128)
        for part in range(2):
            wide = jnp.concatenate([piece[part], jnp.zeros((128, 128), jnp.float32)], axis=1)
            grid[part, :, pl.ds(base, 384)] += pltpu.roll(wide, col % 128, 1)
    size = grid.shape[2]
    inner[...] = grid[:, :, 128 : size - 128]
    edge[...] = jnp.where(lax.axis_index("col") == 0, grid[:, :, size - 128 :], grid[:, :, 0:128])


def fold(here, above, below, near, middle, far, rows, cols):
    return pl.pallas_call(
        fold_kernel,
        out_shape=(f32(2, rows, cols), f32(2, rows, 128)),
        in_specs=[SMEM] * 3 + [VMEM] * 3,
        out_specs=(VMEM, VMEM),
        scratch_shapes=[pltpu.VMEM((2, rows, cols + 256), jnp.float32)],
        compiler_params=params(8),
        name="fold_object",
    )(here, above, below, near, middle, far)


def leg_kernel(low, mine_spot, theirs_spot, came, mine_at, theirs_at, out, mine, theirs, sems):
    pairs = ((mine_at.at[mine_spot], mine), (theirs_at.at[theirs_spot], theirs))
    end(begin([pltpu.make_async_copy(a, b, sems.at[n]) for n, (a, b) in enumerate(pairs)]))
    out[...] = mine[...] + theirs[...]
    out[low : low + came.shape[0]] = out[low : low + came.shape[0]] + came[...]


def add_leg(came, low, mine, mine_spot, theirs, theirs_spot):
    whole = mine.shape[1:]
    return pl.pallas_call(
        functools.partial(leg_kernel, low, mine_spot, theirs_spot),
        out_shape=f32(*whole),
        in_specs=[VMEM] + [ANY] * 2,
        out_specs=VMEM,
        scratch_shapes=[
            pltpu.VMEM(whole, jnp.float32),
            pltpu.VMEM(whole, jnp.float32),
            pltpu.SemaphoreType.DMA((2,)),
        ],
        compiler_params=params(4),
        name="add_leg",
    )(came, mine, theirs)


def close_kernel(ahead, behind, mine_at, theirs_at, den_in, edge, message, mine, theirs, den, sems):
    pairs = ((mine_at.at[mine_at.shape[0] - 1], mine), (theirs_at.at[theirs_at.shape[0] - 1], theirs))
    copies = begin([pltpu.make_async_copy(a, b, sems.at[n]) for n, (a, b) in enumerate(pairs)])
    den[...] = den_in[...]
    cols = den.shape[1]
    side = pl.multiple_of((1 - lax.axis_index("col")) * (cols - 128), 128)
    den[:, pl.ds(side, 128)] += edge[...]
    object_peak = jnp.max(den[...])
    end(copies)
    images = ahead.shape[0]
    for image in range(images):
        total = (mine[image] + theirs[image]) + (ahead[image] + behind[image])
        message[16 * image : 16 * image + 16] = total
    message[16 * images :] = jnp.full((8, 256), object_peak, jnp.float32)


def close(ahead, behind, mine, theirs, den, edge):
    shape = ahead.shape
    return pl.pallas_call(
        close_kernel,
        out_shape=f32(16 * shape[0] + 8, 256),
        in_specs=[VMEM] * 2 + [ANY] * 2 + [VMEM] * 2,
        out_specs=VMEM,
        scratch_shapes=[pltpu.VMEM(shape, jnp.float32)] * 2
        + [pltpu.VMEM(den.shape, jnp.float32), pltpu.SemaphoreType.DMA((2,))],
        compiler_params=params(6),
        name="close_sum",
    )(ahead, behind, mine, theirs, den, edge)


def pack_kernel(*refs):
    edge, messages, out = refs[0], refs[1:-1], refs[-1]
    size = messages[0].shape[0]
    for n, message in enumerate(messages):
        out[size * n : size * n + size] = message[...]
    for part in range(2):
        out[size * len(messages) :, 128 * part : 128 * part + 128] = edge[part]


def pack(edge, messages):
    size = sum(x.shape[0] for x in messages) + edge.shape[1]
    return pl.pallas_call(
        pack_kernel,
        out_shape=f32(size, 256),
        in_specs=[VMEM] * (1 + len(messages)),
        out_specs=VMEM,
        compiler_params=params(4),
        name="pack",
    )(edge, *messages)


def finish_kernel(probe, block, inner, den, den_edge, swapped, packed, packed_parts, *refs):
    per_owner = len(HOPS) + 1
    messages, refs = refs[:per_owner], refs[per_owner:]
    size, cut = messages[0].shape[0], messages[per_owner - 2].shape[0]
    messages += (swapped,) + tuple(packed.at[size * n : size * n + size] for n in range(per_owner - 3))
    messages += (packed_parts.at[0:cut], packed_parts.at[cut:size])
    edge = packed.at[size * (per_owner - 3) :]
    new_block_at, new_probe_at, new_probe, new_block, whole_den, scales, sems = refs
    modes = probe.shape[0]
    core = lax.axis_index("col")
    place = ring_place(lax.axis_index("row"))
    cols = block.shape[2]
    peak = jnp.zeros((8, 256), jnp.float32)
    object_peak = jnp.zeros((8, 256), jnp.float32)
    for n, message in enumerate(messages):
        if n % per_owner != per_owner - 1:
            peak = jnp.maximum(peak, jnp.maximum(message[0:8], message[8:16]))
        if n % per_owner != per_owner - 2:
            object_peak = jnp.maximum(object_peak, message[message.shape[0] - 8 :])
    peak = jnp.max(peak)
    object_peak = jnp.max(object_peak)
    starts = []
    for owner in range(2):
        half = core if owner == 0 else 1 - core
        for n, hop in enumerate(HOPS):
            starts.append(pl.multiple_of(128 * half + 16 * ((place + hop) & 7), 16))
            den_rows = messages[per_owner * owner + n][0:16]
            scales[len(HOPS) * owner + n] = 1.0 / ((1.0 - REGULAR) * den_rows + REGULAR * peak)
    outs = ()
    for m in range(modes):
        for part in range(2):
            at = 16 * (1 + 2 * m + part)
            for owner in range(2):
                for n, hop in enumerate(HOPS):
                    first = per_owner * owner
                    if hop != 4 or at < cut:
                        value = messages[first + n][at : at + 16]
                    else:
                        value = messages[first + n + 1][at - cut : at - cut + 16]
                    spot = len(HOPS) * owner + n
                    rows = pl.ds(starts[spot], 16)
                    new_probe[m, part, rows, :] = probe[m, part, rows, :] + value * scales[spot]
        outs += begin((pltpu.make_async_copy(new_probe.at[m], new_probe_at.at[m], sems.at[m]),))
    side = pl.multiple_of((1 - core) * (cols - 128), 128)
    new_block[...] = inner[...]
    for part in range(2):
        new_block[part, :, pl.ds(side, 128)] += edge[:, 128 * part : 128 * part + 128]
    whole_den[...] = den[...]
    whole_den[:, pl.ds(side, 128)] += den_edge[...]
    scale = 1.0 / ((1.0 - REGULAR) * whole_den[...] + REGULAR * object_peak)
    for part in range(2):
        new_block[part] = block[part] + new_block[part] * scale
    outs += begin((pltpu.make_async_copy(new_block, new_block_at, sems.at[modes]),))
    end(outs)


def finish(probe, block, inner, den, den_edge, swapped, packed, packed_parts, messages):
    modes = probe.shape[0]
    return pl.pallas_call(
        finish_kernel,
        out_shape=(f32(*block.shape), f32(*probe.shape)),
        in_specs=[VMEM] * (8 + len(messages)),
        out_specs=(ANY, ANY),
        scratch_shapes=[pltpu.VMEM(x.shape, jnp.float32) for x in (probe, block, den)]
        + [
            pltpu.VMEM((2 * len(HOPS), 16, 256), jnp.float32),
            pltpu.SemaphoreType.DMA((modes + 1,)),
        ],
        compiler_params=params(12),
        name="finish",
    )(probe, block, inner, den, den_edge, swapped, packed, packed_parts, *messages)


def shards(object_field, probe, measured, offsets):
    rows, cols = object_field.shape[1], object_field.shape[2]
    count = lax.axis_size("row")
    one, two = transform_blocks(probe.shape[-1])
    one, two = jnp.asarray(one), jnp.asarray(two)

    twins = [(i, i ^ 1) for i in range(count)]
    cores = [(0, 1), (1, 0)]
    down = [(i, i + 1) for i in range(count - 1)]
    up = [(i + 1, i) for i in range(count - 1)]
    outward = [(i, i + 2) for i in range(1, count - 2, 2)] + [(i, i - 2) for i in range(2, count, 2)]
    inward = [(b, a) for a, b in outward]
    forward = [
        (block + RING_ORDER[i], block + RING_ORDER[(i + 1) % RING])
        for block in range(0, count, RING)
        for i in range(RING)
    ]
    reverse = [(b, a) for a, b in forward]

    def across(x):
        return lax.ppermute(x, "col", cores)

    def send(x, pairs):
        return lax.ppermute(x, "row", pairs)

    def after(x, y):
        return lax.optimization_barrier((x, y))[0]

    other = across(object_field)
    above = send(offsets, down)
    below = send(offsets, up)
    pattern = send(measured, twins)

    (to_twin,) = cut_slices(("here",), offsets, offsets, offsets, object_field, other, offsets)
    mid_rows = send(to_twin, twins)
    to_beyond, own_rows = cut_slices(
        ("beyond", "twin"), offsets, above, below, object_field, other, to_twin
    )
    far_rows = send(to_beyond, outward)
    power = probe_power(after(probe, own_rows))
    object_den, den_edge = weights(count, offsets, above, below, power, rows, cols)
    den_edge = across(den_edge)

    mine, his0, his1, fold_far, fold_mid, fold_own = position(
        above, below, far_rows, after(mid_rows, den_edge), own_rows, probe, pattern[0], one, two
    )
    images = mine.shape[1]
    cut = images // 2 + 1
    theirs = [across(his0)]
    theirs += [across(after(his1, theirs[0]))]

    mid_got = send(fold_mid, twins)
    far_got = send(fold_far, inward)

    farthest = mine[0] + theirs[0][0]
    ahead, behind = send(farthest[:cut], forward), send(farthest[cut:], reverse)
    low = cut
    for leg in (1, 3, 5):
        ahead = send(add_leg(ahead, 0, mine, leg, theirs[1], leg - 1), forward)
        behind = send(add_leg(behind, low, mine, leg + 1, theirs[1], leg), reverse)
        low = 0
    message = close(ahead, behind, mine, theirs[1], object_den, den_edge)
    if count > RING:
        blocks = [[b * RING + i for b in range(count // RING)] for i in range(RING)]
        total = lax.psum(message[: 16 * images], "row", axis_index_groups=blocks)
        top = lax.pmax(message[16 * images :], "row", axis_index_groups=blocks)
        message = jnp.concatenate([total, top], axis=0)

    message, swapped = lax.optimization_barrier((message, across(message)))
    messages = [message]
    ahead, behind = send(message, forward), send(message, reverse)
    messages += [ahead, behind]
    inner, edge = fold(offsets, above, below, fold_own, mid_got, far_got, rows, cols)
    for hop in range(2):
        ahead, behind = send(ahead, forward), send(behind, reverse)
        messages += [ahead, behind]
    parts = [send(ahead[: 16 * cut], forward), send(behind[16 * cut :], reverse)]
    packed = across(pack(edge, messages[1:]))
    packed_parts = across(jnp.concatenate(parts, axis=0))
    return finish(probe, object_field, inner, object_den, den_edge, swapped, packed, packed_parts, messages + parts)


def solution(mesh):
    placed = (
        P(None, ("groups", "row"), "col"),
        P("groups", None, None, None),
        P(("groups", "row", "col"), None, None),
        P(("groups", "row", "col"), None),
    )
    return jax.shard_map(
        shards,
        mesh=mesh,
        in_specs=placed,
        out_specs=(P(None, ("groups", "row"), "col"), P("groups", None, None, None)),
        check_vma=False,
    )
```

```python
import functools
import math

import jax
import jax.numpy as jnp
import ml_dtypes
import numpy as np
from jax import lax
from jax.experimental import pallas as pl
from jax.experimental.pallas import tpu as pltpu
from jax.sharding import PartitionSpec as P

REGULAR = 0.25
AMP_FLOOR = 2.0
RING = 8
RING_ORDER = (0, 1, 3, 5, 7, 6, 4, 2)
HOPS = (0, -1, 1, -2, 2, -3, 3, 4)

SMEM = pl.BlockSpec(memory_space=pltpu.SMEM)
VMEM = pl.BlockSpec(memory_space=pltpu.VMEM)
ANY = pl.BlockSpec(memory_space=pl.ANY)
HBM = pl.BlockSpec(memory_space=pltpu.HBM)


def transform_blocks(length):
    indices = np.arange(length, dtype=np.int32)
    phases = indices[:, None] * indices[None, :] % length
    angles = phases.astype(np.float32) * np.float32(2.0 * math.pi / length)
    factor = np.float32(1.0 / math.sqrt(length))
    cos = (np.cos(angles) * factor).astype(ml_dtypes.bfloat16)
    sin = (-np.sin(angles) * factor).astype(ml_dtypes.bfloat16)
    one = np.block([[cos, -sin], [sin, cos]])
    return one, np.ascontiguousarray(one.T)


def ring_place(r):
    r = lax.rem(r, RING)
    return jnp.where(r == 0, 0, jnp.where(lax.rem(r, 2) == 1, (r + 1) // 2, RING - r // 2))


def params(mib):
    return pltpu.CompilerParams(vmem_limit_bytes=mib * 1024 * 1024)


def f32(*shape):
    return jax.ShapeDtypeStruct(shape, jnp.float32)


def begin(copies):
    for copy in copies:
        copy.start()
    return copies


def end(copies):
    for copy in copies:
        copy.wait()


def slices_kernel(offsets_at, *refs):
    offsets_in, (block, other, _), outs, (ext, cuts, offsets, sems) = refs[:3], refs[3:6], refs[6:-4], refs[-4:]
    core = lax.axis_index("col")
    cols = block.shape[2]
    end_of = cols + 128
    source = pl.multiple_of(core * (cols - 128), 128)
    target = pl.multiple_of((1 - core) * end_of, 128)
    blank = pl.multiple_of(core * end_of, 128)
    copies = begin(
        (
            pltpu.make_async_copy(block, ext.at[:, :, 128:end_of], sems.at[0]),
            pltpu.make_async_copy(
                other.at[:, :, pl.ds(source, 128)], ext.at[:, :, pl.ds(target, 128)], sems.at[1]
            ),
        )
        + tuple(
            pltpu.make_async_copy(spot, offsets.at[n], sems.at[4 + n]) for n, spot in enumerate(offsets_in)
        )
    )
    ext[:, :, pl.ds(blank, 128)] = jnp.zeros((2, block.shape[1], 128), jnp.float32)
    end(copies)
    columns = {"here": offsets[0, 0, 1], "twin": offsets[1, 0, 1], "beyond": offsets[2, 0, 1]}
    copies = ()
    for number, (which, out) in enumerate(zip(offsets_at, outs)):
        start = columns[which]
        base = pl.multiple_of(start // 128 * 128, 128)
        for part in range(2):
            wide = ext[part, :, pl.ds(base, 384)]
            wide = pltpu.roll(wide, (384 - start % 128) % 384, 1)
            cuts[number, part] = wide[:, 0:256]
        copies += begin((pltpu.make_async_copy(cuts.at[number], out, sems.at[2 + number]),))
    end(copies)


def cut_slices(offsets_at, here, twin, beyond, block, other, ordered):
    rows, cols = block.shape[1], block.shape[2]
    count = len(offsets_at)
    return pl.pallas_call(
        functools.partial(slices_kernel, offsets_at),
        out_shape=(f32(2, rows, 256),) * count,
        in_specs=[ANY] * 3 + [HBM] + [ANY] * 2,
        out_specs=(ANY,) * count,
        scratch_shapes=[
            pltpu.VMEM((2, rows, cols + 256), jnp.float32),
            pltpu.VMEM((count, 2, rows, 256), jnp.float32),
            pltpu.SMEM((3, 1, 2), jnp.int32),
            pltpu.SemaphoreType.DMA((7,)),
        ],
        compiler_params=params(6),
        name="cut_slices",
    )(here, twin, beyond, block, other, ordered)


def power_kernel(probe, out, held, sems):
    modes = probe.shape[0]
    copies = begin([pltpu.make_async_copy(probe.at[m], held.at[m], sems.at[m]) for m in range(modes)])
    for m in range(modes):
        copies[m].wait()
        power = held[m, 0] * held[m, 0] + held[m, 1] * held[m, 1]
        out[...] = power if m == 0 else out[...] + power


def probe_power(probe):
    return pl.pallas_call(
        power_kernel,
        out_shape=f32(*probe.shape[2:]),
        in_specs=[ANY],
        out_specs=VMEM,
        scratch_shapes=[pltpu.VMEM(probe.shape, jnp.float32), pltpu.SemaphoreType.DMA((probe.shape[0],))],
        compiler_params=params(8),
        name="probe_power",
    )(probe)


def weights_kernel(count, here, twin, beyond, power, inner, edge, frame, grid):
    r = lax.axis_index("row")
    odd = lax.rem(r, 2)
    present = jnp.logical_and(r > 0, r < count - 1).astype(jnp.float32)
    tall = jnp.concatenate([power[...], jnp.zeros((128, 256), jnp.float32)], axis=0)
    grid[...] = jnp.zeros(grid.shape, jnp.float32)
    lowers = (128, 256 * odd, 256 * (1 - odd))
    for number, spot in enumerate((here, twin, beyond)):
        row, col = spot[0, 0], spot[0, 1]
        frame[...] = pltpu.roll(tall, row, 0)
        piece = frame[pl.ds(pl.multiple_of(lowers[number], 128), 128), :]
        if number == 2:
            piece = piece * present
        wide = jnp.concatenate([piece, jnp.zeros((128, 128), jnp.float32)], axis=1)
        base = pl.multiple_of(col // 128 * 128, 128)
        grid[:, pl.ds(base, 384)] += pltpu.roll(wide, col % 128, 1)
    size = grid.shape[1]
    inner[...] = grid[:, 128 : size - 128]
    edge[...] = jnp.where(lax.axis_index("col") == 0, grid[:, size - 128 :], grid[:, 0:128])


def weights(count, here, twin, beyond, power, rows, cols):
    return pl.pallas_call(
        functools.partial(weights_kernel, count),
        out_shape=(f32(rows, cols), f32(rows, 128)),
        in_specs=[SMEM] * 3 + [VMEM],
        out_specs=(VMEM, VMEM),
        scratch_shapes=[
            pltpu.VMEM((384, 256), jnp.float32),
            pltpu.VMEM((rows, cols + 256), jnp.float32),
        ],
        compiler_params=params(6),
        name="object_weights",
    )(here, twin, beyond, power)


def position_kernel(
    twin, far_rows, mid_rows, own_rows, probe, pattern, one, two, weight,
    mine, his0, his, fold_far, fold_mid, fold_own,
    stack, window, far, update, strength,
):
    modes = probe.shape[0]
    r = lax.axis_index("row")
    first = lax.axis_index("col") == 0
    odd = lax.rem(r, 2)
    row = twin[0, 0]
    place = ring_place(r)
    far_at = pl.multiple_of(256 * (1 - odd), 128)
    own_at = pl.multiple_of(256 * odd, 128)
    stack[:, pl.ds(far_at, 128), :] = far_rows[...]
    stack[:, 128:256, :] = mid_rows[...]
    stack[:, pl.ds(own_at, 128), :] = own_rows[...]
    for part in range(2):
        window[part] = pltpu.roll(stack[part], (384 - row) % 384, 0)[0:256]

    for m in range(modes):
        p_re, p_im = probe[m, 0], probe[m, 1]
        w_re, w_im = window[0], window[1]
        e_re, e_im = p_re * w_re - p_im * w_im, p_re * w_im + p_im * w_re
        field = jnp.concatenate([e_re.astype(jnp.bfloat16), e_im.astype(jnp.bfloat16)], axis=0)
        half = jnp.dot(one[...], field, preferred_element_type=jnp.float32).astype(jnp.bfloat16)
        half = jnp.concatenate([half[0:256], half[256:512]], axis=1)
        out = jnp.dot(half, two[...], preferred_element_type=jnp.float32)
        far[m] = out
        power = out[:, 0:256] * out[:, 0:256] + out[:, 256:512] * out[:, 256:512]
        strength[...] = power if m == 0 else strength[...] + power

    strength[...] = jnp.sqrt(pattern[...]) / jnp.maximum(jnp.sqrt(strength[...]), AMP_FLOOR)

    spots = []
    for slab in range(8):
        ahead = (slab - place) & 7
        spots.append(jnp.where(ahead < 4, 7 - 2 * ahead, 2 * (ahead - 4)))

    def put(image, value):
        low, high = value[0:128], value[128:256]
        own, other = jnp.where(first, low, high), jnp.where(first, high, low)
        for slab in range(8):
            mine[spots[slab], image] = own[16 * slab : 16 * slab + 16]
            his[spots[slab], image] = other[16 * slab : 16 * slab + 16]

    density = window[0] * window[0] + window[1] * window[1]
    put(0, density)
    for m in range(modes):
        ratio = strength[...]
        fixed = jnp.concatenate(
            [
                (far[m, :, 0:256] * ratio).astype(jnp.bfloat16),
                (far[m, :, 256:512] * ratio).astype(jnp.bfloat16),
            ],
            axis=0,
        )
        back = jnp.dot(two[...], fixed, preferred_element_type=jnp.float32).astype(jnp.bfloat16)
        back = jnp.concatenate([back[0:256], back[256:512]], axis=1)
        near = jnp.dot(back, one[...], preferred_element_type=jnp.float32)
        n_re, n_im = near[:, 0:256], near[:, 256:512]
        p_re, p_im = probe[m, 0], probe[m, 1]
        w_re, w_im = window[0], window[1]
        density = w_re * w_re + w_im * w_im
        u_re = p_re * n_re + p_im * n_im
        u_im = p_re * n_im - p_im * n_re
        update[0] = u_re if m == 0 else update[0] + u_re
        update[1] = u_im if m == 0 else update[1] + u_im
        put(1 + 2 * m, w_re * n_re + w_im * n_im - density * p_re)
        put(2 + 2 * m, w_re * n_im - w_im * n_re - density * p_im)

    his0[0] = his[0]
    for part in range(2):
        whole = update[part] - weight[...] * window[part]
        tall = jnp.concatenate([whole, jnp.zeros((128, 256), jnp.float32)], axis=0)
        stack[part] = pltpu.roll(tall, row, 0)
    fold_far[...] = stack[:, pl.ds(far_at, 128), :]
    fold_mid[...] = stack[:, 128:256, :]
    fold_own[...] = stack[:, pl.ds(own_at, 128), :]


def position(twin, far_rows, mid_rows, own_rows, probe, pattern, one, two, weight):
    modes = probe.shape[0]
    images = 1 + 2 * modes
    return pl.pallas_call(
        position_kernel,
        out_shape=tuple(f32(legs, images, 16, 256) for legs in (8, 1, 8)) + (f32(2, 128, 256),) * 3,
        in_specs=[SMEM] + [VMEM] * 8,
        out_specs=(VMEM,) * 6,
        scratch_shapes=[
            pltpu.VMEM((2, 384, 256), jnp.float32),
            pltpu.VMEM((2, 256, 256), jnp.float32),
            pltpu.VMEM((modes, 256, 512), jnp.float32),
            pltpu.VMEM((2, 256, 256), jnp.float32),
            pltpu.VMEM((256, 256), jnp.float32),
        ],
        compiler_params=params(16),
        name="position_terms",
    )(twin, far_rows, mid_rows, own_rows, probe, pattern, one, two, weight)


def fold_kernel(here, twin, beyond, near, middle, far, inner, edge, grid):
    grid[...] = jnp.zeros(grid.shape, jnp.float32)
    for col, piece in ((twin[0, 1], near), (here[0, 1], middle), (beyond[0, 1], far)):
        base = pl.multiple_of(col // 128 * 128, 128)
        for part in range(2):
            wide = jnp.concatenate([piece[part], jnp.zeros((128, 128), jnp.float32)], axis=1)
            grid[part, :, pl.ds(base, 384)] += pltpu.roll(wide, col % 128, 1)
    size = grid.shape[2]
    inner[...] = grid[:, :, 128 : size - 128]
    edge[...] = jnp.where(lax.axis_index("col") == 0, grid[:, :, size - 128 :], grid[:, :, 0:128])


def fold(here, twin, beyond, near, middle, far, rows, cols):
    return pl.pallas_call(
        fold_kernel,
        out_shape=(f32(2, rows, cols), f32(2, rows, 128)),
        in_specs=[SMEM] * 3 + [VMEM] * 3,
        out_specs=(VMEM, VMEM),
        scratch_shapes=[pltpu.VMEM((2, rows, cols + 256), jnp.float32)],
        compiler_params=params(8),
        name="fold_object",
    )(here, twin, beyond, near, middle, far)


def leg_kernel(low, spot, came, mine_at, theirs_at, out, mine, theirs, sems):
    pairs = ((mine_at.at[spot], mine), (theirs_at.at[spot], theirs))
    end(begin([pltpu.make_async_copy(a, b, sems.at[n]) for n, (a, b) in enumerate(pairs)]))
    out[...] = mine[...] + theirs[...]
    out[low : low + came.shape[0]] = out[low : low + came.shape[0]] + came[...]


def add_leg(came, low, mine, theirs, spot):
    whole = mine.shape[1:]
    return pl.pallas_call(
        functools.partial(leg_kernel, low, spot),
        out_shape=f32(*whole),
        in_specs=[VMEM] + [ANY] * 2,
        out_specs=VMEM,
        scratch_shapes=[
            pltpu.VMEM(whole, jnp.float32),
            pltpu.VMEM(whole, jnp.float32),
            pltpu.SemaphoreType.DMA((2,)),
        ],
        compiler_params=params(4),
        name="add_leg",
    )(came, mine, theirs)


def close_kernel(ahead, behind, mine_at, theirs_at, den_in, edge, message, mine, theirs, den, sems):
    pairs = ((mine_at.at[mine_at.shape[0] - 1], mine), (theirs_at.at[theirs_at.shape[0] - 1], theirs))
    copies = begin([pltpu.make_async_copy(a, b, sems.at[n]) for n, (a, b) in enumerate(pairs)])
    den[...] = den_in[...]
    cols = den.shape[1]
    side = pl.multiple_of((1 - lax.axis_index("col")) * (cols - 128), 128)
    den[:, pl.ds(side, 128)] += edge[...]
    object_peak = jnp.max(den[...])
    end(copies)
    images = ahead.shape[0]
    for image in range(images):
        total = (mine[image] + theirs[image]) + (ahead[image] + behind[image])
        message[16 * image : 16 * image + 16] = total
    message[16 * images :] = jnp.full((8, 256), object_peak, jnp.float32)


def close(ahead, behind, mine, theirs, den, edge):
    shape = ahead.shape
    return pl.pallas_call(
        close_kernel,
        out_shape=f32(16 * shape[0] + 8, 256),
        in_specs=[VMEM] * 2 + [ANY] * 2 + [VMEM] * 2,
        out_specs=VMEM,
        scratch_shapes=[pltpu.VMEM(shape, jnp.float32)] * 2
        + [pltpu.VMEM(den.shape, jnp.float32), pltpu.SemaphoreType.DMA((2,))],
        compiler_params=params(6),
        name="close_sum",
    )(ahead, behind, mine, theirs, den, edge)


def pack_kernel(*refs):
    edge, messages, out = refs[0], refs[1:-1], refs[-1]
    size = messages[0].shape[0]
    for n, message in enumerate(messages):
        out[size * n : size * n + size] = message[...]
    for part in range(2):
        out[size * len(messages) :, 128 * part : 128 * part + 128] = edge[part]


def pack(edge, messages):
    size = sum(x.shape[0] for x in messages) + edge.shape[1]
    return pl.pallas_call(
        pack_kernel,
        out_shape=f32(size, 256),
        in_specs=[VMEM] * (1 + len(messages)),
        out_specs=VMEM,
        compiler_params=params(4),
        name="pack",
    )(edge, *messages)


def finish_kernel(probe, block, inner, den, den_edge, packed, packed_parts, *refs):
    per_owner = len(HOPS) + 1
    messages, refs = refs[:per_owner], refs[per_owner:]
    size, cut = messages[0].shape[0], messages[per_owner - 2].shape[0]
    messages += tuple(packed.at[size * n : size * n + size] for n in range(per_owner - 2))
    messages += (packed_parts.at[0:cut], packed_parts.at[cut:size])
    edge = packed.at[size * (per_owner - 2) :]
    new_block_at, new_probe_at, new_probe, new_block, whole_den, scales, sems = refs
    modes = probe.shape[0]
    core = lax.axis_index("col")
    place = ring_place(lax.axis_index("row"))
    cols = block.shape[2]
    peak = jnp.zeros((8, 256), jnp.float32)
    object_peak = jnp.zeros((8, 256), jnp.float32)
    for n, message in enumerate(messages):
        if n % per_owner != per_owner - 1:
            peak = jnp.maximum(peak, jnp.maximum(message[0:8], message[8:16]))
        if n % per_owner != per_owner - 2:
            object_peak = jnp.maximum(object_peak, message[message.shape[0] - 8 :])
    peak = jnp.max(peak)
    object_peak = jnp.max(object_peak)
    starts = []
    for owner in range(2):
        half = core if owner == 0 else 1 - core
        for n, hop in enumerate(HOPS):
            starts.append(pl.multiple_of(128 * half + 16 * ((place + hop) & 7), 16))
            den_rows = messages[per_owner * owner + n][0:16]
            scales[len(HOPS) * owner + n] = 1.0 / ((1.0 - REGULAR) * den_rows + REGULAR * peak)
    outs = ()
    for m in range(modes):
        for part in range(2):
            at = 16 * (1 + 2 * m + part)
            for owner in range(2):
                for n, hop in enumerate(HOPS):
                    first = per_owner * owner
                    if hop != 4 or at < cut:
                        value = messages[first + n][at : at + 16]
                    else:
                        value = messages[first + n + 1][at - cut : at - cut + 16]
                    spot = len(HOPS) * owner + n
                    rows = pl.ds(starts[spot], 16)
                    new_probe[m, part, rows, :] = probe[m, part, rows, :] + value * scales[spot]
        outs += begin((pltpu.make_async_copy(new_probe.at[m], new_probe_at.at[m], sems.at[m]),))
    side = pl.multiple_of((1 - core) * (cols - 128), 128)
    new_block[...] = inner[...]
    for part in range(2):
        new_block[part, :, pl.ds(side, 128)] += edge[:, 128 * part : 128 * part + 128]
    whole_den[...] = den[...]
    whole_den[:, pl.ds(side, 128)] += den_edge[...]
    scale = 1.0 / ((1.0 - REGULAR) * whole_den[...] + REGULAR * object_peak)
    for part in range(2):
        new_block[part] = block[part] + new_block[part] * scale
    outs += begin((pltpu.make_async_copy(new_block, new_block_at, sems.at[modes]),))
    end(outs)


def finish(probe, block, inner, den, den_edge, packed, packed_parts, messages):
    modes = probe.shape[0]
    return pl.pallas_call(
        finish_kernel,
        out_shape=(f32(*block.shape), f32(*probe.shape)),
        in_specs=[VMEM] * (7 + len(messages)),
        out_specs=(ANY, ANY),
        scratch_shapes=[pltpu.VMEM(x.shape, jnp.float32) for x in (probe, block, den)]
        + [
            pltpu.VMEM((2 * len(HOPS), 16, 256), jnp.float32),
            pltpu.SemaphoreType.DMA((modes + 1,)),
        ],
        compiler_params=params(12),
        name="finish",
    )(probe, block, inner, den, den_edge, packed, packed_parts, *messages)


def shards(object_field, probe, measured, offsets):
    rows, cols = object_field.shape[1], object_field.shape[2]
    count = lax.axis_size("row")
    one, two = transform_blocks(probe.shape[-1])
    one, two = jnp.asarray(one), jnp.asarray(two)

    twins = [(i, i ^ 1) for i in range(count)]
    cores = [(0, 1), (1, 0)]
    others = [(i + 1 if i % 2 else i - 1, i) for i in range(1, count - 1)]
    outward = [(i, i + 2) for i in range(1, count - 2, 2)] + [(i, i - 2) for i in range(2, count, 2)]
    inward = [(b, a) for a, b in outward]
    forward = [
        (block + RING_ORDER[i], block + RING_ORDER[(i + 1) % RING])
        for block in range(0, count, RING)
        for i in range(RING)
    ]
    reverse = [(b, a) for a, b in forward]

    def across(x):
        return lax.ppermute(x, "col", cores)

    def send(x, pairs):
        return lax.ppermute(x, "row", pairs)

    def after(x, y):
        return lax.optimization_barrier((x, y))[0]

    other = across(object_field)
    twin = send(offsets, twins)
    beyond = send(offsets, others)
    pattern = send(measured, twins)

    (to_twin,) = cut_slices(("here",), offsets, offsets, offsets, object_field, other, offsets)
    mid_rows = send(to_twin, twins)
    to_beyond, own_rows = cut_slices(
        ("beyond", "twin"), offsets, twin, beyond, object_field, other, to_twin
    )
    far_rows = send(to_beyond, outward)
    power = probe_power(after(probe, own_rows))
    object_den, den_edge = weights(count, offsets, twin, beyond, power, rows, cols)
    den_edge = across(den_edge)

    mine, his0, his, fold_far, fold_mid, fold_own = position(
        twin, far_rows, after(mid_rows, den_edge), own_rows, probe, pattern[0], one, two, power
    )
    images = mine.shape[1]
    cut = images // 2 + 1
    theirs = [across(his0)]
    theirs += [across(after(his, theirs[0]))]

    mid_got = send(fold_mid, twins)
    far_got = send(fold_far, inward)

    farthest = mine[0] + theirs[0][0]
    ahead, behind = send(farthest[:cut], forward), send(farthest[cut:], reverse)
    low = cut
    for leg in (1, 3, 5):
        ahead = send(add_leg(ahead, 0, mine, theirs[1], leg), forward)
        behind = send(add_leg(behind, low, mine, theirs[1], leg + 1), reverse)
        low = 0
    message = close(ahead, behind, mine, theirs[1], object_den, den_edge)
    if count > RING:
        blocks = [[b * RING + i for b in range(count // RING)] for i in range(RING)]
        total = lax.psum(message[: 16 * images], "row", axis_index_groups=blocks)
        top = lax.pmax(message[16 * images :], "row", axis_index_groups=blocks)
        message = jnp.concatenate([total, top], axis=0)

    messages = [message]
    ahead, behind = send(message, forward), send(message, reverse)
    messages += [ahead, behind]
    ahead, mid_got, far_got = lax.optimization_barrier((ahead, mid_got, far_got))
    inner, edge = fold(offsets, twin, beyond, fold_own, mid_got, far_got, rows, cols)
    for hop in range(2):
        ahead, behind = send(ahead, forward), send(behind, reverse)
        messages += [ahead, behind]
    parts = [send(ahead[: 16 * cut], forward), send(behind[16 * cut :], reverse)]
    packed = across(pack(edge, messages))
    packed_parts = across(jnp.concatenate(parts, axis=0))
    return finish(probe, object_field, inner, object_den, den_edge, packed, packed_parts, messages + parts)


def solution(mesh):
    placed = (
        P(None, ("groups", "row"), "col"),
        P("groups", None, None, None),
        P(("groups", "row", "col"), None, None),
        P(("groups", "row", "col"), None),
    )
    return jax.shard_map(
        shards,
        mesh=mesh,
        in_specs=placed,
        out_specs=(P(None, ("groups", "row"), "col"), P("groups", None, None, None)),
        check_vma=False,
    )
```

```python
import functools
import math

import jax
import jax.numpy as jnp
import ml_dtypes
import numpy as np
from jax import lax
from jax.experimental import pallas as pl
from jax.experimental.pallas import tpu as pltpu
from jax.sharding import PartitionSpec as P

REGULAR = 0.25
AMP_FLOOR = 2.0
RING = 8
RING_ORDER = (0, 1, 3, 5, 7, 6, 4, 2)
HOPS = (0, -1, 1, -2, 2, -3, 3, 4)

SMEM = pl.BlockSpec(memory_space=pltpu.SMEM)
VMEM = pl.BlockSpec(memory_space=pltpu.VMEM)
ANY = pl.BlockSpec(memory_space=pl.ANY)
HBM = pl.BlockSpec(memory_space=pltpu.HBM)


def transform_blocks(length):
    indices = np.arange(length, dtype=np.int32)
    phases = indices[:, None] * indices[None, :] % length
    angles = phases.astype(np.float32) * np.float32(2.0 * math.pi / length)
    factor = np.float32(1.0 / math.sqrt(length))
    cos = (np.cos(angles) * factor).astype(ml_dtypes.bfloat16)
    sin = (-np.sin(angles) * factor).astype(ml_dtypes.bfloat16)
    one = np.block([[cos, -sin], [sin, cos]])
    return one, np.ascontiguousarray(one.T)


def ring_place(r):
    r = lax.rem(r, RING)
    return jnp.where(r == 0, 0, jnp.where(lax.rem(r, 2) == 1, (r + 1) // 2, RING - r // 2))


def params(mib):
    return pltpu.CompilerParams(vmem_limit_bytes=mib * 1024 * 1024)


def f32(*shape):
    return jax.ShapeDtypeStruct(shape, jnp.float32)


def begin(copies):
    for copy in copies:
        copy.start()
    return copies


def end(copies):
    for copy in copies:
        copy.wait()


def slices_kernel(offsets_at, *refs):
    offsets_in, (block, other, _), outs, (ext, cuts, offsets, sems) = refs[:3], refs[3:6], refs[6:-4], refs[-4:]
    core = lax.axis_index("col")
    cols = block.shape[2]
    end_of = cols + 128
    source = pl.multiple_of(core * (cols - 128), 128)
    target = pl.multiple_of((1 - core) * end_of, 128)
    blank = pl.multiple_of(core * end_of, 128)
    copies = begin(
        (
            pltpu.make_async_copy(block, ext.at[:, :, 128:end_of], sems.at[0]),
            pltpu.make_async_copy(
                other.at[:, :, pl.ds(source, 128)], ext.at[:, :, pl.ds(target, 128)], sems.at[1]
            ),
        )
        + tuple(
            pltpu.make_async_copy(spot, offsets.at[n], sems.at[4 + n]) for n, spot in enumerate(offsets_in)
        )
    )
    ext[:, :, pl.ds(blank, 128)] = jnp.zeros((2, block.shape[1], 128), jnp.float32)
    end(copies)
    columns = {"here": offsets[0, 0, 1], "twin": offsets[1, 0, 1], "beyond": offsets[2, 0, 1]}
    copies = ()
    for number, (which, out) in enumerate(zip(offsets_at, outs)):
        start = columns[which]
        base = pl.multiple_of(start // 128 * 128, 128)
        for part in range(2):
            wide = ext[part, :, pl.ds(base, 384)]
            wide = pltpu.roll(wide, (384 - start % 128) % 384, 1)
            cuts[number, part] = wide[:, 0:256]
        copies += begin((pltpu.make_async_copy(cuts.at[number], out, sems.at[2 + number]),))
    end(copies)


def cut_slices(offsets_at, here, twin, beyond, block, other, ordered):
    rows, cols = block.shape[1], block.shape[2]
    count = len(offsets_at)
    return pl.pallas_call(
        functools.partial(slices_kernel, offsets_at),
        out_shape=(f32(2, rows, 256),) * count,
        in_specs=[ANY] * 3 + [HBM] + [ANY] * 2,
        out_specs=(ANY,) * count,
        scratch_shapes=[
            pltpu.VMEM((2, rows, cols + 256), jnp.float32),
            pltpu.VMEM((count, 2, rows, 256), jnp.float32),
            pltpu.SMEM((3, 1, 2), jnp.int32),
            pltpu.SemaphoreType.DMA((7,)),
        ],
        compiler_params=params(6),
        name="cut_slices",
    )(here, twin, beyond, block, other, ordered)


def power_kernel(probe, out, held, sems):
    modes = probe.shape[0]
    copies = begin([pltpu.make_async_copy(probe.at[m], held.at[m], sems.at[m]) for m in range(modes)])
    for m in range(modes):
        copies[m].wait()
        power = held[m, 0] * held[m, 0] + held[m, 1] * held[m, 1]
        out[...] = power if m == 0 else out[...] + power


def probe_power(probe):
    return pl.pallas_call(
        power_kernel,
        out_shape=f32(*probe.shape[2:]),
        in_specs=[ANY],
        out_specs=VMEM,
        scratch_shapes=[pltpu.VMEM(probe.shape, jnp.float32), pltpu.SemaphoreType.DMA((probe.shape[0],))],
        compiler_params=params(8),
        name="probe_power",
    )(probe)


def weights_kernel(count, here, twin, beyond, power, inner, edge, frame, grid):
    r = lax.axis_index("row")
    odd = lax.rem(r, 2)
    present = jnp.logical_and(r > 0, r < count - 1).astype(jnp.float32)
    tall = jnp.concatenate([power[...], jnp.zeros((128, 256), jnp.float32)], axis=0)
    grid[...] = jnp.zeros(grid.shape, jnp.float32)
    lowers = (128, 256 * odd, 256 * (1 - odd))
    for number, spot in enumerate((here, twin, beyond)):
        row, col = spot[0, 0], spot[0, 1]
        frame[...] = pltpu.roll(tall, row, 0)
        piece = frame[pl.ds(pl.multiple_of(lowers[number], 128), 128), :]
        if number == 2:
            piece = piece * present
        wide = jnp.concatenate([piece, jnp.zeros((128, 128), jnp.float32)], axis=1)
        base = pl.multiple_of(col // 128 * 128, 128)
        grid[:, pl.ds(base, 384)] += pltpu.roll(wide, col % 128, 1)
    size = grid.shape[1]
    inner[...] = grid[:, 128 : size - 128]
    edge[...] = jnp.where(lax.axis_index("col") == 0, grid[:, size - 128 :], grid[:, 0:128])


def weights(count, here, twin, beyond, power, rows, cols):
    return pl.pallas_call(
        functools.partial(weights_kernel, count),
        out_shape=(f32(rows, cols), f32(rows, 128)),
        in_specs=[SMEM] * 3 + [VMEM],
        out_specs=(VMEM, VMEM),
        scratch_shapes=[
            pltpu.VMEM((384, 256), jnp.float32),
            pltpu.VMEM((rows, cols + 256), jnp.float32),
        ],
        compiler_params=params(6),
        name="object_weights",
    )(here, twin, beyond, power)


def position_kernel(
    twin, far_rows, mid_rows, own_rows, probe, pattern, one, two, weight,
    mine, his0, his, fold_far, fold_mid, fold_own,
    stack, window, far, update, strength,
):
    modes = probe.shape[0]
    r = lax.axis_index("row")
    first = lax.axis_index("col") == 0
    odd = lax.rem(r, 2)
    row = twin[0, 0]
    place = ring_place(r)
    far_at = pl.multiple_of(256 * (1 - odd), 128)
    own_at = pl.multiple_of(256 * odd, 128)
    stack[:, pl.ds(far_at, 128), :] = far_rows[...]
    stack[:, 128:256, :] = mid_rows[...]
    stack[:, pl.ds(own_at, 128), :] = own_rows[...]
    for part in range(2):
        window[part] = pltpu.roll(stack[part], (384 - row) % 384, 0)[0:256]

    for m in range(modes):
        p_re, p_im = probe[m, 0], probe[m, 1]
        w_re, w_im = window[0], window[1]
        e_re, e_im = p_re * w_re - p_im * w_im, p_re * w_im + p_im * w_re
        field = jnp.concatenate([e_re.astype(jnp.bfloat16), e_im.astype(jnp.bfloat16)], axis=0)
        half = jnp.dot(one[...], field, preferred_element_type=jnp.float32).astype(jnp.bfloat16)
        half = jnp.concatenate([half[0:256], half[256:512]], axis=1)
        out = jnp.dot(half, two[...], preferred_element_type=jnp.float32)
        far[m] = out
        power = out[:, 0:256] * out[:, 0:256] + out[:, 256:512] * out[:, 256:512]
        strength[...] = power if m == 0 else strength[...] + power

    strength[...] = jnp.sqrt(pattern[...]) / jnp.maximum(jnp.sqrt(strength[...]), AMP_FLOOR)

    spots = []
    for slab in range(8):
        ahead = (slab - place) & 7
        spots.append(jnp.where(ahead < 4, 7 - 2 * ahead, 2 * (ahead - 4)))

    def put(image, value):
        low, high = value[0:128], value[128:256]
        own, other = jnp.where(first, low, high), jnp.where(first, high, low)
        for slab in range(8):
            mine[spots[slab], image] = own[16 * slab : 16 * slab + 16]
            his[spots[slab], image] = other[16 * slab : 16 * slab + 16]

    density = window[0] * window[0] + window[1] * window[1]
    put(0, density)
    for m in range(modes):
        ratio = strength[...]
        fixed = jnp.concatenate(
            [
                (far[m, :, 0:256] * ratio).astype(jnp.bfloat16),
                (far[m, :, 256:512] * ratio).astype(jnp.bfloat16),
            ],
            axis=0,
        )
        back = jnp.dot(two[...], fixed, preferred_element_type=jnp.float32).astype(jnp.bfloat16)
        back = jnp.concatenate([back[0:256], back[256:512]], axis=1)
        near = jnp.dot(back, one[...], preferred_element_type=jnp.float32)
        n_re, n_im = near[:, 0:256], near[:, 256:512]
        p_re, p_im = probe[m, 0], probe[m, 1]
        w_re, w_im = window[0], window[1]
        density = w_re * w_re + w_im * w_im
        u_re = p_re * n_re + p_im * n_im
        u_im = p_re * n_im - p_im * n_re
        update[0] = u_re if m == 0 else update[0] + u_re
        update[1] = u_im if m == 0 else update[1] + u_im
        put(1 + 2 * m, w_re * n_re + w_im * n_im - density * p_re)
        put(2 + 2 * m, w_re * n_im - w_im * n_re - density * p_im)

    his0[0] = his[0]
    for part in range(2):
        whole = update[part] - weight[...] * window[part]
        tall = jnp.concatenate([whole, jnp.zeros((128, 256), jnp.float32)], axis=0)
        stack[part] = pltpu.roll(tall, row, 0)
    fold_far[...] = stack[:, pl.ds(far_at, 128), :]
    fold_mid[...] = stack[:, 128:256, :]
    fold_own[...] = stack[:, pl.ds(own_at, 128), :]


def position(twin, far_rows, mid_rows, own_rows, probe, pattern, one, two, weight):
    modes = probe.shape[0]
    images = 1 + 2 * modes
    return pl.pallas_call(
        position_kernel,
        out_shape=tuple(f32(legs, images, 16, 256) for legs in (8, 1, 8)) + (f32(2, 128, 256),) * 3,
        in_specs=[SMEM] + [VMEM] * 8,
        out_specs=(VMEM,) * 6,
        scratch_shapes=[
            pltpu.VMEM((2, 384, 256), jnp.float32),
            pltpu.VMEM((2, 256, 256), jnp.float32),
            pltpu.VMEM((modes, 256, 512), jnp.float32),
            pltpu.VMEM((2, 256, 256), jnp.float32),
            pltpu.VMEM((256, 256), jnp.float32),
        ],
        compiler_params=params(16),
        name="position_terms",
    )(twin, far_rows, mid_rows, own_rows, probe, pattern, one, two, weight)


def fold_kernel(here, twin, beyond, near, middle, far, inner, edge, grid):
    grid[...] = jnp.zeros(grid.shape, jnp.float32)
    for col, piece in ((twin[0, 1], near), (here[0, 1], middle), (beyond[0, 1], far)):
        base = pl.multiple_of(col // 128 * 128, 128)
        for part in range(2):
            wide = jnp.concatenate([piece[part], jnp.zeros((128, 128), jnp.float32)], axis=1)
            grid[part, :, pl.ds(base, 384)] += pltpu.roll(wide, col % 128, 1)
    size = grid.shape[2]
    inner[...] = grid[:, :, 128 : size - 128]
    edge[...] = jnp.where(lax.axis_index("col") == 0, grid[:, :, size - 128 :], grid[:, :, 0:128])


def fold(here, twin, beyond, near, middle, far, rows, cols):
    return pl.pallas_call(
        fold_kernel,
        out_shape=(f32(2, rows, cols), f32(2, rows, 128)),
        in_specs=[SMEM] * 3 + [VMEM] * 3,
        out_specs=(VMEM, VMEM),
        scratch_shapes=[pltpu.VMEM((2, rows, cols + 256), jnp.float32)],
        compiler_params=params(8),
        name="fold_object",
    )(here, twin, beyond, near, middle, far)


def leg_kernel(spot, low, mine_at, theirs_at, *refs):
    came, (out, mine, theirs, sems) = refs[:-4], refs[-4:]
    images = pl.ds(low, out.shape[0])
    pairs = ((mine_at.at[spot, images], mine), (theirs_at.at[spot, images], theirs))
    end(begin([pltpu.make_async_copy(a, b, sems.at[n]) for n, (a, b) in enumerate(pairs)]))
    total = mine[...] + theirs[...]
    out[...] = total + came[0][...] if came else total


def add_leg(came, mine, theirs, spot, low, high):
    whole = (high - low,) + mine.shape[2:]
    came = () if came is None else (came,)
    return pl.pallas_call(
        functools.partial(leg_kernel, spot, low),
        out_shape=f32(*whole),
        in_specs=[ANY] * 2 + [VMEM] * len(came),
        out_specs=VMEM,
        scratch_shapes=[
            pltpu.VMEM(whole, jnp.float32),
            pltpu.VMEM(whole, jnp.float32),
            pltpu.SemaphoreType.DMA((2,)),
        ],
        compiler_params=params(4),
        name="add_leg",
    )(mine, theirs, *came)


def close_kernel(
    ahead_low, ahead_high, behind_low, behind_high, mine_at, theirs_at, den_in, edge,
    low, high, mine, theirs, den, sems,
):
    pairs = ((mine_at.at[mine_at.shape[0] - 1], mine), (theirs_at.at[theirs_at.shape[0] - 1], theirs))
    copies = begin([pltpu.make_async_copy(a, b, sems.at[n]) for n, (a, b) in enumerate(pairs)])
    den[...] = den_in[...]
    cols = den.shape[1]
    side = pl.multiple_of((1 - lax.axis_index("col")) * (cols - 128), 128)
    den[:, pl.ds(side, 128)] += edge[...]
    object_peak = jnp.max(den[...])
    end(copies)
    cut, images = ahead_low.shape[0], mine.shape[0]
    for image in range(images):
        if image < cut:
            out, n, ahead, behind = low, image, ahead_low, behind_low
        else:
            out, n, ahead, behind = high, image - cut, ahead_high, behind_high
        out[16 * n : 16 * n + 16] = (mine[image] + theirs[image]) + (ahead[n] + behind[n])
    high[16 * (images - cut) :] = jnp.full((8, 256), object_peak, jnp.float32)


def close(ahead, behind, mine, theirs, den, edge):
    cut, images = ahead[0].shape[0], mine.shape[1]
    return pl.pallas_call(
        close_kernel,
        out_shape=(f32(16 * cut, 256), f32(16 * (images - cut) + 8, 256)),
        in_specs=[VMEM] * 4 + [ANY] * 2 + [VMEM] * 2,
        out_specs=(VMEM, VMEM),
        scratch_shapes=[pltpu.VMEM(mine.shape[1:], jnp.float32)] * 2
        + [pltpu.VMEM(den.shape, jnp.float32), pltpu.SemaphoreType.DMA((2,))],
        compiler_params=params(6),
        name="close_sum",
    )(*ahead, *behind, mine, theirs, den, edge)


def pack_kernel(edge, *refs):
    parts, out = refs[:-1], refs[-1]
    at = 0
    for part in parts:
        out[at : at + part.shape[0]] = part[...]
        at += part.shape[0]
    for part in range(2):
        out[at:, 128 * part : 128 * part + 128] = edge[part]


def pack(edge, parts):
    size = sum(x.shape[0] for x in parts) + edge.shape[1]
    return pl.pallas_call(
        pack_kernel,
        out_shape=f32(size, 256),
        in_specs=[VMEM] * (1 + len(parts)),
        out_specs=VMEM,
        compiler_params=params(4),
        name="pack",
    )(edge, *parts)


def finish_kernel(probe, block, inner, den, den_edge, packed, packed_last, *refs):
    hops = len(HOPS)
    parts, refs = refs[: 2 * hops], refs[2 * hops :]
    new_block_at, new_probe_at, new_probe, new_block, whole_den, scales, sems = refs
    cut, rest = parts[0].shape[0], parts[1].shape[0]
    size = cut + rest
    lows, highs = list(parts[0::2]), list(parts[1::2])
    for n in range(hops - 1):
        lows.append(packed.at[size * n : size * n + cut])
        highs.append(packed.at[size * n + cut : size * n + size])
    lows.append(packed_last.at[0:cut])
    highs.append(packed_last.at[cut:size])
    edge = packed.at[size * (hops - 1) :]
    modes = probe.shape[0]
    core = lax.axis_index("col")
    place = ring_place(lax.axis_index("row"))
    cols = block.shape[2]
    peak = jnp.zeros((8, 256), jnp.float32)
    object_peak = jnp.zeros((8, 256), jnp.float32)
    for low, high in zip(lows, highs):
        peak = jnp.maximum(peak, jnp.maximum(low[0:8], low[8:16]))
        object_peak = jnp.maximum(object_peak, high[rest - 8 : rest])
    peak = jnp.max(peak)
    object_peak = jnp.max(object_peak)
    starts = []
    for n, low in enumerate(lows):
        half = core if n < hops else 1 - core
        starts.append(pl.multiple_of(128 * half + 16 * ((place + HOPS[n % hops]) & 7), 16))
        scales[n] = 1.0 / ((1.0 - REGULAR) * low[0:16] + REGULAR * peak)
    outs = ()
    for m in range(modes):
        for part in range(2):
            at = 16 * (1 + 2 * m + part)
            for n in range(2 * hops):
                value = lows[n][at : at + 16] if at < cut else highs[n][at - cut : at - cut + 16]
                rows = pl.ds(starts[n], 16)
                new_probe[m, part, rows, :] = probe[m, part, rows, :] + value * scales[n]
        outs += begin((pltpu.make_async_copy(new_probe.at[m], new_probe_at.at[m], sems.at[m]),))
    side = pl.multiple_of((1 - core) * (cols - 128), 128)
    new_block[...] = inner[...]
    for part in range(2):
        new_block[part, :, pl.ds(side, 128)] += edge[:, 128 * part : 128 * part + 128]
    whole_den[...] = den[...]
    whole_den[:, pl.ds(side, 128)] += den_edge[...]
    scale = 1.0 / ((1.0 - REGULAR) * whole_den[...] + REGULAR * object_peak)
    for part in range(2):
        new_block[part] = block[part] + new_block[part] * scale
    outs += begin((pltpu.make_async_copy(new_block, new_block_at, sems.at[modes]),))
    end(outs)


def finish(probe, block, inner, den, den_edge, packed, packed_last, parts):
    modes = probe.shape[0]
    return pl.pallas_call(
        finish_kernel,
        out_shape=(f32(*block.shape), f32(*probe.shape)),
        in_specs=[VMEM] * (7 + len(parts)),
        out_specs=(ANY, ANY),
        scratch_shapes=[pltpu.VMEM(x.shape, jnp.float32) for x in (probe, block, den)]
        + [
            pltpu.VMEM((2 * len(HOPS), 16, 256), jnp.float32),
            pltpu.SemaphoreType.DMA((modes + 1,)),
        ],
        compiler_params=params(12),
        name="finish",
    )(probe, block, inner, den, den_edge, packed, packed_last, *parts)


def shards(object_field, probe, measured, offsets):
    rows, cols = object_field.shape[1], object_field.shape[2]
    count = lax.axis_size("row")
    one, two = transform_blocks(probe.shape[-1])
    one, two = jnp.asarray(one), jnp.asarray(two)

    twins = [(i, i ^ 1) for i in range(count)]
    cores = [(0, 1), (1, 0)]
    others = [(i + 1 if i % 2 else i - 1, i) for i in range(1, count - 1)]
    outward = [(i, i + 2) for i in range(1, count - 2, 2)] + [(i, i - 2) for i in range(2, count, 2)]
    inward = [(b, a) for a, b in outward]
    forward = [
        (block + RING_ORDER[i], block + RING_ORDER[(i + 1) % RING])
        for block in range(0, count, RING)
        for i in range(RING)
    ]
    reverse = [(b, a) for a, b in forward]

    def across(x):
        return lax.ppermute(x, "col", cores)

    def send(x, pairs):
        return lax.ppermute(x, "row", pairs)

    def after(x, y):
        return lax.optimization_barrier((x, y))[0]

    other = across(object_field)
    twin = send(offsets, twins)
    beyond = send(offsets, others)
    pattern = send(measured, twins)

    (to_twin,) = cut_slices(("here",), offsets, offsets, offsets, object_field, other, offsets)
    mid_rows = send(to_twin, twins)
    to_beyond, own_rows = cut_slices(
        ("beyond", "twin"), offsets, twin, beyond, object_field, other, to_twin
    )
    far_rows = send(to_beyond, outward)
    power = probe_power(after(probe, own_rows))
    object_den, den_edge = weights(count, offsets, twin, beyond, power, rows, cols)
    den_edge = across(den_edge)

    mine, his0, his, fold_far, fold_mid, fold_own = position(
        twin, far_rows, after(mid_rows, den_edge), own_rows, probe, pattern[0], one, two, power
    )
    images = mine.shape[1]
    cut = images // 2 + 1
    theirs = [across(his0)]
    theirs += [across(after(his, theirs[0]))]

    mid_got = send(fold_mid, twins)
    far_got = send(fold_far, inward)

    farthest = mine[0] + theirs[0][0]
    ahead = [send(farthest[:cut], forward), None]
    behind = [None, send(farthest[cut:], reverse)]
    bounds = ((0, cut), (cut, images))
    for leg in (1, 3, 5):
        for n in (0, 1):
            ahead[n] = send(add_leg(ahead[n], mine, theirs[1], leg, *bounds[n]), forward)
        for n in (1, 0):
            behind[n] = send(add_leg(behind[n], mine, theirs[1], leg + 1, *bounds[n]), reverse)
    message = close(ahead, behind, mine, theirs[1], object_den, den_edge)
    if count > RING:
        blocks = [[b * RING + i for b in range(count // RING)] for i in range(RING)]
        low = lax.psum(message[0], "row", axis_index_groups=blocks)
        high = lax.psum(message[1][:-8], "row", axis_index_groups=blocks)
        top = lax.pmax(message[1][-8:], "row", axis_index_groups=blocks)
        message = (low, jnp.concatenate([high, top], axis=0))

    parts = list(message)
    ahead = [send(x, forward) for x in message]
    behind = [send(x, reverse) for x in message]
    parts += ahead + behind
    ahead[0], mid_got, far_got = lax.optimization_barrier((ahead[0], mid_got, far_got))
    inner, edge = fold(offsets, twin, beyond, fold_own, mid_got, far_got, rows, cols)
    for hop in range(2):
        ahead = [send(x, forward) for x in ahead]
        behind = [send(x, reverse) for x in behind]
        parts += ahead + behind
    last = [send(ahead[0], forward), send(behind[1], reverse)]
    packed = across(pack(edge, parts))
    packed_last = across(jnp.concatenate(last, axis=0))
    return finish(probe, object_field, inner, object_den, den_edge, packed, packed_last, parts + last)


def solution(mesh):
    placed = (
        P(None, ("groups", "row"), "col"),
        P("groups", None, None, None),
        P(("groups", "row", "col"), None, None),
        P(("groups", "row", "col"), None),
    )
    return jax.shard_map(
        shards,
        mesh=mesh,
        in_specs=placed,
        out_specs=(P(None, ("groups", "row"), "col"), P("groups", None, None, None)),
        check_vma=False,
    )
```

```python
import functools
import math

import jax
import jax.numpy as jnp
import ml_dtypes
import numpy as np
from jax import lax
from jax.experimental import pallas as pl
from jax.experimental.pallas import tpu as pltpu
from jax.sharding import PartitionSpec as P

REGULAR = 0.25
AMP_FLOOR = 2.0
RING = 8
RING_ORDER = (0, 1, 3, 5, 7, 6, 4, 2)
HOPS = (0, -1, 1, -2, 2, -3, 3, 4)

SMEM = pl.BlockSpec(memory_space=pltpu.SMEM)
VMEM = pl.BlockSpec(memory_space=pltpu.VMEM)
ANY = pl.BlockSpec(memory_space=pl.ANY)
HBM = pl.BlockSpec(memory_space=pltpu.HBM)


def transform_blocks(length):
    indices = np.arange(length, dtype=np.int32)
    phases = indices[:, None] * indices[None, :] % length
    angles = phases.astype(np.float32) * np.float32(2.0 * math.pi / length)
    factor = np.float32(1.0 / math.sqrt(length))
    cos = (np.cos(angles) * factor).astype(ml_dtypes.bfloat16)
    sin = (-np.sin(angles) * factor).astype(ml_dtypes.bfloat16)
    one = np.block([[cos, -sin], [sin, cos]])
    return one, np.ascontiguousarray(one.T)


def ring_place(r):
    r = lax.rem(r, RING)
    return jnp.where(r == 0, 0, jnp.where(lax.rem(r, 2) == 1, (r + 1) // 2, RING - r // 2))


def params(mib):
    return pltpu.CompilerParams(vmem_limit_bytes=mib * 1024 * 1024)


def f32(*shape):
    return jax.ShapeDtypeStruct(shape, jnp.float32)


def begin(copies):
    for copy in copies:
        copy.start()
    return copies


def end(copies):
    for copy in copies:
        copy.wait()


def slices_kernel(offsets_at, *refs):
    offsets_in, (block, other, _), outs, (ext, cuts, offsets, sems) = refs[:3], refs[3:6], refs[6:-4], refs[-4:]
    core = lax.axis_index("col")
    cols = block.shape[2]
    end_of = cols + 128
    source = pl.multiple_of(core * (cols - 128), 128)
    target = pl.multiple_of((1 - core) * end_of, 128)
    blank = pl.multiple_of(core * end_of, 128)
    copies = begin(
        (
            pltpu.make_async_copy(block, ext.at[:, :, 128:end_of], sems.at[0]),
            pltpu.make_async_copy(
                other.at[:, :, pl.ds(source, 128)], ext.at[:, :, pl.ds(target, 128)], sems.at[1]
            ),
        )
        + tuple(
            pltpu.make_async_copy(spot, offsets.at[n], sems.at[4 + n]) for n, spot in enumerate(offsets_in)
        )
    )
    ext[:, :, pl.ds(blank, 128)] = jnp.zeros((2, block.shape[1], 128), jnp.float32)
    end(copies)
    columns = {"here": offsets[0, 0, 1], "twin": offsets[1, 0, 1], "beyond": offsets[2, 0, 1]}
    copies = ()
    for number, (which, out) in enumerate(zip(offsets_at, outs)):
        start = columns[which]
        base = pl.multiple_of(start // 128 * 128, 128)
        for part in range(2):
            wide = ext[part, :, pl.ds(base, 384)]
            wide = pltpu.roll(wide, (384 - start % 128) % 384, 1)
            cuts[number, part] = wide[:, 0:256]
        copies += begin((pltpu.make_async_copy(cuts.at[number], out, sems.at[2 + number]),))
    end(copies)


def cut_slices(offsets_at, here, twin, beyond, block, other, ordered):
    rows, cols = block.shape[1], block.shape[2]
    count = len(offsets_at)
    return pl.pallas_call(
        functools.partial(slices_kernel, offsets_at),
        out_shape=(f32(2, rows, 256),) * count,
        in_specs=[ANY] * 3 + [HBM] + [ANY] * 2,
        out_specs=(ANY,) * count,
        scratch_shapes=[
            pltpu.VMEM((2, rows, cols + 256), jnp.float32),
            pltpu.VMEM((count, 2, rows, 256), jnp.float32),
            pltpu.SMEM((3, 1, 2), jnp.int32),
            pltpu.SemaphoreType.DMA((7,)),
        ],
        compiler_params=params(6),
        name="cut_slices",
    )(here, twin, beyond, block, other, ordered)


def power_kernel(probe, out, held, sems):
    modes = probe.shape[0]
    copies = begin([pltpu.make_async_copy(probe.at[m], held.at[m], sems.at[m]) for m in range(modes)])
    for m in range(modes):
        copies[m].wait()
        power = held[m, 0] * held[m, 0] + held[m, 1] * held[m, 1]
        out[...] = power if m == 0 else out[...] + power


def probe_power(probe):
    return pl.pallas_call(
        power_kernel,
        out_shape=f32(*probe.shape[2:]),
        in_specs=[ANY],
        out_specs=VMEM,
        scratch_shapes=[pltpu.VMEM(probe.shape, jnp.float32), pltpu.SemaphoreType.DMA((probe.shape[0],))],
        compiler_params=params(8),
        name="probe_power",
    )(probe)


def weights_kernel(count, here, twin, beyond, power, inner, edge, frame, grid):
    r = lax.axis_index("row")
    odd = lax.rem(r, 2)
    present = jnp.logical_and(r > 0, r < count - 1).astype(jnp.float32)
    tall = jnp.concatenate([power[...], jnp.zeros((128, 256), jnp.float32)], axis=0)
    grid[...] = jnp.zeros(grid.shape, jnp.float32)
    lowers = (128, 256 * odd, 256 * (1 - odd))
    for number, spot in enumerate((here, twin, beyond)):
        row, col = spot[0, 0], spot[0, 1]
        frame[...] = pltpu.roll(tall, row, 0)
        piece = frame[pl.ds(pl.multiple_of(lowers[number], 128), 128), :]
        if number == 2:
            piece = piece * present
        wide = jnp.concatenate([piece, jnp.zeros((128, 128), jnp.float32)], axis=1)
        base = pl.multiple_of(col // 128 * 128, 128)
        grid[:, pl.ds(base, 384)] += pltpu.roll(wide, col % 128, 1)
    size = grid.shape[1]
    inner[...] = grid[:, 128 : size - 128]
    edge[...] = jnp.where(lax.axis_index("col") == 0, grid[:, size - 128 :], grid[:, 0:128])


def weights(count, here, twin, beyond, power, rows, cols):
    return pl.pallas_call(
        functools.partial(weights_kernel, count),
        out_shape=(f32(rows, cols), f32(rows, 128)),
        in_specs=[SMEM] * 3 + [VMEM],
        out_specs=(VMEM, VMEM),
        scratch_shapes=[
            pltpu.VMEM((384, 256), jnp.float32),
            pltpu.VMEM((rows, cols + 256), jnp.float32),
        ],
        compiler_params=params(6),
        name="object_weights",
    )(here, twin, beyond, power)


def position_kernel(
    twin, far_rows, mid_rows, own_rows, probe, pattern, one, two, weight,
    mine, his0, his, fold_far, fold_mid, fold_own,
    stack, window, far, update, strength,
):
    modes = probe.shape[0]
    r = lax.axis_index("row")
    first = lax.axis_index("col") == 0
    odd = lax.rem(r, 2)
    row = twin[0, 0]
    place = ring_place(r)
    far_at = pl.multiple_of(256 * (1 - odd), 128)
    own_at = pl.multiple_of(256 * odd, 128)
    stack[:, pl.ds(far_at, 128), :] = far_rows[...]
    stack[:, 128:256, :] = mid_rows[...]
    stack[:, pl.ds(own_at, 128), :] = own_rows[...]
    for part in range(2):
        window[part] = pltpu.roll(stack[part], (384 - row) % 384, 0)[0:256]

    for m in range(modes):
        p_re, p_im = probe[m, 0], probe[m, 1]
        w_re, w_im = window[0], window[1]
        e_re, e_im = p_re * w_re - p_im * w_im, p_re * w_im + p_im * w_re
        field = jnp.concatenate([e_re.astype(jnp.bfloat16), e_im.astype(jnp.bfloat16)], axis=0)
        half = jnp.dot(one[...], field, preferred_element_type=jnp.float32).astype(jnp.bfloat16)
        half = jnp.concatenate([half[0:256], half[256:512]], axis=1)
        out = jnp.dot(half, two[...], preferred_element_type=jnp.float32)
        far[m] = out
        power = out[:, 0:256] * out[:, 0:256] + out[:, 256:512] * out[:, 256:512]
        strength[...] = power if m == 0 else strength[...] + power

    strength[...] = jnp.sqrt(pattern[...]) / jnp.maximum(jnp.sqrt(strength[...]), AMP_FLOOR)

    spots = []
    for slab in range(8):
        ahead = (slab - place) & 7
        spots.append(jnp.where(ahead < 4, 7 - 2 * ahead, 2 * (ahead - 4)))

    def put(image, value):
        low, high = value[0:128], value[128:256]
        own, other = jnp.where(first, low, high), jnp.where(first, high, low)
        for slab in range(8):
            mine[spots[slab], image] = own[16 * slab : 16 * slab + 16]
            his[spots[slab], image] = other[16 * slab : 16 * slab + 16]

    density = window[0] * window[0] + window[1] * window[1]
    put(0, density)
    for m in range(modes):
        ratio = strength[...]
        fixed = jnp.concatenate(
            [
                (far[m, :, 0:256] * ratio).astype(jnp.bfloat16),
                (far[m, :, 256:512] * ratio).astype(jnp.bfloat16),
            ],
            axis=0,
        )
        back = jnp.dot(two[...], fixed, preferred_element_type=jnp.float32).astype(jnp.bfloat16)
        back = jnp.concatenate([back[0:256], back[256:512]], axis=1)
        near = jnp.dot(back, one[...], preferred_element_type=jnp.float32)
        n_re, n_im = near[:, 0:256], near[:, 256:512]
        p_re, p_im = probe[m, 0], probe[m, 1]
        w_re, w_im = window[0], window[1]
        density = w_re * w_re + w_im * w_im
        u_re = p_re * n_re + p_im * n_im
        u_im = p_re * n_im - p_im * n_re
        update[0] = u_re if m == 0 else update[0] + u_re
        update[1] = u_im if m == 0 else update[1] + u_im
        put(1 + 2 * m, w_re * n_re + w_im * n_im - density * p_re)
        put(2 + 2 * m, w_re * n_im - w_im * n_re - density * p_im)

    his0[...] = his[0:3]
    for part in range(2):
        whole = update[part] - weight[...] * window[part]
        tall = jnp.concatenate([whole, jnp.zeros((128, 256), jnp.float32)], axis=0)
        stack[part] = pltpu.roll(tall, row, 0)
    fold_far[...] = stack[:, pl.ds(far_at, 128), :]
    fold_mid[...] = stack[:, 128:256, :]
    fold_own[...] = stack[:, pl.ds(own_at, 128), :]


def position(twin, far_rows, mid_rows, own_rows, probe, pattern, one, two, weight):
    modes = probe.shape[0]
    images = 1 + 2 * modes
    return pl.pallas_call(
        position_kernel,
        out_shape=tuple(f32(legs, images, 16, 256) for legs in (8, 3, 8)) + (f32(2, 128, 256),) * 3,
        in_specs=[SMEM] + [VMEM] * 8,
        out_specs=(VMEM,) * 6,
        scratch_shapes=[
            pltpu.VMEM((2, 384, 256), jnp.float32),
            pltpu.VMEM((2, 256, 256), jnp.float32),
            pltpu.VMEM((modes, 256, 512), jnp.float32),
            pltpu.VMEM((2, 256, 256), jnp.float32),
            pltpu.VMEM((256, 256), jnp.float32),
        ],
        compiler_params=params(16),
        name="position_terms",
    )(twin, far_rows, mid_rows, own_rows, probe, pattern, one, two, weight)


def fold_kernel(here, twin, beyond, near, middle, far, inner, edge, grid):
    grid[...] = jnp.zeros(grid.shape, jnp.float32)
    for col, piece in ((twin[0, 1], near), (here[0, 1], middle), (beyond[0, 1], far)):
        base = pl.multiple_of(col // 128 * 128, 128)
        for part in range(2):
            wide = jnp.concatenate([piece[part], jnp.zeros((128, 128), jnp.float32)], axis=1)
            grid[part, :, pl.ds(base, 384)] += pltpu.roll(wide, col % 128, 1)
    size = grid.shape[2]
    inner[...] = grid[:, :, 128 : size - 128]
    edge[...] = jnp.where(lax.axis_index("col") == 0, grid[:, :, size - 128 :], grid[:, :, 0:128])


def fold(here, twin, beyond, near, middle, far, rows, cols):
    return pl.pallas_call(
        fold_kernel,
        out_shape=(f32(2, rows, cols), f32(2, rows, 128)),
        in_specs=[SMEM] * 3 + [VMEM] * 3,
        out_specs=(VMEM, VMEM),
        scratch_shapes=[pltpu.VMEM((2, rows, cols + 256), jnp.float32)],
        compiler_params=params(8),
        name="fold_object",
    )(here, twin, beyond, near, middle, far)


def leg_kernel(spot, low, mine, theirs, *refs):
    came, out = refs[:-1], refs[-1]
    high = low + out.shape[0]
    total = mine[spot, low:high] + theirs[spot, low:high]
    out[...] = total + came[0][...] if came else total


def add_leg(came, mine, theirs, spot, low, high):
    came = () if came is None else (came,)
    return pl.pallas_call(
        functools.partial(leg_kernel, spot, low),
        out_shape=f32(high - low, *mine.shape[2:]),
        in_specs=[VMEM] * (2 + len(came)),
        out_specs=VMEM,
        compiler_params=params(2),
        name="add_leg",
    )(mine, theirs, *came)


def close_kernel(
    ahead_low, ahead_high, behind_low, behind_high, mine, theirs, den_in, edge, low, high, den
):
    den[...] = den_in[...]
    cols = den.shape[1]
    side = pl.multiple_of((1 - lax.axis_index("col")) * (cols - 128), 128)
    den[:, pl.ds(side, 128)] += edge[...]
    object_peak = jnp.max(den[...])
    last = mine.shape[0] - 1
    cut, images = ahead_low.shape[0], mine.shape[1]
    for image in range(images):
        if image < cut:
            out, n, ahead, behind = low, image, ahead_low, behind_low
        else:
            out, n, ahead, behind = high, image - cut, ahead_high, behind_high
        out[16 * n : 16 * n + 16] = (mine[last, image] + theirs[last, image]) + (ahead[n] + behind[n])
    high[16 * (images - cut) :] = jnp.full((8, 256), object_peak, jnp.float32)


def close(ahead, behind, mine, theirs, den, edge):
    cut, images = ahead[0].shape[0], mine.shape[1]
    return pl.pallas_call(
        close_kernel,
        out_shape=(f32(16 * cut, 256), f32(16 * (images - cut) + 8, 256)),
        in_specs=[VMEM] * 8,
        out_specs=(VMEM, VMEM),
        scratch_shapes=[pltpu.VMEM(den.shape, jnp.float32)],
        compiler_params=params(2),
        name="close_sum",
    )(*ahead, *behind, mine, theirs, den, edge)


def pack_kernel(edge, *refs):
    parts, out = refs[:-1], refs[-1]
    at = 0
    for part in parts:
        out[at : at + part.shape[0]] = part[...]
        at += part.shape[0]
    for part in range(2):
        out[at:, 128 * part : 128 * part + 128] = edge[part]


def pack(edge, parts):
    size = sum(x.shape[0] for x in parts) + edge.shape[1]
    return pl.pallas_call(
        pack_kernel,
        out_shape=f32(size, 256),
        in_specs=[VMEM] * (1 + len(parts)),
        out_specs=VMEM,
        compiler_params=params(4),
        name="pack",
    )(edge, *parts)


def finish_kernel(probe, block, inner, den, den_edge, packed, packed_last, *refs):
    hops = len(HOPS)
    parts, refs = refs[: 2 * hops], refs[2 * hops :]
    new_block_at, new_probe_at, new_probe, new_block, whole_den, scales, sems = refs
    cut, rest = parts[0].shape[0], parts[1].shape[0]
    size = cut + rest
    lows, highs = list(parts[0::2]), list(parts[1::2])
    for n in range(hops - 1):
        lows.append(packed.at[size * n : size * n + cut])
        highs.append(packed.at[size * n + cut : size * n + size])
    lows.append(packed_last.at[0:cut])
    highs.append(packed_last.at[cut:size])
    edge = packed.at[size * (hops - 1) :]
    modes = probe.shape[0]
    core = lax.axis_index("col")
    place = ring_place(lax.axis_index("row"))
    cols = block.shape[2]
    peak = jnp.zeros((8, 256), jnp.float32)
    object_peak = jnp.zeros((8, 256), jnp.float32)
    for low, high in zip(lows, highs):
        peak = jnp.maximum(peak, jnp.maximum(low[0:8], low[8:16]))
        object_peak = jnp.maximum(object_peak, high[rest - 8 : rest])
    peak = jnp.max(peak)
    object_peak = jnp.max(object_peak)
    starts = []
    for n, low in enumerate(lows):
        half = core if n < hops else 1 - core
        starts.append(pl.multiple_of(128 * half + 16 * ((place + HOPS[n % hops]) & 7), 16))
        scales[n] = 1.0 / ((1.0 - REGULAR) * low[0:16] + REGULAR * peak)
    outs = ()
    for m in range(modes):
        for part in range(2):
            at = 16 * (1 + 2 * m + part)
            for n in range(2 * hops):
                value = lows[n][at : at + 16] if at < cut else highs[n][at - cut : at - cut + 16]
                rows = pl.ds(starts[n], 16)
                new_probe[m, part, rows, :] = probe[m, part, rows, :] + value * scales[n]
        outs += begin((pltpu.make_async_copy(new_probe.at[m], new_probe_at.at[m], sems.at[m]),))
    side = pl.multiple_of((1 - core) * (cols - 128), 128)
    new_block[...] = inner[...]
    for part in range(2):
        new_block[part, :, pl.ds(side, 128)] += edge[:, 128 * part : 128 * part + 128]
    whole_den[...] = den[...]
    whole_den[:, pl.ds(side, 128)] += den_edge[...]
    scale = 1.0 / ((1.0 - REGULAR) * whole_den[...] + REGULAR * object_peak)
    for part in range(2):
        new_block[part] = block[part] + new_block[part] * scale
    outs += begin((pltpu.make_async_copy(new_block, new_block_at, sems.at[modes]),))
    end(outs)


def finish(probe, block, inner, den, den_edge, packed, packed_last, parts):
    modes = probe.shape[0]
    return pl.pallas_call(
        finish_kernel,
        out_shape=(f32(*block.shape), f32(*probe.shape)),
        in_specs=[VMEM] * (7 + len(parts)),
        out_specs=(ANY, ANY),
        scratch_shapes=[pltpu.VMEM(x.shape, jnp.float32) for x in (probe, block, den)]
        + [
            pltpu.VMEM((2 * len(HOPS), 16, 256), jnp.float32),
            pltpu.SemaphoreType.DMA((modes + 1,)),
        ],
        compiler_params=params(12),
        name="finish",
    )(probe, block, inner, den, den_edge, packed, packed_last, *parts)


def shards(object_field, probe, measured, offsets):
    rows, cols = object_field.shape[1], object_field.shape[2]
    count = lax.axis_size("row")
    one, two = transform_blocks(probe.shape[-1])
    one, two = jnp.asarray(one), jnp.asarray(two)

    twins = [(i, i ^ 1) for i in range(count)]
    cores = [(0, 1), (1, 0)]
    others = [(i + 1 if i % 2 else i - 1, i) for i in range(1, count - 1)]
    outward = [(i, i + 2) for i in range(1, count - 2, 2)] + [(i, i - 2) for i in range(2, count, 2)]
    inward = [(b, a) for a, b in outward]
    forward = [
        (block + RING_ORDER[i], block + RING_ORDER[(i + 1) % RING])
        for block in range(0, count, RING)
        for i in range(RING)
    ]
    reverse = [(b, a) for a, b in forward]

    def across(x):
        return lax.ppermute(x, "col", cores)

    def send(x, pairs):
        return lax.ppermute(x, "row", pairs)

    def after(x, y):
        return lax.optimization_barrier((x, y))[0]

    other = across(object_field)
    twin = send(offsets, twins)
    beyond = send(offsets, others)
    pattern = send(measured, twins)

    (to_twin,) = cut_slices(("here",), offsets, offsets, offsets, object_field, other, offsets)
    mid_rows = send(to_twin, twins)
    to_beyond, own_rows = cut_slices(
        ("beyond", "twin"), offsets, twin, beyond, object_field, other, to_twin
    )
    far_rows = send(to_beyond, outward)
    power = probe_power(after(probe, own_rows))
    object_den, den_edge = weights(count, offsets, twin, beyond, power, rows, cols)
    den_edge = across(den_edge)

    mine, his0, his, fold_far, fold_mid, fold_own = position(
        twin, far_rows, after(mid_rows, den_edge), own_rows, probe, pattern[0], one, two, power
    )
    images = mine.shape[1]
    cut = images // 2 + 1
    theirs = [across(his0)]
    theirs += [across(after(his, theirs[0]))]

    mid_got = send(fold_mid, twins)
    far_got = send(fold_far, inward)

    farthest = mine[0] + theirs[0][0]
    ahead = [send(farthest[:cut], forward), None]
    behind = [None, send(farthest[cut:], reverse)]
    bounds = ((0, cut), (cut, images))
    for leg in (1, 3, 5):
        for n in (0, 1):
            ahead[n] = send(add_leg(ahead[n], mine, theirs[leg > 1], leg, *bounds[n]), forward)
        for n in (1, 0):
            behind[n] = send(add_leg(behind[n], mine, theirs[leg > 1], leg + 1, *bounds[n]), reverse)
    message = close(ahead, behind, mine, theirs[1], object_den, den_edge)
    if count > RING:
        blocks = [[b * RING + i for b in range(count // RING)] for i in range(RING)]
        low = lax.psum(message[0], "row", axis_index_groups=blocks)
        high = lax.psum(message[1][:-8], "row", axis_index_groups=blocks)
        top = lax.pmax(message[1][-8:], "row", axis_index_groups=blocks)
        message = (low, jnp.concatenate([high, top], axis=0))

    parts = list(message)
    ahead = [send(x, forward) for x in message]
    behind = [send(x, reverse) for x in message]
    parts += ahead + behind
    ahead[0], mid_got, far_got = lax.optimization_barrier((ahead[0], mid_got, far_got))
    inner, edge = fold(offsets, twin, beyond, fold_own, mid_got, far_got, rows, cols)
    for hop in range(2):
        ahead = [send(x, forward) for x in ahead]
        behind = [send(x, reverse) for x in behind]
        parts += ahead + behind
    last = [send(ahead[0], forward), send(behind[1], reverse)]
    packed = across(pack(edge, parts))
    packed_last = across(jnp.concatenate(last, axis=0))
    return finish(probe, object_field, inner, object_den, den_edge, packed, packed_last, parts + last)


def solution(mesh):
    placed = (
        P(None, ("groups", "row"), "col"),
        P("groups", None, None, None),
        P(("groups", "row", "col"), None, None),
        P(("groups", "row", "col"), None),
    )
    return jax.shard_map(
        shards,
        mesh=mesh,
        in_specs=placed,
        out_specs=(P(None, ("groups", "row"), "col"), P("groups", None, None, None)),
        check_vma=False,
    )
```

```python
import functools
import math

import jax
import jax.numpy as jnp
import ml_dtypes
import numpy as np
from jax import lax
from jax.experimental import pallas as pl
from jax.experimental.pallas import tpu as pltpu
from jax.sharding import PartitionSpec as P

REGULAR = 0.25
AMP_FLOOR = 2.0
RING = 8
RING_ORDER = (0, 1, 3, 5, 7, 6, 4, 2)
HOPS = (0, -1, 1, -2, 2, -3, 3, 4)

SMEM = pl.BlockSpec(memory_space=pltpu.SMEM)
VMEM = pl.BlockSpec(memory_space=pltpu.VMEM)
ANY = pl.BlockSpec(memory_space=pl.ANY)
HBM = pl.BlockSpec(memory_space=pltpu.HBM)


def transform_blocks(length):
    indices = np.arange(length, dtype=np.int32)
    phases = indices[:, None] * indices[None, :] % length
    angles = phases.astype(np.float32) * np.float32(2.0 * math.pi / length)
    factor = np.float32(1.0 / math.sqrt(length))
    cos = (np.cos(angles) * factor).astype(ml_dtypes.bfloat16)
    sin = (-np.sin(angles) * factor).astype(ml_dtypes.bfloat16)
    one = np.block([[cos, -sin], [sin, cos]])
    return one, np.ascontiguousarray(one.T)


def ring_place(r):
    r = lax.rem(r, RING)
    return jnp.where(r == 0, 0, jnp.where(lax.rem(r, 2) == 1, (r + 1) // 2, RING - r // 2))


def params(mib):
    return pltpu.CompilerParams(vmem_limit_bytes=mib * 1024 * 1024)


def f32(*shape):
    return jax.ShapeDtypeStruct(shape, jnp.float32)


def begin(copies):
    for copy in copies:
        copy.start()
    return copies


def end(copies):
    for copy in copies:
        copy.wait()


def slices_kernel(offsets_at, *refs):
    offsets_in, (block, other, _), outs, (ext, cuts, offsets, sems) = refs[:3], refs[3:6], refs[6:-4], refs[-4:]
    core = lax.axis_index("col")
    cols = block.shape[2]
    end_of = cols + 128
    source = pl.multiple_of(core * (cols - 128), 128)
    target = pl.multiple_of((1 - core) * end_of, 128)
    blank = pl.multiple_of(core * end_of, 128)
    copies = begin(
        (
            pltpu.make_async_copy(block, ext.at[:, :, 128:end_of], sems.at[0]),
            pltpu.make_async_copy(
                other.at[:, :, pl.ds(source, 128)], ext.at[:, :, pl.ds(target, 128)], sems.at[1]
            ),
        )
        + tuple(
            pltpu.make_async_copy(spot, offsets.at[n], sems.at[4 + n]) for n, spot in enumerate(offsets_in)
        )
    )
    ext[:, :, pl.ds(blank, 128)] = jnp.zeros((2, block.shape[1], 128), jnp.float32)
    end(copies)
    columns = {"here": offsets[0, 0, 1], "twin": offsets[1, 0, 1], "beyond": offsets[2, 0, 1]}
    copies = ()
    for number, (which, out) in enumerate(zip(offsets_at, outs)):
        start = columns[which]
        base = pl.multiple_of(start // 128 * 128, 128)
        for part in range(2):
            wide = ext[part, :, pl.ds(base, 384)]
            wide = pltpu.roll(wide, (384 - start % 128) % 384, 1)
            cuts[number, part] = wide[:, 0:256]
        copies += begin((pltpu.make_async_copy(cuts.at[number], out, sems.at[2 + number]),))
    end(copies)


def cut_slices(offsets_at, here, twin, beyond, block, other, ordered):
    rows, cols = block.shape[1], block.shape[2]
    count = len(offsets_at)
    return pl.pallas_call(
        functools.partial(slices_kernel, offsets_at),
        out_shape=(f32(2, rows, 256),) * count,
        in_specs=[ANY] * 3 + [HBM] + [ANY] * 2,
        out_specs=(ANY,) * count,
        scratch_shapes=[
            pltpu.VMEM((2, rows, cols + 256), jnp.float32),
            pltpu.VMEM((count, 2, rows, 256), jnp.float32),
            pltpu.SMEM((3, 1, 2), jnp.int32),
            pltpu.SemaphoreType.DMA((7,)),
        ],
        compiler_params=params(6),
        name="cut_slices",
    )(here, twin, beyond, block, other, ordered)


def power_kernel(probe, out, held, sems):
    modes = probe.shape[0]
    copies = begin([pltpu.make_async_copy(probe.at[m], held.at[m], sems.at[m]) for m in range(modes)])
    for m in range(modes):
        copies[m].wait()
        power = held[m, 0] * held[m, 0] + held[m, 1] * held[m, 1]
        out[...] = power if m == 0 else out[...] + power


def probe_power(probe):
    return pl.pallas_call(
        power_kernel,
        out_shape=f32(*probe.shape[2:]),
        in_specs=[ANY],
        out_specs=VMEM,
        scratch_shapes=[pltpu.VMEM(probe.shape, jnp.float32), pltpu.SemaphoreType.DMA((probe.shape[0],))],
        compiler_params=params(8),
        name="probe_power",
    )(probe)


def weights_kernel(count, here, twin, beyond, power, inner, edge, frame, grid):
    r = lax.axis_index("row")
    odd = lax.rem(r, 2)
    present = jnp.logical_and(r > 0, r < count - 1).astype(jnp.float32)
    tall = jnp.concatenate([power[...], jnp.zeros((128, 256), jnp.float32)], axis=0)
    grid[...] = jnp.zeros(grid.shape, jnp.float32)
    lowers = (128, 256 * odd, 256 * (1 - odd))
    for number, spot in enumerate((here, twin, beyond)):
        row, col = spot[0, 0], spot[0, 1]
        frame[...] = pltpu.roll(tall, row, 0)
        piece = frame[pl.ds(pl.multiple_of(lowers[number], 128), 128), :]
        if number == 2:
            piece = piece * present
        wide = jnp.concatenate([piece, jnp.zeros((128, 128), jnp.float32)], axis=1)
        base = pl.multiple_of(col // 128 * 128, 128)
        grid[:, pl.ds(base, 384)] += pltpu.roll(wide, col % 128, 1)
    size = grid.shape[1]
    inner[...] = grid[:, 128 : size - 128]
    edge[...] = jnp.where(lax.axis_index("col") == 0, grid[:, size - 128 :], grid[:, 0:128])


def weights(count, here, twin, beyond, power, rows, cols):
    return pl.pallas_call(
        functools.partial(weights_kernel, count),
        out_shape=(f32(rows, cols), f32(rows, 128)),
        in_specs=[SMEM] * 3 + [VMEM],
        out_specs=(VMEM, VMEM),
        scratch_shapes=[
            pltpu.VMEM((384, 256), jnp.float32),
            pltpu.VMEM((rows, cols + 256), jnp.float32),
        ],
        compiler_params=params(6),
        name="object_weights",
    )(here, twin, beyond, power)


def slab_spots():
    place = ring_place(lax.axis_index("row"))
    spots = []
    for slab in range(8):
        ahead = (slab - place) & 7
        spots.append(jnp.where(ahead < 4, 7 - 2 * ahead, 2 * (ahead - 4)))
    return spots


def put(spots, mine, his, image, value):
    first = lax.axis_index("col") == 0
    low, high = value[0:128], value[128:256]
    own, other = jnp.where(first, low, high), jnp.where(first, high, low)
    for slab in range(8):
        mine[spots[slab], image] = own[16 * slab : 16 * slab + 16]
        his[spots[slab], image] = other[16 * slab : 16 * slab + 16]


def backward(far, ratio, p_re, p_im, w_re, w_im, one, two):
    fixed = jnp.concatenate(
        [(far[:, 0:256] * ratio).astype(jnp.bfloat16), (far[:, 256:512] * ratio).astype(jnp.bfloat16)],
        axis=0,
    )
    back = jnp.dot(two[...], fixed, preferred_element_type=jnp.float32).astype(jnp.bfloat16)
    back = jnp.concatenate([back[0:256], back[256:512]], axis=1)
    near = jnp.dot(back, one[...], preferred_element_type=jnp.float32)
    n_re, n_im = near[:, 0:256], near[:, 256:512]
    density = w_re * w_re + w_im * w_im
    return (
        p_re * n_re + p_im * n_im,
        p_re * n_im - p_im * n_re,
        w_re * n_re + w_im * n_im - density * p_re,
        w_re * n_im - w_im * n_re - density * p_im,
    )


def position_kernel(
    twin, far_rows, mid_rows, own_rows, probe, pattern, one, two,
    mine, his, window, rest, strength, update,
    stack, far,
):
    modes = probe.shape[0]
    cut = modes // 2
    odd = lax.rem(lax.axis_index("row"), 2)
    row = twin[0, 0]
    stack[:, pl.ds(pl.multiple_of(256 * (1 - odd), 128), 128), :] = far_rows[...]
    stack[:, 128:256, :] = mid_rows[...]
    stack[:, pl.ds(pl.multiple_of(256 * odd, 128), 128), :] = own_rows[...]
    for part in range(2):
        window[part] = pltpu.roll(stack[part], (384 - row) % 384, 0)[0:256]

    for m in range(modes):
        p_re, p_im = probe[m, 0], probe[m, 1]
        w_re, w_im = window[0], window[1]
        e_re, e_im = p_re * w_re - p_im * w_im, p_re * w_im + p_im * w_re
        field = jnp.concatenate([e_re.astype(jnp.bfloat16), e_im.astype(jnp.bfloat16)], axis=0)
        half = jnp.dot(one[...], field, preferred_element_type=jnp.float32).astype(jnp.bfloat16)
        half = jnp.concatenate([half[0:256], half[256:512]], axis=1)
        out = jnp.dot(half, two[...], preferred_element_type=jnp.float32)
        if m < cut:
            far[m] = out
        else:
            rest[m - cut] = out
        power = out[:, 0:256] * out[:, 0:256] + out[:, 256:512] * out[:, 256:512]
        strength[...] = power if m == 0 else strength[...] + power

    strength[...] = jnp.sqrt(pattern[...]) / jnp.maximum(jnp.sqrt(strength[...]), AMP_FLOOR)

    spots = slab_spots()
    put(spots, mine, his, 0, window[0] * window[0] + window[1] * window[1])
    for m in range(cut):
        u_re, u_im, t_re, t_im = backward(
            far[m], strength[...], probe[m, 0], probe[m, 1], window[0], window[1], one, two
        )
        update[0] = u_re if m == 0 else update[0] + u_re
        update[1] = u_im if m == 0 else update[1] + u_im
        put(spots, mine, his, 1 + 2 * m, t_re)
        put(spots, mine, his, 2 + 2 * m, t_im)


def position(twin, far_rows, mid_rows, own_rows, probe, pattern, one, two):
    modes = probe.shape[0]
    cut = modes // 2
    return pl.pallas_call(
        position_kernel,
        out_shape=(f32(8, 1 + 2 * cut, 16, 256),) * 2
        + (f32(2, 256, 256), f32(modes - cut, 256, 512), f32(256, 256), f32(2, 256, 256)),
        in_specs=[SMEM] + [VMEM] * 7,
        out_specs=(VMEM,) * 6,
        scratch_shapes=[
            pltpu.VMEM((2, 384, 256), jnp.float32),
            pltpu.VMEM((cut, 256, 512), jnp.float32),
        ],
        compiler_params=params(10),
        name="position_terms",
    )(twin, far_rows, mid_rows, own_rows, probe, pattern, one, two)


def position_rest_kernel(
    twin, window, rest, strength, update, probe, one, two, weight,
    mine, his, fold_far, fold_mid, fold_own,
    stack, total,
):
    modes = probe.shape[0]
    count = rest.shape[0]
    odd = lax.rem(lax.axis_index("row"), 2)
    spots = slab_spots()
    for part in range(2):
        total[part] = update[part] - weight[...] * window[part]
    for n in range(count):
        m = modes - count + n
        u_re, u_im, t_re, t_im = backward(
            rest[n], strength[...], probe[m, 0], probe[m, 1], window[0], window[1], one, two
        )
        total[0] = total[0] + u_re
        total[1] = total[1] + u_im
        put(spots, mine, his, 2 * n, t_re)
        put(spots, mine, his, 2 * n + 1, t_im)
    for part in range(2):
        tall = jnp.concatenate([total[part], jnp.zeros((128, 256), jnp.float32)], axis=0)
        stack[part] = pltpu.roll(tall, twin[0, 0], 0)
    fold_far[...] = stack[:, pl.ds(pl.multiple_of(256 * (1 - odd), 128), 128), :]
    fold_mid[...] = stack[:, 128:256, :]
    fold_own[...] = stack[:, pl.ds(pl.multiple_of(256 * odd, 128), 128), :]


def position_rest(twin, window, rest, strength, update, probe, one, two, weight):
    images = 2 * rest.shape[0]
    return pl.pallas_call(
        position_rest_kernel,
        out_shape=(f32(8, images, 16, 256),) * 2 + (f32(2, 128, 256),) * 3,
        in_specs=[SMEM] + [VMEM] * 8,
        out_specs=(VMEM,) * 5,
        scratch_shapes=[
            pltpu.VMEM((2, 384, 256), jnp.float32),
            pltpu.VMEM((2, 256, 256), jnp.float32),
        ],
        compiler_params=params(8),
        name="position_rest",
    )(twin, window, rest, strength, update, probe, one, two, weight)


def fold_kernel(here, twin, beyond, near, middle, far, inner, edge, grid):
    grid[...] = jnp.zeros(grid.shape, jnp.float32)
    for col, piece in ((twin[0, 1], near), (here[0, 1], middle), (beyond[0, 1], far)):
        base = pl.multiple_of(col // 128 * 128, 128)
        for part in range(2):
            wide = jnp.concatenate([piece[part], jnp.zeros((128, 128), jnp.float32)], axis=1)
            grid[part, :, pl.ds(base, 384)] += pltpu.roll(wide, col % 128, 1)
    size = grid.shape[2]
    inner[...] = grid[:, :, 128 : size - 128]
    edge[...] = jnp.where(lax.axis_index("col") == 0, grid[:, :, size - 128 :], grid[:, :, 0:128])


def fold(here, twin, beyond, near, middle, far, rows, cols):
    return pl.pallas_call(
        fold_kernel,
        out_shape=(f32(2, rows, cols), f32(2, rows, 128)),
        in_specs=[SMEM] * 3 + [VMEM] * 3,
        out_specs=(VMEM, VMEM),
        scratch_shapes=[pltpu.VMEM((2, rows, cols + 256), jnp.float32)],
        compiler_params=params(8),
        name="fold_object",
    )(here, twin, beyond, near, middle, far)


def leg_kernel(spot, mine, theirs, *refs):
    came, out = refs[:-1], refs[-1]
    total = mine[spot] + theirs[spot]
    out[...] = total + came[0][...] if came else total


def add_leg(came, mine, theirs, spot):
    came = () if came is None else (came,)
    return pl.pallas_call(
        functools.partial(leg_kernel, spot),
        out_shape=f32(*mine.shape[1:]),
        in_specs=[VMEM] * (2 + len(came)),
        out_specs=VMEM,
        compiler_params=params(2),
        name="add_leg",
    )(mine, theirs, *came)


def close_kernel(
    ahead_low, ahead_high, behind_low, behind_high, mine_low, mine_high, theirs_low, theirs_high,
    den_in, edge, low, high, den,
):
    den[...] = den_in[...]
    cols = den.shape[1]
    side = pl.multiple_of((1 - lax.axis_index("col")) * (cols - 128), 128)
    den[:, pl.ds(side, 128)] += edge[...]
    object_peak = jnp.max(den[...])
    last = mine_low.shape[0] - 1
    for out, ahead, behind, mine, theirs in (
        (low, ahead_low, behind_low, mine_low, theirs_low),
        (high, ahead_high, behind_high, mine_high, theirs_high),
    ):
        for n in range(ahead.shape[0]):
            out[16 * n : 16 * n + 16] = (mine[last, n] + theirs[last, n]) + (ahead[n] + behind[n])
    high[16 * ahead_high.shape[0] :] = jnp.full((8, 256), object_peak, jnp.float32)


def close(ahead, behind, mine, theirs, den, edge):
    return pl.pallas_call(
        close_kernel,
        out_shape=(f32(16 * mine[0].shape[1], 256), f32(16 * mine[1].shape[1] + 8, 256)),
        in_specs=[VMEM] * 10,
        out_specs=(VMEM, VMEM),
        scratch_shapes=[pltpu.VMEM(den.shape, jnp.float32)],
        compiler_params=params(2),
        name="close_sum",
    )(*ahead, *behind, *mine, *theirs, den, edge)


def pack_kernel(edge, *refs):
    parts, out = refs[:-1], refs[-1]
    at = 0
    for part in parts:
        out[at : at + part.shape[0]] = part[...]
        at += part.shape[0]
    for part in range(2):
        out[at:, 128 * part : 128 * part + 128] = edge[part]


def pack(edge, parts):
    size = sum(x.shape[0] for x in parts) + edge.shape[1]
    return pl.pallas_call(
        pack_kernel,
        out_shape=f32(size, 256),
        in_specs=[VMEM] * (1 + len(parts)),
        out_specs=VMEM,
        compiler_params=params(4),
        name="pack",
    )(edge, *parts)


def finish_kernel(probe, block, inner, den, den_edge, packed, packed_last, *refs):
    hops = len(HOPS)
    parts, refs = refs[: 2 * hops], refs[2 * hops :]
    new_block_at, new_probe_at, new_probe, new_block, whole_den, scales, sems = refs
    cut, rest = parts[0].shape[0], parts[1].shape[0]
    size = cut + rest
    lows, highs = list(parts[0::2]), list(parts[1::2])
    for n in range(hops - 1):
        lows.append(packed.at[size * n : size * n + cut])
        highs.append(packed.at[size * n + cut : size * n + size])
    lows.append(packed_last.at[0:cut])
    highs.append(packed_last.at[cut:size])
    edge = packed.at[size * (hops - 1) :]
    modes = probe.shape[0]
    core = lax.axis_index("col")
    place = ring_place(lax.axis_index("row"))
    cols = block.shape[2]
    peak = jnp.zeros((8, 256), jnp.float32)
    object_peak = jnp.zeros((8, 256), jnp.float32)
    for low, high in zip(lows, highs):
        peak = jnp.maximum(peak, jnp.maximum(low[0:8], low[8:16]))
        object_peak = jnp.maximum(object_peak, high[rest - 8 : rest])
    peak = jnp.max(peak)
    object_peak = jnp.max(object_peak)
    starts = []
    for n, low in enumerate(lows):
        half = core if n < hops else 1 - core
        starts.append(pl.multiple_of(128 * half + 16 * ((place + HOPS[n % hops]) & 7), 16))
        scales[n] = 1.0 / ((1.0 - REGULAR) * low[0:16] + REGULAR * peak)
    outs = ()
    for m in range(modes):
        for part in range(2):
            at = 16 * (1 + 2 * m + part)
            for n in range(2 * hops):
                value = lows[n][at : at + 16] if at < cut else highs[n][at - cut : at - cut + 16]
                rows = pl.ds(starts[n], 16)
                new_probe[m, part, rows, :] = probe[m, part, rows, :] + value * scales[n]
        outs += begin((pltpu.make_async_copy(new_probe.at[m], new_probe_at.at[m], sems.at[m]),))
    side = pl.multiple_of((1 - core) * (cols - 128), 128)
    new_block[...] = inner[...]
    for part in range(2):
        new_block[part, :, pl.ds(side, 128)] += edge[:, 128 * part : 128 * part + 128]
    whole_den[...] = den[...]
    whole_den[:, pl.ds(side, 128)] += den_edge[...]
    scale = 1.0 / ((1.0 - REGULAR) * whole_den[...] + REGULAR * object_peak)
    for part in range(2):
        new_block[part] = block[part] + new_block[part] * scale
    outs += begin((pltpu.make_async_copy(new_block, new_block_at, sems.at[modes]),))
    end(outs)


def finish(probe, block, inner, den, den_edge, packed, packed_last, parts):
    modes = probe.shape[0]
    return pl.pallas_call(
        finish_kernel,
        out_shape=(f32(*block.shape), f32(*probe.shape)),
        in_specs=[VMEM] * (7 + len(parts)),
        out_specs=(ANY, ANY),
        scratch_shapes=[pltpu.VMEM(x.shape, jnp.float32) for x in (probe, block, den)]
        + [
            pltpu.VMEM((2 * len(HOPS), 16, 256), jnp.float32),
            pltpu.SemaphoreType.DMA((modes + 1,)),
        ],
        compiler_params=params(12),
        name="finish",
    )(probe, block, inner, den, den_edge, packed, packed_last, *parts)


def shards(object_field, probe, measured, offsets):
    rows, cols = object_field.shape[1], object_field.shape[2]
    count = lax.axis_size("row")
    one, two = transform_blocks(probe.shape[-1])
    one, two = jnp.asarray(one), jnp.asarray(two)

    twins = [(i, i ^ 1) for i in range(count)]
    cores = [(0, 1), (1, 0)]
    others = [(i + 1 if i % 2 else i - 1, i) for i in range(1, count - 1)]
    outward = [(i, i + 2) for i in range(1, count - 2, 2)] + [(i, i - 2) for i in range(2, count, 2)]
    inward = [(b, a) for a, b in outward]
    forward = [
        (block + RING_ORDER[i], block + RING_ORDER[(i + 1) % RING])
        for block in range(0, count, RING)
        for i in range(RING)
    ]
    reverse = [(b, a) for a, b in forward]

    def across(x):
        return lax.ppermute(x, "col", cores)

    def send(x, pairs):
        return lax.ppermute(x, "row", pairs)

    def after(x, y):
        return lax.optimization_barrier((x, y))[0]

    other = across(object_field)
    twin = send(offsets, twins)
    beyond = send(offsets, others)
    pattern = send(measured, twins)

    (to_twin,) = cut_slices(("here",), offsets, offsets, offsets, object_field, other, offsets)
    mid_rows = send(to_twin, twins)
    to_beyond, own_rows = cut_slices(
        ("beyond", "twin"), offsets, twin, beyond, object_field, other, to_twin
    )
    far_rows = send(to_beyond, outward)
    power = probe_power(after(probe, own_rows))
    object_den, den_edge = weights(count, offsets, twin, beyond, power, rows, cols)
    den_edge = across(den_edge)

    mine_low, his_low, window, rest, strength, update = position(
        twin, far_rows, after(mid_rows, den_edge), own_rows, probe, pattern[0], one, two
    )
    theirs_low = across(his_low)
    mine_high, his_high, fold_far, fold_mid, fold_own = position_rest(
        twin, window, rest, strength, update, probe, one, two, power
    )
    theirs_high = across(his_high)
    mid_got = send(fold_mid, twins)
    far_got = send(fold_far, inward)

    start_ahead = add_leg(None, mine_low, theirs_low, 0)
    start_behind = add_leg(None, mine_low, theirs_low, 2)
    theirs_high = after(theirs_high, start_behind)
    mine, theirs = (mine_low, mine_high), (theirs_low, theirs_high)

    def legs(part, came, spots, pairs):
        for spot in spots:
            came = send(add_leg(came, mine[part], theirs[part], spot), pairs)
        return came

    ahead = [legs(0, send(start_ahead, forward), (1, 3, 5), forward), legs(1, None, (1, 3, 5), forward)]
    behind = [legs(0, send(start_behind, reverse), (4, 6), reverse), legs(1, None, (0, 2, 4, 6), reverse)]
    message = close(ahead, behind, mine, theirs, object_den, den_edge)
    if count > RING:
        blocks = [[b * RING + i for b in range(count // RING)] for i in range(RING)]
        low = lax.psum(message[0], "row", axis_index_groups=blocks)
        high = lax.psum(message[1][:-8], "row", axis_index_groups=blocks)
        top = lax.pmax(message[1][-8:], "row", axis_index_groups=blocks)
        message = (low, jnp.concatenate([high, top], axis=0))

    parts = list(message)
    ahead = [send(x, forward) for x in message]
    behind = [send(x, reverse) for x in message]
    parts += ahead + behind
    ahead[0], mid_got, far_got = lax.optimization_barrier((ahead[0], mid_got, far_got))
    inner, edge = fold(offsets, twin, beyond, fold_own, mid_got, far_got, rows, cols)
    for hop in range(2):
        ahead = [send(x, forward) for x in ahead]
        behind = [send(x, reverse) for x in behind]
        parts += ahead + behind
    last = [send(ahead[0], forward), send(behind[1], reverse)]
    packed = across(pack(edge, parts))
    packed_last = across(jnp.concatenate(last, axis=0))
    return finish(probe, object_field, inner, object_den, den_edge, packed, packed_last, parts + last)


def solution(mesh):
    placed = (
        P(None, ("groups", "row"), "col"),
        P("groups", None, None, None),
        P(("groups", "row", "col"), None, None),
        P(("groups", "row", "col"), None),
    )
    return jax.shard_map(
        shards,
        mesh=mesh,
        in_specs=placed,
        out_specs=(P(None, ("groups", "row"), "col"), P("groups", None, None, None)),
        check_vma=False,
    )
```

```python
import functools
import math

import jax
import jax.numpy as jnp
import ml_dtypes
import numpy as np
from jax import lax
from jax.experimental import pallas as pl
from jax.experimental.pallas import tpu as pltpu
from jax.sharding import PartitionSpec as P

REGULAR = 0.25
AMP_FLOOR = 2.0
RING = 8
RING_ORDER = (0, 1, 3, 5, 7, 6, 4, 2)
HOPS = (0, -1, 1, -2, 2, -3, 3, 4)

SMEM = pl.BlockSpec(memory_space=pltpu.SMEM)
VMEM = pl.BlockSpec(memory_space=pltpu.VMEM)
ANY = pl.BlockSpec(memory_space=pl.ANY)
HBM = pl.BlockSpec(memory_space=pltpu.HBM)


def transform_blocks(length):
    indices = np.arange(length, dtype=np.int32)
    phases = indices[:, None] * indices[None, :] % length
    angles = phases.astype(np.float32) * np.float32(2.0 * math.pi / length)
    factor = np.float32(1.0 / math.sqrt(length))
    cos = (np.cos(angles) * factor).astype(ml_dtypes.bfloat16)
    sin = (-np.sin(angles) * factor).astype(ml_dtypes.bfloat16)
    one = np.block([[cos, -sin], [sin, cos]])
    return one, np.ascontiguousarray(one.T)


def ring_place(r):
    r = lax.rem(r, RING)
    return jnp.where(r == 0, 0, jnp.where(lax.rem(r, 2) == 1, (r + 1) // 2, RING - r // 2))


def params(mib):
    return pltpu.CompilerParams(vmem_limit_bytes=mib * 1024 * 1024)


def f32(*shape):
    return jax.ShapeDtypeStruct(shape, jnp.float32)


def begin(copies):
    for copy in copies:
        copy.start()
    return copies


def end(copies):
    for copy in copies:
        copy.wait()


def slices_kernel(offsets_at, *refs):
    offsets_in, (block, other), outs, (ext, cuts, offsets, sems) = refs[:3], refs[3:5], refs[5:-4], refs[-4:]
    core = lax.axis_index("col")
    cols = block.shape[2]
    end_of = cols + 128
    source = pl.multiple_of(core * (cols - 128), 128)
    target = pl.multiple_of((1 - core) * end_of, 128)
    blank = pl.multiple_of(core * end_of, 128)
    copies = begin(
        (
            pltpu.make_async_copy(block, ext.at[:, :, 128:end_of], sems.at[0]),
            pltpu.make_async_copy(
                other.at[:, :, pl.ds(source, 128)], ext.at[:, :, pl.ds(target, 128)], sems.at[1]
            ),
        )
        + tuple(
            pltpu.make_async_copy(spot, offsets.at[n], sems.at[5 + n]) for n, spot in enumerate(offsets_in)
        )
    )
    ext[:, :, pl.ds(blank, 128)] = jnp.zeros((2, block.shape[1], 128), jnp.float32)
    end(copies)
    columns = {"here": offsets[0, 0, 1], "twin": offsets[1, 0, 1], "beyond": offsets[2, 0, 1]}
    copies = ()
    for number, (which, out) in enumerate(zip(offsets_at, outs)):
        start = columns[which]
        base = pl.multiple_of(start // 128 * 128, 128)
        for part in range(2):
            wide = ext[part, :, pl.ds(base, 384)]
            wide = pltpu.roll(wide, (384 - start % 128) % 384, 1)
            cuts[number, part] = wide[:, 0:256]
        copies += begin((pltpu.make_async_copy(cuts.at[number], out, sems.at[2 + number]),))
    end(copies)


def cut_slices(offsets_at, here, twin, beyond, block, other):
    rows, cols = block.shape[1], block.shape[2]
    count = len(offsets_at)
    return pl.pallas_call(
        functools.partial(slices_kernel, offsets_at),
        out_shape=(f32(2, rows, 256),) * count,
        in_specs=[ANY] * 3 + [HBM, ANY],
        out_specs=(ANY,) * count,
        scratch_shapes=[
            pltpu.VMEM((2, rows, cols + 256), jnp.float32),
            pltpu.VMEM((count, 2, rows, 256), jnp.float32),
            pltpu.SMEM((3, 1, 2), jnp.int32),
            pltpu.SemaphoreType.DMA((8,)),
        ],
        compiler_params=params(6),
        name="cut_slices",
    )(here, twin, beyond, block, other)


def power_kernel(probe, out, held, sems):
    modes = probe.shape[0]
    copies = begin([pltpu.make_async_copy(probe.at[m], held.at[m], sems.at[m]) for m in range(modes)])
    for m in range(modes):
        copies[m].wait()
        power = held[m, 0] * held[m, 0] + held[m, 1] * held[m, 1]
        out[...] = power if m == 0 else out[...] + power


def probe_power(probe):
    return pl.pallas_call(
        power_kernel,
        out_shape=f32(*probe.shape[2:]),
        in_specs=[ANY],
        out_specs=VMEM,
        scratch_shapes=[pltpu.VMEM(probe.shape, jnp.float32), pltpu.SemaphoreType.DMA((probe.shape[0],))],
        compiler_params=params(8),
        name="probe_power",
    )(probe)


def weights_kernel(count, here, twin, beyond, power, inner, edge, frame, grid):
    r = lax.axis_index("row")
    odd = lax.rem(r, 2)
    present = jnp.logical_and(r > 0, r < count - 1).astype(jnp.float32)
    tall = jnp.concatenate([power[...], jnp.zeros((128, 256), jnp.float32)], axis=0)
    grid[...] = jnp.zeros(grid.shape, jnp.float32)
    lowers = (128, 256 * odd, 256 * (1 - odd))
    for number, spot in enumerate((here, twin, beyond)):
        row, col = spot[0, 0], spot[0, 1]
        frame[...] = pltpu.roll(tall, row, 0)
        piece = frame[pl.ds(pl.multiple_of(lowers[number], 128), 128), :]
        if number == 2:
            piece = piece * present
        wide = jnp.concatenate([piece, jnp.zeros((128, 128), jnp.float32)], axis=1)
        base = pl.multiple_of(col // 128 * 128, 128)
        grid[:, pl.ds(base, 384)] += pltpu.roll(wide, col % 128, 1)
    size = grid.shape[1]
    inner[...] = grid[:, 128 : size - 128]
    edge[...] = jnp.where(lax.axis_index("col") == 0, grid[:, size - 128 :], grid[:, 0:128])


def weights(count, here, twin, beyond, power, rows, cols):
    return pl.pallas_call(
        functools.partial(weights_kernel, count),
        out_shape=(f32(rows, cols), f32(rows, 128)),
        in_specs=[SMEM] * 3 + [VMEM],
        out_specs=(VMEM, VMEM),
        scratch_shapes=[
            pltpu.VMEM((384, 256), jnp.float32),
            pltpu.VMEM((rows, cols + 256), jnp.float32),
        ],
        compiler_params=params(6),
        name="object_weights",
    )(here, twin, beyond, power)


def slab_spots():
    place = ring_place(lax.axis_index("row"))
    spots = []
    for slab in range(8):
        ahead = (slab - place) & 7
        spots.append(jnp.where(ahead < 4, 7 - 2 * ahead, 2 * (ahead - 4)))
    return spots


def put(spots, mine, his, image, value):
    first = lax.axis_index("col") == 0
    low, high = value[0:128], value[128:256]
    own, other = jnp.where(first, low, high), jnp.where(first, high, low)
    for slab in range(8):
        mine[spots[slab], image] = own[16 * slab : 16 * slab + 16]
        his[spots[slab], image] = other[16 * slab : 16 * slab + 16]


def backward(far, ratio, p_re, p_im, w_re, w_im, one, two):
    fixed = jnp.concatenate(
        [(far[:, 0:256] * ratio).astype(jnp.bfloat16), (far[:, 256:512] * ratio).astype(jnp.bfloat16)],
        axis=0,
    )
    back = jnp.dot(two[...], fixed, preferred_element_type=jnp.float32).astype(jnp.bfloat16)
    back = jnp.concatenate([back[0:256], back[256:512]], axis=1)
    near = jnp.dot(back, one[...], preferred_element_type=jnp.float32)
    n_re, n_im = near[:, 0:256], near[:, 256:512]
    density = w_re * w_re + w_im * w_im
    return (
        p_re * n_re + p_im * n_im,
        p_re * n_im - p_im * n_re,
        w_re * n_re + w_im * n_im - density * p_re,
        w_re * n_im - w_im * n_re - density * p_im,
    )


def position_kernel(
    twin, far_rows, mid_rows, own_rows, probe, pattern, one, two,
    mine, his, window, rest, strength, update,
    stack, far,
):
    modes = probe.shape[0]
    cut = modes // 2
    odd = lax.rem(lax.axis_index("row"), 2)
    row = twin[0, 0]
    stack[:, pl.ds(pl.multiple_of(256 * (1 - odd), 128), 128), :] = far_rows[...]
    stack[:, 128:256, :] = mid_rows[...]
    stack[:, pl.ds(pl.multiple_of(256 * odd, 128), 128), :] = own_rows[...]
    for part in range(2):
        window[part] = pltpu.roll(stack[part], (384 - row) % 384, 0)[0:256]

    for m in range(modes):
        p_re, p_im = probe[m, 0], probe[m, 1]
        w_re, w_im = window[0], window[1]
        e_re, e_im = p_re * w_re - p_im * w_im, p_re * w_im + p_im * w_re
        field = jnp.concatenate([e_re.astype(jnp.bfloat16), e_im.astype(jnp.bfloat16)], axis=0)
        half = jnp.dot(one[...], field, preferred_element_type=jnp.float32).astype(jnp.bfloat16)
        half = jnp.concatenate([half[0:256], half[256:512]], axis=1)
        out = jnp.dot(half, two[...], preferred_element_type=jnp.float32)
        if m < cut:
            far[m] = out
        else:
            rest[m - cut] = out
        power = out[:, 0:256] * out[:, 0:256] + out[:, 256:512] * out[:, 256:512]
        strength[...] = power if m == 0 else strength[...] + power

    strength[...] = jnp.sqrt(pattern[...]) / jnp.maximum(jnp.sqrt(strength[...]), AMP_FLOOR)

    spots = slab_spots()
    put(spots, mine, his, 0, window[0] * window[0] + window[1] * window[1])
    for m in range(cut):
        u_re, u_im, t_re, t_im = backward(
            far[m], strength[...], probe[m, 0], probe[m, 1], window[0], window[1], one, two
        )
        update[0] = u_re if m == 0 else update[0] + u_re
        update[1] = u_im if m == 0 else update[1] + u_im
        put(spots, mine, his, 1 + 2 * m, t_re)
        put(spots, mine, his, 2 + 2 * m, t_im)


def position(twin, far_rows, mid_rows, own_rows, probe, pattern, one, two):
    modes = probe.shape[0]
    cut = modes // 2
    return pl.pallas_call(
        position_kernel,
        out_shape=(f32(8, 1 + 2 * cut, 16, 256),) * 2
        + (f32(2, 256, 256), f32(modes - cut, 256, 512), f32(256, 256), f32(2, 256, 256)),
        in_specs=[SMEM] + [VMEM] * 7,
        out_specs=(VMEM,) * 6,
        scratch_shapes=[
            pltpu.VMEM((2, 384, 256), jnp.float32),
            pltpu.VMEM((cut, 256, 512), jnp.float32),
        ],
        compiler_params=params(10),
        name="position_terms",
    )(twin, far_rows, mid_rows, own_rows, probe, pattern, one, two)


def position_rest_kernel(
    twin, window, rest, strength, update, probe, one, two, weight,
    mine, his, fold_far, fold_mid, fold_own,
    stack, total,
):
    modes = probe.shape[0]
    count = rest.shape[0]
    odd = lax.rem(lax.axis_index("row"), 2)
    spots = slab_spots()
    for part in range(2):
        total[part] = update[part] - weight[...] * window[part]
    for n in range(count):
        m = modes - count + n
        u_re, u_im, t_re, t_im = backward(
            rest[n], strength[...], probe[m, 0], probe[m, 1], window[0], window[1], one, two
        )
        total[0] = total[0] + u_re
        total[1] = total[1] + u_im
        put(spots, mine, his, 2 * n, t_re)
        put(spots, mine, his, 2 * n + 1, t_im)
    for part in range(2):
        tall = jnp.concatenate([total[part], jnp.zeros((128, 256), jnp.float32)], axis=0)
        stack[part] = pltpu.roll(tall, twin[0, 0], 0)
    fold_far[...] = stack[:, pl.ds(pl.multiple_of(256 * (1 - odd), 128), 128), :]
    fold_mid[...] = stack[:, 128:256, :]
    fold_own[...] = stack[:, pl.ds(pl.multiple_of(256 * odd, 128), 128), :]


def position_rest(twin, window, rest, strength, update, probe, one, two, weight):
    images = 2 * rest.shape[0]
    return pl.pallas_call(
        position_rest_kernel,
        out_shape=(f32(8, images, 16, 256),) * 2 + (f32(2, 128, 256),) * 3,
        in_specs=[SMEM] + [VMEM] * 8,
        out_specs=(VMEM,) * 5,
        scratch_shapes=[
            pltpu.VMEM((2, 384, 256), jnp.float32),
            pltpu.VMEM((2, 256, 256), jnp.float32),
        ],
        compiler_params=params(8),
        name="position_rest",
    )(twin, window, rest, strength, update, probe, one, two, weight)


def fold_kernel(here, twin, beyond, near, middle, far, inner, edge, grid):
    grid[...] = jnp.zeros(grid.shape, jnp.float32)
    for col, piece in ((twin[0, 1], near), (here[0, 1], middle), (beyond[0, 1], far)):
        base = pl.multiple_of(col // 128 * 128, 128)
        for part in range(2):
            wide = jnp.concatenate([piece[part], jnp.zeros((128, 128), jnp.float32)], axis=1)
            grid[part, :, pl.ds(base, 384)] += pltpu.roll(wide, col % 128, 1)
    size = grid.shape[2]
    inner[...] = grid[:, :, 128 : size - 128]
    edge[...] = jnp.where(lax.axis_index("col") == 0, grid[:, :, size - 128 :], grid[:, :, 0:128])


def fold(here, twin, beyond, near, middle, far, rows, cols):
    return pl.pallas_call(
        fold_kernel,
        out_shape=(f32(2, rows, cols), f32(2, rows, 128)),
        in_specs=[SMEM] * 3 + [VMEM] * 3,
        out_specs=(VMEM, VMEM),
        scratch_shapes=[pltpu.VMEM((2, rows, cols + 256), jnp.float32)],
        compiler_params=params(8),
        name="fold_object",
    )(here, twin, beyond, near, middle, far)


def leg_kernel(spot, mine, theirs, *refs):
    came, out = refs[:-1], refs[-1]
    total = mine[spot] + theirs[spot]
    out[...] = total + came[0][...] if came else total


def add_leg(came, mine, theirs, spot):
    came = () if came is None else (came,)
    return pl.pallas_call(
        functools.partial(leg_kernel, spot),
        out_shape=f32(*mine.shape[1:]),
        in_specs=[VMEM] * (2 + len(came)),
        out_specs=VMEM,
        compiler_params=params(2),
        name="add_leg",
    )(mine, theirs, *came)


def close_kernel(
    ahead_low, ahead_high, behind_low, behind_high, mine_low, mine_high, theirs_low, theirs_high,
    den_in, edge, low, high, den,
):
    den[...] = den_in[...]
    cols = den.shape[1]
    side = pl.multiple_of((1 - lax.axis_index("col")) * (cols - 128), 128)
    den[:, pl.ds(side, 128)] += edge[...]
    object_peak = jnp.max(den[...])
    last = mine_low.shape[0] - 1
    for out, ahead, behind, mine, theirs in (
        (low, ahead_low, behind_low, mine_low, theirs_low),
        (high, ahead_high, behind_high, mine_high, theirs_high),
    ):
        for n in range(ahead.shape[0]):
            out[16 * n : 16 * n + 16] = (mine[last, n] + theirs[last, n]) + (ahead[n] + behind[n])
    high[16 * ahead_high.shape[0] :] = jnp.full((8, 256), object_peak, jnp.float32)


def close(ahead, behind, mine, theirs, den, edge):
    return pl.pallas_call(
        close_kernel,
        out_shape=(f32(16 * mine[0].shape[1], 256), f32(16 * mine[1].shape[1] + 8, 256)),
        in_specs=[VMEM] * 10,
        out_specs=(VMEM, VMEM),
        scratch_shapes=[pltpu.VMEM(den.shape, jnp.float32)],
        compiler_params=params(2),
        name="close_sum",
    )(*ahead, *behind, *mine, *theirs, den, edge)


def pack_kernel(edge, *refs):
    parts, out = refs[:-1], refs[-1]
    at = 0
    for part in parts:
        out[at : at + part.shape[0]] = part[...]
        at += part.shape[0]
    for part in range(2):
        out[at:, 128 * part : 128 * part + 128] = edge[part]


def pack(edge, parts):
    size = sum(x.shape[0] for x in parts) + edge.shape[1]
    return pl.pallas_call(
        pack_kernel,
        out_shape=f32(size, 256),
        in_specs=[VMEM] * (1 + len(parts)),
        out_specs=VMEM,
        compiler_params=params(4),
        name="pack",
    )(edge, *parts)


def finish_kernel(probe, block, inner, den, den_edge, packed, packed_last, *refs):
    hops = len(HOPS)
    parts, refs = refs[: 2 * hops], refs[2 * hops :]
    new_block_at, new_probe_at, new_probe, new_block, whole_den, scales, sems = refs
    cut, rest = parts[0].shape[0], parts[1].shape[0]
    size = cut + rest
    lows, highs = list(parts[0::2]), list(parts[1::2])
    for n in range(hops - 1):
        lows.append(packed.at[size * n : size * n + cut])
        highs.append(packed.at[size * n + cut : size * n + size])
    lows.append(packed_last.at[0:cut])
    highs.append(packed_last.at[cut:size])
    edge = packed.at[size * (hops - 1) :]
    modes = probe.shape[0]
    core = lax.axis_index("col")
    place = ring_place(lax.axis_index("row"))
    cols = block.shape[2]
    peak = jnp.zeros((8, 256), jnp.float32)
    object_peak = jnp.zeros((8, 256), jnp.float32)
    for low, high in zip(lows, highs):
        peak = jnp.maximum(peak, jnp.maximum(low[0:8], low[8:16]))
        object_peak = jnp.maximum(object_peak, high[rest - 8 : rest])
    peak = jnp.max(peak)
    object_peak = jnp.max(object_peak)
    starts = []
    for n, low in enumerate(lows):
        half = core if n < hops else 1 - core
        starts.append(pl.multiple_of(128 * half + 16 * ((place + HOPS[n % hops]) & 7), 16))
        scales[n] = 1.0 / ((1.0 - REGULAR) * low[0:16] + REGULAR * peak)
    outs = ()
    for m in range(modes):
        for part in range(2):
            at = 16 * (1 + 2 * m + part)
            for n in range(2 * hops):
                value = lows[n][at : at + 16] if at < cut else highs[n][at - cut : at - cut + 16]
                rows = pl.ds(starts[n], 16)
                new_probe[m, part, rows, :] = probe[m, part, rows, :] + value * scales[n]
        outs += begin((pltpu.make_async_copy(new_probe.at[m], new_probe_at.at[m], sems.at[m]),))
    side = pl.multiple_of((1 - core) * (cols - 128), 128)
    new_block[...] = inner[...]
    for part in range(2):
        new_block[part, :, pl.ds(side, 128)] += edge[:, 128 * part : 128 * part + 128]
    whole_den[...] = den[...]
    whole_den[:, pl.ds(side, 128)] += den_edge[...]
    scale = 1.0 / ((1.0 - REGULAR) * whole_den[...] + REGULAR * object_peak)
    for part in range(2):
        new_block[part] = block[part] + new_block[part] * scale
    outs += begin((pltpu.make_async_copy(new_block, new_block_at, sems.at[modes]),))
    end(outs)


def finish(probe, block, inner, den, den_edge, packed, packed_last, parts):
    modes = probe.shape[0]
    return pl.pallas_call(
        finish_kernel,
        out_shape=(f32(*block.shape), f32(*probe.shape)),
        in_specs=[VMEM] * (7 + len(parts)),
        out_specs=(ANY, ANY),
        scratch_shapes=[pltpu.VMEM(x.shape, jnp.float32) for x in (probe, block, den)]
        + [
            pltpu.VMEM((2 * len(HOPS), 16, 256), jnp.float32),
            pltpu.SemaphoreType.DMA((modes + 1,)),
        ],
        compiler_params=params(12),
        name="finish",
    )(probe, block, inner, den, den_edge, packed, packed_last, *parts)


def shards(object_field, probe, measured, offsets):
    rows, cols = object_field.shape[1], object_field.shape[2]
    count = lax.axis_size("row")
    one, two = transform_blocks(probe.shape[-1])
    one, two = jnp.asarray(one), jnp.asarray(two)

    twins = [(i, i ^ 1) for i in range(count)]
    cores = [(0, 1), (1, 0)]
    others = [(i + 1 if i % 2 else i - 1, i) for i in range(1, count - 1)]
    outward = [(i, i + 2) for i in range(1, count - 2, 2)] + [(i, i - 2) for i in range(2, count, 2)]
    inward = [(b, a) for a, b in outward]
    forward = [
        (block + RING_ORDER[i], block + RING_ORDER[(i + 1) % RING])
        for block in range(0, count, RING)
        for i in range(RING)
    ]
    reverse = [(b, a) for a, b in forward]

    def across(x):
        return lax.ppermute(x, "col", cores)

    def send(x, pairs):
        return lax.ppermute(x, "row", pairs)

    def after(x, y):
        return lax.optimization_barrier((x, y))[0]

    twin = send(offsets, twins)
    beyond = send(offsets, others)
    pattern = send(measured, twins)
    other = across(after(object_field, twin))

    to_beyond, to_twin, own_rows = cut_slices(
        ("beyond", "here", "twin"), offsets, twin, beyond, object_field, other
    )
    far_rows = send(to_beyond, outward)
    mid_rows = send(to_twin, twins)
    power = probe_power(after(probe, own_rows))
    object_den, den_edge = weights(count, offsets, twin, beyond, power, rows, cols)
    den_edge = across(den_edge)

    mine_low, his_low, window, rest, strength, update = position(
        twin, far_rows, after(mid_rows, den_edge), own_rows, probe, pattern[0], one, two
    )
    theirs_low = across(his_low)
    mine_high, his_high, fold_far, fold_mid, fold_own = position_rest(
        twin, window, rest, strength, update, probe, one, two, power
    )
    theirs_high = across(his_high)
    mid_got = send(fold_mid, twins)
    far_got = send(fold_far, inward)

    start_ahead = add_leg(None, mine_low, theirs_low, 0)
    start_behind = add_leg(None, mine_low, theirs_low, 2)
    theirs_high = after(theirs_high, start_behind)
    mine, theirs = (mine_low, mine_high), (theirs_low, theirs_high)

    def legs(part, came, spots, pairs):
        for spot in spots:
            came = send(add_leg(came, mine[part], theirs[part], spot), pairs)
        return came

    ahead = [legs(0, send(start_ahead, forward), (1, 3, 5), forward), legs(1, None, (1, 3, 5), forward)]
    behind = [legs(0, send(start_behind, reverse), (4, 6), reverse), legs(1, None, (0, 2, 4, 6), reverse)]
    message = close(ahead, behind, mine, theirs, object_den, den_edge)
    if count > RING:
        blocks = [[b * RING + i for b in range(count // RING)] for i in range(RING)]
        low = lax.psum(message[0], "row", axis_index_groups=blocks)
        high = lax.psum(message[1][:-8], "row", axis_index_groups=blocks)
        top = lax.pmax(message[1][-8:], "row", axis_index_groups=blocks)
        message = (low, jnp.concatenate([high, top], axis=0))

    parts = list(message)
    ahead = [send(x, forward) for x in message]
    behind = [send(x, reverse) for x in message]
    parts += ahead + behind
    ahead[0], mid_got, far_got = lax.optimization_barrier((ahead[0], mid_got, far_got))
    inner, edge = fold(offsets, twin, beyond, fold_own, mid_got, far_got, rows, cols)
    for hop in range(2):
        ahead = [send(x, forward) for x in ahead]
        behind = [send(x, reverse) for x in behind]
        parts += ahead + behind
    last = [send(ahead[0], forward), send(behind[1], reverse)]
    packed = across(pack(edge, parts))
    packed_last = across(jnp.concatenate(last, axis=0))
    return finish(probe, object_field, inner, object_den, den_edge, packed, packed_last, parts + last)


def solution(mesh):
    placed = (
        P(None, ("groups", "row"), "col"),
        P("groups", None, None, None),
        P(("groups", "row", "col"), None, None),
        P(("groups", "row", "col"), None),
    )
    return jax.shard_map(
        shards,
        mesh=mesh,
        in_specs=placed,
        out_specs=(P(None, ("groups", "row"), "col"), P("groups", None, None, None)),
        check_vma=False,
    )
```

```python
import functools
import math

import jax
import jax.numpy as jnp
import ml_dtypes
import numpy as np
from jax import lax
from jax.experimental import pallas as pl
from jax.experimental.pallas import tpu as pltpu
from jax.sharding import PartitionSpec as P

REGULAR = 0.25
AMP_FLOOR = 2.0
RING = 8
RING_ORDER = (0, 1, 3, 5, 7, 6, 4, 2)
HOPS = (0, -1, 1, -2, 2, -3, 3, 4)

SMEM = pl.BlockSpec(memory_space=pltpu.SMEM)
VMEM = pl.BlockSpec(memory_space=pltpu.VMEM)
ANY = pl.BlockSpec(memory_space=pl.ANY)
HBM = pl.BlockSpec(memory_space=pltpu.HBM)


def transform_blocks(length):
    indices = np.arange(length, dtype=np.int32)
    phases = indices[:, None] * indices[None, :] % length
    angles = phases.astype(np.float32) * np.float32(2.0 * math.pi / length)
    factor = np.float32(1.0 / math.sqrt(length))
    cos = (np.cos(angles) * factor).astype(ml_dtypes.bfloat16)
    sin = (-np.sin(angles) * factor).astype(ml_dtypes.bfloat16)
    one = np.block([[cos, -sin], [sin, cos]])
    return one, np.ascontiguousarray(one.T)


def ring_place(r):
    r = lax.rem(r, RING)
    return jnp.where(r == 0, 0, jnp.where(lax.rem(r, 2) == 1, (r + 1) // 2, RING - r // 2))


def params(mib):
    return pltpu.CompilerParams(vmem_limit_bytes=mib * 1024 * 1024)


def f32(*shape):
    return jax.ShapeDtypeStruct(shape, jnp.float32)


def begin(copies):
    for copy in copies:
        copy.start()
    return copies


def end(copies):
    for copy in copies:
        copy.wait()


def slices_kernel(offsets_at, *refs):
    offsets_in, (block, other, _), outs, (ext, cuts, offsets, sems) = refs[:3], refs[3:6], refs[6:-4], refs[-4:]
    core = lax.axis_index("col")
    cols = block.shape[2]
    end_of = cols + 128
    source = pl.multiple_of(core * (cols - 128), 128)
    target = pl.multiple_of((1 - core) * end_of, 128)
    blank = pl.multiple_of(core * end_of, 128)
    copies = begin(
        (
            pltpu.make_async_copy(block, ext.at[:, :, 128:end_of], sems.at[0]),
            pltpu.make_async_copy(
                other.at[:, :, pl.ds(source, 128)], ext.at[:, :, pl.ds(target, 128)], sems.at[1]
            ),
        )
        + tuple(
            pltpu.make_async_copy(spot, offsets.at[n], sems.at[4 + n]) for n, spot in enumerate(offsets_in)
        )
    )
    ext[:, :, pl.ds(blank, 128)] = jnp.zeros((2, block.shape[1], 128), jnp.float32)
    end(copies)
    columns = {"here": offsets[0, 0, 1], "twin": offsets[1, 0, 1], "beyond": offsets[2, 0, 1]}
    copies = ()
    for number, (which, out) in enumerate(zip(offsets_at, outs)):
        start = columns[which]
        base = pl.multiple_of(start // 128 * 128, 128)
        for part in range(2):
            wide = ext[part, :, pl.ds(base, 384)]
            wide = pltpu.roll(wide, (384 - start % 128) % 384, 1)
            cuts[number, part] = wide[:, 0:256]
        copies += begin((pltpu.make_async_copy(cuts.at[number], out, sems.at[2 + number]),))
    end(copies)


def cut_slices(offsets_at, here, twin, beyond, block, other, ordered):
    rows, cols = block.shape[1], block.shape[2]
    count = len(offsets_at)
    return pl.pallas_call(
        functools.partial(slices_kernel, offsets_at),
        out_shape=(f32(2, rows, 256),) * count,
        in_specs=[ANY] * 3 + [HBM] + [ANY] * 2,
        out_specs=(ANY,) * count,
        scratch_shapes=[
            pltpu.VMEM((2, rows, cols + 256), jnp.float32),
            pltpu.VMEM((count, 2, rows, 256), jnp.float32),
            pltpu.SMEM((3, 1, 2), jnp.int32),
            pltpu.SemaphoreType.DMA((7,)),
        ],
        compiler_params=params(6),
        name="cut_slices",
    )(here, twin, beyond, block, other, ordered)


def power_kernel(probe, out, held, sems):
    modes = probe.shape[0]
    copies = begin([pltpu.make_async_copy(probe.at[m], held.at[m], sems.at[m]) for m in range(modes)])
    for m in range(modes):
        copies[m].wait()
        power = held[m, 0] * held[m, 0] + held[m, 1] * held[m, 1]
        out[...] = power if m == 0 else out[...] + power


def probe_power(probe):
    return pl.pallas_call(
        power_kernel,
        out_shape=f32(*probe.shape[2:]),
        in_specs=[ANY],
        out_specs=VMEM,
        scratch_shapes=[pltpu.VMEM(probe.shape, jnp.float32), pltpu.SemaphoreType.DMA((probe.shape[0],))],
        compiler_params=params(8),
        name="probe_power",
    )(probe)


def weights_kernel(count, here, twin, beyond, power, inner, edge, frame, grid):
    r = lax.axis_index("row")
    odd = lax.rem(r, 2)
    present = jnp.logical_and(r > 0, r < count - 1).astype(jnp.float32)
    tall = jnp.concatenate([power[...], jnp.zeros((128, 256), jnp.float32)], axis=0)
    grid[...] = jnp.zeros(grid.shape, jnp.float32)
    lowers = (128, 256 * odd, 256 * (1 - odd))
    for number, spot in enumerate((here, twin, beyond)):
        row, col = spot[0, 0], spot[0, 1]
        frame[...] = pltpu.roll(tall, row, 0)
        piece = frame[pl.ds(pl.multiple_of(lowers[number], 128), 128), :]
        if number == 2:
            piece = piece * present
        wide = jnp.concatenate([piece, jnp.zeros((128, 128), jnp.float32)], axis=1)
        base = pl.multiple_of(col // 128 * 128, 128)
        grid[:, pl.ds(base, 384)] += pltpu.roll(wide, col % 128, 1)
    size = grid.shape[1]
    inner[...] = grid[:, 128 : size - 128]
    edge[...] = jnp.where(lax.axis_index("col") == 0, grid[:, size - 128 :], grid[:, 0:128])


def weights(count, here, twin, beyond, power, rows, cols):
    return pl.pallas_call(
        functools.partial(weights_kernel, count),
        out_shape=(f32(rows, cols), f32(rows, 128)),
        in_specs=[SMEM] * 3 + [VMEM],
        out_specs=(VMEM, VMEM),
        scratch_shapes=[
            pltpu.VMEM((384, 256), jnp.float32),
            pltpu.VMEM((rows, cols + 256), jnp.float32),
        ],
        compiler_params=params(6),
        name="object_weights",
    )(here, twin, beyond, power)


def slab_spots():
    place = ring_place(lax.axis_index("row"))
    spots = []
    for slab in range(8):
        ahead = (slab - place) & 7
        spots.append(jnp.where(ahead < 4, 7 - 2 * ahead, 2 * (ahead - 4)))
    return spots


def put(spots, mine, his, image, value):
    first = lax.axis_index("col") == 0
    low, high = value[0:128], value[128:256]
    own, other = jnp.where(first, low, high), jnp.where(first, high, low)
    for slab in range(8):
        mine[spots[slab], image] = own[16 * slab : 16 * slab + 16]
        his[spots[slab], image] = other[16 * slab : 16 * slab + 16]


def backward(far, ratio, p_re, p_im, w_re, w_im, one, two):
    fixed = jnp.concatenate(
        [(far[:, 0:256] * ratio).astype(jnp.bfloat16), (far[:, 256:512] * ratio).astype(jnp.bfloat16)],
        axis=0,
    )
    back = jnp.dot(two[...], fixed, preferred_element_type=jnp.float32).astype(jnp.bfloat16)
    back = jnp.concatenate([back[0:256], back[256:512]], axis=1)
    near = jnp.dot(back, one[...], preferred_element_type=jnp.float32)
    n_re, n_im = near[:, 0:256], near[:, 256:512]
    density = w_re * w_re + w_im * w_im
    return (
        p_re * n_re + p_im * n_im,
        p_re * n_im - p_im * n_re,
        w_re * n_re + w_im * n_im - density * p_re,
        w_re * n_im - w_im * n_re - density * p_im,
    )


def position_kernel(
    twin, far_rows, mid_rows, own_rows, probe, pattern, one, two,
    mine, his, window, rest, strength, update,
    stack, far,
):
    modes = probe.shape[0]
    cut = modes // 2
    odd = lax.rem(lax.axis_index("row"), 2)
    row = twin[0, 0]
    stack[:, pl.ds(pl.multiple_of(256 * (1 - odd), 128), 128), :] = far_rows[...]
    stack[:, 128:256, :] = mid_rows[...]
    stack[:, pl.ds(pl.multiple_of(256 * odd, 128), 128), :] = own_rows[...]
    for part in range(2):
        window[part] = pltpu.roll(stack[part], (384 - row) % 384, 0)[0:256]

    for m in range(modes):
        p_re, p_im = probe[m, 0], probe[m, 1]
        w_re, w_im = window[0], window[1]
        e_re, e_im = p_re * w_re - p_im * w_im, p_re * w_im + p_im * w_re
        field = jnp.concatenate([e_re.astype(jnp.bfloat16), e_im.astype(jnp.bfloat16)], axis=0)
        half = jnp.dot(one[...], field, preferred_element_type=jnp.float32).astype(jnp.bfloat16)
        half = jnp.concatenate([half[0:256], half[256:512]], axis=1)
        out = jnp.dot(half, two[...], preferred_element_type=jnp.float32)
        if m < cut:
            far[m] = out
        else:
            rest[m - cut] = out
        power = out[:, 0:256] * out[:, 0:256] + out[:, 256:512] * out[:, 256:512]
        strength[...] = power if m == 0 else strength[...] + power

    strength[...] = jnp.sqrt(pattern[...]) / jnp.maximum(jnp.sqrt(strength[...]), AMP_FLOOR)

    spots = slab_spots()
    put(spots, mine, his, 0, window[0] * window[0] + window[1] * window[1])
    for m in range(cut):
        u_re, u_im, t_re, t_im = backward(
            far[m], strength[...], probe[m, 0], probe[m, 1], window[0], window[1], one, two
        )
        update[0] = u_re if m == 0 else update[0] + u_re
        update[1] = u_im if m == 0 else update[1] + u_im
        put(spots, mine, his, 1 + 2 * m, t_re)
        put(spots, mine, his, 2 + 2 * m, t_im)


def position(twin, far_rows, mid_rows, own_rows, probe, pattern, one, two):
    modes = probe.shape[0]
    cut = modes // 2
    return pl.pallas_call(
        position_kernel,
        out_shape=(f32(8, 1 + 2 * cut, 16, 256),) * 2
        + (f32(2, 256, 256), f32(modes - cut, 256, 512), f32(256, 256), f32(2, 256, 256)),
        in_specs=[SMEM] + [VMEM] * 7,
        out_specs=(VMEM,) * 6,
        scratch_shapes=[
            pltpu.VMEM((2, 384, 256), jnp.float32),
            pltpu.VMEM((cut, 256, 512), jnp.float32),
        ],
        compiler_params=params(10),
        name="position_terms",
    )(twin, far_rows, mid_rows, own_rows, probe, pattern, one, two)


def position_rest_kernel(
    twin, window, rest, strength, update, probe, one, two, weight,
    mine, his, fold_out, fold_own,
    stack, total,
):
    modes = probe.shape[0]
    count = rest.shape[0]
    odd = lax.rem(lax.axis_index("row"), 2)
    spots = slab_spots()
    for part in range(2):
        total[part] = update[part] - weight[...] * window[part]
    for n in range(count):
        m = modes - count + n
        u_re, u_im, t_re, t_im = backward(
            rest[n], strength[...], probe[m, 0], probe[m, 1], window[0], window[1], one, two
        )
        total[0] = total[0] + u_re
        total[1] = total[1] + u_im
        put(spots, mine, his, 2 * n, t_re)
        put(spots, mine, his, 2 * n + 1, t_im)
    for part in range(2):
        tall = jnp.concatenate([total[part], jnp.zeros((128, 256), jnp.float32)], axis=0)
        stack[part] = pltpu.roll(tall, twin[0, 0], 0)
    fold_out[0] = stack[:, 128:256, :]
    fold_out[1] = stack[:, pl.ds(pl.multiple_of(256 * (1 - odd), 128), 128), :]
    fold_own[...] = stack[:, pl.ds(pl.multiple_of(256 * odd, 128), 128), :]


def position_rest(twin, window, rest, strength, update, probe, one, two, weight):
    images = 2 * rest.shape[0]
    return pl.pallas_call(
        position_rest_kernel,
        out_shape=(f32(8, images, 16, 256),) * 2 + (f32(2, 2, 128, 256), f32(2, 128, 256)),
        in_specs=[SMEM] + [VMEM] * 8,
        out_specs=(VMEM,) * 4,
        scratch_shapes=[
            pltpu.VMEM((2, 384, 256), jnp.float32),
            pltpu.VMEM((2, 256, 256), jnp.float32),
        ],
        compiler_params=params(8),
        name="position_rest",
    )(twin, window, rest, strength, update, probe, one, two, weight)


def pair_kernel(here, there, mid, far):
    for piece, out in enumerate((mid, far)):
        out[0] = here[piece]
        out[1] = there[piece]


def pair(here, there):
    return pl.pallas_call(
        pair_kernel,
        out_shape=(f32(*here.shape), f32(*here.shape)),
        in_specs=[VMEM] * 2,
        out_specs=(VMEM, VMEM),
        compiler_params=params(2),
        name="pair_fold",
    )(here, there)


def merge_kernel(mid, far, out):
    out[0] = mid[1]
    out[1] = far[1]


def merge(mid, far):
    return pl.pallas_call(
        merge_kernel,
        out_shape=f32(*mid.shape),
        in_specs=[VMEM] * 2,
        out_specs=VMEM,
        compiler_params=params(2),
        name="merge_fold",
    )(mid, far)


def fold_kernel(here, twin, beyond, near, mid, far, back, inner, edge, grid):
    first = lax.axis_index("col") == 0
    grid[...] = jnp.zeros(grid.shape, jnp.float32)
    for col, came, number in ((twin[0, 1], near, None), (here[0, 1], mid, 0), (beyond[0, 1], far, 1)):
        base = pl.multiple_of(col // 128 * 128, 128)
        for part in range(2):
            piece = came[part] if number is None else jnp.where(first, back[number, part], came[0, part])
            wide = jnp.concatenate([piece, jnp.zeros((128, 128), jnp.float32)], axis=1)
            grid[part, :, pl.ds(base, 384)] += pltpu.roll(wide, col % 128, 1)
    size = grid.shape[2]
    inner[...] = grid[:, :, 128 : size - 128]
    edge[...] = jnp.where(first, grid[:, :, size - 128 :], grid[:, :, 0:128])


def fold(here, twin, beyond, near, pieces, rows, cols):
    return pl.pallas_call(
        fold_kernel,
        out_shape=(f32(2, rows, cols), f32(2, rows, 128)),
        in_specs=[SMEM] * 3 + [VMEM] * 4,
        out_specs=(VMEM, VMEM),
        scratch_shapes=[pltpu.VMEM((2, rows, cols + 256), jnp.float32)],
        compiler_params=params(6),
        name="fold_object",
    )(here, twin, beyond, near, *pieces)


def leg_kernel(spot, mine, theirs, *refs):
    came, out = refs[:-1], refs[-1]
    total = mine[spot] + theirs[spot]
    out[...] = total + came[0][...] if came else total


def add_leg(came, mine, theirs, spot):
    came = () if came is None else (came,)
    return pl.pallas_call(
        functools.partial(leg_kernel, spot),
        out_shape=f32(*mine.shape[1:]),
        in_specs=[VMEM] * (2 + len(came)),
        out_specs=VMEM,
        compiler_params=params(2),
        name="add_leg",
    )(mine, theirs, *came)


def close_kernel(
    ahead_low, ahead_high, behind_low, behind_high, mine_low, mine_high, theirs_low, theirs_high,
    den_in, edge, low, high, den,
):
    den[...] = den_in[...]
    cols = den.shape[1]
    side = pl.multiple_of((1 - lax.axis_index("col")) * (cols - 128), 128)
    den[:, pl.ds(side, 128)] += edge[...]
    object_peak = jnp.max(den[...])
    last = mine_low.shape[0] - 1
    for out, ahead, behind, mine, theirs in (
        (low, ahead_low, behind_low, mine_low, theirs_low),
        (high, ahead_high, behind_high, mine_high, theirs_high),
    ):
        for n in range(ahead.shape[0]):
            out[16 * n : 16 * n + 16] = (mine[last, n] + theirs[last, n]) + (ahead[n] + behind[n])
    high[16 * ahead_high.shape[0] :] = jnp.full((8, 256), object_peak, jnp.float32)


def close(ahead, behind, mine, theirs, den, edge):
    return pl.pallas_call(
        close_kernel,
        out_shape=(f32(16 * mine[0].shape[1], 256), f32(16 * mine[1].shape[1] + 8, 256)),
        in_specs=[VMEM] * 10,
        out_specs=(VMEM, VMEM),
        scratch_shapes=[pltpu.VMEM(den.shape, jnp.float32)],
        compiler_params=params(2),
        name="close_sum",
    )(*ahead, *behind, *mine, *theirs, den, edge)


def pack_kernel(edge, *refs):
    parts, out = refs[:-1], refs[-1]
    at = 0
    for part in parts:
        out[at : at + part.shape[0]] = part[...]
        at += part.shape[0]
    for part in range(2):
        out[at:, 128 * part : 128 * part + 128] = edge[part]


def pack(edge, parts):
    size = sum(x.shape[0] for x in parts) + edge.shape[1]
    return pl.pallas_call(
        pack_kernel,
        out_shape=f32(size, 256),
        in_specs=[VMEM] * (1 + len(parts)),
        out_specs=VMEM,
        compiler_params=params(4),
        name="pack",
    )(edge, *parts)


def finish_kernel(probe, block, inner, den, den_edge, packed, packed_last, *refs):
    hops = len(HOPS)
    parts, refs = refs[: 2 * hops], refs[2 * hops :]
    new_block_at, new_probe_at, new_probe, new_block, whole_den, scales, sems = refs
    cut, rest = parts[0].shape[0], parts[1].shape[0]
    size = cut + rest
    lows, highs = list(parts[0::2]), list(parts[1::2])
    for n in range(hops - 1):
        lows.append(packed.at[size * n : size * n + cut])
        highs.append(packed.at[size * n + cut : size * n + size])
    lows.append(packed_last.at[0:cut])
    highs.append(packed_last.at[cut:size])
    edge = packed.at[size * (hops - 1) :]
    modes = probe.shape[0]
    core = lax.axis_index("col")
    place = ring_place(lax.axis_index("row"))
    cols = block.shape[2]
    peak = jnp.zeros((8, 256), jnp.float32)
    object_peak = jnp.zeros((8, 256), jnp.float32)
    for low, high in zip(lows, highs):
        peak = jnp.maximum(peak, jnp.maximum(low[0:8], low[8:16]))
        object_peak = jnp.maximum(object_peak, high[rest - 8 : rest])
    peak = jnp.max(peak)
    object_peak = jnp.max(object_peak)
    starts = []
    for n, low in enumerate(lows):
        half = core if n < hops else 1 - core
        starts.append(pl.multiple_of(128 * half + 16 * ((place + HOPS[n % hops]) & 7), 16))
        scales[n] = 1.0 / ((1.0 - REGULAR) * low[0:16] + REGULAR * peak)
    outs = ()
    for m in range(modes):
        for part in range(2):
            at = 16 * (1 + 2 * m + part)
            for n in range(2 * hops):
                value = lows[n][at : at + 16] if at < cut else highs[n][at - cut : at - cut + 16]
                rows = pl.ds(starts[n], 16)
                new_probe[m, part, rows, :] = probe[m, part, rows, :] + value * scales[n]
        outs += begin((pltpu.make_async_copy(new_probe.at[m], new_probe_at.at[m], sems.at[m]),))
    side = pl.multiple_of((1 - core) * (cols - 128), 128)
    new_block[...] = inner[...]
    for part in range(2):
        new_block[part, :, pl.ds(side, 128)] += edge[:, 128 * part : 128 * part + 128]
    whole_den[...] = den[...]
    whole_den[:, pl.ds(side, 128)] += den_edge[...]
    scale = 1.0 / ((1.0 - REGULAR) * whole_den[...] + REGULAR * object_peak)
    for part in range(2):
        new_block[part] = block[part] + new_block[part] * scale
    outs += begin((pltpu.make_async_copy(new_block, new_block_at, sems.at[modes]),))
    end(outs)


def finish(probe, block, inner, den, den_edge, packed, packed_last, parts):
    modes = probe.shape[0]
    return pl.pallas_call(
        finish_kernel,
        out_shape=(f32(*block.shape), f32(*probe.shape)),
        in_specs=[VMEM] * (7 + len(parts)),
        out_specs=(ANY, ANY),
        scratch_shapes=[pltpu.VMEM(x.shape, jnp.float32) for x in (probe, block, den)]
        + [
            pltpu.VMEM((2 * len(HOPS), 16, 256), jnp.float32),
            pltpu.SemaphoreType.DMA((modes + 1,)),
        ],
        compiler_params=params(12),
        name="finish",
    )(probe, block, inner, den, den_edge, packed, packed_last, *parts)


def shards(object_field, probe, measured, offsets):
    rows, cols = object_field.shape[1], object_field.shape[2]
    count = lax.axis_size("row")
    one, two = transform_blocks(probe.shape[-1])
    one, two = jnp.asarray(one), jnp.asarray(two)

    twins = [(i, i ^ 1) for i in range(count)]
    cores = [(0, 1), (1, 0)]
    others = [(i + 1 if i % 2 else i - 1, i) for i in range(1, count - 1)]
    outward = [(i, i + 2) for i in range(1, count - 2, 2)] + [(i, i - 2) for i in range(2, count, 2)]
    inward = [(b, a) for a, b in outward]
    forward = [
        (block + RING_ORDER[i], block + RING_ORDER[(i + 1) % RING])
        for block in range(0, count, RING)
        for i in range(RING)
    ]
    reverse = [(b, a) for a, b in forward]

    def across(x):
        return lax.ppermute(x, "col", cores)

    def send(x, pairs):
        return lax.ppermute(x, "row", pairs)

    def after(x, y):
        return lax.optimization_barrier((x, y))[0]

    other = across(object_field)
    twin = send(offsets, twins)
    beyond = send(offsets, others)
    pattern = send(measured, twins)

    (to_twin,) = cut_slices(("here",), offsets, offsets, offsets, object_field, other, offsets)
    mid_rows = send(to_twin, twins)
    to_beyond, own_rows = cut_slices(
        ("beyond", "twin"), offsets, twin, beyond, object_field, other, to_twin
    )
    far_rows = send(to_beyond, outward)
    power = probe_power(after(probe, own_rows))
    object_den, den_edge = weights(count, offsets, twin, beyond, power, rows, cols)
    den_edge = across(den_edge)

    mine_low, his_low, window, rest, strength, update = position(
        twin, far_rows, after(mid_rows, den_edge), own_rows, probe, pattern[0], one, two
    )
    theirs_low = across(his_low)
    mine_high, his_high, fold_out, fold_own = position_rest(
        twin, window, rest, strength, update, probe, one, two, power
    )
    theirs_high = across(his_high)
    mid_both, far_both = pair(fold_out, lax.ppermute(fold_out, "col", [(0, 1)]))
    mid_got = lax.ppermute(mid_both, ("row", "col"), [(2 * a + 1, 2 * b + 1) for a, b in twins])
    far_got = lax.ppermute(far_both, ("row", "col"), [(2 * a + 1, 2 * b + 1) for a, b in inward])

    start_ahead = add_leg(None, mine_low, theirs_low, 0)
    start_behind = add_leg(None, mine_low, theirs_low, 2)
    theirs_high = after(theirs_high, start_behind)
    mine, theirs = (mine_low, mine_high), (theirs_low, theirs_high)

    def legs(part, came, spots, pairs):
        for spot in spots:
            came = send(add_leg(came, mine[part], theirs[part], spot), pairs)
        return came

    ahead = [legs(0, send(start_ahead, forward), (1, 3, 5), forward), legs(1, None, (1, 3, 5), forward)]
    behind = [legs(0, send(start_behind, reverse), (4, 6), reverse), legs(1, None, (0, 2, 4, 6), reverse)]
    message = close(ahead, behind, mine, theirs, object_den, den_edge)
    if count > RING:
        blocks = [[b * RING + i for b in range(count // RING)] for i in range(RING)]
        low = lax.psum(message[0], "row", axis_index_groups=blocks)
        high = lax.psum(message[1][:-8], "row", axis_index_groups=blocks)
        top = lax.pmax(message[1][-8:], "row", axis_index_groups=blocks)
        message = (low, jnp.concatenate([high, top], axis=0))

    low, high, mid_got, far_got = lax.optimization_barrier((*message, mid_got, far_got))
    message = (low, high)
    parts = list(message)
    ahead = [send(x, forward) for x in message]
    behind = [send(x, reverse) for x in message]
    parts += ahead + behind
    pieces = [mid_got, far_got, lax.ppermute(merge(mid_got, far_got), "col", [(1, 0)])]
    inner, edge = fold(offsets, twin, beyond, fold_own, pieces, rows, cols)
    for hop in range(2):
        ahead = [send(x, forward) for x in ahead]
        behind = [send(x, reverse) for x in behind]
        parts += ahead + behind
    last = [send(ahead[0], forward), send(behind[1], reverse)]
    packed = across(pack(edge, parts))
    packed_last = across(jnp.concatenate(last, axis=0))
    return finish(probe, object_field, inner, object_den, den_edge, packed, packed_last, parts + last)


def solution(mesh):
    placed = (
        P(None, ("groups", "row"), "col"),
        P("groups", None, None, None),
        P(("groups", "row", "col"), None, None),
        P(("groups", "row", "col"), None),
    )
    return jax.shard_map(
        shards,
        mesh=mesh,
        in_specs=placed,
        out_specs=(P(None, ("groups", "row"), "col"), P("groups", None, None, None)),
        check_vma=False,
    )
```

```python
import functools
import math

import jax
import jax.numpy as jnp
import ml_dtypes
import numpy as np
from jax import lax
from jax.experimental import pallas as pl
from jax.experimental.pallas import tpu as pltpu
from jax.sharding import PartitionSpec as P

REGULAR = 0.25
AMP_FLOOR = 2.0
RING = 8
RING_ORDER = (0, 1, 3, 5, 7, 6, 4, 2)
HOPS = (0, -1, 1, -2, 2, -3, 3, 4)

SMEM = pl.BlockSpec(memory_space=pltpu.SMEM)
VMEM = pl.BlockSpec(memory_space=pltpu.VMEM)
ANY = pl.BlockSpec(memory_space=pl.ANY)
HBM = pl.BlockSpec(memory_space=pltpu.HBM)


def transform_blocks(length):
    indices = np.arange(length, dtype=np.int32)
    phases = indices[:, None] * indices[None, :] % length
    angles = phases.astype(np.float32) * np.float32(2.0 * math.pi / length)
    factor = np.float32(1.0 / math.sqrt(length))
    cos = (np.cos(angles) * factor).astype(ml_dtypes.bfloat16)
    sin = (-np.sin(angles) * factor).astype(ml_dtypes.bfloat16)
    one = np.block([[cos, -sin], [sin, cos]])
    return one, np.ascontiguousarray(one.T)


def ring_place(r):
    r = lax.rem(r, RING)
    return jnp.where(r == 0, 0, jnp.where(lax.rem(r, 2) == 1, (r + 1) // 2, RING - r // 2))


def params(mib):
    return pltpu.CompilerParams(vmem_limit_bytes=mib * 1024 * 1024)


def f32(*shape):
    return jax.ShapeDtypeStruct(shape, jnp.float32)


def begin(copies):
    for copy in copies:
        copy.start()
    return copies


def end(copies):
    for copy in copies:
        copy.wait()


def slices_kernel(offsets_at, *refs):
    offsets_in, (block, other), outs, (ext, cuts, offsets, sems) = refs[:3], refs[3:5], refs[5:-4], refs[-4:]
    core = lax.axis_index("col")
    cols = block.shape[2]
    end_of = cols + 128
    source = pl.multiple_of(core * (cols - 128), 128)
    target = pl.multiple_of((1 - core) * end_of, 128)
    blank = pl.multiple_of(core * end_of, 128)
    copies = begin(
        (
            pltpu.make_async_copy(block, ext.at[:, :, 128:end_of], sems.at[0]),
            pltpu.make_async_copy(
                other.at[:, :, pl.ds(source, 128)], ext.at[:, :, pl.ds(target, 128)], sems.at[1]
            ),
        )
        + tuple(
            pltpu.make_async_copy(spot, offsets.at[n], sems.at[5 + n]) for n, spot in enumerate(offsets_in)
        )
    )
    ext[:, :, pl.ds(blank, 128)] = jnp.zeros((2, block.shape[1], 128), jnp.float32)
    end(copies)
    columns = {"here": offsets[0, 0, 1], "twin": offsets[1, 0, 1], "beyond": offsets[2, 0, 1]}
    copies = ()
    for number, (which, out) in enumerate(zip(offsets_at, outs)):
        start = columns[which]
        base = pl.multiple_of(start // 128 * 128, 128)
        for part in range(2):
            wide = ext[part, :, pl.ds(base, 384)]
            wide = pltpu.roll(wide, (384 - start % 128) % 384, 1)
            cuts[number, part] = wide[:, 0:256]
        copies += begin((pltpu.make_async_copy(cuts.at[number], out, sems.at[2 + number]),))
    end(copies)


def cut_slices(offsets_at, here, twin, beyond, block, other):
    rows, cols = block.shape[1], block.shape[2]
    count = len(offsets_at)
    return pl.pallas_call(
        functools.partial(slices_kernel, offsets_at),
        out_shape=(f32(2, rows, 256),) * count,
        in_specs=[ANY] * 3 + [HBM, ANY],
        out_specs=(ANY,) * count,
        scratch_shapes=[
            pltpu.VMEM((2, rows, cols + 256), jnp.float32),
            pltpu.VMEM((count, 2, rows, 256), jnp.float32),
            pltpu.SMEM((3, 1, 2), jnp.int32),
            pltpu.SemaphoreType.DMA((8,)),
        ],
        compiler_params=params(6),
        name="cut_slices",
    )(here, twin, beyond, block, other)


def power_kernel(probe, out, held, sems):
    modes = probe.shape[0]
    copies = begin([pltpu.make_async_copy(probe.at[m], held.at[m], sems.at[m]) for m in range(modes)])
    for m in range(modes):
        copies[m].wait()
        power = held[m, 0] * held[m, 0] + held[m, 1] * held[m, 1]
        out[...] = power if m == 0 else out[...] + power


def probe_power(probe):
    return pl.pallas_call(
        power_kernel,
        out_shape=f32(*probe.shape[2:]),
        in_specs=[ANY],
        out_specs=VMEM,
        scratch_shapes=[pltpu.VMEM(probe.shape, jnp.float32), pltpu.SemaphoreType.DMA((probe.shape[0],))],
        compiler_params=params(8),
        name="probe_power",
    )(probe)


def weights_kernel(count, here, twin, beyond, power, inner, edge, frame, grid):
    r = lax.axis_index("row")
    odd = lax.rem(r, 2)
    present = jnp.logical_and(r > 0, r < count - 1).astype(jnp.float32)
    tall = jnp.concatenate([power[...], jnp.zeros((128, 256), jnp.float32)], axis=0)
    grid[...] = jnp.zeros(grid.shape, jnp.float32)
    lowers = (128, 256 * odd, 256 * (1 - odd))
    for number, spot in enumerate((here, twin, beyond)):
        row, col = spot[0, 0], spot[0, 1]
        frame[...] = pltpu.roll(tall, row, 0)
        piece = frame[pl.ds(pl.multiple_of(lowers[number], 128), 128), :]
        if number == 2:
            piece = piece * present
        wide = jnp.concatenate([piece, jnp.zeros((128, 128), jnp.float32)], axis=1)
        base = pl.multiple_of(col // 128 * 128, 128)
        grid[:, pl.ds(base, 384)] += pltpu.roll(wide, col % 128, 1)
    size = grid.shape[1]
    inner[...] = grid[:, 128 : size - 128]
    edge[...] = jnp.where(lax.axis_index("col") == 0, grid[:, size - 128 :], grid[:, 0:128])


def weights(count, here, twin, beyond, power, rows, cols):
    return pl.pallas_call(
        functools.partial(weights_kernel, count),
        out_shape=(f32(rows, cols), f32(rows, 128)),
        in_specs=[SMEM] * 3 + [VMEM],
        out_specs=(VMEM, VMEM),
        scratch_shapes=[
            pltpu.VMEM((384, 256), jnp.float32),
            pltpu.VMEM((rows, cols + 256), jnp.float32),
        ],
        compiler_params=params(6),
        name="object_weights",
    )(here, twin, beyond, power)


def slab_spots():
    place = ring_place(lax.axis_index("row"))
    spots = []
    for slab in range(8):
        ahead = (slab - place) & 7
        spots.append(jnp.where(ahead < 4, 7 - 2 * ahead, 2 * (ahead - 4)))
    return spots


def put(spots, mine, his, image, value):
    first = lax.axis_index("col") == 0
    low, high = value[0:128], value[128:256]
    own, other = jnp.where(first, low, high), jnp.where(first, high, low)
    for slab in range(8):
        mine[spots[slab], image] = own[16 * slab : 16 * slab + 16]
        his[spots[slab], image] = other[16 * slab : 16 * slab + 16]


def backward(far, ratio, p_re, p_im, w_re, w_im, one, two):
    fixed = jnp.concatenate(
        [(far[:, 0:256] * ratio).astype(jnp.bfloat16), (far[:, 256:512] * ratio).astype(jnp.bfloat16)],
        axis=0,
    )
    back = jnp.dot(two[...], fixed, preferred_element_type=jnp.float32).astype(jnp.bfloat16)
    back = jnp.concatenate([back[0:256], back[256:512]], axis=1)
    near = jnp.dot(back, one[...], preferred_element_type=jnp.float32)
    n_re, n_im = near[:, 0:256], near[:, 256:512]
    density = w_re * w_re + w_im * w_im
    return (
        p_re * n_re + p_im * n_im,
        p_re * n_im - p_im * n_re,
        w_re * n_re + w_im * n_im - density * p_re,
        w_re * n_im - w_im * n_re - density * p_im,
    )


def position_kernel(
    twin, far_rows, mid_rows, own_rows, probe, pattern, one, two,
    mine, his, window, rest, strength, update,
    stack, far,
):
    modes = probe.shape[0]
    cut = modes // 2
    odd = lax.rem(lax.axis_index("row"), 2)
    row = twin[0, 0]
    stack[:, pl.ds(pl.multiple_of(256 * (1 - odd), 128), 128), :] = far_rows[...]
    stack[:, 128:256, :] = mid_rows[...]
    stack[:, pl.ds(pl.multiple_of(256 * odd, 128), 128), :] = own_rows[...]
    for part in range(2):
        window[part] = pltpu.roll(stack[part], (384 - row) % 384, 0)[0:256]

    for m in range(modes):
        p_re, p_im = probe[m, 0], probe[m, 1]
        w_re, w_im = window[0], window[1]
        e_re, e_im = p_re * w_re - p_im * w_im, p_re * w_im + p_im * w_re
        field = jnp.concatenate([e_re.astype(jnp.bfloat16), e_im.astype(jnp.bfloat16)], axis=0)
        half = jnp.dot(one[...], field, preferred_element_type=jnp.float32).astype(jnp.bfloat16)
        half = jnp.concatenate([half[0:256], half[256:512]], axis=1)
        out = jnp.dot(half, two[...], preferred_element_type=jnp.float32)
        if m < cut:
            far[m] = out
        else:
            rest[m - cut] = out
        power = out[:, 0:256] * out[:, 0:256] + out[:, 256:512] * out[:, 256:512]
        strength[...] = power if m == 0 else strength[...] + power

    strength[...] = jnp.sqrt(pattern[...]) / jnp.maximum(jnp.sqrt(strength[...]), AMP_FLOOR)

    spots = slab_spots()
    put(spots, mine, his, 0, window[0] * window[0] + window[1] * window[1])
    for m in range(cut):
        u_re, u_im, t_re, t_im = backward(
            far[m], strength[...], probe[m, 0], probe[m, 1], window[0], window[1], one, two
        )
        update[0] = u_re if m == 0 else update[0] + u_re
        update[1] = u_im if m == 0 else update[1] + u_im
        put(spots, mine, his, 1 + 2 * m, t_re)
        put(spots, mine, his, 2 + 2 * m, t_im)


def position(twin, far_rows, mid_rows, own_rows, probe, pattern, one, two):
    modes = probe.shape[0]
    cut = modes // 2
    return pl.pallas_call(
        position_kernel,
        out_shape=(f32(8, 1 + 2 * cut, 16, 256),) * 2
        + (f32(2, 256, 256), f32(modes - cut, 256, 512), f32(256, 256), f32(2, 256, 256)),
        in_specs=[SMEM] + [VMEM] * 7,
        out_specs=(VMEM,) * 6,
        scratch_shapes=[
            pltpu.VMEM((2, 384, 256), jnp.float32),
            pltpu.VMEM((cut, 256, 512), jnp.float32),
        ],
        compiler_params=params(10),
        name="position_terms",
    )(twin, far_rows, mid_rows, own_rows, probe, pattern, one, two)


def position_rest_kernel(
    twin, window, rest, strength, update, probe, one, two, weight,
    mine, his, fold_far, fold_mid, fold_own,
    stack, total,
):
    modes = probe.shape[0]
    count = rest.shape[0]
    odd = lax.rem(lax.axis_index("row"), 2)
    spots = slab_spots()
    for part in range(2):
        total[part] = update[part] - weight[...] * window[part]
    for n in range(count):
        m = modes - count + n
        u_re, u_im, t_re, t_im = backward(
            rest[n], strength[...], probe[m, 0], probe[m, 1], window[0], window[1], one, two
        )
        total[0] = total[0] + u_re
        total[1] = total[1] + u_im
        put(spots, mine, his, 2 * n, t_re)
        put(spots, mine, his, 2 * n + 1, t_im)
    for part in range(2):
        tall = jnp.concatenate([total[part], jnp.zeros((128, 256), jnp.float32)], axis=0)
        stack[part] = pltpu.roll(tall, twin[0, 0], 0)
    fold_far[...] = stack[:, pl.ds(pl.multiple_of(256 * (1 - odd), 128), 128), :]
    fold_mid[...] = stack[:, 128:256, :]
    fold_own[...] = stack[:, pl.ds(pl.multiple_of(256 * odd, 128), 128), :]


def position_rest(twin, window, rest, strength, update, probe, one, two, weight):
    images = 2 * rest.shape[0]
    return pl.pallas_call(
        position_rest_kernel,
        out_shape=(f32(8, images, 16, 256),) * 2 + (f32(2, 128, 256),) * 3,
        in_specs=[SMEM] + [VMEM] * 8,
        out_specs=(VMEM,) * 5,
        scratch_shapes=[
            pltpu.VMEM((2, 384, 256), jnp.float32),
            pltpu.VMEM((2, 256, 256), jnp.float32),
        ],
        compiler_params=params(8),
        name="position_rest",
    )(twin, window, rest, strength, update, probe, one, two, weight)


def fold_kernel(here, twin, beyond, near, middle, far, inner, edge, grid):
    grid[...] = jnp.zeros(grid.shape, jnp.float32)
    for col, piece in ((twin[0, 1], near), (here[0, 1], middle), (beyond[0, 1], far)):
        base = pl.multiple_of(col // 128 * 128, 128)
        for part in range(2):
            wide = jnp.concatenate([piece[part], jnp.zeros((128, 128), jnp.float32)], axis=1)
            grid[part, :, pl.ds(base, 384)] += pltpu.roll(wide, col % 128, 1)
    size = grid.shape[2]
    inner[...] = grid[:, :, 128 : size - 128]
    edge[...] = jnp.where(lax.axis_index("col") == 0, grid[:, :, size - 128 :], grid[:, :, 0:128])


def fold(here, twin, beyond, near, middle, far, rows, cols):
    return pl.pallas_call(
        fold_kernel,
        out_shape=(f32(2, rows, cols), f32(2, rows, 128)),
        in_specs=[SMEM] * 3 + [VMEM] * 3,
        out_specs=(VMEM, VMEM),
        scratch_shapes=[pltpu.VMEM((2, rows, cols + 256), jnp.float32)],
        compiler_params=params(8),
        name="fold_object",
    )(here, twin, beyond, near, middle, far)


def leg_kernel(spot, mine, theirs, *refs):
    came, out = refs[:-1], refs[-1]
    total = mine[spot] + theirs[spot]
    out[...] = total + came[0][...] if came else total


def add_leg(came, mine, theirs, spot):
    came = () if came is None else (came,)
    return pl.pallas_call(
        functools.partial(leg_kernel, spot),
        out_shape=f32(*mine.shape[1:]),
        in_specs=[VMEM] * (2 + len(came)),
        out_specs=VMEM,
        compiler_params=params(2),
        name="add_leg",
    )(mine, theirs, *came)


def close_kernel(
    ahead_low, ahead_high, behind_low, behind_high, mine_low, mine_high, theirs_low, theirs_high,
    den_in, edge, low, high, den,
):
    den[...] = den_in[...]
    cols = den.shape[1]
    side = pl.multiple_of((1 - lax.axis_index("col")) * (cols - 128), 128)
    den[:, pl.ds(side, 128)] += edge[...]
    object_peak = jnp.max(den[...])
    last = mine_low.shape[0] - 1
    for out, ahead, behind, mine, theirs in (
        (low, ahead_low, behind_low, mine_low, theirs_low),
        (high, ahead_high, behind_high, mine_high, theirs_high),
    ):
        for n in range(ahead.shape[0]):
            out[16 * n : 16 * n + 16] = (mine[last, n] + theirs[last, n]) + (ahead[n] + behind[n])
    high[16 * ahead_high.shape[0] :] = jnp.full((8, 256), object_peak, jnp.float32)


def close(ahead, behind, mine, theirs, den, edge):
    return pl.pallas_call(
        close_kernel,
        out_shape=(f32(16 * mine[0].shape[1], 256), f32(16 * mine[1].shape[1] + 8, 256)),
        in_specs=[VMEM] * 10,
        out_specs=(VMEM, VMEM),
        scratch_shapes=[pltpu.VMEM(den.shape, jnp.float32)],
        compiler_params=params(2),
        name="close_sum",
    )(*ahead, *behind, *mine, *theirs, den, edge)


def pack_kernel(edge, *refs):
    parts, out = refs[:-1], refs[-1]
    at = 0
    for part in parts:
        out[at : at + part.shape[0]] = part[...]
        at += part.shape[0]
    for part in range(2):
        out[at:, 128 * part : 128 * part + 128] = edge[part]


def pack(edge, parts):
    size = sum(x.shape[0] for x in parts) + edge.shape[1]
    return pl.pallas_call(
        pack_kernel,
        out_shape=f32(size, 256),
        in_specs=[VMEM] * (1 + len(parts)),
        out_specs=VMEM,
        compiler_params=params(4),
        name="pack",
    )(edge, *parts)


def finish_kernel(probe, block, inner, den, den_edge, packed, packed_last, *refs):
    hops = len(HOPS)
    parts, refs = refs[: 2 * hops], refs[2 * hops :]
    new_block_at, new_probe_at, new_probe, new_block, whole_den, scales, sems = refs
    cut, rest = parts[0].shape[0], parts[1].shape[0]
    size = cut + rest
    lows, highs = list(parts[0::2]), list(parts[1::2])
    for n in range(hops - 1):
        lows.append(packed.at[size * n : size * n + cut])
        highs.append(packed.at[size * n + cut : size * n + size])
    lows.append(packed_last.at[0:cut])
    highs.append(packed_last.at[cut:size])
    edge = packed.at[size * (hops - 1) :]
    modes = probe.shape[0]
    core = lax.axis_index("col")
    place = ring_place(lax.axis_index("row"))
    cols = block.shape[2]
    peak = jnp.zeros((8, 256), jnp.float32)
    object_peak = jnp.zeros((8, 256), jnp.float32)
    for low, high in zip(lows, highs):
        peak = jnp.maximum(peak, jnp.maximum(low[0:8], low[8:16]))
        object_peak = jnp.maximum(object_peak, high[rest - 8 : rest])
    peak = jnp.max(peak)
    object_peak = jnp.max(object_peak)
    side = pl.multiple_of((1 - core) * (cols - 128), 128)
    new_block[...] = inner[...]
    for part in range(2):
        new_block[part, :, pl.ds(side, 128)] += edge[:, 128 * part : 128 * part + 128]
    whole_den[...] = den[...]
    whole_den[:, pl.ds(side, 128)] += den_edge[...]
    scale = 1.0 / ((1.0 - REGULAR) * whole_den[...] + REGULAR * object_peak)
    for part in range(2):
        new_block[part] = block[part] + new_block[part] * scale
    outs = begin((pltpu.make_async_copy(new_block, new_block_at, sems.at[modes]),))
    starts = []
    for n, low in enumerate(lows):
        half = core if n < hops else 1 - core
        starts.append(pl.multiple_of(128 * half + 16 * ((place + HOPS[n % hops]) & 7), 16))
        scales[n] = 1.0 / ((1.0 - REGULAR) * low[0:16] + REGULAR * peak)
    for m in range(modes):
        for part in range(2):
            at = 16 * (1 + 2 * m + part)
            for n in range(2 * hops):
                value = lows[n][at : at + 16] if at < cut else highs[n][at - cut : at - cut + 16]
                rows = pl.ds(starts[n], 16)
                new_probe[m, part, rows, :] = probe[m, part, rows, :] + value * scales[n]
        outs += begin((pltpu.make_async_copy(new_probe.at[m], new_probe_at.at[m], sems.at[m]),))
    end(outs)


def finish(probe, block, inner, den, den_edge, packed, packed_last, parts):
    modes = probe.shape[0]
    return pl.pallas_call(
        finish_kernel,
        out_shape=(f32(*block.shape), f32(*probe.shape)),
        in_specs=[VMEM] * (7 + len(parts)),
        out_specs=(ANY, ANY),
        scratch_shapes=[pltpu.VMEM(x.shape, jnp.float32) for x in (probe, block, den)]
        + [
            pltpu.VMEM((2 * len(HOPS), 16, 256), jnp.float32),
            pltpu.SemaphoreType.DMA((modes + 1,)),
        ],
        compiler_params=params(12),
        name="finish",
    )(probe, block, inner, den, den_edge, packed, packed_last, *parts)


def shards(object_field, probe, measured, offsets):
    rows, cols = object_field.shape[1], object_field.shape[2]
    count = lax.axis_size("row")
    one, two = transform_blocks(probe.shape[-1])
    one, two = jnp.asarray(one), jnp.asarray(two)

    twins = [(i, i ^ 1) for i in range(count)]
    cores = [(0, 1), (1, 0)]
    others = [(i + 1 if i % 2 else i - 1, i) for i in range(1, count - 1)]
    outward = [(i, i + 2) for i in range(1, count - 2, 2)] + [(i, i - 2) for i in range(2, count, 2)]
    inward = [(b, a) for a, b in outward]
    forward = [
        (block + RING_ORDER[i], block + RING_ORDER[(i + 1) % RING])
        for block in range(0, count, RING)
        for i in range(RING)
    ]
    reverse = [(b, a) for a, b in forward]

    def across(x):
        return lax.ppermute(x, "col", cores)

    def send(x, pairs):
        return lax.ppermute(x, "row", pairs)

    def after(x, y):
        return lax.optimization_barrier((x, y))[0]

    other = across(object_field)
    twin = send(offsets, twins)
    beyond = send(offsets, others)
    pattern = send(measured, twins)

    to_beyond, to_twin, own_rows = cut_slices(
        ("beyond", "here", "twin"), offsets, twin, beyond, object_field, other
    )
    far_rows = send(to_beyond, outward)
    mid_rows = send(to_twin, twins)
    power = probe_power(after(after(probe, own_rows), pattern))
    object_den, den_edge = weights(count, offsets, twin, beyond, power, rows, cols)
    den_edge = across(den_edge)

    mine_low, his_low, window, rest, strength, update = position(
        twin, far_rows, after(mid_rows, den_edge), own_rows, probe, pattern[0], one, two
    )
    theirs_low = across(his_low)
    mine_high, his_high, fold_far, fold_mid, fold_own = position_rest(
        twin, window, rest, strength, update, probe, one, two, power
    )
    theirs_high = across(his_high)
    mid_got = send(fold_mid, twins)
    far_got = send(fold_far, inward)

    start_ahead = add_leg(None, mine_low, theirs_low, 0)
    start_behind = add_leg(None, mine_low, theirs_low, 2)
    theirs_high = after(theirs_high, start_behind)
    mine, theirs = (mine_low, mine_high), (theirs_low, theirs_high)

    def legs(part, came, spots, pairs):
        for spot in spots:
            came = send(add_leg(came, mine[part], theirs[part], spot), pairs)
        return came

    ahead = [legs(0, send(start_ahead, forward), (1, 3, 5), forward), legs(1, None, (1, 3, 5), forward)]
    behind = [legs(0, send(start_behind, reverse), (4, 6), reverse), legs(1, None, (0, 2, 4, 6), reverse)]
    message = close(ahead, behind, mine, theirs, object_den, den_edge)
    if count > RING:
        blocks = [[b * RING + i for b in range(count // RING)] for i in range(RING)]
        low = lax.psum(message[0], "row", axis_index_groups=blocks)
        high = lax.psum(message[1][:-8], "row", axis_index_groups=blocks)
        top = lax.pmax(message[1][-8:], "row", axis_index_groups=blocks)
        message = (low, jnp.concatenate([high, top], axis=0))

    parts = list(message)
    ahead = [send(x, forward) for x in message]
    behind = [send(x, reverse) for x in message]
    parts += ahead + behind
    ahead[0], mid_got, far_got = lax.optimization_barrier((ahead[0], mid_got, far_got))
    inner, edge = fold(offsets, twin, beyond, fold_own, mid_got, far_got, rows, cols)
    for hop in range(2):
        ahead = [send(x, forward) for x in ahead]
        behind = [send(x, reverse) for x in behind]
        parts += ahead + behind
    last = [send(ahead[0], forward), send(behind[1], reverse)]
    packed = across(pack(edge, parts))
    packed_last = across(jnp.concatenate(last, axis=0))
    return finish(probe, object_field, inner, object_den, den_edge, packed, packed_last, parts + last)


def solution(mesh):
    placed = (
        P(None, ("groups", "row"), "col"),
        P("groups", None, None, None),
        P(("groups", "row", "col"), None, None),
        P(("groups", "row", "col"), None),
    )
    return jax.shard_map(
        shards,
        mesh=mesh,
        in_specs=placed,
        out_specs=(P(None, ("groups", "row"), "col"), P("groups", None, None, None)),
        check_vma=False,
    )
```

```python
import functools
import math

import jax
import jax.numpy as jnp
import ml_dtypes
import numpy as np
from jax import lax
from jax.experimental import pallas as pl
from jax.experimental.pallas import tpu as pltpu
from jax.sharding import PartitionSpec as P

REGULAR = 0.25
AMP_FLOOR = 2.0
RING = 8
RING_ORDER = (0, 1, 3, 5, 7, 6, 4, 2)
HOPS = (0, -1, 1, -2, 2, -3, 3, 4)

SMEM = pl.BlockSpec(memory_space=pltpu.SMEM)
VMEM = pl.BlockSpec(memory_space=pltpu.VMEM)
ANY = pl.BlockSpec(memory_space=pl.ANY)
HBM = pl.BlockSpec(memory_space=pltpu.HBM)


def transform_blocks(length):
    indices = np.arange(length, dtype=np.int32)
    phases = indices[:, None] * indices[None, :] % length
    angles = phases.astype(np.float32) * np.float32(2.0 * math.pi / length)
    factor = np.float32(1.0 / math.sqrt(length))
    cos = (np.cos(angles) * factor).astype(ml_dtypes.bfloat16)
    sin = (-np.sin(angles) * factor).astype(ml_dtypes.bfloat16)
    one = np.block([[cos, -sin], [sin, cos]])
    return one, np.ascontiguousarray(one.T)


def ring_place(r):
    r = lax.rem(r, RING)
    return jnp.where(r == 0, 0, jnp.where(lax.rem(r, 2) == 1, (r + 1) // 2, RING - r // 2))


def params(mib):
    return pltpu.CompilerParams(vmem_limit_bytes=mib * 1024 * 1024)


def f32(*shape):
    return jax.ShapeDtypeStruct(shape, jnp.float32)


def begin(copies):
    for copy in copies:
        copy.start()
    return copies


def end(copies):
    for copy in copies:
        copy.wait()


def slices_kernel(offsets_at, *refs):
    offsets_in, (block, other), outs, (ext, cuts, offsets, sems) = refs[:3], refs[3:5], refs[5:-4], refs[-4:]
    core = lax.axis_index("col")
    cols = block.shape[2]
    end_of = cols + 128
    source = pl.multiple_of(core * (cols - 128), 128)
    target = pl.multiple_of((1 - core) * end_of, 128)
    blank = pl.multiple_of(core * end_of, 128)
    copies = begin(
        (
            pltpu.make_async_copy(block, ext.at[:, :, 128:end_of], sems.at[0]),
            pltpu.make_async_copy(
                other.at[:, :, pl.ds(source, 128)], ext.at[:, :, pl.ds(target, 128)], sems.at[1]
            ),
        )
        + tuple(
            pltpu.make_async_copy(spot, offsets.at[n], sems.at[5 + n]) for n, spot in enumerate(offsets_in)
        )
    )
    ext[:, :, pl.ds(blank, 128)] = jnp.zeros((2, block.shape[1], 128), jnp.float32)
    end(copies)
    columns = {"here": offsets[0, 0, 1], "twin": offsets[1, 0, 1], "beyond": offsets[2, 0, 1]}
    copies = ()
    for number, (which, out) in enumerate(zip(offsets_at, outs)):
        start = columns[which]
        base = pl.multiple_of(start // 128 * 128, 128)
        for part in range(2):
            wide = ext[part, :, pl.ds(base, 384)]
            wide = pltpu.roll(wide, (384 - start % 128) % 384, 1)
            cuts[number, part] = wide[:, 0:256]
        copies += begin((pltpu.make_async_copy(cuts.at[number], out, sems.at[2 + number]),))
    end(copies)


def cut_slices(offsets_at, here, twin, beyond, block, other):
    rows, cols = block.shape[1], block.shape[2]
    count = len(offsets_at)
    return pl.pallas_call(
        functools.partial(slices_kernel, offsets_at),
        out_shape=(f32(2, rows, 256),) * count,
        in_specs=[ANY] * 3 + [HBM, ANY],
        out_specs=(ANY,) * count,
        scratch_shapes=[
            pltpu.VMEM((2, rows, cols + 256), jnp.float32),
            pltpu.VMEM((count, 2, rows, 256), jnp.float32),
            pltpu.SMEM((3, 1, 2), jnp.int32),
            pltpu.SemaphoreType.DMA((8,)),
        ],
        compiler_params=params(6),
        name="cut_slices",
    )(here, twin, beyond, block, other)


def power_kernel(probe, out, held, sems):
    modes = probe.shape[0]
    copies = begin([pltpu.make_async_copy(probe.at[m], held.at[m], sems.at[m]) for m in range(modes)])
    for m in range(modes):
        copies[m].wait()
        power = held[m, 0] * held[m, 0] + held[m, 1] * held[m, 1]
        out[...] = power if m == 0 else out[...] + power


def probe_power(probe):
    return pl.pallas_call(
        power_kernel,
        out_shape=f32(*probe.shape[2:]),
        in_specs=[ANY],
        out_specs=VMEM,
        scratch_shapes=[pltpu.VMEM(probe.shape, jnp.float32), pltpu.SemaphoreType.DMA((probe.shape[0],))],
        compiler_params=params(8),
        name="probe_power",
    )(probe)


def weights_kernel(count, here, twin, beyond, power, inner, edge, frame, grid):
    r = lax.axis_index("row")
    odd = lax.rem(r, 2)
    present = jnp.logical_and(r > 0, r < count - 1).astype(jnp.float32)
    tall = jnp.concatenate([power[...], jnp.zeros((128, 256), jnp.float32)], axis=0)
    grid[...] = jnp.zeros(grid.shape, jnp.float32)
    lowers = (128, 256 * odd, 256 * (1 - odd))
    for number, spot in enumerate((here, twin, beyond)):
        row, col = spot[0, 0], spot[0, 1]
        frame[...] = pltpu.roll(tall, row, 0)
        piece = frame[pl.ds(pl.multiple_of(lowers[number], 128), 128), :]
        if number == 2:
            piece = piece * present
        wide = jnp.concatenate([piece, jnp.zeros((128, 128), jnp.float32)], axis=1)
        base = pl.multiple_of(col // 128 * 128, 128)
        grid[:, pl.ds(base, 384)] += pltpu.roll(wide, col % 128, 1)
    size = grid.shape[1]
    inner[...] = grid[:, 128 : size - 128]
    edge[...] = jnp.where(lax.axis_index("col") == 0, grid[:, size - 128 :], grid[:, 0:128])


def weights(count, here, twin, beyond, power, rows, cols):
    return pl.pallas_call(
        functools.partial(weights_kernel, count),
        out_shape=(f32(rows, cols), f32(rows, 128)),
        in_specs=[SMEM] * 3 + [VMEM],
        out_specs=(VMEM, VMEM),
        scratch_shapes=[
            pltpu.VMEM((384, 256), jnp.float32),
            pltpu.VMEM((rows, cols + 256), jnp.float32),
        ],
        compiler_params=params(6),
        name="object_weights",
    )(here, twin, beyond, power)


def slab_spots():
    place = ring_place(lax.axis_index("row"))
    spots = []
    for slab in range(8):
        ahead = (slab - place) & 7
        spots.append(jnp.where(ahead < 4, 7 - 2 * ahead, 2 * (ahead - 4)))
    return spots


def put(spots, mine, his, image, value):
    first = lax.axis_index("col") == 0
    low, high = value[0:128], value[128:256]
    own, other = jnp.where(first, low, high), jnp.where(first, high, low)
    for slab in range(8):
        mine[spots[slab], image] = own[16 * slab : 16 * slab + 16]
        his[spots[slab], image] = other[16 * slab : 16 * slab + 16]


def backward(far, ratio, p_re, p_im, w_re, w_im, one, two):
    fixed = jnp.concatenate(
        [(far[:, 0:256] * ratio).astype(jnp.bfloat16), (far[:, 256:512] * ratio).astype(jnp.bfloat16)],
        axis=0,
    )
    back = jnp.dot(two[...], fixed, preferred_element_type=jnp.float32).astype(jnp.bfloat16)
    back = jnp.concatenate([back[0:256], back[256:512]], axis=1)
    near = jnp.dot(back, one[...], preferred_element_type=jnp.float32)
    n_re, n_im = near[:, 0:256], near[:, 256:512]
    density = w_re * w_re + w_im * w_im
    return (
        p_re * n_re + p_im * n_im,
        p_re * n_im - p_im * n_re,
        w_re * n_re + w_im * n_im - density * p_re,
        w_re * n_im - w_im * n_re - density * p_im,
    )


def position_kernel(
    twin, far_rows, mid_rows, own_rows, probe, pattern, one, two,
    mine, his, window, rest, strength, update,
    stack, far,
):
    modes = probe.shape[0]
    cut = modes // 2
    odd = lax.rem(lax.axis_index("row"), 2)
    row = twin[0, 0]
    stack[:, pl.ds(pl.multiple_of(256 * (1 - odd), 128), 128), :] = far_rows[...]
    stack[:, 128:256, :] = mid_rows[...]
    stack[:, pl.ds(pl.multiple_of(256 * odd, 128), 128), :] = own_rows[...]
    for part in range(2):
        window[part] = pltpu.roll(stack[part], (384 - row) % 384, 0)[0:256]

    for m in range(modes):
        p_re, p_im = probe[m, 0], probe[m, 1]
        w_re, w_im = window[0], window[1]
        e_re, e_im = p_re * w_re - p_im * w_im, p_re * w_im + p_im * w_re
        field = jnp.concatenate([e_re.astype(jnp.bfloat16), e_im.astype(jnp.bfloat16)], axis=0)
        half = jnp.dot(one[...], field, preferred_element_type=jnp.float32).astype(jnp.bfloat16)
        half = jnp.concatenate([half[0:256], half[256:512]], axis=1)
        out = jnp.dot(half, two[...], preferred_element_type=jnp.float32)
        if m < cut:
            far[m] = out
        else:
            rest[m - cut] = out
        power = out[:, 0:256] * out[:, 0:256] + out[:, 256:512] * out[:, 256:512]
        strength[...] = power if m == 0 else strength[...] + power

    strength[...] = jnp.sqrt(pattern[...]) / jnp.maximum(jnp.sqrt(strength[...]), AMP_FLOOR)

    spots = slab_spots()
    put(spots, mine, his, 0, window[0] * window[0] + window[1] * window[1])
    for m in range(cut):
        u_re, u_im, t_re, t_im = backward(
            far[m], strength[...], probe[m, 0], probe[m, 1], window[0], window[1], one, two
        )
        update[0] = u_re if m == 0 else update[0] + u_re
        update[1] = u_im if m == 0 else update[1] + u_im
        put(spots, mine, his, 1 + 2 * m, t_re)
        put(spots, mine, his, 2 + 2 * m, t_im)


def position(twin, far_rows, mid_rows, own_rows, probe, pattern, one, two):
    modes = probe.shape[0]
    cut = modes // 2
    return pl.pallas_call(
        position_kernel,
        out_shape=(f32(8, 1 + 2 * cut, 16, 256),) * 2
        + (f32(2, 256, 256), f32(modes - cut, 256, 512), f32(256, 256), f32(2, 256, 256)),
        in_specs=[SMEM] + [VMEM] * 7,
        out_specs=(VMEM,) * 6,
        scratch_shapes=[
            pltpu.VMEM((2, 384, 256), jnp.float32),
            pltpu.VMEM((cut, 256, 512), jnp.float32),
        ],
        compiler_params=params(10),
        name="position_terms",
    )(twin, far_rows, mid_rows, own_rows, probe, pattern, one, two)


def position_rest_kernel(
    twin, window, rest, strength, update, probe, one, two, weight,
    mine, his, fold_far, fold_mid, fold_own,
    stack, total,
):
    modes = probe.shape[0]
    count = rest.shape[0]
    odd = lax.rem(lax.axis_index("row"), 2)
    spots = slab_spots()
    for part in range(2):
        total[part] = update[part] - weight[...] * window[part]
    for n in range(count):
        m = modes - count + n
        u_re, u_im, t_re, t_im = backward(
            rest[n], strength[...], probe[m, 0], probe[m, 1], window[0], window[1], one, two
        )
        total[0] = total[0] + u_re
        total[1] = total[1] + u_im
        put(spots, mine, his, 2 * n, t_re)
        put(spots, mine, his, 2 * n + 1, t_im)
    for part in range(2):
        tall = jnp.concatenate([total[part], jnp.zeros((128, 256), jnp.float32)], axis=0)
        stack[part] = pltpu.roll(tall, twin[0, 0], 0)
    fold_far[...] = stack[:, pl.ds(pl.multiple_of(256 * (1 - odd), 128), 128), :]
    fold_mid[...] = stack[:, 128:256, :]
    fold_own[...] = stack[:, pl.ds(pl.multiple_of(256 * odd, 128), 128), :]


def position_rest(twin, window, rest, strength, update, probe, one, two, weight):
    images = 2 * rest.shape[0]
    return pl.pallas_call(
        position_rest_kernel,
        out_shape=(f32(8, images, 16, 256),) * 2 + (f32(2, 128, 256),) * 3,
        in_specs=[SMEM] + [VMEM] * 8,
        out_specs=(VMEM,) * 5,
        scratch_shapes=[
            pltpu.VMEM((2, 384, 256), jnp.float32),
            pltpu.VMEM((2, 256, 256), jnp.float32),
        ],
        compiler_params=params(8),
        name="position_rest",
    )(twin, window, rest, strength, update, probe, one, two, weight)


def fold_kernel(here, twin, beyond, near, middle, far, inner, edge, grid):
    grid[...] = jnp.zeros(grid.shape, jnp.float32)
    for col, piece in ((twin[0, 1], near), (here[0, 1], middle), (beyond[0, 1], far)):
        base = pl.multiple_of(col // 128 * 128, 128)
        for part in range(2):
            wide = jnp.concatenate([piece[part], jnp.zeros((128, 128), jnp.float32)], axis=1)
            grid[part, :, pl.ds(base, 384)] += pltpu.roll(wide, col % 128, 1)
    size = grid.shape[2]
    inner[...] = grid[:, :, 128 : size - 128]
    edge[...] = jnp.where(lax.axis_index("col") == 0, grid[:, :, size - 128 :], grid[:, :, 0:128])


def fold(here, twin, beyond, near, middle, far, rows, cols):
    return pl.pallas_call(
        fold_kernel,
        out_shape=(f32(2, rows, cols), f32(2, rows, 128)),
        in_specs=[SMEM] * 3 + [VMEM] * 3,
        out_specs=(VMEM, VMEM),
        scratch_shapes=[pltpu.VMEM((2, rows, cols + 256), jnp.float32)],
        compiler_params=params(8),
        name="fold_object",
    )(here, twin, beyond, near, middle, far)


def leg_kernel(spot, mine, theirs, *refs):
    came, out = refs[:-1], refs[-1]
    total = mine[spot] + theirs[spot]
    out[...] = total + came[0][...] if came else total


def add_leg(came, mine, theirs, spot):
    came = () if came is None else (came,)
    return pl.pallas_call(
        functools.partial(leg_kernel, spot),
        out_shape=f32(*mine.shape[1:]),
        in_specs=[VMEM] * (2 + len(came)),
        out_specs=VMEM,
        compiler_params=params(2),
        name="add_leg",
    )(mine, theirs, *came)


def close_kernel(
    ahead_low, ahead_high, behind_low, behind_high, mine_low, mine_high, theirs_low, theirs_high,
    den_in, edge, low, high, den,
):
    den[...] = den_in[...]
    cols = den.shape[1]
    side = pl.multiple_of((1 - lax.axis_index("col")) * (cols - 128), 128)
    den[:, pl.ds(side, 128)] += edge[...]
    object_peak = jnp.max(den[...])
    last = mine_low.shape[0] - 1
    for out, ahead, behind, mine, theirs in (
        (low, ahead_low, behind_low, mine_low, theirs_low),
        (high, ahead_high, behind_high, mine_high, theirs_high),
    ):
        for n in range(ahead.shape[0]):
            out[16 * n : 16 * n + 16] = (mine[last, n] + theirs[last, n]) + (ahead[n] + behind[n])
    high[16 * ahead_high.shape[0] :] = jnp.full((8, 256), object_peak, jnp.float32)


def close(ahead, behind, mine, theirs, den, edge):
    return pl.pallas_call(
        close_kernel,
        out_shape=(f32(16 * mine[0].shape[1], 256), f32(16 * mine[1].shape[1] + 8, 256)),
        in_specs=[VMEM] * 10,
        out_specs=(VMEM, VMEM),
        scratch_shapes=[pltpu.VMEM(den.shape, jnp.float32)],
        compiler_params=params(2),
        name="close_sum",
    )(*ahead, *behind, *mine, *theirs, den, edge)


def pack_kernel(edge, *refs):
    parts, out = refs[:-1], refs[-1]
    at = 0
    for part in parts:
        out[at : at + part.shape[0]] = part[...]
        at += part.shape[0]
    for part in range(2):
        out[at:, 128 * part : 128 * part + 128] = edge[part]


def pack(edge, parts):
    size = sum(x.shape[0] for x in parts) + edge.shape[1]
    return pl.pallas_call(
        pack_kernel,
        out_shape=f32(size, 256),
        in_specs=[VMEM] * (1 + len(parts)),
        out_specs=VMEM,
        compiler_params=params(4),
        name="pack",
    )(edge, *parts)


def finish_kernel(probe, block, inner, den, den_edge, packed, packed_last, *refs):
    hops = len(HOPS)
    parts, refs = refs[: 2 * hops], refs[2 * hops :]
    new_block_at, new_probe_at, new_probe, new_block, whole_den, scales, sems = refs
    cut, rest = parts[0].shape[0], parts[1].shape[0]
    size = cut + rest
    lows, highs = list(parts[0::2]), list(parts[1::2])
    for n in range(hops - 1):
        lows.append(packed.at[size * n : size * n + cut])
        highs.append(packed.at[size * n + cut : size * n + size])
    lows.append(packed_last.at[0:cut])
    highs.append(packed_last.at[cut:size])
    edge = packed.at[size * (hops - 1) :]
    modes = probe.shape[0]
    core = lax.axis_index("col")
    place = ring_place(lax.axis_index("row"))
    cols = block.shape[2]
    peak = jnp.zeros((8, 256), jnp.float32)
    object_peak = jnp.zeros((8, 256), jnp.float32)
    for low, high in zip(lows, highs):
        peak = jnp.maximum(peak, jnp.maximum(low[0:8], low[8:16]))
        object_peak = jnp.maximum(object_peak, high[rest - 8 : rest])
    peak = jnp.max(peak)
    object_peak = jnp.max(object_peak)
    side = pl.multiple_of((1 - core) * (cols - 128), 128)
    new_block[...] = inner[...]
    for part in range(2):
        new_block[part, :, pl.ds(side, 128)] += edge[:, 128 * part : 128 * part + 128]
    whole_den[...] = den[...]
    whole_den[:, pl.ds(side, 128)] += den_edge[...]
    scale = 1.0 / ((1.0 - REGULAR) * whole_den[...] + REGULAR * object_peak)
    for part in range(2):
        new_block[part] = block[part] + new_block[part] * scale
    outs = begin((pltpu.make_async_copy(new_block, new_block_at, sems.at[modes]),))
    starts = []
    for n, low in enumerate(lows):
        half = core if n < hops else 1 - core
        starts.append(pl.multiple_of(128 * half + 16 * ((place + HOPS[n % hops]) & 7), 16))
        scales[n] = 1.0 / ((1.0 - REGULAR) * low[0:16] + REGULAR * peak)
    for m in range(modes):
        for part in range(2):
            at = 16 * (1 + 2 * m + part)
            for n in range(2 * hops):
                value = lows[n][at : at + 16] if at < cut else highs[n][at - cut : at - cut + 16]
                rows = pl.ds(starts[n], 16)
                new_probe[m, part, rows, :] = probe[m, part, rows, :] + value * scales[n]
        outs += begin((pltpu.make_async_copy(new_probe.at[m], new_probe_at.at[m], sems.at[m]),))
    end(outs)


def finish(probe, block, inner, den, den_edge, packed, packed_last, parts):
    modes = probe.shape[0]
    return pl.pallas_call(
        finish_kernel,
        out_shape=(f32(*block.shape), f32(*probe.shape)),
        in_specs=[VMEM] * (7 + len(parts)),
        out_specs=(ANY, ANY),
        scratch_shapes=[pltpu.VMEM(x.shape, jnp.float32) for x in (probe, block, den)]
        + [
            pltpu.VMEM((2 * len(HOPS), 16, 256), jnp.float32),
            pltpu.SemaphoreType.DMA((modes + 1,)),
        ],
        compiler_params=params(12),
        name="finish",
    )(probe, block, inner, den, den_edge, packed, packed_last, *parts)


def shards(object_field, probe, measured, offsets):
    rows, cols = object_field.shape[1], object_field.shape[2]
    count = lax.axis_size("row")
    one, two = transform_blocks(probe.shape[-1])
    one, two = jnp.asarray(one), jnp.asarray(two)

    twins = [(i, i ^ 1) for i in range(count)]
    cores = [(0, 1), (1, 0)]
    others = [(i + 1 if i % 2 else i - 1, i) for i in range(1, count - 1)]
    outward = [(i, i + 2) for i in range(1, count - 2, 2)] + [(i, i - 2) for i in range(2, count, 2)]
    inward = [(b, a) for a, b in outward]
    forward = [
        (block + RING_ORDER[i], block + RING_ORDER[(i + 1) % RING])
        for block in range(0, count, RING)
        for i in range(RING)
    ]
    reverse = [(b, a) for a, b in forward]

    def across(x):
        return lax.ppermute(x, "col", cores)

    def send(x, pairs):
        return lax.ppermute(x, "row", pairs)

    def after(x, y):
        return lax.optimization_barrier((x, y))[0]

    twin = send(offsets, twins)
    beyond = send(offsets, others)
    twin, beyond = lax.optimization_barrier((twin, beyond))
    other = across(after(object_field, twin))
    pattern = send(after(measured, twin), twins)

    to_beyond, to_twin, own_rows = cut_slices(
        ("beyond", "here", "twin"), offsets, twin, beyond, object_field, other
    )
    far_rows = send(to_beyond, outward)
    mid_rows = send(to_twin, twins)
    power = probe_power(after(after(probe, own_rows), pattern))
    object_den, den_edge = weights(count, offsets, twin, beyond, power, rows, cols)
    den_edge = across(den_edge)

    mine_low, his_low, window, rest, strength, update = position(
        twin, far_rows, after(mid_rows, den_edge), own_rows, probe, pattern[0], one, two
    )
    theirs_low = across(his_low)
    mine_high, his_high, fold_far, fold_mid, fold_own = position_rest(
        twin, window, rest, strength, update, probe, one, two, power
    )
    theirs_high = across(his_high)
    mid_got = send(fold_mid, twins)
    far_got = send(fold_far, inward)

    start_ahead = add_leg(None, mine_low, theirs_low, 0)
    start_behind = add_leg(None, mine_low, theirs_low, 2)
    theirs_high = after(theirs_high, start_behind)
    mine, theirs = (mine_low, mine_high), (theirs_low, theirs_high)

    def legs(part, came, spots, pairs):
        for spot in spots:
            came = send(add_leg(came, mine[part], theirs[part], spot), pairs)
        return came

    ahead = [legs(0, send(start_ahead, forward), (1, 3, 5), forward), legs(1, None, (1, 3, 5), forward)]
    behind = [legs(0, send(start_behind, reverse), (4, 6), reverse), legs(1, None, (0, 2, 4, 6), reverse)]
    message = close(ahead, behind, mine, theirs, object_den, den_edge)
    if count > RING:
        blocks = [[b * RING + i for b in range(count // RING)] for i in range(RING)]
        low = lax.psum(message[0], "row", axis_index_groups=blocks)
        high = lax.psum(message[1][:-8], "row", axis_index_groups=blocks)
        top = lax.pmax(message[1][-8:], "row", axis_index_groups=blocks)
        message = (low, jnp.concatenate([high, top], axis=0))

    parts = list(message)
    ahead = [send(x, forward) for x in message]
    behind = [send(x, reverse) for x in message]
    parts += ahead + behind
    ahead[0], mid_got, far_got = lax.optimization_barrier((ahead[0], mid_got, far_got))
    inner, edge = fold(offsets, twin, beyond, fold_own, mid_got, far_got, rows, cols)
    for hop in range(2):
        ahead = [send(x, forward) for x in ahead]
        behind = [send(x, reverse) for x in behind]
        parts += ahead + behind
    last = [send(ahead[0], forward), send(behind[1], reverse)]
    packed = across(pack(edge, parts))
    packed_last = across(jnp.concatenate(last, axis=0))
    return finish(probe, object_field, inner, object_den, den_edge, packed, packed_last, parts + last)


def solution(mesh):
    placed = (
        P(None, ("groups", "row"), "col"),
        P("groups", None, None, None),
        P(("groups", "row", "col"), None, None),
        P(("groups", "row", "col"), None),
    )
    return jax.shard_map(
        shards,
        mesh=mesh,
        in_specs=placed,
        out_specs=(P(None, ("groups", "row"), "col"), P("groups", None, None, None)),
        check_vma=False,
    )
```

```python
import functools
import math

import jax
import jax.numpy as jnp
import ml_dtypes
import numpy as np
from jax import lax
from jax.experimental import pallas as pl
from jax.experimental.pallas import tpu as pltpu
from jax.sharding import PartitionSpec as P

REGULAR = 0.25
AMP_FLOOR = 2.0
RING = 8
RING_ORDER = (0, 1, 3, 5, 7, 6, 4, 2)
HOPS = (0, -1, 1, -2, 2, -3, 3, 4)

SMEM = pl.BlockSpec(memory_space=pltpu.SMEM)
VMEM = pl.BlockSpec(memory_space=pltpu.VMEM)
ANY = pl.BlockSpec(memory_space=pl.ANY)
HBM = pl.BlockSpec(memory_space=pltpu.HBM)


def transform_blocks(length):
    indices = np.arange(length, dtype=np.int32)
    phases = indices[:, None] * indices[None, :] % length
    angles = phases.astype(np.float32) * np.float32(2.0 * math.pi / length)
    factor = np.float32(1.0 / math.sqrt(length))
    cos = (np.cos(angles) * factor).astype(ml_dtypes.bfloat16)
    sin = (-np.sin(angles) * factor).astype(ml_dtypes.bfloat16)
    one = np.block([[cos, -sin], [sin, cos]])
    return one, np.ascontiguousarray(one.T)


def ring_place(r):
    r = lax.rem(r, RING)
    return jnp.where(r == 0, 0, jnp.where(lax.rem(r, 2) == 1, (r + 1) // 2, RING - r // 2))


def params(mib):
    return pltpu.CompilerParams(vmem_limit_bytes=mib * 1024 * 1024)


def f32(*shape):
    return jax.ShapeDtypeStruct(shape, jnp.float32)


def begin(copies):
    for copy in copies:
        copy.start()
    return copies


def end(copies):
    for copy in copies:
        copy.wait()


def slices_kernel(offsets_at, *refs):
    offsets_in, (block, other, _), outs, (ext, cuts, offsets, sems) = refs[:3], refs[3:6], refs[6:-4], refs[-4:]
    core = lax.axis_index("col")
    cols = block.shape[2]
    end_of = cols + 128
    source = pl.multiple_of(core * (cols - 128), 128)
    target = pl.multiple_of((1 - core) * end_of, 128)
    blank = pl.multiple_of(core * end_of, 128)
    copies = begin(
        (
            pltpu.make_async_copy(block, ext.at[:, :, 128:end_of], sems.at[0]),
            pltpu.make_async_copy(
                other.at[:, :, pl.ds(source, 128)], ext.at[:, :, pl.ds(target, 128)], sems.at[1]
            ),
        )
        + tuple(
            pltpu.make_async_copy(spot, offsets.at[n], sems.at[4 + n]) for n, spot in enumerate(offsets_in)
        )
    )
    ext[:, :, pl.ds(blank, 128)] = jnp.zeros((2, block.shape[1], 128), jnp.float32)
    end(copies)
    columns = {"here": offsets[0, 0, 1], "twin": offsets[1, 0, 1], "beyond": offsets[2, 0, 1]}
    copies = ()
    for number, (which, out) in enumerate(zip(offsets_at, outs)):
        start = columns[which]
        base = pl.multiple_of(start // 128 * 128, 128)
        for part in range(2):
            wide = ext[part, :, pl.ds(base, 384)]
            wide = pltpu.roll(wide, (384 - start % 128) % 384, 1)
            cuts[number, part] = wide[:, 0:256]
        copies += begin((pltpu.make_async_copy(cuts.at[number], out, sems.at[2 + number]),))
    end(copies)


def cut_slices(offsets_at, here, twin, beyond, block, other, ordered):
    rows, cols = block.shape[1], block.shape[2]
    count = len(offsets_at)
    return pl.pallas_call(
        functools.partial(slices_kernel, offsets_at),
        out_shape=(f32(2, rows, 256),) * count,
        in_specs=[ANY] * 3 + [HBM] + [ANY] * 2,
        out_specs=(ANY,) * count,
        scratch_shapes=[
            pltpu.VMEM((2, rows, cols + 256), jnp.float32),
            pltpu.VMEM((count, 2, rows, 256), jnp.float32),
            pltpu.SMEM((3, 1, 2), jnp.int32),
            pltpu.SemaphoreType.DMA((7,)),
        ],
        compiler_params=params(6),
        name="cut_slices",
    )(here, twin, beyond, block, other, ordered)


def power_kernel(probe, out, held, sems):
    modes = probe.shape[0]
    copies = begin([pltpu.make_async_copy(probe.at[m], held.at[m], sems.at[m]) for m in range(modes)])
    for m in range(modes):
        copies[m].wait()
        power = held[m, 0] * held[m, 0] + held[m, 1] * held[m, 1]
        out[...] = power if m == 0 else out[...] + power


def probe_power(probe):
    return pl.pallas_call(
        power_kernel,
        out_shape=f32(*probe.shape[2:]),
        in_specs=[ANY],
        out_specs=VMEM,
        scratch_shapes=[pltpu.VMEM(probe.shape, jnp.float32), pltpu.SemaphoreType.DMA((probe.shape[0],))],
        compiler_params=params(8),
        name="probe_power",
    )(probe)


def weights_kernel(count, here, twin, beyond, power, inner, edge, frame, grid):
    r = lax.axis_index("row")
    odd = lax.rem(r, 2)
    present = jnp.logical_and(r > 0, r < count - 1).astype(jnp.float32)
    tall = jnp.concatenate([power[...], jnp.zeros((128, 256), jnp.float32)], axis=0)
    grid[...] = jnp.zeros(grid.shape, jnp.float32)
    lowers = (128, 256 * odd, 256 * (1 - odd))
    for number, spot in enumerate((here, twin, beyond)):
        row, col = spot[0, 0], spot[0, 1]
        frame[...] = pltpu.roll(tall, row, 0)
        piece = frame[pl.ds(pl.multiple_of(lowers[number], 128), 128), :]
        if number == 2:
            piece = piece * present
        wide = jnp.concatenate([piece, jnp.zeros((128, 128), jnp.float32)], axis=1)
        base = pl.multiple_of(col // 128 * 128, 128)
        grid[:, pl.ds(base, 384)] += pltpu.roll(wide, col % 128, 1)
    size = grid.shape[1]
    inner[...] = grid[:, 128 : size - 128]
    edge[...] = jnp.where(lax.axis_index("col") == 0, grid[:, size - 128 :], grid[:, 0:128])


def weights(count, here, twin, beyond, power, rows, cols):
    return pl.pallas_call(
        functools.partial(weights_kernel, count),
        out_shape=(f32(rows, cols), f32(rows, 128)),
        in_specs=[SMEM] * 3 + [VMEM],
        out_specs=(VMEM, VMEM),
        scratch_shapes=[
            pltpu.VMEM((384, 256), jnp.float32),
            pltpu.VMEM((rows, cols + 256), jnp.float32),
        ],
        compiler_params=params(6),
        name="object_weights",
    )(here, twin, beyond, power)


def slab_spots():
    place = ring_place(lax.axis_index("row"))
    spots = []
    for slab in range(8):
        ahead = (slab - place) & 7
        spots.append(jnp.where(ahead < 4, 7 - 2 * ahead, 2 * (ahead - 4)))
    return spots


def put(spots, mine, his, image, value):
    first = lax.axis_index("col") == 0
    low, high = value[0:128], value[128:256]
    own, other = jnp.where(first, low, high), jnp.where(first, high, low)
    for slab in range(8):
        mine[spots[slab], image] = own[16 * slab : 16 * slab + 16]
        his[spots[slab], image] = other[16 * slab : 16 * slab + 16]


def backward(far, ratio, p_re, p_im, w_re, w_im, one, two):
    fixed = jnp.concatenate(
        [(far[:, 0:256] * ratio).astype(jnp.bfloat16), (far[:, 256:512] * ratio).astype(jnp.bfloat16)],
        axis=0,
    )
    back = jnp.dot(two[...], fixed, preferred_element_type=jnp.float32).astype(jnp.bfloat16)
    back = jnp.concatenate([back[0:256], back[256:512]], axis=1)
    near = jnp.dot(back, one[...], preferred_element_type=jnp.float32)
    n_re, n_im = near[:, 0:256], near[:, 256:512]
    density = w_re * w_re + w_im * w_im
    return (
        p_re * n_re + p_im * n_im,
        p_re * n_im - p_im * n_re,
        w_re * n_re + w_im * n_im - density * p_re,
        w_re * n_im - w_im * n_re - density * p_im,
    )


def position_kernel(
    twin, far_rows, mid_rows, own_rows, probe, pattern, one, two,
    mine, his, window, rest, strength, update,
    stack, far,
):
    modes = probe.shape[0]
    cut = modes // 2
    odd = lax.rem(lax.axis_index("row"), 2)
    row = twin[0, 0]
    stack[:, pl.ds(pl.multiple_of(256 * (1 - odd), 128), 128), :] = far_rows[...]
    stack[:, 128:256, :] = mid_rows[...]
    stack[:, pl.ds(pl.multiple_of(256 * odd, 128), 128), :] = own_rows[...]
    for part in range(2):
        window[part] = pltpu.roll(stack[part], (384 - row) % 384, 0)[0:256]

    for m in range(modes):
        p_re, p_im = probe[m, 0], probe[m, 1]
        w_re, w_im = window[0], window[1]
        e_re, e_im = p_re * w_re - p_im * w_im, p_re * w_im + p_im * w_re
        field = jnp.concatenate([e_re.astype(jnp.bfloat16), e_im.astype(jnp.bfloat16)], axis=0)
        half = jnp.dot(one[...], field, preferred_element_type=jnp.float32).astype(jnp.bfloat16)
        half = jnp.concatenate([half[0:256], half[256:512]], axis=1)
        out = jnp.dot(half, two[...], preferred_element_type=jnp.float32)
        if m < cut:
            far[m] = out
        else:
            rest[m - cut] = out
        power = out[:, 0:256] * out[:, 0:256] + out[:, 256:512] * out[:, 256:512]
        strength[...] = power if m == 0 else strength[...] + power

    strength[...] = jnp.sqrt(pattern[...]) / jnp.maximum(jnp.sqrt(strength[...]), AMP_FLOOR)

    spots = slab_spots()
    put(spots, mine, his, 0, window[0] * window[0] + window[1] * window[1])
    for m in range(cut):
        u_re, u_im, t_re, t_im = backward(
            far[m], strength[...], probe[m, 0], probe[m, 1], window[0], window[1], one, two
        )
        update[0] = u_re if m == 0 else update[0] + u_re
        update[1] = u_im if m == 0 else update[1] + u_im
        put(spots, mine, his, 1 + 2 * m, t_re)
        put(spots, mine, his, 2 + 2 * m, t_im)


def position(twin, far_rows, mid_rows, own_rows, probe, pattern, one, two):
    modes = probe.shape[0]
    cut = modes // 2
    return pl.pallas_call(
        position_kernel,
        out_shape=(f32(8, 1 + 2 * cut, 16, 256),) * 2
        + (f32(2, 256, 256), f32(modes - cut, 256, 512), f32(256, 256), f32(2, 256, 256)),
        in_specs=[SMEM] + [VMEM] * 7,
        out_specs=(VMEM,) * 6,
        scratch_shapes=[
            pltpu.VMEM((2, 384, 256), jnp.float32),
            pltpu.VMEM((cut, 256, 512), jnp.float32),
        ],
        compiler_params=params(10),
        name="position_terms",
    )(twin, far_rows, mid_rows, own_rows, probe, pattern, one, two)


def position_rest_kernel(
    twin, window, rest, strength, update, probe, one, two, weight,
    mine, his, his_first, fold_far, fold_mid, fold_own,
    stack, total,
):
    modes = probe.shape[0]
    count = rest.shape[0]
    odd = lax.rem(lax.axis_index("row"), 2)
    spots = slab_spots()
    for part in range(2):
        total[part] = update[part] - weight[...] * window[part]
    for n in range(count):
        m = modes - count + n
        u_re, u_im, t_re, t_im = backward(
            rest[n], strength[...], probe[m, 0], probe[m, 1], window[0], window[1], one, two
        )
        total[0] = total[0] + u_re
        total[1] = total[1] + u_im
        put(spots, mine, his, 2 * n, t_re)
        put(spots, mine, his, 2 * n + 1, t_im)
    his_first[0] = his[0]
    for part in range(2):
        tall = jnp.concatenate([total[part], jnp.zeros((128, 256), jnp.float32)], axis=0)
        stack[part] = pltpu.roll(tall, twin[0, 0], 0)
    fold_far[...] = stack[:, pl.ds(pl.multiple_of(256 * (1 - odd), 128), 128), :]
    fold_mid[...] = stack[:, 128:256, :]
    fold_own[...] = stack[:, pl.ds(pl.multiple_of(256 * odd, 128), 128), :]


def position_rest(twin, window, rest, strength, update, probe, one, two, weight):
    images = 2 * rest.shape[0]
    return pl.pallas_call(
        position_rest_kernel,
        out_shape=(f32(8, images, 16, 256),) * 2 + (f32(1, images, 16, 256),) + (f32(2, 128, 256),) * 3,
        in_specs=[SMEM] + [VMEM] * 8,
        out_specs=(VMEM,) * 6,
        scratch_shapes=[
            pltpu.VMEM((2, 384, 256), jnp.float32),
            pltpu.VMEM((2, 256, 256), jnp.float32),
        ],
        compiler_params=params(8),
        name="position_rest",
    )(twin, window, rest, strength, update, probe, one, two, weight)


def fold_kernel(here, twin, beyond, near, middle, far, inner, edge, grid):
    grid[...] = jnp.zeros(grid.shape, jnp.float32)
    for col, piece in ((twin[0, 1], near), (here[0, 1], middle), (beyond[0, 1], far)):
        base = pl.multiple_of(col // 128 * 128, 128)
        for part in range(2):
            wide = jnp.concatenate([piece[part], jnp.zeros((128, 128), jnp.float32)], axis=1)
            grid[part, :, pl.ds(base, 384)] += pltpu.roll(wide, col % 128, 1)
    size = grid.shape[2]
    inner[...] = grid[:, :, 128 : size - 128]
    edge[...] = jnp.where(lax.axis_index("col") == 0, grid[:, :, size - 128 :], grid[:, :, 0:128])


def fold(here, twin, beyond, near, middle, far, rows, cols):
    return pl.pallas_call(
        fold_kernel,
        out_shape=(f32(2, rows, cols), f32(2, rows, 128)),
        in_specs=[SMEM] * 3 + [VMEM] * 3,
        out_specs=(VMEM, VMEM),
        scratch_shapes=[pltpu.VMEM((2, rows, cols + 256), jnp.float32)],
        compiler_params=params(8),
        name="fold_object",
    )(here, twin, beyond, near, middle, far)


def leg_kernel(spot, mine, theirs, *refs):
    came, out = refs[:-1], refs[-1]
    total = mine[spot] + theirs[spot]
    out[...] = total + came[0][...] if came else total


def add_leg(came, mine, theirs, spot):
    came = () if came is None else (came,)
    return pl.pallas_call(
        functools.partial(leg_kernel, spot),
        out_shape=f32(*mine.shape[1:]),
        in_specs=[VMEM] * (2 + len(came)),
        out_specs=VMEM,
        compiler_params=params(2),
        name="add_leg",
    )(mine, theirs, *came)


def close_kernel(
    ahead_low, ahead_high, behind_low, behind_high, mine_low, mine_high, theirs_low, theirs_high,
    den_in, edge, low, high, den,
):
    den[...] = den_in[...]
    cols = den.shape[1]
    side = pl.multiple_of((1 - lax.axis_index("col")) * (cols - 128), 128)
    den[:, pl.ds(side, 128)] += edge[...]
    object_peak = jnp.max(den[...])
    last = mine_low.shape[0] - 1
    for out, ahead, behind, mine, theirs in (
        (low, ahead_low, behind_low, mine_low, theirs_low),
        (high, ahead_high, behind_high, mine_high, theirs_high),
    ):
        for n in range(ahead.shape[0]):
            out[16 * n : 16 * n + 16] = (mine[last, n] + theirs[last, n]) + (ahead[n] + behind[n])
    high[16 * ahead_high.shape[0] :] = jnp.full((8, 256), object_peak, jnp.float32)


def close(ahead, behind, mine, theirs, den, edge):
    return pl.pallas_call(
        close_kernel,
        out_shape=(f32(16 * mine[0].shape[1], 256), f32(16 * mine[1].shape[1] + 8, 256)),
        in_specs=[VMEM] * 10,
        out_specs=(VMEM, VMEM),
        scratch_shapes=[pltpu.VMEM(den.shape, jnp.float32)],
        compiler_params=params(2),
        name="close_sum",
    )(*ahead, *behind, *mine, *theirs, den, edge)


def pack_kernel(edge, *refs):
    parts, out = refs[:-1], refs[-1]
    at = 0
    for part in parts:
        out[at : at + part.shape[0]] = part[...]
        at += part.shape[0]
    for part in range(2):
        out[at:, 128 * part : 128 * part + 128] = edge[part]


def pack(edge, parts):
    size = sum(x.shape[0] for x in parts) + edge.shape[1]
    return pl.pallas_call(
        pack_kernel,
        out_shape=f32(size, 256),
        in_specs=[VMEM] * (1 + len(parts)),
        out_specs=VMEM,
        compiler_params=params(4),
        name="pack",
    )(edge, *parts)


def finish_kernel(probe, block, inner, den, den_edge, packed, last_low, last_high, *refs):
    hops = len(HOPS)
    parts, refs = refs[: 2 * hops], refs[2 * hops :]
    new_block_at, new_probe_at, new_probe, new_block, whole_den, scales, sems = refs
    cut, rest = parts[0].shape[0], parts[1].shape[0]
    size = cut + rest
    lows, highs = list(parts[0::2]), list(parts[1::2])
    for n in range(hops - 1):
        lows.append(packed.at[size * n : size * n + cut])
        highs.append(packed.at[size * n + cut : size * n + size])
    lows.append(last_low)
    highs.append(last_high)
    edge = packed.at[size * (hops - 1) :]
    modes = probe.shape[0]
    core = lax.axis_index("col")
    place = ring_place(lax.axis_index("row"))
    cols = block.shape[2]
    peak = jnp.zeros((8, 256), jnp.float32)
    object_peak = jnp.zeros((8, 256), jnp.float32)
    for low, high in zip(lows, highs):
        peak = jnp.maximum(peak, jnp.maximum(low[0:8], low[8:16]))
        object_peak = jnp.maximum(object_peak, high[rest - 8 : rest])
    peak = jnp.max(peak)
    object_peak = jnp.max(object_peak)
    side = pl.multiple_of((1 - core) * (cols - 128), 128)
    new_block[...] = inner[...]
    for part in range(2):
        new_block[part, :, pl.ds(side, 128)] += edge[:, 128 * part : 128 * part + 128]
    whole_den[...] = den[...]
    whole_den[:, pl.ds(side, 128)] += den_edge[...]
    scale = 1.0 / ((1.0 - REGULAR) * whole_den[...] + REGULAR * object_peak)
    for part in range(2):
        new_block[part] = block[part] + new_block[part] * scale
    outs = begin((pltpu.make_async_copy(new_block, new_block_at, sems.at[modes]),))
    starts = []
    for n, low in enumerate(lows):
        half = core if n < hops else 1 - core
        starts.append(pl.multiple_of(128 * half + 16 * ((place + HOPS[n % hops]) & 7), 16))
        scales[n] = 1.0 / ((1.0 - REGULAR) * low[0:16] + REGULAR * peak)
    for m in range(modes):
        for part in range(2):
            at = 16 * (1 + 2 * m + part)
            for n in range(2 * hops):
                value = lows[n][at : at + 16] if at < cut else highs[n][at - cut : at - cut + 16]
                rows = pl.ds(starts[n], 16)
                new_probe[m, part, rows, :] = probe[m, part, rows, :] + value * scales[n]
        outs += begin((pltpu.make_async_copy(new_probe.at[m], new_probe_at.at[m], sems.at[m]),))
    end(outs)


def finish(probe, block, inner, den, den_edge, packed, last_low, last_high, parts):
    modes = probe.shape[0]
    return pl.pallas_call(
        finish_kernel,
        out_shape=(f32(*block.shape), f32(*probe.shape)),
        in_specs=[VMEM] * (8 + len(parts)),
        out_specs=(ANY, ANY),
        scratch_shapes=[pltpu.VMEM(x.shape, jnp.float32) for x in (probe, block, den)]
        + [
            pltpu.VMEM((2 * len(HOPS), 16, 256), jnp.float32),
            pltpu.SemaphoreType.DMA((modes + 1,)),
        ],
        compiler_params=params(12),
        name="finish",
    )(probe, block, inner, den, den_edge, packed, last_low, last_high, *parts)


def shards(object_field, probe, measured, offsets):
    rows, cols = object_field.shape[1], object_field.shape[2]
    count = lax.axis_size("row")
    one, two = transform_blocks(probe.shape[-1])
    one, two = jnp.asarray(one), jnp.asarray(two)

    twins = [(i, i ^ 1) for i in range(count)]
    cores = [(0, 1), (1, 0)]
    others = [(i + 1 if i % 2 else i - 1, i) for i in range(1, count - 1)]
    outward = [(i, i + 2) for i in range(1, count - 2, 2)] + [(i, i - 2) for i in range(2, count, 2)]
    inward = [(b, a) for a, b in outward]
    forward = [
        (block + RING_ORDER[i], block + RING_ORDER[(i + 1) % RING])
        for block in range(0, count, RING)
        for i in range(RING)
    ]
    reverse = [(b, a) for a, b in forward]

    def across(x):
        return lax.ppermute(x, "col", cores)

    def send(x, pairs):
        return lax.ppermute(x, "row", pairs)

    def after(x, y):
        return lax.optimization_barrier((x, y))[0]

    other = across(object_field)
    twin = send(offsets, twins)
    beyond = send(offsets, others)
    pattern = send(measured, twins)

    (to_twin,) = cut_slices(("here",), offsets, offsets, offsets, object_field, other, offsets)
    mid_rows = send(to_twin, twins)
    to_beyond, own_rows = cut_slices(
        ("beyond", "twin"), offsets, twin, beyond, object_field, other, to_twin
    )
    far_rows = send(to_beyond, outward)
    power = probe_power(after(probe, own_rows))
    object_den, den_edge = weights(count, offsets, twin, beyond, power, rows, cols)
    den_edge = across(den_edge)

    mine_low, his_low, window, rest, strength, update = position(
        twin, far_rows, after(mid_rows, den_edge), own_rows, probe, pattern[0], one, two
    )
    theirs_low = across(his_low)
    mine_high, his_high, his_first, fold_far, fold_mid, fold_own = position_rest(
        twin, window, rest, strength, update, probe, one, two, power
    )
    first_high = across(his_first)
    mid_got = send(fold_mid, twins)
    far_got = send(fold_far, inward)

    start_ahead = add_leg(None, mine_low, theirs_low, 0)
    start_behind = add_leg(None, mine_low, theirs_low, 2)
    first_high = after(after(first_high, start_ahead), start_behind)
    theirs_high = across(after(his_high, first_high))
    start_high = add_leg(None, mine_high, first_high, 0)
    mine, theirs = (mine_low, mine_high), (theirs_low, theirs_high)

    def legs(part, came, spots, pairs):
        for spot in spots:
            came = send(add_leg(came, mine[part], theirs[part], spot), pairs)
        return came

    ahead = [legs(0, send(start_ahead, forward), (1, 3, 5), forward), legs(1, None, (1, 3, 5), forward)]
    behind = [legs(0, send(start_behind, reverse), (4, 6), reverse), legs(1, send(start_high, reverse), (2, 4, 6), reverse)]
    message = close(ahead, behind, mine, theirs, object_den, den_edge)
    if count > RING:
        blocks = [[b * RING + i for b in range(count // RING)] for i in range(RING)]
        low = lax.psum(message[0], "row", axis_index_groups=blocks)
        high = lax.psum(message[1][:-8], "row", axis_index_groups=blocks)
        top = lax.pmax(message[1][-8:], "row", axis_index_groups=blocks)
        message = (low, jnp.concatenate([high, top], axis=0))

    parts = list(message)
    ahead = [send(x, forward) for x in message]
    behind = [send(x, reverse) for x in message]
    parts += ahead + behind
    ahead[0], mid_got, far_got = lax.optimization_barrier((ahead[0], mid_got, far_got))
    inner, edge = fold(offsets, twin, beyond, fold_own, mid_got, far_got, rows, cols)
    for hop in range(2):
        ahead = [send(x, forward) for x in ahead]
        behind = [send(x, reverse) for x in behind]
        parts += ahead + behind
    last = [send(ahead[0], forward), send(behind[1], reverse)]
    packed = across(pack(edge, parts))
    crossed = [across(x) for x in last]
    return finish(probe, object_field, inner, object_den, den_edge, packed, *crossed, parts + last)


def solution(mesh):
    placed = (
        P(None, ("groups", "row"), "col"),
        P("groups", None, None, None),
        P(("groups", "row", "col"), None, None),
        P(("groups", "row", "col"), None),
    )
    return jax.shard_map(
        shards,
        mesh=mesh,
        in_specs=placed,
        out_specs=(P(None, ("groups", "row"), "col"), P("groups", None, None, None)),
        check_vma=False,
    )
```
